32 devices in a mesh: group: 2 (over x), loop: 16 (over z, y, core).
Axes of the slice: x: 2, y: 2, z: 4, core: 2. Of those that a mesh axis runs over, the one named last changes fastest.
Arguments:
- users: float32 [8192, 512], P(('group', 'loop')), parts along dimension 0, may hold values from -1.3 to 1.3
- items: bfloat16 [4096, 512], P(('group', 'loop')), parts along dimension 0, may hold values from -1.296875 to 1.296875
- tile_blocks: int32 [32, 8], P(('group', 'loop')), parts along dimension 0, may hold values from 0 to 15, as said below
- tile_count: int32 [32], P(('group', 'loop')), parts along dimension 0, may hold values from 1 to 8, as said below
- labels: int32 [8192, 1024], P(('group', 'loop')), parts along dimension 0, may hold values 0 or 1
Outputs:
- new_users: float32 [8192, 512], P(('group', 'loop')), parts along dimension 0
The draws below stay inside these ranges and needn't reach their ends.
There are 2 independent parts, one for each index of `group`. The reference program is written for one: setup_inputs(seed, part) draws one part's arguments, and reference() takes and returns one part's arrays. A program takes and returns all parts, laid end to end along the dimension named above; each array names one. Nothing has to cross between parts.
Inputs may be any that keep to these rules, and one draw needn't show every extreme that they name: `tile_blocks`: in each row the entries are distinct item blocks; only the first tile_count of them are used. `tile_count`: some user block has all 8 tiles live.
All inputs are finite; a program needn't handle non-finite values. No bound on the sum of `labels` on one device may be relied on, other than what follows from the above.
Results may differ from the reference program's by a relative error of at most 0.0003.
Values may be sent and summed in bfloat16 or wider, within the bound.
No kernel may reach another device: no remote copies, remote signals or barrier semaphores. Data moves between devices by JAX's collectives and lax.ppermute only.
A program may use at most 64 MiB of HBM per device.

```python
import jax
import jax.numpy as jnp
from jax import lax

K = 512
USR_DEV = 256
ITEM_DEV = 128
SLOTS = 8
NU = 4096
NI = 2048
N_LOOP = 16


def draw_tile_blocks(key, part):
    row_keys = jax.random.split(jax.random.fold_in(key, 7), N_LOOP)
    shuffled = jax.vmap(lambda row_key: jax.random.permutation(row_key, N_LOOP))(row_keys)
    return shuffled[:, :SLOTS].astype(jnp.int32)


def draw_tile_count(key, part):
    shifts = jax.random.randint(jax.random.fold_in(key, 11), (N_LOOP,), 0, 4)
    counts_drawn = jnp.floor_divide(SLOTS, jnp.left_shift(1, shifts))
    busiest = jax.random.randint(jax.random.fold_in(key, 13), (), 0, N_LOOP)
    positions = jnp.arange(N_LOOP)
    return jnp.where(positions == busiest, SLOTS, counts_drawn).astype(jnp.int32)


def plant(values, rng, least, largest):
    longest = values.shape.index(max(values.shape))
    spots = []
    for shift in (0, 1):
        where = [jax.random.randint(jax.random.fold_in(rng, axis), (), 0, length) for axis, length in enumerate(values.shape)]
        where[longest] = (where[longest] + shift) % values.shape[longest]
        spots.append(tuple(where))
    return values.at[spots[0]].set(least).at[spots[1]].set(largest)


def shard_levels(own_key, dims, shards, low, top_value):
    loudness = 1.0
    for axis_at, shards_of in shards:
        heights = jax.random.uniform(jax.random.fold_in(jax.random.fold_in(own_key, 6), axis_at), (shards_of,), jnp.float32, low / len(shards), top_value / len(shards))
        loudness = loudness * jnp.repeat(jnp.exp(heights), dims[axis_at] // shards_of).reshape((-1,) + (1,) * (len(dims) - 1 - axis_at))
    return loudness


def centred(own_key, shape, spread, most, cuts=(), kind=jnp.bfloat16):
    values = spread * jax.random.normal(own_key, shape, jnp.float32)
    if cuts:
        values = values * shard_levels(own_key, shape, cuts, -0.22, 0.18)
    return jnp.clip(values, -most, most).astype(kind)


def setup_inputs(seed: int = 0, part: int = 0) -> dict:
    seeds = jax.random.split(jax.random.key(seed), 6)
    part_splits = jax.random.split(jax.random.fold_in(seeds[5], part), 6)
    users = centred(part_splits[0], (NU, K), 0.21, 1.3, ((0, 16),), jnp.float32)
    items = centred(part_splits[1], (NI, K), 0.21, 1.296875, ((0, 16),))
    tile_blocks = draw_tile_blocks(jax.random.fold_in(jax.random.fold_in(seeds[5], part), 71), part)
    tile_count = draw_tile_count(jax.random.fold_in(jax.random.fold_in(seeds[5], part), 71), part)
    labels = plant((jax.random.randint(part_splits[4], (NU, SLOTS * ITEM_DEV), 0, 4) < 1).astype(jnp.int32), jax.random.fold_in(part_splits[4], 1), 0, 1)
    return {"users": users, "items": items, "tile_blocks": tile_blocks, "tile_count": tile_count, "labels": labels}


def reference(users, items, tile_blocks, tile_count, labels):
    item_groups = items.astype(jnp.float32).reshape(N_LOOP, ITEM_DEV, K)
    user_groups = users.reshape(N_LOOP, USR_DEV, K)
    label_groups = labels.reshape(N_LOOP, USR_DEV, SLOTS, ITEM_DEV)

    def block_gradient(packed_args):
        user_rows, block_list, live_count, label_tile = packed_args

        def slot_step(running, slot_index):

            def work(current):
                item_block = item_groups[block_list[slot_index]]
                scores = jnp.dot(user_rows, item_block.T, precision=lax.Precision.HIGHEST, preferred_element_type=jnp.float32)
                target = label_tile[:, slot_index, :].astype(jnp.float32)
                residual = jax.nn.sigmoid(scores) - target
                return current + jnp.dot(residual, item_block, precision=lax.Precision.HIGHEST, preferred_element_type=jnp.float32)
            return (lax.cond(slot_index < live_count, work, lambda current: current, running), None)
        start_grad = jnp.zeros((USR_DEV, K), jnp.float32)
        result, _ = lax.scan(slot_step, start_grad, jnp.arange(SLOTS, dtype=jnp.int32))
        return result
    gradient = lax.map(block_gradient, (user_groups, tile_blocks, tile_count, label_groups)).reshape(NU, K)
    grad_rms = jnp.sqrt(jnp.sum(gradient * gradient) / (NU * K) + 1e-06)
    step_scale = 0.5 / grad_rms
    return users - step_scale * gradient
```

```python
import functools

import jax
import jax.numpy as jnp
from jax import lax
from jax.experimental import pallas as pl
from jax.experimental.pallas import tpu as pltpu
from jax.sharding import PartitionSpec as P

CHUNK = 8
DIRECT_LIMIT = 16


def split_loop(loop_size):
    cores = 2 if loop_size % 2 == 0 else 1
    chips = loop_size // cores
    inner = 1
    while inner * inner * 4 <= chips:
        inner *= 2
    if chips % inner:
        inner = 1
    return chips // inner, inner, cores


def shifted(array, dims, axis, shift):
    outer, inner, cores = dims
    pairs = []
    for source in range(outer * inner * cores):
        place = [source // (inner * cores), source // cores % inner, source % cores]
        place[axis] = (place[axis] + shift) % dims[axis]
        pairs.append((source, (place[0] * inner + place[1]) * cores + place[2]))
    return lax.ppermute(array, "loop", pairs)


def spread(array, dims):
    held = [((0, 0, 0), array)]
    for axis in range(3):
        for shifts, piece in list(held):
            for shift in range(1, dims[axis]):
                moved = list(shifts)
                moved[axis] = shift
                held.append((tuple(moved), shifted(piece, dims, axis, shift)))
    return held


def halves(values):
    upper = values.astype(jnp.bfloat16)
    return jnp.concatenate([upper, (values - upper.astype(jnp.float32)).astype(jnp.bfloat16)], 0)


def gradient_kernel(
    fetch, refs, list_ref, count_ref, users_ref, labels_ref, *rest
):
    pieces = rest[:refs]
    grad_ref, square_ref, tiles, parts, sems = rest[refs:]
    rows, width = users_ref.shape
    tile = tiles.shape[0] // CHUNK
    step = pl.program_id(0)
    live = jnp.minimum(count_ref[0] - step * CHUNK, CHUNK)

    @pl.when(step == 0)
    def _():
        grad_ref[...] = jnp.zeros_like(grad_ref)

    fetch(list_ref, step, live, pieces, tiles, sems, False)

    @pl.when(step == 0)
    def _():
        parts[...] = halves(users_ref[...])

    @pl.when((live > 0) & (live % 2 == 1))
    def _():
        blank = pl.multiple_of(live * tile, tile)
        tiles[pl.ds(blank, tile), :] = jnp.zeros((tile, width), tiles.dtype)

    fetch(list_ref, step, live, pieces, tiles, sems, True)

    def pair(index, carry):
        start = pl.multiple_of(index * 2 * tile, 2 * tile)
        block = tiles[pl.ds(start, 2 * tile), :]
        both = lax.dot_general(
            parts[...], block, (((1,), (1,)), ((), ())), preferred_element_type=jnp.float32
        )
        scores = both[:rows] + both[rows:]
        chance = 0.5 * jnp.tanh(0.5 * scores) + 0.5
        labels = labels_ref[:, pl.ds(start, 2 * tile)].astype(jnp.float32)
        column = start + lax.broadcasted_iota(jnp.int32, scores.shape, 1)
        residual = jnp.where(column < live * tile, chance - labels, 0.0)
        both = jnp.dot(halves(residual), block, preferred_element_type=jnp.float32)
        grad_ref[...] += both[:rows] + both[rows:]
        return carry

    lax.fori_loop(0, (jnp.maximum(live, 0) + 1) // 2, pair, 0)

    @pl.when(step == pl.num_programs(0) - 1)
    def _():
        gradient = grad_ref[...]
        square = jnp.sum(gradient * gradient, axis=0, keepdims=True)
        square_ref[...] = sum(square[:, at : at + 128] for at in range(0, width, 128))


def fetch_list(dims, shifts, list_ref, step, live, pieces, tiles, sems, wait):
    tile = pieces[0].shape[0]
    outer, inner, cores = dims
    me = lax.axis_index("loop")
    place = (me // (inner * cores), me // cores % inner, me % cores)
    wanted = [jnp.where(slot < live, list_ref[0, step * CHUNK + slot], -1) for slot in range(CHUNK)]
    for piece, shift in zip(pieces, shifts):
        at = [lax.rem(p - s + d, d) for p, s, d in zip(place, shift, dims)]
        block = (at[0] * inner + at[1]) * cores + at[2]
        found = jnp.int32(-1)
        for slot in range(CHUNK):
            found = jnp.where(wanted[slot] == block, slot, found)

        @pl.when(found >= 0)
        def _():
            start = pl.multiple_of(found * tile, tile)
            copy = pltpu.make_async_copy(piece, tiles.at[pl.ds(start, tile), :], sems.at[found])
            if wait:
                copy.wait()
            else:
                copy.start()


def fetch_whole(list_ref, step, live, pieces, tiles, sems, wait):
    tile = tiles.shape[0] // CHUNK
    for slot in range(CHUNK):

        @pl.when(slot < live)
        def _():
            start = pl.multiple_of(list_ref[0, step * CHUNK + slot] * tile, tile)
            copy = pltpu.make_async_copy(
                pieces[0].at[pl.ds(start, tile), :], tiles.at[pl.ds(slot * tile, tile), :], sems.at[slot]
            )
            if wait:
                copy.wait()
            else:
                copy.start()


def update_kernel(entries, users_ref, grad_ref, *rest):
    squares, out_ref = rest[:-1], rest[-1]
    total = squares[0][...]
    for square in squares[1:]:
        total = total + square[...]
    total = jnp.sum(total, axis=1, keepdims=True)
    scale = 0.5 / jnp.sqrt(total / entries + 1e-06)
    out_ref[...] = users_ref[...] - scale * grad_ref[...]


def local(users, items, tile_blocks, tile_count, labels):
    loop_size = lax.axis_size("loop")
    rows, width = users.shape
    tile = items.shape[0]
    slots = tile_blocks.shape[1]
    dims = split_loop(loop_size)
    direct = loop_size <= DIRECT_LIMIT
    if direct:
        held = spread(items, dims)
        pieces = [piece for _, piece in held]
        fetch = functools.partial(fetch_list, dims, [shifts for shifts, _ in held])
    else:
        pieces = [lax.all_gather(items, "loop", axis=0, tiled=True)]
        fetch = fetch_whole

    gradient, square = pl.pallas_call(
        functools.partial(gradient_kernel, fetch, len(pieces)),
        grid=(slots // CHUNK,),
        out_shape=[
            jax.ShapeDtypeStruct((rows, width), jnp.float32),
            jax.ShapeDtypeStruct((1, 128), jnp.float32),
        ],
        in_specs=[
            pl.BlockSpec(memory_space=pltpu.SMEM),
            pl.BlockSpec(memory_space=pltpu.SMEM),
            pl.BlockSpec((rows, width), lambda step: (0, 0)),
            pl.BlockSpec((rows, CHUNK * tile), lambda step: (0, step)),
        ]
        + [pl.BlockSpec(memory_space=pl.ANY)] * len(pieces),
        out_specs=[
            pl.BlockSpec((rows, width), lambda step: (0, 0)),
            pl.BlockSpec((1, 128), lambda step: (0, 0)),
        ],
        scratch_shapes=[
            pltpu.VMEM((CHUNK * tile, width), jnp.bfloat16),
            pltpu.VMEM((2 * rows, width), jnp.bfloat16),
            pltpu.SemaphoreType.DMA((CHUNK,)),
        ],
        compiler_params=pltpu.CompilerParams(vmem_limit_bytes=32 * 1024 * 1024),
        cost_estimate=pl.CostEstimate(
            flops=8 * rows * width * slots * tile,
            bytes_accessed=4 * rows * (slots * tile + 2 * width) + 2 * slots * tile * width,
            transcendentals=rows * slots * tile,
        ),
        name="gradient",
    )(tile_blocks, tile_count, users, labels, *pieces)

    if direct:
        squares = [piece for _, piece in [((0, 0, 0), square)]]
        squares += [
            lax.ppermute(square, "loop", [(at, (at + shift) % loop_size) for at in range(loop_size)])
            for shift in range(1, loop_size)
        ]
    else:
        squares = [lax.psum(square, "loop")]

    return pl.pallas_call(
        functools.partial(update_kernel, rows * loop_size * width),
        out_shape=jax.ShapeDtypeStruct((rows, width), jnp.float32),
        in_specs=[pl.BlockSpec(memory_space=pltpu.VMEM)] * (2 + len(squares)),
        out_specs=pl.BlockSpec(memory_space=pltpu.VMEM),
        compiler_params=pltpu.CompilerParams(vmem_limit_bytes=16 * 1024 * 1024),
        cost_estimate=pl.CostEstimate(
            flops=2 * rows * width, bytes_accessed=12 * rows * width, transcendentals=0
        ),
        name="update",
    )(users, gradient, *squares)


def solution(mesh):
    in_specs = (
        P(("group", "loop"), None),
        P(("group", "loop"), None),
        P(("group", "loop"), None),
        P(("group", "loop")),
        P(("group", "loop"), None),
    )
    out_specs = P(("group", "loop"), None)
    return jax.shard_map(local, mesh=mesh, in_specs=in_specs, out_specs=out_specs, check_vma=False)
```

```python
import functools

import jax
import jax.numpy as jnp
from jax import lax
from jax.experimental import pallas as pl
from jax.experimental.pallas import tpu as pltpu
from jax.sharding import PartitionSpec as P

CHUNK = 8
DIRECT_LIMIT = 16


def split_loop(loop_size):
    cores = 2 if loop_size % 2 == 0 else 1
    chips = loop_size // cores
    inner = 1
    while inner * inner * 4 <= chips:
        inner *= 2
    if chips % inner:
        inner = 1
    return chips // inner, inner, cores


def shifted(array, dims, axis, shift):
    outer, inner, cores = dims
    pairs = []
    for source in range(outer * inner * cores):
        place = [source // (inner * cores), source // cores % inner, source % cores]
        place[axis] = (place[axis] + shift) % dims[axis]
        pairs.append((source, (place[0] * inner + place[1]) * cores + place[2]))
    return lax.ppermute(array, "loop", pairs)


def spread(array, dims):
    held = [((0, 0, 0), array)]
    for axis in range(3):
        for shifts, piece in list(held):
            for shift in range(1, dims[axis]):
                moved = list(shifts)
                moved[axis] = shift
                held.append((tuple(moved), shifted(piece, dims, axis, shift)))
    return held


def halves(values):
    upper = values.astype(jnp.bfloat16)
    return jnp.concatenate([upper, (values - upper.astype(jnp.float32)).astype(jnp.bfloat16)], 0)


def gradient_kernel(
    fetch, refs, list_ref, count_ref, users_ref, labels_ref, *rest
):
    pieces = rest[:refs]
    grad_ref, square_ref, tiles, parts, sems = rest[refs:]
    rows, width = users_ref.shape
    tile = tiles.shape[0] // CHUNK
    step = pl.program_id(0)
    live = jnp.minimum(count_ref[0] - step * CHUNK, CHUNK)

    @pl.when(step == 0)
    def _():
        grad_ref[...] = jnp.zeros_like(grad_ref)

    fetch(list_ref, step, live, pieces, tiles, sems, False)

    @pl.when(step == 0)
    def _():
        parts[...] = halves(users_ref[...])

    @pl.when((live > 0) & (live % 2 == 1))
    def _():
        blank = pl.multiple_of(live * tile, tile)
        tiles[pl.ds(blank, tile), :] = jnp.zeros((tile, width), tiles.dtype)

    fetch(list_ref, step, live, pieces, tiles, sems, True)

    def pair(index, carry):
        start = pl.multiple_of(index * 2 * tile, 2 * tile)
        block = tiles[pl.ds(start, 2 * tile), :]
        both = lax.dot_general(
            parts[...], block, (((1,), (1,)), ((), ())), preferred_element_type=jnp.float32
        )
        scores = both[:rows] + both[rows:]
        chance = 0.5 * jnp.tanh(0.5 * scores) + 0.5
        labels = labels_ref[:, pl.ds(start, 2 * tile)].astype(jnp.float32)
        column = start + lax.broadcasted_iota(jnp.int32, scores.shape, 1)
        residual = jnp.where(column < live * tile, chance - labels, 0.0)
        both = jnp.dot(halves(residual), block, preferred_element_type=jnp.float32)
        grad_ref[...] += both[:rows] + both[rows:]
        return carry

    lax.fori_loop(0, (jnp.maximum(live, 0) + 1) // 2, pair, 0)

    @pl.when(step == pl.num_programs(0) - 1)
    def _():
        gradient = grad_ref[...]
        square = jnp.sum(gradient * gradient, axis=0, keepdims=True)
        square = sum(square[:, at : at + 128] for at in range(0, width, 128))
        square_ref[...] = jnp.broadcast_to(square, square_ref.shape)


def fetch_list(dims, shifts, list_ref, step, live, pieces, tiles, sems, wait):
    tile = pieces[0].shape[0]
    outer, inner, cores = dims
    me = lax.axis_index("loop")
    place = (me // (inner * cores), me // cores % inner, me % cores)
    wanted = [jnp.where(slot < live, list_ref[0, step * CHUNK + slot], -1) for slot in range(CHUNK)]
    for piece, shift in zip(pieces, shifts):
        at = [lax.rem(p - s + d, d) for p, s, d in zip(place, shift, dims)]
        block = (at[0] * inner + at[1]) * cores + at[2]
        found = jnp.int32(-1)
        for slot in range(CHUNK):
            found = jnp.where(wanted[slot] == block, slot, found)

        @pl.when(found >= 0)
        def _():
            start = pl.multiple_of(found * tile, tile)
            copy = pltpu.make_async_copy(piece, tiles.at[pl.ds(start, tile), :], sems.at[found])
            if wait:
                copy.wait()
            else:
                copy.start()


def fetch_whole(list_ref, step, live, pieces, tiles, sems, wait):
    tile = tiles.shape[0] // CHUNK
    for slot in range(CHUNK):

        @pl.when(slot < live)
        def _():
            start = pl.multiple_of(list_ref[0, step * CHUNK + slot] * tile, tile)
            copy = pltpu.make_async_copy(
                pieces[0].at[pl.ds(start, tile), :], tiles.at[pl.ds(slot * tile, tile), :], sems.at[slot]
            )
            if wait:
                copy.wait()
            else:
                copy.start()


def update_kernel(entries, users_ref, grad_ref, squares_ref, out_ref):
    total = jnp.sum(squares_ref[...], axis=0, keepdims=True)
    total = jnp.sum(total, axis=1, keepdims=True)
    scale = 0.5 / jnp.sqrt(total / entries + 1e-06)
    out_ref[...] = users_ref[...] - scale * grad_ref[...]


def local(users, items, tile_blocks, tile_count, labels):
    loop_size = lax.axis_size("loop")
    rows, width = users.shape
    tile = items.shape[0]
    slots = tile_blocks.shape[1]
    dims = split_loop(loop_size)
    direct = loop_size <= DIRECT_LIMIT
    if direct:
        held = spread(items, dims)
        pieces = [piece for _, piece in held]
        fetch = functools.partial(fetch_list, dims, [shifts for shifts, _ in held])
    else:
        pieces = [lax.all_gather(items, "loop", axis=0, tiled=True)]
        fetch = fetch_whole

    gradient, square = pl.pallas_call(
        functools.partial(gradient_kernel, fetch, len(pieces)),
        grid=(slots // CHUNK,),
        out_shape=[
            jax.ShapeDtypeStruct((rows, width), jnp.float32),
            jax.ShapeDtypeStruct((loop_size, 128), jnp.float32),
        ],
        in_specs=[
            pl.BlockSpec(memory_space=pltpu.SMEM),
            pl.BlockSpec(memory_space=pltpu.SMEM),
            pl.BlockSpec((rows, width), lambda step: (0, 0)),
            pl.BlockSpec((rows, CHUNK * tile), lambda step: (0, step)),
        ]
        + [pl.BlockSpec(memory_space=pl.ANY)] * len(pieces),
        out_specs=[
            pl.BlockSpec((rows, width), lambda step: (0, 0)),
            pl.BlockSpec((loop_size, 128), lambda step: (0, 0)),
        ],
        scratch_shapes=[
            pltpu.VMEM((CHUNK * tile, width), jnp.bfloat16),
            pltpu.VMEM((2 * rows, width), jnp.bfloat16),
            pltpu.SemaphoreType.DMA((CHUNK,)),
        ],
        compiler_params=pltpu.CompilerParams(vmem_limit_bytes=32 * 1024 * 1024),
        cost_estimate=pl.CostEstimate(
            flops=8 * rows * width * slots * tile,
            bytes_accessed=4 * rows * (slots * tile + 2 * width) + 2 * slots * tile * width,
            transcendentals=rows * slots * tile,
        ),
        name="gradient",
    )(tile_blocks, tile_count, users, labels, *pieces)

    squares = lax.all_to_all(square, "loop", 0, 0, tiled=True)

    return pl.pallas_call(
        functools.partial(update_kernel, rows * loop_size * width),
        out_shape=jax.ShapeDtypeStruct((rows, width), jnp.float32),
        in_specs=[pl.BlockSpec(memory_space=pltpu.VMEM)] * 3,
        out_specs=pl.BlockSpec(memory_space=pltpu.VMEM),
        compiler_params=pltpu.CompilerParams(vmem_limit_bytes=16 * 1024 * 1024),
        cost_estimate=pl.CostEstimate(
            flops=2 * rows * width, bytes_accessed=12 * rows * width, transcendentals=0
        ),
        name="update",
    )(users, gradient, squares)


def solution(mesh):
    in_specs = (
        P(("group", "loop"), None),
        P(("group", "loop"), None),
        P(("group", "loop"), None),
        P(("group", "loop")),
        P(("group", "loop"), None),
    )
    out_specs = P(("group", "loop"), None)
    return jax.shard_map(local, mesh=mesh, in_specs=in_specs, out_specs=out_specs, check_vma=False)
```

```python
import functools

import jax
import jax.numpy as jnp
from jax import lax
from jax.experimental import pallas as pl
from jax.experimental.pallas import tpu as pltpu
from jax.sharding import PartitionSpec as P

CHUNK = 8
RING_LIMIT = 16


def ring_place(loop_size):
    outer = loop_size // 4

    def device(position, core):
        position = position % (2 * outer)
        chip = 2 * position if position < outer else 2 * (2 * outer - 1 - position) + 1
        return 2 * chip + core

    return 2 * outer, device


def to_next(array, loop_size):
    chips, device = ring_place(loop_size)
    pairs = [(device(at, 0), device(at + 1, 0)) for at in range(chips)]
    pairs += [(device(at, 1), device(at - 1, 1)) for at in range(chips)]
    return lax.ppermute(array, "loop", pairs)


def to_other_core(array, loop_size):
    return lax.ppermute(array, "loop", [(at, at ^ 1) for at in range(loop_size)])


def join_kernel(own_ref, other_ref, both_ref):
    tile = own_ref.shape[0]
    core = lax.axis_index("loop") % 2
    both_ref[pl.ds(pl.multiple_of(core * tile, tile), tile), :] = own_ref[...]
    both_ref[pl.ds(pl.multiple_of((1 - core) * tile, tile), tile), :] = other_ref[...]


def join(own, other):
    tile, width = own.shape
    return pl.pallas_call(
        join_kernel,
        out_shape=jax.ShapeDtypeStruct((2 * tile, width), own.dtype),
        in_specs=[pl.BlockSpec(memory_space=pltpu.VMEM)] * 2,
        out_specs=pl.BlockSpec(memory_space=pltpu.VMEM),
        cost_estimate=pl.CostEstimate(
            flops=0, bytes_accessed=8 * tile * width, transcendentals=0
        ),
        name="join",
    )(own, other)


def halves(values):
    upper = values.astype(jnp.bfloat16)
    return jnp.concatenate([upper, (values - upper.astype(jnp.float32)).astype(jnp.bfloat16)], 0)


def add_tiles(grad_ref, parts_ref, tiles, live, labels_at):
    rows = grad_ref.shape[0]
    tile = tiles.shape[0] // CHUNK

    @pl.when(live % 2 == 1)
    def _():
        blank = pl.multiple_of(live * tile, tile)
        tiles[pl.ds(blank, tile), :] = jnp.zeros((tile, tiles.shape[1]), tiles.dtype)

    def pair(index, carry):
        block = tiles[pl.ds(pl.multiple_of(index * 2 * tile, 2 * tile), 2 * tile), :]
        both = lax.dot_general(
            parts_ref[...], block, (((1,), (1,)), ((), ())), preferred_element_type=jnp.float32
        )
        chance = 0.5 * jnp.tanh(0.5 * (both[:rows] + both[rows:])) + 0.5
        labels = jnp.concatenate([labels_at(2 * index), labels_at(2 * index + 1)], 1)
        position = 2 * index + lax.broadcasted_iota(jnp.int32, chance.shape, 1) // tile
        residual = jnp.where(position < live, chance - labels.astype(jnp.float32), 0.0)
        both = jnp.dot(halves(residual), block, preferred_element_type=jnp.float32)
        grad_ref[...] += both[:rows] + both[rows:]
        return carry

    lax.fori_loop(0, (live + 1) // 2, pair, 0)


def store_square(grad_ref, square_ref):
    gradient = grad_ref[...]
    square = jnp.sum(gradient * gradient, axis=0, keepdims=True)
    square = sum(square[:, at : at + 128] for at in range(0, square.shape[1], 128))
    square_ref[...] = jnp.broadcast_to(square, square_ref.shape)


def chip_behind(hops, loop_size):
    chips = loop_size // 2
    me = lax.axis_index("loop")
    core, row, outer = me % 2, me // 2 % 2, me // 4
    position = jnp.where(row == 0, outer, chips - 1 - outer)
    at = lax.rem(position + chips + jnp.where(core == 0, -hops, hops), chips)
    return jnp.where(at < chips // 2, 2 * at, 2 * (chips - 1 - at) + 1)


def pieces_kernel(loop_size, hops, first, last, list_ref, count_ref, *rest):
    rest = list(rest)
    given_ref, labels_ref = rest.pop(0), rest.pop(0)
    pieces = [rest.pop(0) for _ in hops]
    before_ref = None if first else rest.pop(0)
    grad_ref = rest.pop(0)
    parts_ref = rest.pop(0) if first else given_ref
    square_ref = rest.pop(0) if last else None
    tiles, slots = rest
    tile = tiles.shape[0] // CHUNK
    if first:
        parts_ref[...] = halves(given_ref[...])
        grad_ref[...] = jnp.zeros_like(grad_ref)
    else:
        grad_ref[...] = before_ref[...]
    wanted = [
        jnp.where(slot < count_ref[0], list_ref[0, slot], -1) for slot in range(list_ref.shape[1])
    ]
    live = jnp.int32(0)
    for piece, hop in zip(pieces, hops):
        chip = chip_behind(hop, loop_size)
        for core in range(2):
            found = jnp.int32(-1)
            for slot, name in enumerate(wanted):
                found = jnp.where(name == 2 * chip + core, slot, found)

            @pl.when(found >= 0)
            def _():
                into = pl.ds(pl.multiple_of(live * tile, tile), tile)
                tiles[into, :] = piece[core * tile : (core + 1) * tile, :]
                slots[live] = found

            live = live + (found >= 0).astype(jnp.int32)
    slots[live] = 0

    def labels_at(position):
        return labels_ref[:, pl.ds(pl.multiple_of(slots[position] * tile, tile), tile)]

    add_tiles(grad_ref, parts_ref, tiles, live, labels_at)
    if last:
        store_square(grad_ref, square_ref)


def add_pieces(loop_size, held, lists, given, labels, before, last):
    first = before is None
    width = given.shape[1]
    rows = given.shape[0] // (1 if first else 2)
    pieces = [piece for _, piece in held]
    tile = pieces[0].shape[0] // 2
    most = min(2 * len(pieces), CHUNK)
    out_shape = [jax.ShapeDtypeStruct((rows, width), jnp.float32)]
    if first:
        out_shape.append(jax.ShapeDtypeStruct((2 * rows, width), jnp.bfloat16))
    if last:
        out_shape.append(jax.ShapeDtypeStruct((loop_size, 128), jnp.float32))
    extra = [] if first else [before]
    return pl.pallas_call(
        functools.partial(pieces_kernel, loop_size, [hops for hops, _ in held], first, last),
        out_shape=out_shape,
        in_specs=[pl.BlockSpec(memory_space=pltpu.SMEM)] * 2
        + [pl.BlockSpec(memory_space=pltpu.VMEM)] * (2 + len(pieces) + len(extra)),
        out_specs=[pl.BlockSpec(memory_space=pltpu.VMEM)] * len(out_shape),
        scratch_shapes=[
            pltpu.VMEM((CHUNK * tile, width), jnp.bfloat16),
            pltpu.SMEM((CHUNK + 1,), jnp.int32),
        ],
        compiler_params=pltpu.CompilerParams(vmem_limit_bytes=24 * 1024 * 1024),
        cost_estimate=pl.CostEstimate(
            flops=8 * rows * width * most * tile,
            bytes_accessed=8 * rows * width,
            transcendentals=rows * most * tile,
        ),
        name="add_pieces",
    )(*lists, given, labels, *pieces, *extra)


def ring_gradient(users, items, lists, labels):
    loop_size = lax.axis_size("loop")
    far = loop_size // 4
    near = join(items, to_other_core(items, loop_size))
    ready, gradient, parts = [(0, near)], None, None
    for hop in range(1, far + 1):
        near = to_next(near, loop_size)
        if hop < 2:
            late = []
        elif gradient is None:
            gradient, parts = add_pieces(loop_size, ready, lists, users, labels, None, False)
            ready = []
        else:
            (gradient,) = add_pieces(loop_size, ready, lists, parts, labels, gradient, False)
            ready = []
        if gradient is not None:
            near, gradient = lax.optimization_barrier((near, gradient))
        ready = ready + late + [(hop, near)]
        late = []
        if hop < far:
            late = [(-hop, to_other_core(near, loop_size))]
            if hop == far - 1:
                ready, late = ready + late, []
    return add_pieces(loop_size, ready, lists, parts, labels, gradient, True)


def chunks_kernel(
    list_ref, count_ref, users_ref, labels_ref, items_ref, grad_ref, square_ref, tiles, parts_ref, sems
):
    tile = tiles.shape[0] // CHUNK
    step = pl.program_id(0)
    live = jnp.clip(count_ref[0] - step * CHUNK, 0, CHUNK)

    @pl.when(step == 0)
    def _():
        parts_ref[...] = halves(users_ref[...])
        grad_ref[...] = jnp.zeros_like(grad_ref)

    def move(slot):
        start = pl.multiple_of(list_ref[0, step * CHUNK + slot] * tile, tile)
        return pltpu.make_async_copy(
            items_ref.at[pl.ds(start, tile), :], tiles.at[pl.ds(slot * tile, tile), :], sems.at[slot]
        )

    for slot in range(CHUNK):
        pl.when(slot < live)(lambda slot=slot: move(slot).start())
    for slot in range(CHUNK):
        pl.when(slot < live)(lambda slot=slot: move(slot).wait())

    def labels_at(position):
        return labels_ref[:, pl.ds(pl.multiple_of(position * tile, tile), tile)]

    add_tiles(grad_ref, parts_ref, tiles, live, labels_at)

    @pl.when(step == pl.num_programs(0) - 1)
    def _():
        store_square(grad_ref, square_ref)


def add_chunks(loop_size, items, lists, users, labels):
    rows, width = users.shape
    slots = lists[0].shape[1]
    tile = labels.shape[1] // slots
    return pl.pallas_call(
        chunks_kernel,
        grid=(slots // CHUNK,),
        out_shape=[
            jax.ShapeDtypeStruct((rows, width), jnp.float32),
            jax.ShapeDtypeStruct((loop_size, 128), jnp.float32),
        ],
        in_specs=[
            pl.BlockSpec(memory_space=pltpu.SMEM),
            pl.BlockSpec(memory_space=pltpu.SMEM),
            pl.BlockSpec((rows, width), lambda step: (0, 0)),
            pl.BlockSpec((rows, CHUNK * tile), lambda step: (0, step)),
            pl.BlockSpec(memory_space=pl.ANY),
        ],
        out_specs=[
            pl.BlockSpec((rows, width), lambda step: (0, 0)),
            pl.BlockSpec((loop_size, 128), lambda step: (0, 0)),
        ],
        scratch_shapes=[
            pltpu.VMEM((CHUNK * tile, width), jnp.bfloat16),
            pltpu.VMEM((2 * rows, width), jnp.bfloat16),
            pltpu.SemaphoreType.DMA((CHUNK,)),
        ],
        compiler_params=pltpu.CompilerParams(vmem_limit_bytes=32 * 1024 * 1024),
        cost_estimate=pl.CostEstimate(
            flops=8 * rows * width * slots * tile,
            bytes_accessed=4 * rows * (slots * tile + 2 * width) + 2 * slots * tile * width,
            transcendentals=rows * slots * tile,
        ),
        name="add_chunks",
    )(*lists, users, labels, items)


def update_kernel(entries, users_ref, grad_ref, squares_ref, out_ref):
    total = jnp.sum(squares_ref[...], axis=0, keepdims=True)
    total = jnp.sum(total, axis=1, keepdims=True)
    scale = 0.5 / jnp.sqrt(total / entries + 1e-06)
    out_ref[...] = users_ref[...] - scale * grad_ref[...]


def local(users, items, tile_blocks, tile_count, labels):
    loop_size = lax.axis_size("loop")
    rows, width = users.shape
    slots = tile_blocks.shape[1]
    lists = (tile_blocks, tile_count)
    if loop_size <= RING_LIMIT and loop_size % 8 == 0 and slots <= CHUNK:
        gradient, square = ring_gradient(users, items, lists, labels)
    else:
        whole = lax.all_gather(items, "loop", axis=0, tiled=True)
        gradient, square = add_chunks(loop_size, whole, lists, users, labels)

    squares = lax.all_to_all(square, "loop", 0, 0, tiled=True)
    return pl.pallas_call(
        functools.partial(update_kernel, rows * loop_size * width),
        out_shape=jax.ShapeDtypeStruct((rows, width), jnp.float32),
        in_specs=[pl.BlockSpec(memory_space=pltpu.VMEM)] * 3,
        out_specs=pl.BlockSpec(memory_space=pltpu.VMEM),
        compiler_params=pltpu.CompilerParams(vmem_limit_bytes=16 * 1024 * 1024),
        cost_estimate=pl.CostEstimate(
            flops=2 * rows * width, bytes_accessed=12 * rows * width, transcendentals=0
        ),
        name="update",
    )(users, gradient, squares)


def solution(mesh):
    in_specs = (
        P(("group", "loop"), None),
        P(("group", "loop"), None),
        P(("group", "loop"), None),
        P(("group", "loop")),
        P(("group", "loop"), None),
    )
    out_specs = P(("group", "loop"), None)
    return jax.shard_map(local, mesh=mesh, in_specs=in_specs, out_specs=out_specs, check_vma=False)
```

```python
import functools

import jax
import jax.numpy as jnp
from jax import lax
from jax.experimental import pallas as pl
from jax.experimental.pallas import tpu as pltpu
from jax.sharding import PartitionSpec as P

CHUNK = 8
RING_LIMIT = 16


def ring_place(loop_size):
    outer = loop_size // 4

    def device(position, core):
        position = position % (2 * outer)
        chip = 2 * position if position < outer else 2 * (2 * outer - 1 - position) + 1
        return 2 * chip + core

    return 2 * outer, device


def to_next(array, direction, loop_size):
    chips, device = ring_place(loop_size)
    pairs = [(device(at, 0), device(at + direction, 0)) for at in range(chips)]
    pairs += [(device(at, 1), device(at - direction, 1)) for at in range(chips)]
    return lax.ppermute(array, "loop", pairs)


def to_other_core(array, loop_size):
    return lax.ppermute(array, "loop", [(at, at ^ 1) for at in range(loop_size)])


def halves(values):
    upper = values.astype(jnp.bfloat16)
    return jnp.concatenate([upper, (values - upper.astype(jnp.float32)).astype(jnp.bfloat16)], 0)


def add_tiles(grad_ref, parts_ref, tiles, live, labels_at):
    rows = grad_ref.shape[0]
    tile = tiles.shape[0] // CHUNK

    @pl.when(live % 2 == 1)
    def _():
        blank = pl.multiple_of(live * tile, tile)
        tiles[pl.ds(blank, tile), :] = jnp.zeros((tile, tiles.shape[1]), tiles.dtype)

    def pair(index, carry):
        block = tiles[pl.ds(pl.multiple_of(index * 2 * tile, 2 * tile), 2 * tile), :]
        both = lax.dot_general(
            parts_ref[...], block, (((1,), (1,)), ((), ())), preferred_element_type=jnp.float32
        )
        chance = 0.5 * jnp.tanh(0.5 * (both[:rows] + both[rows:])) + 0.5
        labels = jnp.concatenate([labels_at(2 * index), labels_at(2 * index + 1)], 1)
        position = 2 * index + lax.broadcasted_iota(jnp.int32, chance.shape, 1) // tile
        residual = jnp.where(position < live, chance - labels.astype(jnp.float32), 0.0)
        both = jnp.dot(halves(residual), block, preferred_element_type=jnp.float32)
        grad_ref[...] += both[:rows] + both[rows:]
        return carry

    lax.fori_loop(0, (live + 1) // 2, pair, 0)


def store_square(grad_ref, square_ref):
    gradient = grad_ref[...]
    square = jnp.sum(gradient * gradient, axis=0, keepdims=True)
    square = sum(square[:, at : at + 128] for at in range(0, square.shape[1], 128))
    square_ref[...] = jnp.broadcast_to(square, square_ref.shape)


def origin_block(origin, loop_size):
    hops, other = origin
    chips = loop_size // 2
    me = lax.axis_index("loop")
    core, row, outer = me % 2, me // 2 % 2, me // 4
    position = jnp.where(row == 0, outer, chips - 1 - outer)
    at = lax.rem(position + chips + jnp.where(core == 0, -hops, hops), chips)
    chip = jnp.where(at < chips // 2, 2 * at, 2 * (chips - 1 - at) + 1)
    return 2 * chip + (1 - core if other else core)


def pieces_kernel(loop_size, origins, first, last, list_ref, count_ref, *rest):
    rest = list(rest)
    given_ref, labels_ref = rest.pop(0), rest.pop(0)
    pieces = [rest.pop(0) for _ in origins]
    before_ref = None if first else rest.pop(0)
    grad_ref = rest.pop(0)
    parts_ref = rest.pop(0) if first else given_ref
    square_ref = rest.pop(0) if last else None
    tiles, slots = rest
    tile = tiles.shape[0] // CHUNK
    if first:
        parts_ref[...] = halves(given_ref[...])
        grad_ref[...] = jnp.zeros_like(grad_ref)
    else:
        grad_ref[...] = before_ref[...]
    wanted = [
        jnp.where(slot < count_ref[0], list_ref[0, slot], -1) for slot in range(list_ref.shape[1])
    ]
    live = jnp.int32(0)
    for piece, origin in zip(pieces, origins):
        block = origin_block(origin, loop_size)
        found = jnp.int32(-1)
        for slot, name in enumerate(wanted):
            found = jnp.where(name == block, slot, found)

        @pl.when(found >= 0)
        def _():
            tiles[pl.ds(pl.multiple_of(live * tile, tile), tile), :] = piece[...]
            slots[live] = found

        live = live + (found >= 0).astype(jnp.int32)
    slots[live] = 0

    def labels_at(position):
        return labels_ref[:, pl.ds(pl.multiple_of(slots[position] * tile, tile), tile)]

    add_tiles(grad_ref, parts_ref, tiles, live, labels_at)
    if last:
        store_square(grad_ref, square_ref)


def add_pieces(loop_size, held, lists, given, labels, before, last):
    first = before is None
    width = given.shape[1]
    rows = given.shape[0] // (1 if first else 2)
    pieces = [piece for _, piece in held]
    tile = pieces[0].shape[0]
    most = min(len(pieces), CHUNK)
    out_shape = [jax.ShapeDtypeStruct((rows, width), jnp.float32)]
    if first:
        out_shape.append(jax.ShapeDtypeStruct((2 * rows, width), jnp.bfloat16))
    if last:
        out_shape.append(jax.ShapeDtypeStruct((loop_size, 128), jnp.float32))
    extra = [] if first else [before]
    results = pl.pallas_call(
        functools.partial(pieces_kernel, loop_size, [origin for origin, _ in held], first, last),
        out_shape=out_shape,
        in_specs=[pl.BlockSpec(memory_space=pltpu.SMEM)] * 2
        + [pl.BlockSpec(memory_space=pltpu.VMEM)] * (2 + len(pieces) + len(extra)),
        out_specs=[pl.BlockSpec(memory_space=pltpu.VMEM)] * len(out_shape),
        scratch_shapes=[
            pltpu.VMEM((CHUNK * tile, width), jnp.bfloat16),
            pltpu.SMEM((CHUNK + 1,), jnp.int32),
        ],
        compiler_params=pltpu.CompilerParams(vmem_limit_bytes=24 * 1024 * 1024),
        cost_estimate=pl.CostEstimate(
            flops=8 * rows * width * most * tile,
            bytes_accessed=8 * rows * width,
            transcendentals=rows * most * tile,
        ),
        name="add_pieces",
    )(*lists, given, labels, *pieces, *extra)
    return results if first or last else (results[0], given)


def ring_gradient(users, items, lists, labels):
    loop_size = lax.axis_size("loop")
    far = loop_size // 4
    held = [[((0, 0), items), ((0, 1), to_other_core(items, loop_size))]]
    given, gradient = users, None
    up = down = items
    for hop in range(1, far + 1):
        if hop > 2:
            gradient, given = add_pieces(loop_size, held[hop - 3], lists, given, labels, gradient, False)
            up, gradient = lax.optimization_barrier((up, gradient))
        up = to_next(up, 1, loop_size)
        if hop < far:
            down = to_next(down, -1, loop_size)
            arrived = [((hop, 0), up), ((-hop, 0), down)]
            arrived += [((-hop, 1), to_other_core(up, loop_size)), ((hop, 1), to_other_core(down, loop_size))]
            held.append(arrived)
    gradient, given = add_pieces(loop_size, held[far - 2], lists, given, labels, gradient, False)
    up, gradient = lax.optimization_barrier((up, gradient))
    last = held[far - 1] + [((far, 0), up), ((far, 1), to_other_core(up, loop_size))]
    return add_pieces(loop_size, last, lists, given, labels, gradient, True)


def chunks_kernel(
    list_ref, count_ref, users_ref, labels_ref, items_ref, grad_ref, square_ref, tiles, parts_ref, sems
):
    tile = tiles.shape[0] // CHUNK
    step = pl.program_id(0)
    live = jnp.clip(count_ref[0] - step * CHUNK, 0, CHUNK)

    @pl.when(step == 0)
    def _():
        parts_ref[...] = halves(users_ref[...])
        grad_ref[...] = jnp.zeros_like(grad_ref)

    def move(slot):
        start = pl.multiple_of(list_ref[0, step * CHUNK + slot] * tile, tile)
        return pltpu.make_async_copy(
            items_ref.at[pl.ds(start, tile), :], tiles.at[pl.ds(slot * tile, tile), :], sems.at[slot]
        )

    for slot in range(CHUNK):
        pl.when(slot < live)(lambda slot=slot: move(slot).start())
    for slot in range(CHUNK):
        pl.when(slot < live)(lambda slot=slot: move(slot).wait())

    def labels_at(position):
        return labels_ref[:, pl.ds(pl.multiple_of(position * tile, tile), tile)]

    add_tiles(grad_ref, parts_ref, tiles, live, labels_at)

    @pl.when(step == pl.num_programs(0) - 1)
    def _():
        store_square(grad_ref, square_ref)


def add_chunks(loop_size, items, lists, users, labels):
    rows, width = users.shape
    slots = lists[0].shape[1]
    tile = labels.shape[1] // slots
    return pl.pallas_call(
        chunks_kernel,
        grid=(slots // CHUNK,),
        out_shape=[
            jax.ShapeDtypeStruct((rows, width), jnp.float32),
            jax.ShapeDtypeStruct((loop_size, 128), jnp.float32),
        ],
        in_specs=[
            pl.BlockSpec(memory_space=pltpu.SMEM),
            pl.BlockSpec(memory_space=pltpu.SMEM),
            pl.BlockSpec((rows, width), lambda step: (0, 0)),
            pl.BlockSpec((rows, CHUNK * tile), lambda step: (0, step)),
            pl.BlockSpec(memory_space=pl.ANY),
        ],
        out_specs=[
            pl.BlockSpec((rows, width), lambda step: (0, 0)),
            pl.BlockSpec((loop_size, 128), lambda step: (0, 0)),
        ],
        scratch_shapes=[
            pltpu.VMEM((CHUNK * tile, width), jnp.bfloat16),
            pltpu.VMEM((2 * rows, width), jnp.bfloat16),
            pltpu.SemaphoreType.DMA((CHUNK,)),
        ],
        compiler_params=pltpu.CompilerParams(vmem_limit_bytes=32 * 1024 * 1024),
        cost_estimate=pl.CostEstimate(
            flops=8 * rows * width * slots * tile,
            bytes_accessed=4 * rows * (slots * tile + 2 * width) + 2 * slots * tile * width,
            transcendentals=rows * slots * tile,
        ),
        name="add_chunks",
    )(*lists, users, labels, items)


def update_kernel(entries, users_ref, grad_ref, squares_ref, out_ref):
    total = jnp.sum(squares_ref[...], axis=0, keepdims=True)
    total = jnp.sum(total, axis=1, keepdims=True)
    scale = 0.5 / jnp.sqrt(total / entries + 1e-06)
    out_ref[...] = users_ref[...] - scale * grad_ref[...]


def local(users, items, tile_blocks, tile_count, labels):
    loop_size = lax.axis_size("loop")
    rows, width = users.shape
    slots = tile_blocks.shape[1]
    lists = (tile_blocks, tile_count)
    if loop_size <= RING_LIMIT and loop_size % 8 == 0 and slots <= CHUNK:
        gradient, square = ring_gradient(users, items, lists, labels)
    else:
        whole = lax.all_gather(items, "loop", axis=0, tiled=True)
        gradient, square = add_chunks(loop_size, whole, lists, users, labels)

    squares = lax.all_to_all(square, "loop", 0, 0, tiled=True)
    return pl.pallas_call(
        functools.partial(update_kernel, rows * loop_size * width),
        out_shape=jax.ShapeDtypeStruct((rows, width), jnp.float32),
        in_specs=[pl.BlockSpec(memory_space=pltpu.VMEM)] * 3,
        out_specs=pl.BlockSpec(memory_space=pltpu.VMEM),
        compiler_params=pltpu.CompilerParams(vmem_limit_bytes=16 * 1024 * 1024),
        cost_estimate=pl.CostEstimate(
            flops=2 * rows * width, bytes_accessed=12 * rows * width, transcendentals=0
        ),
        name="update",
    )(users, gradient, squares)


def solution(mesh):
    in_specs = (
        P(("group", "loop"), None),
        P(("group", "loop"), None),
        P(("group", "loop"), None),
        P(("group", "loop")),
        P(("group", "loop"), None),
    )
    out_specs = P(("group", "loop"), None)
    return jax.shard_map(local, mesh=mesh, in_specs=in_specs, out_specs=out_specs, check_vma=False)
```

```python
import functools

import jax
import jax.numpy as jnp
from jax import lax
from jax.experimental import pallas as pl
from jax.experimental.pallas import tpu as pltpu
from jax.sharding import PartitionSpec as P

CHUNK = 8
RING_LIMIT = 16


def ring_place(loop_size):
    outer = loop_size // 4

    def device(position, core):
        position = position % (2 * outer)
        chip = 2 * position if position < outer else 2 * (2 * outer - 1 - position) + 1
        return 2 * chip + core

    return 2 * outer, device


def to_next(array, direction, loop_size):
    chips, device = ring_place(loop_size)
    pairs = [(device(at, 0), device(at + direction, 0)) for at in range(chips)]
    pairs += [(device(at, 1), device(at - direction, 1)) for at in range(chips)]
    return lax.ppermute(array, "loop", pairs)


def to_other_core(array, loop_size):
    return lax.ppermute(array, "loop", [(at, at ^ 1) for at in range(loop_size)])


def halves(values):
    upper = values.astype(jnp.bfloat16)
    return jnp.concatenate([upper, (values - upper.astype(jnp.float32)).astype(jnp.bfloat16)], 0)


def table_kernel(loop_size, origins, list_ref, count_ref, table_ref):
    wanted = [
        jnp.where(slot < count_ref[0], list_ref[0, slot], -1) for slot in range(list_ref.shape[1])
    ]
    for at, origin in enumerate(origins):
        block = origin_block(origin, loop_size)
        found = jnp.int32(-1)
        for slot, name in enumerate(wanted):
            found = jnp.where(name == block, slot, found)
        table_ref[at] = found


def slot_table(loop_size, origins, block_list, live_count):
    return pl.pallas_call(
        functools.partial(table_kernel, loop_size, origins),
        out_shape=jax.ShapeDtypeStruct((len(origins),), jnp.int32),
        in_specs=[pl.BlockSpec(memory_space=pltpu.SMEM)] * 2,
        out_specs=pl.BlockSpec(memory_space=pltpu.SMEM),
        cost_estimate=pl.CostEstimate(flops=2**32, bytes_accessed=1024, transcendentals=0),
        name="slot_table",
    )(block_list, live_count)


def add_some(grad_ref, parts_ref, tiles, start, count, labels_at):
    rows = grad_ref.shape[0]
    tile = tiles.shape[0] // CHUNK
    block = tiles[pl.ds(pl.multiple_of(start * tile, 2 * tile), count * tile), :]
    upper, lower = [], []
    for at in range(0, count, 2):
        both = lax.dot_general(
            parts_ref[...],
            block[at * tile : (at + 2) * tile],
            (((1,), (1,)), ((), ())),
            preferred_element_type=jnp.float32,
        )
        labels = jnp.concatenate([labels_at(start + at), labels_at(start + at + 1)], 1)
        residual = 0.5 * jnp.tanh(both[:rows] + both[rows:]) + (0.5 - labels.astype(jnp.float32))
        upper.append(residual.astype(jnp.bfloat16))
        lower.append((residual - upper[-1].astype(jnp.float32)).astype(jnp.bfloat16))
    grad_ref[...] += jnp.dot(
        jnp.concatenate(upper + lower, 1),
        jnp.concatenate([block, block], 0),
        preferred_element_type=jnp.float32,
    )


def add_tiles(grad_ref, parts_ref, tiles, live, most, labels_at):
    tile = tiles.shape[0] // CHUNK

    @pl.when(live % 2 == 1)
    def _():
        blank = pl.multiple_of(live * tile, tile)
        tiles[pl.ds(blank, tile), :] = jnp.zeros((tile, tiles.shape[1]), tiles.dtype)

    fours = (live + 1) // 4 if most > 2 else jnp.int32(0)
    if most > 2:

        def four(index, carry):
            add_some(grad_ref, parts_ref, tiles, index * 4, 4, labels_at)
            return carry

        lax.fori_loop(0, fours, four, 0)

    @pl.when(live > 4 * fours)
    def _():
        add_some(grad_ref, parts_ref, tiles, 4 * fours, 2, labels_at)


def store_square(grad_ref, square_ref):
    gradient = grad_ref[...]
    square = jnp.sum(gradient * gradient, axis=0, keepdims=True)
    square = sum(square[:, at : at + 128] for at in range(0, square.shape[1], 128))
    square_ref[...] = jnp.broadcast_to(square, square_ref.shape)


def origin_block(origin, loop_size):
    hops, other = origin
    chips = loop_size // 2
    me = lax.axis_index("loop")
    core, row, outer = me % 2, me // 2 % 2, me // 4
    position = jnp.where(row == 0, outer, chips - 1 - outer)
    at = lax.rem(position + chips + jnp.where(core == 0, -hops, hops), chips)
    chip = jnp.where(at < chips // 2, 2 * at, 2 * (chips - 1 - at) + 1)
    return 2 * chip + (1 - core if other else core)


def pieces_kernel(places, sizes, packed, first, last, table_ref, given_ref, labels_ref, *rest):
    rest = list(rest)
    arrays = [rest.pop(0) for _ in sizes]
    before_ref = None if first else rest.pop(0)
    grad_ref = rest.pop(0)
    parts_ref = rest.pop(0) if first else given_ref
    pack_ref = rest.pop(0) if packed else None
    square_ref = rest.pop(0) if last else None
    tiles, slots = rest
    tile = tiles.shape[0] // CHUNK
    for at, index in enumerate(packed):
        pack_ref[at * tile : (at + 1) * tile, :] = arrays[index][...]
    if first:
        parts_ref[...] = halves(0.5 * given_ref[...])
        grad_ref[...] = jnp.zeros_like(grad_ref)
    else:
        grad_ref[...] = before_ref[...]
    live = jnp.int32(0)
    for at, index, row in places:
        found = table_ref[at]

        @pl.when(found >= 0)
        def _():
            into = pl.ds(pl.multiple_of(live * tile, tile), tile)
            tiles[into, :] = arrays[index][row * tile : (row + 1) * tile, :]
            slots[live] = found

        live = live + (found >= 0).astype(jnp.int32)
    slots[live] = 0

    def labels_at(position):
        return labels_ref[:, pl.ds(pl.multiple_of(slots[position] * tile, tile), tile)]

    add_tiles(grad_ref, parts_ref, tiles, live, min(len(places), CHUNK), labels_at)
    if last:
        store_square(grad_ref, square_ref)


def add_pieces(held, packed, loop_size, table, given, labels, before, last):
    first = before is None
    width = given.shape[1]
    rows = given.shape[0] // (1 if first else 2)
    arrays = [array for array, _ in held]
    tile = arrays[0].shape[0] // len(held[0][1])
    places = [(at, index, row) for index, (_, entries) in enumerate(held) for row, at in enumerate(entries)]
    most = min(len(places), CHUNK)
    out_shape = [jax.ShapeDtypeStruct((rows, width), jnp.float32)]
    if first:
        out_shape.append(jax.ShapeDtypeStruct((2 * rows, width), jnp.bfloat16))
    if packed:
        out_shape.append(jax.ShapeDtypeStruct((len(packed) * tile, width), jnp.bfloat16))
    if last:
        out_shape.append(jax.ShapeDtypeStruct((loop_size, 128), jnp.float32))
    extra = [] if first else [before]
    return pl.pallas_call(
        functools.partial(pieces_kernel, places, [a.shape for a in arrays], packed, first, last),
        out_shape=out_shape,
        in_specs=[pl.BlockSpec(memory_space=pltpu.SMEM)]
        + [pl.BlockSpec(memory_space=pltpu.VMEM)] * (2 + len(arrays) + len(extra)),
        out_specs=[pl.BlockSpec(memory_space=pltpu.VMEM)] * len(out_shape),
        scratch_shapes=[
            pltpu.VMEM((CHUNK * tile, width), jnp.bfloat16),
            pltpu.SMEM((CHUNK + 1,), jnp.int32),
        ],
        compiler_params=pltpu.CompilerParams(vmem_limit_bytes=24 * 1024 * 1024),
        cost_estimate=pl.CostEstimate(
            flops=128 * rows * width * most * tile,
            bytes_accessed=8 * rows * width,
            transcendentals=rows * most * tile,
        ),
        name="add_pieces",
    )(table, given, labels, *arrays, *extra)


def ring_gradient(users, items, lists, labels):
    loop_size = lax.axis_size("loop")
    far = loop_size // 4
    origins = [(hops, 0) for hops in range(1 - far, far + 1)]
    origins += [(-hops, 1) for hops, _ in origins]
    table = slot_table(loop_size, origins, *lists)
    where = {origin: at for at, origin in enumerate(origins)}

    def held(hops, array):
        return array, [where[hops, 0]]

    def other(arrays, hops):
        return to_other_core(arrays, loop_size), [where[-hop, 1] for hop in hops]

    up = to_next(items, 1, loop_size)
    down = to_next(items, -1, loop_size)
    up, table = lax.optimization_barrier((up, table))
    here, hops, early, late = [held(0, items), held(1, up), held(-1, down)], [0, 1, -1], [], []
    given, gradient = users, None
    for hop in range(2, far + 1):
        up = to_next(up, 1, loop_size)
        if hop < far:
            down = to_next(down, -1, loop_size)
        if gradient is None:
            gradient, given, pack = add_pieces(
                here, [0, 1, 2], loop_size, table, given, labels, None, False
            )
        else:
            gradient, pack = add_pieces(
                here + early, [0, 1], loop_size, table, given, labels, gradient, False
            )
        up, gradient = lax.optimization_barrier((up, gradient))
        early, late = late, [other(pack, hops)]
        here, hops = [held(hop, up)], [hop, -hop]
        if hop < far:
            here.append(held(-hop, down))
    final = other(up, [far])
    (gradient,) = add_pieces(early, [], loop_size, table, given, labels, gradient, False)
    final = here + late + [final]
    return *add_pieces(final, [], loop_size, table, given, labels, gradient, True), users


def chunks_kernel(
    list_ref, count_ref, users_ref, labels_ref, items_ref, grad_ref, square_ref, tiles, parts_ref, sems
):
    tile = tiles.shape[0] // CHUNK
    step = pl.program_id(0)
    live = jnp.clip(count_ref[0] - step * CHUNK, 0, CHUNK)

    @pl.when(step == 0)
    def _():
        parts_ref[...] = halves(0.5 * users_ref[...])
        grad_ref[...] = jnp.zeros_like(grad_ref)

    def move(slot):
        start = pl.multiple_of(list_ref[0, step * CHUNK + slot] * tile, tile)
        return pltpu.make_async_copy(
            items_ref.at[pl.ds(start, tile), :], tiles.at[pl.ds(slot * tile, tile), :], sems.at[slot]
        )

    for slot in range(CHUNK):
        pl.when(slot < live)(lambda slot=slot: move(slot).start())
    for slot in range(CHUNK):
        pl.when(slot < live)(lambda slot=slot: move(slot).wait())

    def labels_at(position):
        return labels_ref[:, pl.ds(pl.multiple_of(position * tile, tile), tile)]

    add_tiles(grad_ref, parts_ref, tiles, live, CHUNK, labels_at)

    @pl.when(step == pl.num_programs(0) - 1)
    def _():
        store_square(grad_ref, square_ref)


def add_chunks(loop_size, items, lists, users, labels):
    rows, width = users.shape
    slots = lists[0].shape[1]
    tile = labels.shape[1] // slots
    return pl.pallas_call(
        chunks_kernel,
        grid=(slots // CHUNK,),
        out_shape=[
            jax.ShapeDtypeStruct((rows, width), jnp.float32),
            jax.ShapeDtypeStruct((loop_size, 128), jnp.float32),
        ],
        in_specs=[
            pl.BlockSpec(memory_space=pltpu.SMEM),
            pl.BlockSpec(memory_space=pltpu.SMEM),
            pl.BlockSpec((rows, width), lambda step: (0, 0)),
            pl.BlockSpec((rows, CHUNK * tile), lambda step: (0, step)),
            pl.BlockSpec(memory_space=pl.ANY),
        ],
        out_specs=[
            pl.BlockSpec((rows, width), lambda step: (0, 0)),
            pl.BlockSpec((loop_size, 128), lambda step: (0, 0)),
        ],
        scratch_shapes=[
            pltpu.VMEM((CHUNK * tile, width), jnp.bfloat16),
            pltpu.VMEM((2 * rows, width), jnp.bfloat16),
            pltpu.SemaphoreType.DMA((CHUNK,)),
        ],
        compiler_params=pltpu.CompilerParams(vmem_limit_bytes=32 * 1024 * 1024),
        cost_estimate=pl.CostEstimate(
            flops=8 * rows * width * slots * tile,
            bytes_accessed=4 * rows * (slots * tile + 2 * width) + 2 * slots * tile * width,
            transcendentals=rows * slots * tile,
        ),
        name="add_chunks",
    )(*lists, users, labels, items)


def update_kernel(entries, users_ref, grad_ref, squares_ref, out_ref):
    total = jnp.sum(squares_ref[...], axis=0, keepdims=True)
    total = jnp.sum(total, axis=1, keepdims=True)
    scale = 0.5 / jnp.sqrt(total / entries + 1e-06)
    out_ref[...] = users_ref[...] - scale * grad_ref[...]


def local(users, items, tile_blocks, tile_count, labels):
    loop_size = lax.axis_size("loop")
    rows, width = users.shape
    slots = tile_blocks.shape[1]
    lists = (tile_blocks, tile_count)
    if loop_size <= RING_LIMIT and loop_size % 8 == 0 and slots <= CHUNK:
        gradient, square, users = ring_gradient(users, items, lists, labels)
    else:
        whole = lax.all_gather(items, "loop", axis=0, tiled=True)
        gradient, square = add_chunks(loop_size, whole, lists, users, labels)

    squares = lax.all_to_all(square, "loop", 0, 0, tiled=True)
    return pl.pallas_call(
        functools.partial(update_kernel, rows * loop_size * width),
        out_shape=jax.ShapeDtypeStruct((rows, width), jnp.float32),
        in_specs=[pl.BlockSpec(memory_space=pltpu.VMEM)] * 3,
        out_specs=pl.BlockSpec(memory_space=pltpu.VMEM),
        compiler_params=pltpu.CompilerParams(vmem_limit_bytes=16 * 1024 * 1024),
        cost_estimate=pl.CostEstimate(
            flops=2 * rows * width, bytes_accessed=12 * rows * width, transcendentals=0
        ),
        name="update",
    )(users, gradient, squares)


def solution(mesh):
    in_specs = (
        P(("group", "loop"), None),
        P(("group", "loop"), None),
        P(("group", "loop"), None),
        P(("group", "loop")),
        P(("group", "loop"), None),
    )
    out_specs = P(("group", "loop"), None)
    return jax.shard_map(local, mesh=mesh, in_specs=in_specs, out_specs=out_specs, check_vma=False)
```

```python
import functools

import jax
import jax.numpy as jnp
from jax import lax
from jax.experimental import pallas as pl
from jax.experimental.pallas import tpu as pltpu
from jax.sharding import PartitionSpec as P

CHUNK = 8
RING = 16


def ring_place(loop_size):
    outer = loop_size // 4

    def device(position, core):
        position = position % (2 * outer)
        chip = 2 * position if position < outer else 2 * (2 * outer - 1 - position) + 1
        return 2 * chip + core

    return 2 * outer, device


def to_next(array, direction, loop_size):
    chips, device = ring_place(loop_size)
    pairs = [(device(at, 0), device(at + direction, 0)) for at in range(chips)]
    pairs += [(device(at, 1), device(at - direction, 1)) for at in range(chips)]
    return lax.ppermute(array, "loop", pairs)


def across(array, loop_size):
    chips, device = ring_place(loop_size)
    pairs = [
        (device(at, core), device(at + (3 if at % 2 == 0 else -3), core))
        for at in range(chips)
        for core in range(2)
    ]
    return lax.ppermute(array, "loop", pairs)


def to_other_core(array, loop_size):
    return lax.ppermute(array, "loop", [(at, at ^ 1) for at in range(loop_size)])


def halves(values):
    upper = values.astype(jnp.bfloat16)
    return jnp.concatenate([upper, (values - upper.astype(jnp.float32)).astype(jnp.bfloat16)], 0)


def table_kernel(loop_size, origins, list_ref, count_ref, table_ref):
    wanted = [
        jnp.where(slot < count_ref[0], list_ref[0, slot], -1) for slot in range(list_ref.shape[1])
    ]
    for at, origin in enumerate(origins):
        block = origin_block(origin, loop_size)
        found = jnp.int32(-1)
        for slot, name in enumerate(wanted):
            found = jnp.where(name == block, slot, found)
        table_ref[at] = found


def slot_table(loop_size, origins, block_list, live_count):
    return pl.pallas_call(
        functools.partial(table_kernel, loop_size, origins),
        out_shape=jax.ShapeDtypeStruct((len(origins),), jnp.int32),
        in_specs=[pl.BlockSpec(memory_space=pltpu.SMEM)] * 2,
        out_specs=pl.BlockSpec(memory_space=pltpu.SMEM),
        cost_estimate=pl.CostEstimate(flops=2**32, bytes_accessed=1024, transcendentals=0),
        name="slot_table",
    )(block_list, live_count)


def add_some(grad_ref, parts_ref, tiles, start, count, labels_at):
    rows = grad_ref.shape[0]
    tile = tiles.shape[0] // CHUNK
    block = tiles[pl.ds(pl.multiple_of(start * tile, 2 * tile), count * tile), :]
    upper, lower = [], []
    for at in range(0, count, 2):
        both = lax.dot_general(
            parts_ref[...],
            block[at * tile : (at + 2) * tile],
            (((1,), (1,)), ((), ())),
            preferred_element_type=jnp.float32,
        )
        labels = jnp.concatenate([labels_at(start + at), labels_at(start + at + 1)], 1)
        residual = 0.5 * jnp.tanh(both[:rows] + both[rows:]) + (0.5 - labels.astype(jnp.float32))
        upper.append(residual.astype(jnp.bfloat16))
        lower.append((residual - upper[-1].astype(jnp.float32)).astype(jnp.bfloat16))
    grad_ref[...] += jnp.dot(
        jnp.concatenate(upper + lower, 1),
        jnp.concatenate([block, block], 0),
        preferred_element_type=jnp.float32,
    )


def add_tiles(grad_ref, parts_ref, tiles, live, most, labels_at):
    tile = tiles.shape[0] // CHUNK

    @pl.when(live % 2 == 1)
    def _():
        blank = pl.multiple_of(live * tile, tile)
        tiles[pl.ds(blank, tile), :] = jnp.zeros((tile, tiles.shape[1]), tiles.dtype)

    fours = (live + 1) // 4 if most > 2 else jnp.int32(0)
    if most > 2:

        def four(index, carry):
            add_some(grad_ref, parts_ref, tiles, index * 4, 4, labels_at)
            return carry

        lax.fori_loop(0, fours, four, 0)

    @pl.when(live > 4 * fours)
    def _():
        add_some(grad_ref, parts_ref, tiles, 4 * fours, 2, labels_at)


def store_square(grad_ref, square_ref):
    gradient = grad_ref[...]
    square = jnp.sum(gradient * gradient, axis=0, keepdims=True)
    square = sum(square[:, at : at + 128] for at in range(0, square.shape[1], 128))
    square_ref[...] = jnp.broadcast_to(square, square_ref.shape)


def core_and_position(loop_size):
    me = lax.axis_index("loop")
    core, row, outer = me % 2, me // 2 % 2, me // 4
    return core, jnp.where(row == 0, outer, loop_size // 2 - 1 - outer)


def origin_block(origin, loop_size):
    hops, other = origin
    chips = loop_size // 2
    core, position = core_and_position(loop_size)
    at = lax.rem(position + chips + jnp.where(core == 0, -hops, hops), chips)
    chip = jnp.where(at < chips // 2, 2 * at, 2 * (chips - 1 - at) + 1)
    return 2 * chip + (1 - core if other else core)


def pieces_kernel(places, count, packed, loop_size, first, last, table_ref, given_ref, labels_ref, *rest):
    rest = list(rest)
    arrays = [rest.pop(0) for _ in range(count)]
    if not first:
        rest.pop(0)
    grad_ref = rest.pop(0)
    parts_ref = rest.pop(0) if first else given_ref
    across_ref = rest.pop(0) if first else None
    pack_ref = rest.pop(0) if packed else None
    square_ref = rest.pop(0) if last else None
    tiles, slots = rest
    tile = tiles.shape[0] // CHUNK
    for at, index in enumerate(packed):
        pack_ref[at * tile : (at + 1) * tile, :] = arrays[index][...]
    if first:
        core, position = core_and_position(loop_size)
        for at in range(2):

            @pl.when((core + position) % 2 == at)
            def _():
                across_ref[...] = arrays[1 + at][...]

        parts_ref[...] = halves(0.5 * given_ref[...])
        grad_ref[...] = jnp.zeros_like(grad_ref)
    live = jnp.int32(0)
    for at, index, row in places:
        found = table_ref[at]

        @pl.when(found >= 0)
        def _():
            into = pl.ds(pl.multiple_of(live * tile, tile), tile)
            tiles[into, :] = arrays[index][row * tile : (row + 1) * tile, :]
            slots[live] = found

        live = live + (found >= 0).astype(jnp.int32)
    slots[live] = 0

    def labels_at(position):
        return labels_ref[:, pl.ds(pl.multiple_of(slots[position] * tile, tile), tile)]

    add_tiles(grad_ref, parts_ref, tiles, live, min(len(places), CHUNK), labels_at)
    if last:
        store_square(grad_ref, square_ref)


def add_pieces(held, packed, loop_size, table, given, labels, before, last):
    first = before is None
    width = given.shape[1]
    rows = given.shape[0] // (1 if first else 2)
    arrays = [array for array, _ in held]
    tile = labels.shape[1] // CHUNK
    places = [(at, index, row) for index, (_, entries) in enumerate(held) for row, at in enumerate(entries)]
    most = min(len(places), CHUNK)
    out_shape = [jax.ShapeDtypeStruct((rows, width), jnp.float32)]
    if first:
        out_shape.append(jax.ShapeDtypeStruct((2 * rows, width), jnp.bfloat16))
        out_shape.append(jax.ShapeDtypeStruct((tile, width), jnp.bfloat16))
    if packed:
        out_shape.append(jax.ShapeDtypeStruct((len(packed) * tile, width), jnp.bfloat16))
    if last:
        out_shape.append(jax.ShapeDtypeStruct((loop_size, 128), jnp.float32))
    extra = [] if first else [before]
    return pl.pallas_call(
        functools.partial(pieces_kernel, places, len(arrays), packed, loop_size, first, last),
        out_shape=out_shape,
        in_specs=[pl.BlockSpec(memory_space=pltpu.SMEM)]
        + [pl.BlockSpec(memory_space=pltpu.VMEM)] * (2 + len(arrays) + len(extra)),
        out_specs=[pl.BlockSpec(memory_space=pltpu.VMEM)] * len(out_shape),
        input_output_aliases={} if first else {3 + len(arrays): 0},
        scratch_shapes=[
            pltpu.VMEM((CHUNK * tile, width), jnp.bfloat16),
            pltpu.SMEM((CHUNK + 1,), jnp.int32),
        ],
        compiler_params=pltpu.CompilerParams(vmem_limit_bytes=24 * 1024 * 1024),
        cost_estimate=pl.CostEstimate(
            flops=128 * rows * width * most * tile,
            bytes_accessed=8 * rows * width,
            transcendentals=rows * most * tile,
        ),
        name="add_pieces",
    )(table, given, labels, *arrays, *extra)


def ring_gradient(users, items, lists, labels):
    loop_size = lax.axis_size("loop")
    far = loop_size // 4
    origins = [(hops, 0) for hops in range(1 - far, far + 1)]
    origins += [(-hops, 1) for hops, _ in origins]
    table = slot_table(loop_size, origins, *lists)
    where = {origin: at for at, origin in enumerate(origins)}

    def held(hops, array):
        return array, [where[hops, 0]]

    def other(arrays, hops):
        return to_other_core(arrays, loop_size), [where[-hop, 1] for hop in hops]

    up = to_next(items, 1, loop_size)
    down = to_next(items, -1, loop_size)
    up, table = lax.optimization_barrier((up, table))
    first = [held(0, items), held(1, up), held(-1, down)]
    second = [held(2, to_next(up, 1, loop_size)), held(-2, to_next(down, -1, loop_size))]
    gradient, parts, opposite, pack = add_pieces(
        first, [0, 1, 2], loop_size, table, users, labels, None, False
    )
    opposite = across(opposite, loop_size)
    first = other(pack, [0, 1, -1])
    third = [held(3, to_next(second[0][0], 1, loop_size)), held(-3, to_next(second[1][0], -1, loop_size))]
    gradient, pack = add_pieces(second, [0, 1], loop_size, table, parts, labels, gradient, False)
    second = other(pack, [2, -2])
    third.append(held(4, opposite))
    gradient, pack = add_pieces(third, [0, 1, 2], loop_size, table, parts, labels, gradient, False)
    third = other(pack, [3, -3, 4])
    (gradient,) = add_pieces([first, second], [], loop_size, table, parts, labels, gradient, False)
    return *add_pieces([third], [], loop_size, table, parts, labels, gradient, True), users


def chunks_kernel(
    list_ref, count_ref, users_ref, labels_ref, items_ref, grad_ref, square_ref, tiles, parts_ref, sems
):
    tile = tiles.shape[0] // CHUNK
    step = pl.program_id(0)
    live = jnp.clip(count_ref[0] - step * CHUNK, 0, CHUNK)

    @pl.when(step == 0)
    def _():
        parts_ref[...] = halves(0.5 * users_ref[...])
        grad_ref[...] = jnp.zeros_like(grad_ref)

    def move(slot):
        start = pl.multiple_of(list_ref[0, step * CHUNK + slot] * tile, tile)
        return pltpu.make_async_copy(
            items_ref.at[pl.ds(start, tile), :], tiles.at[pl.ds(slot * tile, tile), :], sems.at[slot]
        )

    for slot in range(CHUNK):
        pl.when(slot < live)(lambda slot=slot: move(slot).start())
    for slot in range(CHUNK):
        pl.when(slot < live)(lambda slot=slot: move(slot).wait())

    def labels_at(position):
        return labels_ref[:, pl.ds(pl.multiple_of(position * tile, tile), tile)]

    add_tiles(grad_ref, parts_ref, tiles, live, CHUNK, labels_at)

    @pl.when(step == pl.num_programs(0) - 1)
    def _():
        store_square(grad_ref, square_ref)


def add_chunks(loop_size, items, lists, users, labels):
    rows, width = users.shape
    slots = lists[0].shape[1]
    tile = labels.shape[1] // slots
    return pl.pallas_call(
        chunks_kernel,
        grid=(slots // CHUNK,),
        out_shape=[
            jax.ShapeDtypeStruct((rows, width), jnp.float32),
            jax.ShapeDtypeStruct((loop_size, 128), jnp.float32),
        ],
        in_specs=[
            pl.BlockSpec(memory_space=pltpu.SMEM),
            pl.BlockSpec(memory_space=pltpu.SMEM),
            pl.BlockSpec((rows, width), lambda step: (0, 0)),
            pl.BlockSpec((rows, CHUNK * tile), lambda step: (0, step)),
            pl.BlockSpec(memory_space=pl.ANY),
        ],
        out_specs=[
            pl.BlockSpec((rows, width), lambda step: (0, 0)),
            pl.BlockSpec((loop_size, 128), lambda step: (0, 0)),
        ],
        scratch_shapes=[
            pltpu.VMEM((CHUNK * tile, width), jnp.bfloat16),
            pltpu.VMEM((2 * rows, width), jnp.bfloat16),
            pltpu.SemaphoreType.DMA((CHUNK,)),
        ],
        compiler_params=pltpu.CompilerParams(vmem_limit_bytes=32 * 1024 * 1024),
        cost_estimate=pl.CostEstimate(
            flops=8 * rows * width * slots * tile,
            bytes_accessed=4 * rows * (slots * tile + 2 * width) + 2 * slots * tile * width,
            transcendentals=rows * slots * tile,
        ),
        name="add_chunks",
    )(*lists, users, labels, items)


def update_kernel(entries, users_ref, grad_ref, squares_ref, out_ref):
    total = jnp.sum(squares_ref[...], axis=0, keepdims=True)
    total = jnp.sum(total, axis=1, keepdims=True)
    scale = 0.5 / jnp.sqrt(total / entries + 1e-06)
    out_ref[...] = users_ref[...] - scale * grad_ref[...]


def local(users, items, tile_blocks, tile_count, labels):
    loop_size = lax.axis_size("loop")
    rows, width = users.shape
    slots = tile_blocks.shape[1]
    lists = (tile_blocks, tile_count)
    if loop_size == RING and slots == CHUNK:
        gradient, square, users = ring_gradient(users, items, lists, labels)
    else:
        whole = lax.all_gather(items, "loop", axis=0, tiled=True)
        gradient, square = add_chunks(loop_size, whole, lists, users, labels)

    squares = lax.all_to_all(square, "loop", 0, 0, tiled=True)
    return pl.pallas_call(
        functools.partial(update_kernel, rows * loop_size * width),
        out_shape=jax.ShapeDtypeStruct((rows, width), jnp.float32),
        in_specs=[pl.BlockSpec(memory_space=pltpu.VMEM)] * 3,
        out_specs=pl.BlockSpec(memory_space=pltpu.VMEM),
        compiler_params=pltpu.CompilerParams(vmem_limit_bytes=16 * 1024 * 1024),
        cost_estimate=pl.CostEstimate(
            flops=2 * rows * width, bytes_accessed=12 * rows * width, transcendentals=0
        ),
        name="update",
    )(users, gradient, squares)


def solution(mesh):
    in_specs = (
        P(("group", "loop"), None),
        P(("group", "loop"), None),
        P(("group", "loop"), None),
        P(("group", "loop")),
        P(("group", "loop"), None),
    )
    out_specs = P(("group", "loop"), None)
    return jax.shard_map(local, mesh=mesh, in_specs=in_specs, out_specs=out_specs, check_vma=False)
```

```python
import functools

import jax
import jax.numpy as jnp
from jax import lax
from jax.experimental import pallas as pl
from jax.experimental.pallas import tpu as pltpu
from jax.sharding import PartitionSpec as P

CHUNK = 8
RING = 16


def ring_place(loop_size):
    outer = loop_size // 4

    def device(position, core):
        position = position % (2 * outer)
        chip = 2 * position if position < outer else 2 * (2 * outer - 1 - position) + 1
        return 2 * chip + core

    return 2 * outer, device


def to_next(array, direction, loop_size):
    chips, device = ring_place(loop_size)
    pairs = [(device(at, 0), device(at + direction, 0)) for at in range(chips)]
    pairs += [(device(at, 1), device(at - direction, 1)) for at in range(chips)]
    return lax.ppermute(array, "loop", pairs)


def across(array, loop_size):
    chips, device = ring_place(loop_size)
    pairs = [
        (device(at, core), device(at + (3 if at % 2 == 0 else -3), core))
        for at in range(chips)
        for core in range(2)
    ]
    return lax.ppermute(array, "loop", pairs)


def to_other_core(array, loop_size):
    return lax.ppermute(array, "loop", [(at, at ^ 1) for at in range(loop_size)])


def halves(values):
    upper = values.astype(jnp.bfloat16)
    return jnp.concatenate([upper, (values - upper.astype(jnp.float32)).astype(jnp.bfloat16)], 0)


def table_kernel(loop_size, origins, list_ref, count_ref, table_ref):
    wanted = [
        jnp.where(slot < count_ref[0], list_ref[0, slot], -1) for slot in range(list_ref.shape[1])
    ]
    for at, origin in enumerate(origins):
        block = origin_block(origin, loop_size)
        found = jnp.int32(-1)
        for slot, name in enumerate(wanted):
            found = jnp.where(name == block, slot, found)
        table_ref[at] = found


def slot_table(loop_size, origins, block_list, live_count):
    return pl.pallas_call(
        functools.partial(table_kernel, loop_size, origins),
        out_shape=jax.ShapeDtypeStruct((len(origins),), jnp.int32),
        in_specs=[pl.BlockSpec(memory_space=pltpu.SMEM)] * 2,
        out_specs=pl.BlockSpec(memory_space=pltpu.SMEM),
        cost_estimate=pl.CostEstimate(flops=2**32, bytes_accessed=1024, transcendentals=0),
        name="slot_table",
    )(block_list, live_count)


def add_some(grad_ref, parts_ref, tiles, start, count, labels_at):
    rows = grad_ref.shape[0]
    tile = tiles.shape[0] // CHUNK
    block = tiles[pl.ds(pl.multiple_of(start * tile, 2 * tile), count * tile), :]
    upper, lower = [], []
    for at in range(0, count, 2):
        both = lax.dot_general(
            parts_ref[...],
            block[at * tile : (at + 2) * tile],
            (((1,), (1,)), ((), ())),
            preferred_element_type=jnp.float32,
        )
        labels = jnp.concatenate([labels_at(start + at), labels_at(start + at + 1)], 1)
        residual = 0.5 * jnp.tanh(both[:rows] + both[rows:]) + (0.5 - labels.astype(jnp.float32))
        upper.append(residual.astype(jnp.bfloat16))
        lower.append((residual - upper[-1].astype(jnp.float32)).astype(jnp.bfloat16))
    grad_ref[...] += jnp.dot(
        jnp.concatenate(upper + lower, 1),
        jnp.concatenate([block, block], 0),
        preferred_element_type=jnp.float32,
    )


def add_tiles(grad_ref, parts_ref, tiles, live, most, labels_at):
    tile = tiles.shape[0] // CHUNK

    @pl.when(live % 2 == 1)
    def _():
        blank = pl.multiple_of(live * tile, tile)
        tiles[pl.ds(blank, tile), :] = jnp.zeros((tile, tiles.shape[1]), tiles.dtype)

    fours = (live + 1) // 4 if most > 2 else jnp.int32(0)
    if most > 2:

        def four(index, carry):
            add_some(grad_ref, parts_ref, tiles, index * 4, 4, labels_at)
            return carry

        lax.fori_loop(0, fours, four, 0)

    @pl.when(live > 4 * fours)
    def _():
        add_some(grad_ref, parts_ref, tiles, 4 * fours, 2, labels_at)


def store_square(grad_ref, square_ref):
    gradient = grad_ref[...]
    square = jnp.sum(gradient * gradient, axis=0, keepdims=True)
    square = sum(square[:, at : at + 128] for at in range(0, square.shape[1], 128))
    square_ref[...] = jnp.broadcast_to(square, square_ref.shape)


def core_and_position(loop_size):
    me = lax.axis_index("loop")
    core, row, outer = me % 2, me // 2 % 2, me // 4
    return core, jnp.where(row == 0, outer, loop_size // 2 - 1 - outer)


def origin_block(origin, loop_size):
    hops, other = origin
    chips = loop_size // 2
    core, position = core_and_position(loop_size)
    at = lax.rem(position + chips + jnp.where(core == 0, -hops, hops), chips)
    chip = jnp.where(at < chips // 2, 2 * at, 2 * (chips - 1 - at) + 1)
    return 2 * chip + (1 - core if other else core)


def pack_kernel(*refs):
    tile = refs[0].shape[0]
    for at, ref in enumerate(refs[:-1]):
        refs[-1][at * tile : (at + 1) * tile, :] = ref[...]


def pick_kernel(loop_size, ahead_ref, behind_ref, picked_ref):
    core, position = core_and_position(loop_size)
    for at, ref in enumerate((ahead_ref, behind_ref)):

        @pl.when((core + position) % 2 == at)
        def _():
            picked_ref[...] = ref[...]


def copies(kernel, name, rows, *arrays):
    width = arrays[0].shape[1]
    return pl.pallas_call(
        kernel,
        out_shape=jax.ShapeDtypeStruct((rows, width), arrays[0].dtype),
        in_specs=[pl.BlockSpec(memory_space=pltpu.VMEM)] * len(arrays),
        out_specs=pl.BlockSpec(memory_space=pltpu.VMEM),
        compiler_params=pltpu.CompilerParams(vmem_limit_bytes=16 * 1024 * 1024),
        cost_estimate=pl.CostEstimate(
            flops=2**34, bytes_accessed=4 * rows * width, transcendentals=0
        ),
        name=name,
    )(*arrays)


def pack(arrays):
    return copies(pack_kernel, "pack", sum(array.shape[0] for array in arrays), *arrays)


def pieces_kernel(places, count, packed, first, last, table_ref, given_ref, labels_ref, *rest):
    rest = list(rest)
    arrays = [rest.pop(0) for _ in range(count)]
    if not first:
        rest.pop(0)
    grad_ref = rest.pop(0)
    parts_ref = rest.pop(0) if first else given_ref
    pack_ref = rest.pop(0) if packed else None
    square_ref = rest.pop(0) if last else None
    tiles, slots = rest
    tile = tiles.shape[0] // CHUNK
    for at, index in enumerate(packed):
        pack_ref[at * tile : (at + 1) * tile, :] = arrays[index][...]
    if first:
        parts_ref[...] = halves(0.5 * given_ref[...])
        grad_ref[...] = jnp.zeros_like(grad_ref)
    live = jnp.int32(0)
    for at, index, row in places:
        found = table_ref[at]

        @pl.when(found >= 0)
        def _():
            into = pl.ds(pl.multiple_of(live * tile, tile), tile)
            tiles[into, :] = arrays[index][row * tile : (row + 1) * tile, :]
            slots[live] = found

        live = live + (found >= 0).astype(jnp.int32)
    slots[live] = 0

    def labels_at(position):
        return labels_ref[:, pl.ds(pl.multiple_of(slots[position] * tile, tile), tile)]

    add_tiles(grad_ref, parts_ref, tiles, live, min(len(places), CHUNK), labels_at)
    if last:
        store_square(grad_ref, square_ref)


def add_pieces(held, packed, loop_size, table, given, labels, before, last):
    first = before is None
    width = given.shape[1]
    rows = given.shape[0] // (1 if first else 2)
    arrays = [array for array, _ in held]
    tile = labels.shape[1] // CHUNK
    places = [(at, index, row) for index, (_, entries) in enumerate(held) for row, at in enumerate(entries)]
    most = min(len(places), CHUNK)
    out_shape = [jax.ShapeDtypeStruct((rows, width), jnp.float32)]
    if first:
        out_shape.append(jax.ShapeDtypeStruct((2 * rows, width), jnp.bfloat16))
    if packed:
        out_shape.append(jax.ShapeDtypeStruct((len(packed) * tile, width), jnp.bfloat16))
    if last:
        out_shape.append(jax.ShapeDtypeStruct((loop_size, 128), jnp.float32))
    extra = [] if first else [before]
    return pl.pallas_call(
        functools.partial(pieces_kernel, places, len(arrays), packed, first, last),
        out_shape=out_shape,
        in_specs=[pl.BlockSpec(memory_space=pltpu.SMEM)]
        + [pl.BlockSpec(memory_space=pltpu.VMEM)] * (2 + len(arrays) + len(extra)),
        out_specs=[pl.BlockSpec(memory_space=pltpu.VMEM)] * len(out_shape),
        input_output_aliases={} if first else {3 + len(arrays): 0},
        scratch_shapes=[
            pltpu.VMEM((CHUNK * tile, width), jnp.bfloat16),
            pltpu.SMEM((CHUNK + 1,), jnp.int32),
        ],
        compiler_params=pltpu.CompilerParams(vmem_limit_bytes=24 * 1024 * 1024),
        cost_estimate=pl.CostEstimate(
            flops=128 * rows * width * most * tile,
            bytes_accessed=8 * rows * width,
            transcendentals=rows * most * tile,
        ),
        name="add_pieces",
    )(table, given, labels, *arrays, *extra)


def ring_gradient(users, items, lists, labels):
    loop_size = lax.axis_size("loop")
    far = loop_size // 4
    origins = [(hops, 0) for hops in range(1 - far, far + 1)]
    origins += [(-hops, 1) for hops, _ in origins]
    table = slot_table(loop_size, origins, *lists)
    where = {origin: at for at, origin in enumerate(origins)}

    def held(hops, array):
        return array, [where[hops, 0]]

    def other(arrays, hops):
        return to_other_core(arrays, loop_size), [where[-hop, 1] for hop in hops]

    up = to_next(items, 1, loop_size)
    down = to_next(items, -1, loop_size)
    up, table = lax.optimization_barrier((up, table))
    first = [held(0, items), held(1, up), held(-1, down)]
    opposite = copies(functools.partial(pick_kernel, loop_size), "pick", up.shape[0], up, down)
    opposite = across(opposite, loop_size)
    first += [held(2, to_next(up, 1, loop_size)), held(-2, to_next(down, -1, loop_size))]
    then = [held(3, to_next(first[3][0], 1, loop_size)), held(-3, to_next(first[4][0], -1, loop_size))]
    then.append(held(4, opposite))
    gradient, parts, packed = add_pieces(
        first, [0, 1, 2, 3, 4], loop_size, table, users, labels, None, False
    )
    given = other(packed, [0, 1, -1, 2, -2])
    arrived, gradient = lax.optimization_barrier(([array for array, _ in then], gradient))
    last = other(pack(arrived), [3, -3, 4])
    (gradient,) = add_pieces(then + [given], [], loop_size, table, parts, labels, gradient, False)
    return *add_pieces([last], [], loop_size, table, parts, labels, gradient, True), users


def chunks_kernel(
    list_ref, count_ref, users_ref, labels_ref, items_ref, grad_ref, square_ref, tiles, parts_ref, sems
):
    tile = tiles.shape[0] // CHUNK
    step = pl.program_id(0)
    live = jnp.clip(count_ref[0] - step * CHUNK, 0, CHUNK)

    @pl.when(step == 0)
    def _():
        parts_ref[...] = halves(0.5 * users_ref[...])
        grad_ref[...] = jnp.zeros_like(grad_ref)

    def move(slot):
        start = pl.multiple_of(list_ref[0, step * CHUNK + slot] * tile, tile)
        return pltpu.make_async_copy(
            items_ref.at[pl.ds(start, tile), :], tiles.at[pl.ds(slot * tile, tile), :], sems.at[slot]
        )

    for slot in range(CHUNK):
        pl.when(slot < live)(lambda slot=slot: move(slot).start())
    for slot in range(CHUNK):
        pl.when(slot < live)(lambda slot=slot: move(slot).wait())

    def labels_at(position):
        return labels_ref[:, pl.ds(pl.multiple_of(position * tile, tile), tile)]

    add_tiles(grad_ref, parts_ref, tiles, live, CHUNK, labels_at)

    @pl.when(step == pl.num_programs(0) - 1)
    def _():
        store_square(grad_ref, square_ref)


def add_chunks(loop_size, items, lists, users, labels):
    rows, width = users.shape
    slots = lists[0].shape[1]
    tile = labels.shape[1] // slots
    return pl.pallas_call(
        chunks_kernel,
        grid=(slots // CHUNK,),
        out_shape=[
            jax.ShapeDtypeStruct((rows, width), jnp.float32),
            jax.ShapeDtypeStruct((loop_size, 128), jnp.float32),
        ],
        in_specs=[
            pl.BlockSpec(memory_space=pltpu.SMEM),
            pl.BlockSpec(memory_space=pltpu.SMEM),
            pl.BlockSpec((rows, width), lambda step: (0, 0)),
            pl.BlockSpec((rows, CHUNK * tile), lambda step: (0, step)),
            pl.BlockSpec(memory_space=pl.ANY),
        ],
        out_specs=[
            pl.BlockSpec((rows, width), lambda step: (0, 0)),
            pl.BlockSpec((loop_size, 128), lambda step: (0, 0)),
        ],
        scratch_shapes=[
            pltpu.VMEM((CHUNK * tile, width), jnp.bfloat16),
            pltpu.VMEM((2 * rows, width), jnp.bfloat16),
            pltpu.SemaphoreType.DMA((CHUNK,)),
        ],
        compiler_params=pltpu.CompilerParams(vmem_limit_bytes=32 * 1024 * 1024),
        cost_estimate=pl.CostEstimate(
            flops=8 * rows * width * slots * tile,
            bytes_accessed=4 * rows * (slots * tile + 2 * width) + 2 * slots * tile * width,
            transcendentals=rows * slots * tile,
        ),
        name="add_chunks",
    )(*lists, users, labels, items)


def update_kernel(entries, users_ref, grad_ref, squares_ref, out_ref):
    total = jnp.sum(squares_ref[...], axis=0, keepdims=True)
    total = jnp.sum(total, axis=1, keepdims=True)
    scale = 0.5 / jnp.sqrt(total / entries + 1e-06)
    out_ref[...] = users_ref[...] - scale * grad_ref[...]


def local(users, items, tile_blocks, tile_count, labels):
    loop_size = lax.axis_size("loop")
    rows, width = users.shape
    slots = tile_blocks.shape[1]
    lists = (tile_blocks, tile_count)
    if loop_size == RING and slots == CHUNK:
        gradient, square, users = ring_gradient(users, items, lists, labels)
    else:
        whole = lax.all_gather(items, "loop", axis=0, tiled=True)
        gradient, square = add_chunks(loop_size, whole, lists, users, labels)

    squares = lax.all_to_all(square, "loop", 0, 0, tiled=True)
    return pl.pallas_call(
        functools.partial(update_kernel, rows * loop_size * width),
        out_shape=jax.ShapeDtypeStruct((rows, width), jnp.float32),
        in_specs=[pl.BlockSpec(memory_space=pltpu.VMEM)] * 3,
        out_specs=pl.BlockSpec(memory_space=pltpu.VMEM),
        compiler_params=pltpu.CompilerParams(vmem_limit_bytes=16 * 1024 * 1024),
        cost_estimate=pl.CostEstimate(
            flops=2 * rows * width, bytes_accessed=12 * rows * width, transcendentals=0
        ),
        name="update",
    )(users, gradient, squares)


def solution(mesh):
    in_specs = (
        P(("group", "loop"), None),
        P(("group", "loop"), None),
        P(("group", "loop"), None),
        P(("group", "loop")),
        P(("group", "loop"), None),
    )
    out_specs = P(("group", "loop"), None)
    return jax.shard_map(local, mesh=mesh, in_specs=in_specs, out_specs=out_specs, check_vma=False)
```

```python
import functools

import jax
import jax.numpy as jnp
from jax import lax
from jax.experimental import pallas as pl
from jax.experimental.pallas import tpu as pltpu
from jax.sharding import PartitionSpec as P

CHUNK = 8
RING = 16


def ring_place(loop_size):
    outer = loop_size // 4

    def device(position, core):
        position = position % (2 * outer)
        chip = 2 * position if position < outer else 2 * (2 * outer - 1 - position) + 1
        return 2 * chip + core

    return 2 * outer, device


def to_next(array, direction, loop_size):
    chips, device = ring_place(loop_size)
    pairs = [(device(at, 0), device(at + direction, 0)) for at in range(chips)]
    pairs += [(device(at, 1), device(at - direction, 1)) for at in range(chips)]
    return lax.ppermute(array, "loop", pairs)


def across(array, loop_size):
    chips, device = ring_place(loop_size)
    pairs = [
        (device(at, core), device(at + (3 if at % 2 == 0 else -3), core))
        for at in range(chips)
        for core in range(2)
    ]
    return lax.ppermute(array, "loop", pairs)


def to_other_core(array, loop_size):
    return lax.ppermute(array, "loop", [(at, at ^ 1) for at in range(loop_size)])


def halves(values):
    upper = values.astype(jnp.bfloat16)
    return jnp.concatenate([upper, (values - upper.astype(jnp.float32)).astype(jnp.bfloat16)], 0)


def table_kernel(loop_size, origins, list_ref, count_ref, table_ref):
    chips = loop_size // 2
    lane = lax.broadcasted_iota(jnp.int32, table_ref.shape, 1)
    core, position = core_and_position(loop_size)
    hops, other = jnp.zeros_like(lane), jnp.zeros_like(lane)
    for at, origin in enumerate(origins):
        hops = jnp.where(lane == at, origin[0], hops)
        other = jnp.where(lane == at, origin[1], other)
    at = (position + chips + jnp.where(core == 0, -hops, hops)) & (chips - 1)
    chip = jnp.where(at < chips // 2, 2 * at, 2 * (chips - 1 - at) + 1)
    block = 2 * chip + jnp.where(other == 1, 1 - core, core)
    found = jnp.full_like(lane, -1)
    for slot in range(list_ref.shape[1]):
        name = jnp.where(slot < count_ref[...], list_ref[:, slot : slot + 1], -1)
        found = jnp.where(name == block, slot, found)
    table_ref[...] = jnp.where(lane < len(origins), found, -1)


def slot_table(loop_size, origins, block_list, live_count):
    return pl.pallas_call(
        functools.partial(table_kernel, loop_size, origins),
        out_shape=jax.ShapeDtypeStruct((1, 128), jnp.int32),
        in_specs=[pl.BlockSpec(memory_space=pltpu.VMEM)] * 2,
        out_specs=pl.BlockSpec(memory_space=pltpu.VMEM),
        cost_estimate=pl.CostEstimate(flops=2**32, bytes_accessed=1024, transcendentals=0),
        name="slot_table",
    )(block_list, live_count.reshape(1, 1))


def add_some(grad_ref, parts_ref, tiles, start, count, labels_at):
    rows = grad_ref.shape[0]
    tile = tiles.shape[0] // CHUNK
    block = tiles[pl.ds(pl.multiple_of(start * tile, 2 * tile), count * tile), :]
    upper, lower = [], []
    for at in range(0, count, 2):
        both = lax.dot_general(
            parts_ref[...],
            block[at * tile : (at + 2) * tile],
            (((1,), (1,)), ((), ())),
            preferred_element_type=jnp.float32,
        )
        labels = jnp.concatenate([labels_at(start + at), labels_at(start + at + 1)], 1)
        residual = 0.5 * jnp.tanh(both[:rows] + both[rows:]) + (0.5 - labels.astype(jnp.float32))
        upper.append(residual.astype(jnp.bfloat16))
        lower.append((residual - upper[-1].astype(jnp.float32)).astype(jnp.bfloat16))
    grad_ref[...] += jnp.dot(
        jnp.concatenate(upper + lower, 1),
        jnp.concatenate([block, block], 0),
        preferred_element_type=jnp.float32,
    )


def add_tiles(grad_ref, parts_ref, tiles, live, most, labels_at):
    tile = tiles.shape[0] // CHUNK

    @pl.when(live % 2 == 1)
    def _():
        blank = pl.multiple_of(live * tile, tile)
        tiles[pl.ds(blank, tile), :] = jnp.zeros((tile, tiles.shape[1]), tiles.dtype)

    fours = (live + 1) // 4 if most > 2 else jnp.int32(0)
    if most > 2:

        def four(index, carry):
            add_some(grad_ref, parts_ref, tiles, index * 4, 4, labels_at)
            return carry

        lax.fori_loop(0, fours, four, 0)

    @pl.when(live > 4 * fours)
    def _():
        add_some(grad_ref, parts_ref, tiles, 4 * fours, 2, labels_at)


def store_square(grad_ref, square_ref):
    gradient = grad_ref[...]
    square = jnp.sum(gradient * gradient, axis=0, keepdims=True)
    square = sum(square[:, at : at + 128] for at in range(0, square.shape[1], 128))
    square_ref[...] = jnp.broadcast_to(square, square_ref.shape)


def core_and_position(loop_size):
    me = lax.axis_index("loop")
    core, row, outer = me % 2, me // 2 % 2, me // 4
    return core, jnp.where(row == 0, outer, loop_size // 2 - 1 - outer)


def table_kernel(loop_size, origins, list_ref, count_ref, table_ref):
    chips = loop_size // 2
    lane = lax.broadcasted_iota(jnp.int32, table_ref.shape, 1)
    core, position = core_and_position(loop_size)
    hops, other = jnp.zeros_like(lane), jnp.zeros_like(lane)
    for at, origin in enumerate(origins):
        hops = jnp.where(lane == at, origin[0], hops)
        other = jnp.where(lane == at, origin[1], other)
    at = (position + chips + jnp.where(core == 0, -hops, hops)) & (chips - 1)
    chip = jnp.where(at < chips // 2, 2 * at, 2 * (chips - 1 - at) + 1)
    block = 2 * chip + jnp.where(other == 1, 1 - core, core)
    found = jnp.full_like(lane, -1)
    for slot in range(list_ref.shape[1]):
        name = jnp.where(slot < count_ref[...], list_ref[:, slot : slot + 1], -1)
        found = jnp.where(name == block, slot, found)
    table_ref[...] = jnp.where(lane < len(origins), found, -1)


def slot_table(loop_size, origins, block_list, live_count):
    return pl.pallas_call(
        functools.partial(table_kernel, loop_size, origins),
        out_shape=jax.ShapeDtypeStruct((1, 128), jnp.int32),
        in_specs=[pl.BlockSpec(memory_space=pltpu.VMEM)] * 2,
        out_specs=pl.BlockSpec(memory_space=pltpu.VMEM),
        cost_estimate=pl.CostEstimate(flops=2**32, bytes_accessed=1024, transcendentals=0),
        name="slot_table",
    )(block_list, live_count.reshape(1, 1))


def add_some(grad_ref, parts_ref, tiles, start, count, labels_at):
    rows = grad_ref.shape[0]
    tile = tiles.shape[0] // CHUNK
    block = tiles[pl.ds(pl.multiple_of(start * tile, 2 * tile), count * tile), :]
    upper, lower = [], []
    for at in range(0, count, 2):
        both = lax.dot_general(
            parts_ref[...],
            block[at * tile : (at + 2) * tile],
            (((1,), (1,)), ((), ())),
            preferred_element_type=jnp.float32,
        )
        labels = jnp.concatenate([labels_at(start + at), labels_at(start + at + 1)], 1)
        residual = 0.5 * jnp.tanh(both[:rows] + both[rows:]) + (0.5 - labels.astype(jnp.float32))
        upper.append(residual.astype(jnp.bfloat16))
        lower.append((residual - upper[-1].astype(jnp.float32)).astype(jnp.bfloat16))
    grad_ref[...] += jnp.dot(
        jnp.concatenate(upper + lower, 1),
        jnp.concatenate([block, block], 0),
        preferred_element_type=jnp.float32,
    )


def add_tiles(grad_ref, parts_ref, tiles, live, most, labels_at):
    tile = tiles.shape[0] // CHUNK

    @pl.when(live % 2 == 1)
    def _():
        blank = pl.multiple_of(live * tile, tile)
        tiles[pl.ds(blank, tile), :] = jnp.zeros((tile, tiles.shape[1]), tiles.dtype)

    fours = (live + 1) // 4 if most > 2 else jnp.int32(0)
    if most > 2:

        def four(index, carry):
            add_some(grad_ref, parts_ref, tiles, index * 4, 4, labels_at)
            return carry

        lax.fori_loop(0, fours, four, 0)

    @pl.when(live > 4 * fours)
    def _():
        add_some(grad_ref, parts_ref, tiles, 4 * fours, 2, labels_at)


def store_square(grad_ref, square_ref):
    gradient = grad_ref[...]
    square = jnp.sum(gradient * gradient, axis=0, keepdims=True)
    square = sum(square[:, at : at + 128] for at in range(0, square.shape[1], 128))
    square_ref[...] = jnp.broadcast_to(square, square_ref.shape)


def core_and_position(loop_size):
    me = lax.axis_index("loop")
    core, row, outer = me % 2, me // 2 % 2, me // 4
    return core, jnp.where(row == 0, outer, loop_size // 2 - 1 - outer)


def origin_block(origin, loop_size):
    hops, other = origin
    chips = loop_size // 2
    core, position = core_and_position(loop_size)
    at = lax.rem(position + chips + jnp.where(core == 0, -hops, hops), chips)
    chip = jnp.where(at < chips // 2, 2 * at, 2 * (chips - 1 - at) + 1)
    return 2 * chip + (1 - core if other else core)


def pieces_kernel(places, count, packed, loop_size, first, last, table_ref, given_ref, labels_ref, *rest):
    rest = list(rest)
    arrays = [rest.pop(0) for _ in range(count)]
    if not first:
        rest.pop(0)
    grad_ref = rest.pop(0)
    parts_ref = rest.pop(0) if first else given_ref
    across_ref = rest.pop(0) if first else None
    pack_ref = rest.pop(0) if packed else None
    square_ref = rest.pop(0) if last else None
    tiles, slots = rest
    tile = tiles.shape[0] // CHUNK
    for at, index in enumerate(packed):
        pack_ref[at * tile : (at + 1) * tile, :] = arrays[index][...]
    if first:
        core, position = core_and_position(loop_size)
        for at in range(2):

            @pl.when((core + position) % 2 == at)
            def _():
                across_ref[...] = arrays[1 + at][...]

        parts_ref[...] = halves(0.5 * given_ref[...])
        grad_ref[...] = jnp.zeros_like(grad_ref)
    live = jnp.int32(0)
    table = table_ref[...]
    entries = [table[0, at] for at, _, _ in places]
    for found, (_, index, row) in zip(entries, places):

        @pl.when(found >= 0)
        def _():
            into = pl.ds(pl.multiple_of(live * tile, tile), tile)
            tiles[into, :] = arrays[index][row * tile : (row + 1) * tile, :]
            slots[live] = found

        live = live + (found >= 0).astype(jnp.int32)
    slots[live] = 0

    def labels_at(position):
        return labels_ref[:, pl.ds(pl.multiple_of(slots[position] * tile, tile), tile)]

    add_tiles(grad_ref, parts_ref, tiles, live, min(len(places), CHUNK), labels_at)
    if last:
        store_square(grad_ref, square_ref)


def add_pieces(held, packed, loop_size, table, given, labels, before, last):
    first = before is None
    width = given.shape[1]
    rows = given.shape[0] // (1 if first else 2)
    arrays = [array for array, _ in held]
    tile = labels.shape[1] // CHUNK
    places = [(at, index, row) for index, (_, entries) in enumerate(held) for row, at in enumerate(entries)]
    most = min(len(places), CHUNK)
    out_shape = [jax.ShapeDtypeStruct((rows, width), jnp.float32)]
    if first:
        out_shape.append(jax.ShapeDtypeStruct((2 * rows, width), jnp.bfloat16))
        out_shape.append(jax.ShapeDtypeStruct((tile, width), jnp.bfloat16))
    if packed:
        out_shape.append(jax.ShapeDtypeStruct((len(packed) * tile, width), jnp.bfloat16))
    if last:
        out_shape.append(jax.ShapeDtypeStruct((loop_size, 128), jnp.float32))
    extra = [] if first else [before]
    return pl.pallas_call(
        functools.partial(pieces_kernel, places, len(arrays), packed, loop_size, first, last),
        out_shape=out_shape,
        in_specs=[pl.BlockSpec(memory_space=pltpu.VMEM)] * (3 + len(arrays) + len(extra)),
        out_specs=[pl.BlockSpec(memory_space=pltpu.VMEM)] * len(out_shape),
        input_output_aliases={} if first else {3 + len(arrays): 0},
        scratch_shapes=[
            pltpu.VMEM((CHUNK * tile, width), jnp.bfloat16),
            pltpu.SMEM((CHUNK + 1,), jnp.int32),
        ],
        compiler_params=pltpu.CompilerParams(vmem_limit_bytes=24 * 1024 * 1024),
        cost_estimate=pl.CostEstimate(
            flops=128 * rows * width * most * tile,
            bytes_accessed=8 * rows * width,
            transcendentals=rows * most * tile,
        ),
        name="add_pieces",
    )(table, given, labels, *arrays, *extra)


def ring_gradient(users, items, lists, labels):
    loop_size = lax.axis_size("loop")
    far = loop_size // 4
    origins = [(hops, 0) for hops in range(1 - far, far + 1)]
    origins += [(-hops, 1) for hops, _ in origins]
    table = slot_table(loop_size, origins, *lists)
    where = {origin: at for at, origin in enumerate(origins)}

    def held(hops, array):
        return array, [where[hops, 0]]

    def other(arrays, hops):
        return to_other_core(arrays, loop_size), [where[-hop, 1] for hop in hops]

    up = to_next(items, 1, loop_size)
    down = to_next(items, -1, loop_size)
    up, table = lax.optimization_barrier((up, table))
    first = [held(0, items), held(1, up), held(-1, down)]
    second = [held(2, to_next(up, 1, loop_size)), held(-2, to_next(down, -1, loop_size))]
    gradient, parts, opposite, pack = add_pieces(
        first, [0, 1, 2], loop_size, table, users, labels, None, False
    )
    opposite = across(opposite, loop_size)
    first = other(pack, [0, 1, -1])
    third = [held(3, to_next(second[0][0], 1, loop_size)), held(-3, to_next(second[1][0], -1, loop_size))]
    gradient, pack = add_pieces(second, [0, 1], loop_size, table, parts, labels, gradient, False)
    second = other(pack, [2, -2])
    third.append(held(4, opposite))
    gradient, pack = add_pieces(third, [0, 1, 2], loop_size, table, parts, labels, gradient, False)
    third = other(pack, [3, -3, 4])
    (gradient,) = add_pieces([first, second], [], loop_size, table, parts, labels, gradient, False)
    return *add_pieces([third], [], loop_size, table, parts, labels, gradient, True), users


def chunks_kernel(
    list_ref, count_ref, users_ref, labels_ref, items_ref, grad_ref, square_ref, tiles, parts_ref, sems
):
    tile = tiles.shape[0] // CHUNK
    step = pl.program_id(0)
    live = jnp.clip(count_ref[0] - step * CHUNK, 0, CHUNK)

    @pl.when(step == 0)
    def _():
        parts_ref[...] = halves(0.5 * users_ref[...])
        grad_ref[...] = jnp.zeros_like(grad_ref)

    def move(slot):
        start = pl.multiple_of(list_ref[0, step * CHUNK + slot] * tile, tile)
        return pltpu.make_async_copy(
            items_ref.at[pl.ds(start, tile), :], tiles.at[pl.ds(slot * tile, tile), :], sems.at[slot]
        )

    for slot in range(CHUNK):
        pl.when(slot < live)(lambda slot=slot: move(slot).start())
    for slot in range(CHUNK):
        pl.when(slot < live)(lambda slot=slot: move(slot).wait())

    def labels_at(position):
        return labels_ref[:, pl.ds(pl.multiple_of(position * tile, tile), tile)]

    add_tiles(grad_ref, parts_ref, tiles, live, CHUNK, labels_at)

    @pl.when(step == pl.num_programs(0) - 1)
    def _():
        store_square(grad_ref, square_ref)


def add_chunks(loop_size, items, lists, users, labels):
    rows, width = users.shape
    slots = lists[0].shape[1]
    tile = labels.shape[1] // slots
    return pl.pallas_call(
        chunks_kernel,
        grid=(slots // CHUNK,),
        out_shape=[
            jax.ShapeDtypeStruct((rows, width), jnp.float32),
            jax.ShapeDtypeStruct((loop_size, 128), jnp.float32),
        ],
        in_specs=[
            pl.BlockSpec(memory_space=pltpu.SMEM),
            pl.BlockSpec(memory_space=pltpu.SMEM),
            pl.BlockSpec((rows, width), lambda step: (0, 0)),
            pl.BlockSpec((rows, CHUNK * tile), lambda step: (0, step)),
            pl.BlockSpec(memory_space=pl.ANY),
        ],
        out_specs=[
            pl.BlockSpec((rows, width), lambda step: (0, 0)),
            pl.BlockSpec((loop_size, 128), lambda step: (0, 0)),
        ],
        scratch_shapes=[
            pltpu.VMEM((CHUNK * tile, width), jnp.bfloat16),
            pltpu.VMEM((2 * rows, width), jnp.bfloat16),
            pltpu.SemaphoreType.DMA((CHUNK,)),
        ],
        compiler_params=pltpu.CompilerParams(vmem_limit_bytes=32 * 1024 * 1024),
        cost_estimate=pl.CostEstimate(
            flops=8 * rows * width * slots * tile,
            bytes_accessed=4 * rows * (slots * tile + 2 * width) + 2 * slots * tile * width,
            transcendentals=rows * slots * tile,
        ),
        name="add_chunks",
    )(*lists, users, labels, items)


def update_kernel(entries, users_ref, grad_ref, squares_ref, out_ref):
    total = jnp.sum(squares_ref[...], axis=0, keepdims=True)
    total = jnp.sum(total, axis=1, keepdims=True)
    scale = 0.5 / jnp.sqrt(total / entries + 1e-06)
    out_ref[...] = users_ref[...] - scale * grad_ref[...]


def local(users, items, tile_blocks, tile_count, labels):
    loop_size = lax.axis_size("loop")
    rows, width = users.shape
    slots = tile_blocks.shape[1]
    lists = (tile_blocks, tile_count)
    if loop_size == RING and slots == CHUNK:
        gradient, square, users = ring_gradient(users, items, lists, labels)
    else:
        whole = lax.all_gather(items, "loop", axis=0, tiled=True)
        gradient, square = add_chunks(loop_size, whole, lists, users, labels)

    squares = lax.all_to_all(square, "loop", 0, 0, tiled=True)
    return pl.pallas_call(
        functools.partial(update_kernel, rows * loop_size * width),
        out_shape=jax.ShapeDtypeStruct((rows, width), jnp.float32),
        in_specs=[pl.BlockSpec(memory_space=pltpu.VMEM)] * 3,
        out_specs=pl.BlockSpec(memory_space=pltpu.VMEM),
        compiler_params=pltpu.CompilerParams(vmem_limit_bytes=16 * 1024 * 1024),
        cost_estimate=pl.CostEstimate(
            flops=2 * rows * width, bytes_accessed=12 * rows * width, transcendentals=0
        ),
        name="update",
    )(users, gradient, squares)


def solution(mesh):
    in_specs = (
        P(("group", "loop"), None),
        P(("group", "loop"), None),
        P(("group", "loop"), None),
        P(("group", "loop")),
        P(("group", "loop"), None),
    )
    out_specs = P(("group", "loop"), None)
    return jax.shard_map(local, mesh=mesh, in_specs=in_specs, out_specs=out_specs, check_vma=False)
```

```python
import functools

import jax
import jax.numpy as jnp
from jax import lax
from jax.experimental import pallas as pl
from jax.experimental.pallas import tpu as pltpu
from jax.sharding import PartitionSpec as P

CHUNK = 8
RING = 16


def ring_place(loop_size):
    outer = loop_size // 4

    def device(position, core):
        position = position % (2 * outer)
        chip = 2 * position if position < outer else 2 * (2 * outer - 1 - position) + 1
        return 2 * chip + core

    return 2 * outer, device


def to_next(array, direction, loop_size):
    chips, device = ring_place(loop_size)
    pairs = [(device(at, 0), device(at + direction, 0)) for at in range(chips)]
    pairs += [(device(at, 1), device(at - direction, 1)) for at in range(chips)]
    return lax.ppermute(array, "loop", pairs)


def across(array, loop_size):
    chips, device = ring_place(loop_size)
    pairs = [
        (device(at, core), device(at + (3 if at % 2 == 0 else -3), core))
        for at in range(chips)
        for core in range(2)
    ]
    return lax.ppermute(array, "loop", pairs)


def to_other_core(array, loop_size):
    return lax.ppermute(array, "loop", [(at, at ^ 1) for at in range(loop_size)])


def halves(values):
    upper = values.astype(jnp.bfloat16)
    return jnp.concatenate([upper, (values - upper.astype(jnp.float32)).astype(jnp.bfloat16)], 0)


def table_kernel(loop_size, origins, list_ref, count_ref, table_ref):
    chips = loop_size // 2
    lane = lax.broadcasted_iota(jnp.int32, table_ref.shape, 1)
    core, position = core_and_position(loop_size)
    hops, other = jnp.zeros_like(lane), jnp.zeros_like(lane)
    for at, origin in enumerate(origins):
        hops = jnp.where(lane == at, origin[0], hops)
        other = jnp.where(lane == at, origin[1], other)
    at = (position + chips + jnp.where(core == 0, -hops, hops)) & (chips - 1)
    chip = jnp.where(at < chips // 2, 2 * at, 2 * (chips - 1 - at) + 1)
    block = 2 * chip + jnp.where(other == 1, 1 - core, core)
    found = jnp.full_like(lane, -1)
    for slot in range(list_ref.shape[1]):
        name = jnp.where(slot < count_ref[...], list_ref[:, slot : slot + 1], -1)
        found = jnp.where(name == block, slot, found)
    table_ref[...] = jnp.where(lane < len(origins), found, -1)


def slot_table(loop_size, origins, block_list, live_count):
    return pl.pallas_call(
        functools.partial(table_kernel, loop_size, origins),
        out_shape=jax.ShapeDtypeStruct((1, 128), jnp.int32),
        in_specs=[pl.BlockSpec(memory_space=pltpu.VMEM)] * 2,
        out_specs=pl.BlockSpec(memory_space=pltpu.VMEM),
        compiler_params=pltpu.CompilerParams(vmem_limit_bytes=16 * 1024 * 1024),
        cost_estimate=pl.CostEstimate(flops=2**32, bytes_accessed=1024, transcendentals=0),
        name="slot_table",
    )(block_list, live_count.reshape(1, 1))


def add_some(grad_ref, parts_ref, tiles, start, count, labels_at):
    rows = grad_ref.shape[0]
    tile = tiles.shape[0] // CHUNK
    block = tiles[pl.ds(pl.multiple_of(start * tile, 2 * tile), count * tile), :]
    upper, lower = [], []
    for at in range(0, count, 2):
        both = lax.dot_general(
            parts_ref[...],
            block[at * tile : (at + 2) * tile],
            (((1,), (1,)), ((), ())),
            preferred_element_type=jnp.float32,
        )
        labels = jnp.concatenate([labels_at(start + at), labels_at(start + at + 1)], 1)
        residual = 0.5 * jnp.tanh(both[:rows] + both[rows:]) + (0.5 - labels.astype(jnp.float32))
        upper.append(residual.astype(jnp.bfloat16))
        lower.append((residual - upper[-1].astype(jnp.float32)).astype(jnp.bfloat16))
    grad_ref[...] += jnp.dot(
        jnp.concatenate(upper + lower, 1),
        jnp.concatenate([block, block], 0),
        preferred_element_type=jnp.float32,
    )


def add_tiles(grad_ref, parts_ref, tiles, live, most, labels_at):
    tile = tiles.shape[0] // CHUNK

    @pl.when(live % 2 == 1)
    def _():
        blank = pl.multiple_of(live * tile, tile)
        tiles[pl.ds(blank, tile), :] = jnp.zeros((tile, tiles.shape[1]), tiles.dtype)

    fours = (live + 1) // 4 if most > 2 else jnp.int32(0)
    if most > 2:

        def four(index, carry):
            add_some(grad_ref, parts_ref, tiles, index * 4, 4, labels_at)
            return carry

        lax.fori_loop(0, fours, four, 0)

    @pl.when(live > 4 * fours)
    def _():
        add_some(grad_ref, parts_ref, tiles, 4 * fours, 2, labels_at)


def store_square(grad_ref, square_ref):
    gradient = grad_ref[...]
    square = jnp.sum(gradient * gradient, axis=0, keepdims=True)
    square = sum(square[:, at : at + 128] for at in range(0, square.shape[1], 128))
    square_ref[...] = jnp.broadcast_to(square, square_ref.shape)


def core_and_position(loop_size):
    me = lax.axis_index("loop")
    core, row, outer = me % 2, me // 2 % 2, me // 4
    return core, jnp.where(row == 0, outer, loop_size // 2 - 1 - outer)


def table_kernel(loop_size, origins, list_ref, count_ref, table_ref):
    chips = loop_size // 2
    lane = lax.broadcasted_iota(jnp.int32, table_ref.shape, 1)
    core, position = core_and_position(loop_size)
    hops, other = jnp.zeros_like(lane), jnp.zeros_like(lane)
    for at, origin in enumerate(origins):
        hops = jnp.where(lane == at, origin[0], hops)
        other = jnp.where(lane == at, origin[1], other)
    at = (position + chips + jnp.where(core == 0, -hops, hops)) & (chips - 1)
    chip = jnp.where(at < chips // 2, 2 * at, 2 * (chips - 1 - at) + 1)
    block = 2 * chip + jnp.where(other == 1, 1 - core, core)
    found = jnp.full_like(lane, -1)
    for slot in range(list_ref.shape[1]):
        name = jnp.where(slot < count_ref[...], list_ref[:, slot : slot + 1], -1)
        found = jnp.where(name == block, slot, found)
    table_ref[...] = jnp.where(lane < len(origins), found, -1)


def slot_table(loop_size, origins, block_list, live_count):
    return pl.pallas_call(
        functools.partial(table_kernel, loop_size, origins),
        out_shape=jax.ShapeDtypeStruct((1, 128), jnp.int32),
        in_specs=[pl.BlockSpec(memory_space=pltpu.VMEM)] * 2,
        out_specs=pl.BlockSpec(memory_space=pltpu.VMEM),
        compiler_params=pltpu.CompilerParams(vmem_limit_bytes=16 * 1024 * 1024),
        cost_estimate=pl.CostEstimate(flops=2**32, bytes_accessed=1024, transcendentals=0),
        name="slot_table",
    )(block_list, live_count.reshape(1, 1))


def add_some(grad_ref, parts_ref, tiles, start, count, labels_at):
    rows = grad_ref.shape[0]
    tile = tiles.shape[0] // CHUNK
    block = tiles[pl.ds(pl.multiple_of(start * tile, 2 * tile), count * tile), :]
    upper, lower = [], []
    for at in range(0, count, 2):
        both = lax.dot_general(
            parts_ref[...],
            block[at * tile : (at + 2) * tile],
            (((1,), (1,)), ((), ())),
            preferred_element_type=jnp.float32,
        )
        labels = jnp.concatenate([labels_at(start + at), labels_at(start + at + 1)], 1)
        residual = 0.5 * jnp.tanh(both[:rows] + both[rows:]) + (0.5 - labels.astype(jnp.float32))
        upper.append(residual.astype(jnp.bfloat16))
        lower.append((residual - upper[-1].astype(jnp.float32)).astype(jnp.bfloat16))
    grad_ref[...] += jnp.dot(
        jnp.concatenate(upper + lower, 1),
        jnp.concatenate([block, block], 0),
        preferred_element_type=jnp.float32,
    )


def add_tiles(grad_ref, parts_ref, tiles, live, most, labels_at):
    tile = tiles.shape[0] // CHUNK

    @pl.when(live % 2 == 1)
    def _():
        blank = pl.multiple_of(live * tile, tile)
        tiles[pl.ds(blank, tile), :] = jnp.zeros((tile, tiles.shape[1]), tiles.dtype)

    fours = (live + 1) // 4 if most > 2 else jnp.int32(0)
    if most > 2:

        def four(index, carry):
            add_some(grad_ref, parts_ref, tiles, index * 4, 4, labels_at)
            return carry

        lax.fori_loop(0, fours, four, 0)

    @pl.when(live > 4 * fours)
    def _():
        add_some(grad_ref, parts_ref, tiles, 4 * fours, 2, labels_at)


def store_square(grad_ref, square_ref):
    gradient = grad_ref[...]
    square = jnp.sum(gradient * gradient, axis=0, keepdims=True)
    square = sum(square[:, at : at + 128] for at in range(0, square.shape[1], 128))
    square_ref[...] = jnp.broadcast_to(square, square_ref.shape)


def core_and_position(loop_size):
    me = lax.axis_index("loop")
    core, row, outer = me % 2, me // 2 % 2, me // 4
    return core, jnp.where(row == 0, outer, loop_size // 2 - 1 - outer)


def origin_block(origin, loop_size):
    hops, other = origin
    chips = loop_size // 2
    core, position = core_and_position(loop_size)
    at = lax.rem(position + chips + jnp.where(core == 0, -hops, hops), chips)
    chip = jnp.where(at < chips // 2, 2 * at, 2 * (chips - 1 - at) + 1)
    return 2 * chip + (1 - core if other else core)


def pieces_kernel(places, count, packed, loop_size, first, last, table_ref, given_ref, labels_ref, *rest):
    rest = list(rest)
    arrays = [rest.pop(0) for _ in range(count)]
    if not first:
        rest.pop(0)
    grad_ref = rest.pop(0)
    parts_ref = rest.pop(0) if first else given_ref
    across_ref = rest.pop(0) if first else None
    pack_ref = rest.pop(0) if packed else None
    square_ref = rest.pop(0) if last else None
    tiles, slots = rest
    tile = tiles.shape[0] // CHUNK
    for at, index in enumerate(packed):
        pack_ref[at * tile : (at + 1) * tile, :] = arrays[index][...]
    if first:
        core, position = core_and_position(loop_size)
        for at in range(2):

            @pl.when((core + position) % 2 == at)
            def _():
                across_ref[...] = arrays[1 + at][...]

        parts_ref[...] = halves(0.5 * given_ref[...])
        grad_ref[...] = jnp.zeros_like(grad_ref)
    live = jnp.int32(0)
    table = table_ref[...]
    entries = [table[0, at] for at, _, _ in places]
    for found, (_, index, row) in zip(entries, places):

        @pl.when(found >= 0)
        def _():
            into = pl.ds(pl.multiple_of(live * tile, tile), tile)
            tiles[into, :] = arrays[index][row * tile : (row + 1) * tile, :]
            slots[live] = found

        live = live + (found >= 0).astype(jnp.int32)
    slots[live] = 0

    def labels_at(position):
        return labels_ref[:, pl.ds(pl.multiple_of(slots[position] * tile, tile), tile)]

    add_tiles(grad_ref, parts_ref, tiles, live, min(len(places), CHUNK), labels_at)
    if last:
        store_square(grad_ref, square_ref)


def add_pieces(held, packed, loop_size, table, given, labels, before, last):
    first = before is None
    width = given.shape[1]
    rows = given.shape[0] // (1 if first else 2)
    arrays = [array for array, _ in held]
    tile = labels.shape[1] // CHUNK
    places = [(at, index, row) for index, (_, entries) in enumerate(held) for row, at in enumerate(entries)]
    most = min(len(places), CHUNK)
    out_shape = [jax.ShapeDtypeStruct((rows, width), jnp.float32)]
    if first:
        out_shape.append(jax.ShapeDtypeStruct((2 * rows, width), jnp.bfloat16))
        out_shape.append(jax.ShapeDtypeStruct((tile, width), jnp.bfloat16))
    if packed:
        out_shape.append(jax.ShapeDtypeStruct((len(packed) * tile, width), jnp.bfloat16))
    if last:
        out_shape.append(jax.ShapeDtypeStruct((len(sum_groups(loop_size)[0][0]), 128), jnp.float32))
    extra = [] if first else [before]
    return pl.pallas_call(
        functools.partial(pieces_kernel, places, len(arrays), packed, loop_size, first, last),
        out_shape=out_shape,
        in_specs=[pl.BlockSpec(memory_space=pltpu.VMEM)] * (3 + len(arrays) + len(extra)),
        out_specs=[pl.BlockSpec(memory_space=pltpu.VMEM)] * len(out_shape),
        input_output_aliases={} if first else {3 + len(arrays): 0},
        scratch_shapes=[
            pltpu.VMEM((CHUNK * tile, width), jnp.bfloat16),
            pltpu.SMEM((CHUNK + 1,), jnp.int32),
        ],
        compiler_params=pltpu.CompilerParams(vmem_limit_bytes=24 * 1024 * 1024),
        cost_estimate=pl.CostEstimate(
            flops=128 * rows * width * most * tile,
            bytes_accessed=8 * rows * width,
            transcendentals=rows * most * tile,
        ),
        name="add_pieces",
    )(table, given, labels, *arrays, *extra)


def ring_gradient(users, items, lists, labels):
    loop_size = lax.axis_size("loop")
    far = loop_size // 4
    origins = [(hops, 0) for hops in range(1 - far, far + 1)]
    origins += [(-hops, 1) for hops, _ in origins]
    table = slot_table(loop_size, origins, *lists)
    where = {origin: at for at, origin in enumerate(origins)}

    def held(hops, array):
        return array, [where[hops, 0]]

    def other(arrays, hops):
        return to_other_core(arrays, loop_size), [where[-hop, 1] for hop in hops]

    up = to_next(items, 1, loop_size)
    down = to_next(items, -1, loop_size)
    up, table = lax.optimization_barrier((up, table))
    first = [held(0, items), held(1, up), held(-1, down)]
    second = [held(2, to_next(up, 1, loop_size)), held(-2, to_next(down, -1, loop_size))]
    gradient, parts, opposite, pack = add_pieces(
        first, [0, 1, 2], loop_size, table, users, labels, None, False
    )
    opposite = across(opposite, loop_size)
    first = other(pack, [0, 1, -1])
    third = [held(3, to_next(second[0][0], 1, loop_size)), held(-3, to_next(second[1][0], -1, loop_size))]
    gradient, pack = add_pieces(second, [0, 1], loop_size, table, parts, labels, gradient, False)
    second = other(pack, [2, -2])
    third.append(held(4, opposite))
    gradient, pack = add_pieces(third, [0, 1, 2], loop_size, table, parts, labels, gradient, False)
    third = other(pack, [3, -3, 4])
    (gradient,) = add_pieces([first, second], [], loop_size, table, parts, labels, gradient, False)
    return *add_pieces([third], [], loop_size, table, parts, labels, gradient, True), users


def chunks_kernel(
    list_ref, count_ref, users_ref, labels_ref, items_ref, grad_ref, square_ref, tiles, parts_ref, sems
):
    tile = tiles.shape[0] // CHUNK
    step = pl.program_id(0)
    live = jnp.clip(count_ref[0] - step * CHUNK, 0, CHUNK)

    @pl.when(step == 0)
    def _():
        parts_ref[...] = halves(0.5 * users_ref[...])
        grad_ref[...] = jnp.zeros_like(grad_ref)

    def move(slot):
        start = pl.multiple_of(list_ref[0, step * CHUNK + slot] * tile, tile)
        return pltpu.make_async_copy(
            items_ref.at[pl.ds(start, tile), :], tiles.at[pl.ds(slot * tile, tile), :], sems.at[slot]
        )

    for slot in range(CHUNK):
        pl.when(slot < live)(lambda slot=slot: move(slot).start())
    for slot in range(CHUNK):
        pl.when(slot < live)(lambda slot=slot: move(slot).wait())

    def labels_at(position):
        return labels_ref[:, pl.ds(pl.multiple_of(position * tile, tile), tile)]

    add_tiles(grad_ref, parts_ref, tiles, live, CHUNK, labels_at)

    @pl.when(step == pl.num_programs(0) - 1)
    def _():
        store_square(grad_ref, square_ref)


def add_chunks(loop_size, items, lists, users, labels):
    rows, width = users.shape
    slots = lists[0].shape[1]
    tile = labels.shape[1] // slots
    near = len(sum_groups(loop_size)[0][0])
    return pl.pallas_call(
        chunks_kernel,
        grid=(slots // CHUNK,),
        out_shape=[
            jax.ShapeDtypeStruct((rows, width), jnp.float32),
            jax.ShapeDtypeStruct((near, 128), jnp.float32),
        ],
        in_specs=[
            pl.BlockSpec(memory_space=pltpu.SMEM),
            pl.BlockSpec(memory_space=pltpu.SMEM),
            pl.BlockSpec((rows, width), lambda step: (0, 0)),
            pl.BlockSpec((rows, CHUNK * tile), lambda step: (0, step)),
            pl.BlockSpec(memory_space=pl.ANY),
        ],
        out_specs=[
            pl.BlockSpec((rows, width), lambda step: (0, 0)),
            pl.BlockSpec((near, 128), lambda step: (0, 0)),
        ],
        scratch_shapes=[
            pltpu.VMEM((CHUNK * tile, width), jnp.bfloat16),
            pltpu.VMEM((2 * rows, width), jnp.bfloat16),
            pltpu.SemaphoreType.DMA((CHUNK,)),
        ],
        compiler_params=pltpu.CompilerParams(vmem_limit_bytes=32 * 1024 * 1024),
        cost_estimate=pl.CostEstimate(
            flops=8 * rows * width * slots * tile,
            bytes_accessed=4 * rows * (slots * tile + 2 * width) + 2 * slots * tile * width,
            transcendentals=rows * slots * tile,
        ),
        name="add_chunks",
    )(*lists, users, labels, items)


def sum_groups(loop_size):
    near = 4 if loop_size % 4 == 0 else 1
    starts = range(0, loop_size, near)
    return [
        [[start + at for at in range(near)] for start in starts],
        [[start + at for start in starts] for at in range(near)],
    ]


def spread_kernel(squares_ref, sums_ref):
    total = jnp.sum(squares_ref[...], axis=0, keepdims=True)
    sums_ref[...] = jnp.broadcast_to(total, sums_ref.shape)


def spread_sum(squares, copies):
    return pl.pallas_call(
        spread_kernel,
        out_shape=jax.ShapeDtypeStruct((copies, squares.shape[1]), jnp.float32),
        in_specs=[pl.BlockSpec(memory_space=pltpu.VMEM)],
        out_specs=pl.BlockSpec(memory_space=pltpu.VMEM),
        compiler_params=pltpu.CompilerParams(vmem_limit_bytes=16 * 1024 * 1024),
        name="spread_sum",
    )(squares)


def update_kernel(entries, users_ref, grad_ref, squares_ref, out_ref):
    total = jnp.sum(squares_ref[...], axis=0, keepdims=True)
    total = jnp.sum(total, axis=1, keepdims=True)
    scale = 0.5 / jnp.sqrt(total / entries + 1e-06)
    out_ref[...] = users_ref[...] - scale * grad_ref[...]


def local(users, items, tile_blocks, tile_count, labels):
    loop_size = lax.axis_size("loop")
    rows, width = users.shape
    slots = tile_blocks.shape[1]
    lists = (tile_blocks, tile_count)
    if loop_size == RING and slots == CHUNK:
        gradient, square, users = ring_gradient(users, items, lists, labels)
    else:
        whole = lax.all_gather(items, "loop", axis=0, tiled=True)
        gradient, square = add_chunks(loop_size, whole, lists, users, labels)

    near, far = sum_groups(loop_size)
    square = lax.all_to_all(square, "loop", 0, 0, axis_index_groups=near, tiled=True)
    square = spread_sum(square, len(far[0]))
    squares = lax.all_to_all(square, "loop", 0, 0, axis_index_groups=far, tiled=True)
    return pl.pallas_call(
        functools.partial(update_kernel, rows * loop_size * width),
        out_shape=jax.ShapeDtypeStruct((rows, width), jnp.float32),
        in_specs=[pl.BlockSpec(memory_space=pltpu.VMEM)] * 3,
        out_specs=pl.BlockSpec(memory_space=pltpu.VMEM),
        compiler_params=pltpu.CompilerParams(vmem_limit_bytes=16 * 1024 * 1024),
        cost_estimate=pl.CostEstimate(
            flops=2 * rows * width, bytes_accessed=12 * rows * width, transcendentals=0
        ),
        name="update",
    )(users, gradient, squares)


def solution(mesh):
    in_specs = (
        P(("group", "loop"), None),
        P(("group", "loop"), None),
        P(("group", "loop"), None),
        P(("group", "loop")),
        P(("group", "loop"), None),
    )
    out_specs = P(("group", "loop"), None)
    return jax.shard_map(local, mesh=mesh, in_specs=in_specs, out_specs=out_specs, check_vma=False)
```

```python
import functools

import jax
import jax.numpy as jnp
from jax import lax
from jax.experimental import pallas as pl
from jax.experimental.pallas import tpu as pltpu
from jax.sharding import PartitionSpec as P

CHUNK = 8
RING = 16


def ring_place(loop_size):
    outer = loop_size // 4

    def device(position, core):
        position = position % (2 * outer)
        chip = 2 * position if position < outer else 2 * (2 * outer - 1 - position) + 1
        return 2 * chip + core

    return 2 * outer, device


def to_next(array, direction, loop_size):
    chips, device = ring_place(loop_size)
    pairs = [(device(at, 0), device(at + direction, 0)) for at in range(chips)]
    pairs += [(device(at, 1), device(at - direction, 1)) for at in range(chips)]
    return lax.ppermute(array, "loop", pairs)


def across(array, loop_size):
    chips, device = ring_place(loop_size)
    pairs = [
        (device(at, core), device(at + (3 if at % 2 == 0 else -3), core))
        for at in range(chips)
        for core in range(2)
    ]
    return lax.ppermute(array, "loop", pairs)


def to_other_core(array, loop_size):
    return lax.ppermute(array, "loop", [(at, at ^ 1) for at in range(loop_size)])


def halves(values):
    upper = values.astype(jnp.bfloat16)
    return jnp.concatenate([upper, (values - upper.astype(jnp.float32)).astype(jnp.bfloat16)], 0)


def table_kernel(loop_size, origins, list_ref, count_ref, table_ref):
    chips = loop_size // 2
    lane = lax.broadcasted_iota(jnp.int32, table_ref.shape, 1)
    core, position = core_and_position(loop_size)
    hops, other = jnp.zeros_like(lane), jnp.zeros_like(lane)
    for at, origin in enumerate(origins):
        hops = jnp.where(lane == at, origin[0], hops)
        other = jnp.where(lane == at, origin[1], other)
    at = (position + chips + jnp.where(core == 0, -hops, hops)) & (chips - 1)
    chip = jnp.where(at < chips // 2, 2 * at, 2 * (chips - 1 - at) + 1)
    block = 2 * chip + jnp.where(other == 1, 1 - core, core)
    found = jnp.full_like(lane, -1)
    for slot in range(list_ref.shape[1]):
        name = jnp.where(slot < count_ref[...], list_ref[:, slot : slot + 1], -1)
        found = jnp.where(name == block, slot, found)
    table_ref[...] = jnp.where(lane < len(origins), found, -1)


def slot_table(loop_size, origins, block_list, live_count):
    return pl.pallas_call(
        functools.partial(table_kernel, loop_size, origins),
        out_shape=jax.ShapeDtypeStruct((1, 128), jnp.int32),
        in_specs=[pl.BlockSpec(memory_space=pltpu.VMEM)] * 2,
        out_specs=pl.BlockSpec(memory_space=pltpu.VMEM),
        compiler_params=pltpu.CompilerParams(vmem_limit_bytes=16 * 1024 * 1024),
        cost_estimate=pl.CostEstimate(flops=2**32, bytes_accessed=1024, transcendentals=0),
        name="slot_table",
    )(block_list, live_count.reshape(1, 1))


def add_some(grad_ref, parts_ref, tiles, start, count, labels_at):
    rows = grad_ref.shape[0]
    tile = tiles.shape[0] // CHUNK
    block = tiles[pl.ds(pl.multiple_of(start * tile, 2 * tile), count * tile), :]
    upper, lower = [], []
    for at in range(0, count, 2):
        both = lax.dot_general(
            parts_ref[...],
            block[at * tile : (at + 2) * tile],
            (((1,), (1,)), ((), ())),
            preferred_element_type=jnp.float32,
        )
        labels = jnp.concatenate([labels_at(start + at), labels_at(start + at + 1)], 1)
        residual = 0.5 * jnp.tanh(both[:rows] + both[rows:]) + (0.5 - labels.astype(jnp.float32))
        upper.append(residual.astype(jnp.bfloat16))
        lower.append((residual - upper[-1].astype(jnp.float32)).astype(jnp.bfloat16))
    grad_ref[...] += jnp.dot(
        jnp.concatenate(upper + lower, 1),
        jnp.concatenate([block, block], 0),
        preferred_element_type=jnp.float32,
    )


def add_tiles(grad_ref, parts_ref, tiles, live, most, labels_at):
    tile = tiles.shape[0] // CHUNK

    @pl.when(live % 2 == 1)
    def _():
        blank = pl.multiple_of(live * tile, tile)
        tiles[pl.ds(blank, tile), :] = jnp.zeros((tile, tiles.shape[1]), tiles.dtype)

    fours = (live + 1) // 4 if most > 2 else jnp.int32(0)
    if most > 2:

        def four(index, carry):
            add_some(grad_ref, parts_ref, tiles, index * 4, 4, labels_at)
            return carry

        lax.fori_loop(0, fours, four, 0)

    @pl.when(live > 4 * fours)
    def _():
        add_some(grad_ref, parts_ref, tiles, 4 * fours, 2, labels_at)


def store_square(grad_ref, square_ref):
    gradient = grad_ref[...]
    square = jnp.sum(gradient * gradient, axis=0, keepdims=True)
    square = sum(square[:, at : at + 128] for at in range(0, square.shape[1], 128))
    square_ref[...] = jnp.broadcast_to(square, square_ref.shape)


def core_and_position(loop_size):
    me = lax.axis_index("loop")
    core, row, outer = me % 2, me // 2 % 2, me // 4
    return core, jnp.where(row == 0, outer, loop_size // 2 - 1 - outer)


def table_kernel(loop_size, origins, list_ref, count_ref, table_ref):
    chips = loop_size // 2
    lane = lax.broadcasted_iota(jnp.int32, table_ref.shape, 1)
    core, position = core_and_position(loop_size)
    hops, other = jnp.zeros_like(lane), jnp.zeros_like(lane)
    for at, origin in enumerate(origins):
        hops = jnp.where(lane == at, origin[0], hops)
        other = jnp.where(lane == at, origin[1], other)
    at = (position + chips + jnp.where(core == 0, -hops, hops)) & (chips - 1)
    chip = jnp.where(at < chips // 2, 2 * at, 2 * (chips - 1 - at) + 1)
    block = 2 * chip + jnp.where(other == 1, 1 - core, core)
    found = jnp.full_like(lane, -1)
    for slot in range(list_ref.shape[1]):
        name = jnp.where(slot < count_ref[...], list_ref[:, slot : slot + 1], -1)
        found = jnp.where(name == block, slot, found)
    table_ref[...] = jnp.where(lane < len(origins), found, -1)


def slot_table(loop_size, origins, block_list, live_count):
    return pl.pallas_call(
        functools.partial(table_kernel, loop_size, origins),
        out_shape=jax.ShapeDtypeStruct((1, 128), jnp.int32),
        in_specs=[pl.BlockSpec(memory_space=pltpu.VMEM)] * 2,
        out_specs=pl.BlockSpec(memory_space=pltpu.VMEM),
        compiler_params=pltpu.CompilerParams(vmem_limit_bytes=16 * 1024 * 1024),
        cost_estimate=pl.CostEstimate(flops=2**32, bytes_accessed=1024, transcendentals=0),
        name="slot_table",
    )(block_list, live_count.reshape(1, 1))


def add_some(grad_ref, parts_ref, tiles, start, count, labels_at):
    rows = grad_ref.shape[0]
    tile = tiles.shape[0] // CHUNK
    block = tiles[pl.ds(pl.multiple_of(start * tile, 2 * tile), count * tile), :]
    upper, lower = [], []
    for at in range(0, count, 2):
        both = lax.dot_general(
            parts_ref[...],
            block[at * tile : (at + 2) * tile],
            (((1,), (1,)), ((), ())),
            preferred_element_type=jnp.float32,
        )
        labels = jnp.concatenate([labels_at(start + at), labels_at(start + at + 1)], 1)
        residual = 0.5 * jnp.tanh(both[:rows] + both[rows:]) + (0.5 - labels.astype(jnp.float32))
        upper.append(residual.astype(jnp.bfloat16))
        lower.append((residual - upper[-1].astype(jnp.float32)).astype(jnp.bfloat16))
    grad_ref[...] += jnp.dot(
        jnp.concatenate(upper + lower, 1),
        jnp.concatenate([block, block], 0),
        preferred_element_type=jnp.float32,
    )


def add_tiles(grad_ref, parts_ref, tiles, live, most, labels_at):
    tile = tiles.shape[0] // CHUNK

    @pl.when(live % 2 == 1)
    def _():
        blank = pl.multiple_of(live * tile, tile)
        tiles[pl.ds(blank, tile), :] = jnp.zeros((tile, tiles.shape[1]), tiles.dtype)

    fours = (live + 1) // 4 if most > 2 else jnp.int32(0)
    if most > 2:

        def four(index, carry):
            add_some(grad_ref, parts_ref, tiles, index * 4, 4, labels_at)
            return carry

        lax.fori_loop(0, fours, four, 0)

    @pl.when(live > 4 * fours)
    def _():
        add_some(grad_ref, parts_ref, tiles, 4 * fours, 2, labels_at)


def store_square(grad_ref, square_ref):
    gradient = grad_ref[...]
    square = jnp.sum(gradient * gradient, axis=0, keepdims=True)
    square = sum(square[:, at : at + 128] for at in range(0, square.shape[1], 128))
    square_ref[...] = jnp.broadcast_to(square, square_ref.shape)


def core_and_position(loop_size):
    me = lax.axis_index("loop")
    core, row, outer = me % 2, me // 2 % 2, me // 4
    return core, jnp.where(row == 0, outer, loop_size // 2 - 1 - outer)


def origin_block(origin, loop_size):
    hops, other = origin
    chips = loop_size // 2
    core, position = core_and_position(loop_size)
    at = lax.rem(position + chips + jnp.where(core == 0, -hops, hops), chips)
    chip = jnp.where(at < chips // 2, 2 * at, 2 * (chips - 1 - at) + 1)
    return 2 * chip + (1 - core if other else core)


def pack_kernel(*refs):
    tile = refs[0].shape[0]
    for at, ref in enumerate(refs[:-1]):
        refs[-1][at * tile : (at + 1) * tile, :] = ref[...]


def pack(arrays):
    tile, width = arrays[0].shape
    return pl.pallas_call(
        pack_kernel,
        out_shape=jax.ShapeDtypeStruct((len(arrays) * tile, width), arrays[0].dtype),
        in_specs=[pl.BlockSpec(memory_space=pltpu.VMEM)] * len(arrays),
        out_specs=pl.BlockSpec(memory_space=pltpu.VMEM),
        compiler_params=pltpu.CompilerParams(vmem_limit_bytes=16 * 1024 * 1024),
        cost_estimate=pl.CostEstimate(
            flops=2**34, bytes_accessed=4 * len(arrays) * tile * width, transcendentals=0
        ),
        name="pack",
    )(*arrays)


def pieces_kernel(places, count, packed, loop_size, first, last, table_ref, given_ref, labels_ref, *rest):
    rest = list(rest)
    arrays = [rest.pop(0) for _ in range(count)]
    if not first:
        rest.pop(0)
    grad_ref = rest.pop(0)
    parts_ref = rest.pop(0) if first else given_ref
    across_ref = rest.pop(0) if first else None
    pack_ref = rest.pop(0) if packed else None
    square_ref = rest.pop(0) if last else None
    tiles, slots = rest
    tile = tiles.shape[0] // CHUNK
    for at, index in enumerate(packed):
        pack_ref[at * tile : (at + 1) * tile, :] = arrays[index][...]
    if first:
        core, position = core_and_position(loop_size)
        for at in range(2):

            @pl.when((core + position) % 2 == at)
            def _():
                across_ref[...] = arrays[1 + at][...]

        parts_ref[...] = halves(0.5 * given_ref[...])
        grad_ref[...] = jnp.zeros_like(grad_ref)
    live = jnp.int32(0)
    table = table_ref[...]
    entries = [table[0, at] for at, _, _ in places]
    for found, (_, index, row) in zip(entries, places):

        @pl.when(found >= 0)
        def _():
            into = pl.ds(pl.multiple_of(live * tile, tile), tile)
            tiles[into, :] = arrays[index][row * tile : (row + 1) * tile, :]
            slots[live] = found

        live = live + (found >= 0).astype(jnp.int32)
    slots[live] = 0

    def labels_at(position):
        return labels_ref[:, pl.ds(pl.multiple_of(slots[position] * tile, tile), tile)]

    add_tiles(grad_ref, parts_ref, tiles, live, min(len(places), CHUNK), labels_at)
    if last:
        store_square(grad_ref, square_ref)


def add_pieces(held, packed, loop_size, table, given, labels, before, last):
    first = before is None
    width = given.shape[1]
    rows = given.shape[0] // (1 if first else 2)
    arrays = [array for array, _ in held]
    tile = labels.shape[1] // CHUNK
    places = [(at, index, row) for index, (_, entries) in enumerate(held) for row, at in enumerate(entries)]
    most = min(len(places), CHUNK)
    out_shape = [jax.ShapeDtypeStruct((rows, width), jnp.float32)]
    if first:
        out_shape.append(jax.ShapeDtypeStruct((2 * rows, width), jnp.bfloat16))
        out_shape.append(jax.ShapeDtypeStruct((tile, width), jnp.bfloat16))
    if packed:
        out_shape.append(jax.ShapeDtypeStruct((len(packed) * tile, width), jnp.bfloat16))
    if last:
        out_shape.append(jax.ShapeDtypeStruct((loop_size, 128), jnp.float32))
    extra = [] if first else [before]
    return pl.pallas_call(
        functools.partial(pieces_kernel, places, len(arrays), packed, loop_size, first, last),
        out_shape=out_shape,
        in_specs=[pl.BlockSpec(memory_space=pltpu.VMEM)] * (3 + len(arrays) + len(extra)),
        out_specs=[pl.BlockSpec(memory_space=pltpu.VMEM)] * len(out_shape),
        input_output_aliases={} if first else {3 + len(arrays): 0},
        scratch_shapes=[
            pltpu.VMEM((CHUNK * tile, width), jnp.bfloat16),
            pltpu.SMEM((CHUNK + 1,), jnp.int32),
        ],
        compiler_params=pltpu.CompilerParams(vmem_limit_bytes=24 * 1024 * 1024),
        cost_estimate=pl.CostEstimate(
            flops=128 * rows * width * most * tile,
            bytes_accessed=8 * rows * width,
            transcendentals=rows * most * tile,
        ),
        name="add_pieces",
    )(table, given, labels, *arrays, *extra)


def ring_gradient(users, items, lists, labels):
    loop_size = lax.axis_size("loop")
    far = loop_size // 4
    origins = [(hops, 0) for hops in range(1 - far, far + 1)]
    origins += [(-hops, 1) for hops, _ in origins]
    table = slot_table(loop_size, origins, *lists)
    where = {origin: at for at, origin in enumerate(origins)}

    def held(hops, array):
        return array, [where[hops, 0]]

    def other(arrays, hops):
        return to_other_core(arrays, loop_size), [where[-hop, 1] for hop in hops]

    up = to_next(items, 1, loop_size)
    down = to_next(items, -1, loop_size)
    up, table = lax.optimization_barrier((up, table))
    first = [held(0, items), held(1, up), held(-1, down)]
    second = [held(2, to_next(up, 1, loop_size)), held(-2, to_next(down, -1, loop_size))]
    gradient, parts, opposite, packed = add_pieces(
        first, [0, 1, 2], loop_size, table, users, labels, None, False
    )
    opposite = across(opposite, loop_size)
    first = other(packed, [0, 1, -1])
    third = [held(3, to_next(second[0][0], 1, loop_size)), held(-3, to_next(second[1][0], -1, loop_size))]
    gradient, packed = add_pieces(second, [0, 1], loop_size, table, parts, labels, gradient, False)
    second = other(packed, [2, -2])
    third.append(held(4, opposite))
    arrived, gradient = lax.optimization_barrier(([array for array, _ in third], gradient))
    last = other(pack(arrived), [3, -3, 4])
    (gradient,) = add_pieces(
        third + [first, second], [], loop_size, table, parts, labels, gradient, False
    )
    return *add_pieces([last], [], loop_size, table, parts, labels, gradient, True), users


def chunks_kernel(
    list_ref, count_ref, users_ref, labels_ref, items_ref, grad_ref, square_ref, tiles, parts_ref, sems
):
    tile = tiles.shape[0] // CHUNK
    step = pl.program_id(0)
    live = jnp.clip(count_ref[0] - step * CHUNK, 0, CHUNK)

    @pl.when(step == 0)
    def _():
        parts_ref[...] = halves(0.5 * users_ref[...])
        grad_ref[...] = jnp.zeros_like(grad_ref)

    def move(slot):
        start = pl.multiple_of(list_ref[0, step * CHUNK + slot] * tile, tile)
        return pltpu.make_async_copy(
            items_ref.at[pl.ds(start, tile), :], tiles.at[pl.ds(slot * tile, tile), :], sems.at[slot]
        )

    for slot in range(CHUNK):
        pl.when(slot < live)(lambda slot=slot: move(slot).start())
    for slot in range(CHUNK):
        pl.when(slot < live)(lambda slot=slot: move(slot).wait())

    def labels_at(position):
        return labels_ref[:, pl.ds(pl.multiple_of(position * tile, tile), tile)]

    add_tiles(grad_ref, parts_ref, tiles, live, CHUNK, labels_at)

    @pl.when(step == pl.num_programs(0) - 1)
    def _():
        store_square(grad_ref, square_ref)


def add_chunks(loop_size, items, lists, users, labels):
    rows, width = users.shape
    slots = lists[0].shape[1]
    tile = labels.shape[1] // slots
    return pl.pallas_call(
        chunks_kernel,
        grid=(slots // CHUNK,),
        out_shape=[
            jax.ShapeDtypeStruct((rows, width), jnp.float32),
            jax.ShapeDtypeStruct((loop_size, 128), jnp.float32),
        ],
        in_specs=[
            pl.BlockSpec(memory_space=pltpu.SMEM),
            pl.BlockSpec(memory_space=pltpu.SMEM),
            pl.BlockSpec((rows, width), lambda step: (0, 0)),
            pl.BlockSpec((rows, CHUNK * tile), lambda step: (0, step)),
            pl.BlockSpec(memory_space=pl.ANY),
        ],
        out_specs=[
            pl.BlockSpec((rows, width), lambda step: (0, 0)),
            pl.BlockSpec((loop_size, 128), lambda step: (0, 0)),
        ],
        scratch_shapes=[
            pltpu.VMEM((CHUNK * tile, width), jnp.bfloat16),
            pltpu.VMEM((2 * rows, width), jnp.bfloat16),
            pltpu.SemaphoreType.DMA((CHUNK,)),
        ],
        compiler_params=pltpu.CompilerParams(vmem_limit_bytes=32 * 1024 * 1024),
        cost_estimate=pl.CostEstimate(
            flops=8 * rows * width * slots * tile,
            bytes_accessed=4 * rows * (slots * tile + 2 * width) + 2 * slots * tile * width,
            transcendentals=rows * slots * tile,
        ),
        name="add_chunks",
    )(*lists, users, labels, items)


def update_kernel(entries, users_ref, grad_ref, squares_ref, out_ref):
    total = jnp.sum(squares_ref[...], axis=0, keepdims=True)
    total = jnp.sum(total, axis=1, keepdims=True)
    scale = 0.5 / jnp.sqrt(total / entries + 1e-06)
    out_ref[...] = users_ref[...] - scale * grad_ref[...]


def local(users, items, tile_blocks, tile_count, labels):
    loop_size = lax.axis_size("loop")
    rows, width = users.shape
    slots = tile_blocks.shape[1]
    lists = (tile_blocks, tile_count)
    if loop_size == RING and slots == CHUNK:
        gradient, square, users = ring_gradient(users, items, lists, labels)
    else:
        whole = lax.all_gather(items, "loop", axis=0, tiled=True)
        gradient, square = add_chunks(loop_size, whole, lists, users, labels)

    squares = lax.all_to_all(square, "loop", 0, 0, tiled=True)
    return pl.pallas_call(
        functools.partial(update_kernel, rows * loop_size * width),
        out_shape=jax.ShapeDtypeStruct((rows, width), jnp.float32),
        in_specs=[pl.BlockSpec(memory_space=pltpu.VMEM)] * 3,
        out_specs=pl.BlockSpec(memory_space=pltpu.VMEM),
        compiler_params=pltpu.CompilerParams(vmem_limit_bytes=16 * 1024 * 1024),
        cost_estimate=pl.CostEstimate(
            flops=2 * rows * width, bytes_accessed=12 * rows * width, transcendentals=0
        ),
        name="update",
    )(users, gradient, squares)


def solution(mesh):
    in_specs = (
        P(("group", "loop"), None),
        P(("group", "loop"), None),
        P(("group", "loop"), None),
        P(("group", "loop")),
        P(("group", "loop"), None),
    )
    out_specs = P(("group", "loop"), None)
    return jax.shard_map(local, mesh=mesh, in_specs=in_specs, out_specs=out_specs, check_vma=False)
```

```python
import functools

import jax
import jax.numpy as jnp
from jax import lax
from jax.experimental import pallas as pl
from jax.experimental.pallas import tpu as pltpu
from jax.sharding import PartitionSpec as P

CHUNK = 8
RING = 16


def ring_place(loop_size):
    outer = loop_size // 4

    def device(position, core):
        position = position % (2 * outer)
        chip = 2 * position if position < outer else 2 * (2 * outer - 1 - position) + 1
        return 2 * chip + core

    return 2 * outer, device


def to_next(array, direction, loop_size):
    chips, device = ring_place(loop_size)
    pairs = [(device(at, 0), device(at + direction, 0)) for at in range(chips)]
    pairs += [(device(at, 1), device(at - direction, 1)) for at in range(chips)]
    return lax.ppermute(array, "loop", pairs)


def to_opposite(array, loop_size):
    chips, device = ring_place(loop_size)
    pairs = [(device(at, core), device(at + chips // 2, core)) for at in range(chips) for core in range(2)]
    return lax.ppermute(array, "loop", pairs)


def to_other_core(array, loop_size):
    return lax.ppermute(array, "loop", [(at, at ^ 1) for at in range(loop_size)])


def halves(values):
    upper = values.astype(jnp.bfloat16)
    return jnp.concatenate([upper, (values - upper.astype(jnp.float32)).astype(jnp.bfloat16)], 0)


def table_kernel(loop_size, origins, list_ref, count_ref, table_ref):
    chips = loop_size // 2
    lane = lax.broadcasted_iota(jnp.int32, table_ref.shape, 1)
    core, position = core_and_position(loop_size)
    hops, other = jnp.zeros_like(lane), jnp.zeros_like(lane)
    for at, origin in enumerate(origins):
        hops = jnp.where(lane == at, origin[0], hops)
        other = jnp.where(lane == at, origin[1], other)
    at = (position + chips + jnp.where(core == 0, -hops, hops)) & (chips - 1)
    chip = jnp.where(at < chips // 2, 2 * at, 2 * (chips - 1 - at) + 1)
    block = 2 * chip + jnp.where(other == 1, 1 - core, core)
    found = jnp.full_like(lane, -1)
    for slot in range(list_ref.shape[1]):
        name = jnp.where(slot < count_ref[...], list_ref[:, slot : slot + 1], -1)
        found = jnp.where(name == block, slot, found)
    table_ref[...] = jnp.where(lane < len(origins), found, -1)


def slot_table(loop_size, origins, block_list, live_count):
    return pl.pallas_call(
        functools.partial(table_kernel, loop_size, origins),
        out_shape=jax.ShapeDtypeStruct((1, 128), jnp.int32),
        in_specs=[pl.BlockSpec(memory_space=pltpu.VMEM)] * 2,
        out_specs=pl.BlockSpec(memory_space=pltpu.VMEM),
        compiler_params=pltpu.CompilerParams(vmem_limit_bytes=16 * 1024 * 1024),
        cost_estimate=pl.CostEstimate(flops=2**32, bytes_accessed=1024, transcendentals=0),
        name="slot_table",
    )(block_list, live_count.reshape(1, 1))


def add_some(grad_ref, parts_ref, tiles, start, count, labels_at):
    rows = grad_ref.shape[0]
    tile = tiles.shape[0] // CHUNK
    block = tiles[pl.ds(pl.multiple_of(start * tile, 2 * tile), count * tile), :]
    upper, lower = [], []
    for at in range(0, count, 2):
        both = lax.dot_general(
            parts_ref[...],
            block[at * tile : (at + 2) * tile],
            (((1,), (1,)), ((), ())),
            preferred_element_type=jnp.float32,
        )
        labels = jnp.concatenate([labels_at(start + at), labels_at(start + at + 1)], 1)
        residual = 0.5 * jnp.tanh(both[:rows] + both[rows:]) + (0.5 - labels.astype(jnp.float32))
        upper.append(residual.astype(jnp.bfloat16))
        lower.append((residual - upper[-1].astype(jnp.float32)).astype(jnp.bfloat16))
    grad_ref[...] += jnp.dot(
        jnp.concatenate(upper + lower, 1),
        jnp.concatenate([block, block], 0),
        preferred_element_type=jnp.float32,
    )


def add_tiles(grad_ref, parts_ref, tiles, live, most, labels_at):
    tile = tiles.shape[0] // CHUNK

    @pl.when(live % 2 == 1)
    def _():
        blank = pl.multiple_of(live * tile, tile)
        tiles[pl.ds(blank, tile), :] = jnp.zeros((tile, tiles.shape[1]), tiles.dtype)

    fours = (live + 1) // 4 if most > 2 else jnp.int32(0)
    if most > 2:

        def four(index, carry):
            add_some(grad_ref, parts_ref, tiles, index * 4, 4, labels_at)
            return carry

        lax.fori_loop(0, fours, four, 0)

    @pl.when(live > 4 * fours)
    def _():
        add_some(grad_ref, parts_ref, tiles, 4 * fours, 2, labels_at)


def store_square(grad_ref, square_ref):
    gradient = grad_ref[...]
    square = jnp.sum(gradient * gradient, axis=0, keepdims=True)
    square = sum(square[:, at : at + 128] for at in range(0, square.shape[1], 128))
    square_ref[...] = jnp.broadcast_to(square, square_ref.shape)


def core_and_position(loop_size):
    me = lax.axis_index("loop")
    core, row, outer = me % 2, me // 2 % 2, me // 4
    return core, jnp.where(row == 0, outer, loop_size // 2 - 1 - outer)


def table_kernel(loop_size, origins, list_ref, count_ref, table_ref):
    chips = loop_size // 2
    lane = lax.broadcasted_iota(jnp.int32, table_ref.shape, 1)
    core, position = core_and_position(loop_size)
    hops, other = jnp.zeros_like(lane), jnp.zeros_like(lane)
    for at, origin in enumerate(origins):
        hops = jnp.where(lane == at, origin[0], hops)
        other = jnp.where(lane == at, origin[1], other)
    at = (position + chips + jnp.where(core == 0, -hops, hops)) & (chips - 1)
    chip = jnp.where(at < chips // 2, 2 * at, 2 * (chips - 1 - at) + 1)
    block = 2 * chip + jnp.where(other == 1, 1 - core, core)
    found = jnp.full_like(lane, -1)
    for slot in range(list_ref.shape[1]):
        name = jnp.where(slot < count_ref[...], list_ref[:, slot : slot + 1], -1)
        found = jnp.where(name == block, slot, found)
    table_ref[...] = jnp.where(lane < len(origins), found, -1)


def slot_table(loop_size, origins, block_list, live_count):
    return pl.pallas_call(
        functools.partial(table_kernel, loop_size, origins),
        out_shape=jax.ShapeDtypeStruct((1, 128), jnp.int32),
        in_specs=[pl.BlockSpec(memory_space=pltpu.VMEM)] * 2,
        out_specs=pl.BlockSpec(memory_space=pltpu.VMEM),
        compiler_params=pltpu.CompilerParams(vmem_limit_bytes=16 * 1024 * 1024),
        cost_estimate=pl.CostEstimate(flops=2**32, bytes_accessed=1024, transcendentals=0),
        name="slot_table",
    )(block_list, live_count.reshape(1, 1))


def add_some(grad_ref, parts_ref, tiles, start, count, labels_at):
    rows = grad_ref.shape[0]
    tile = tiles.shape[0] // CHUNK
    block = tiles[pl.ds(pl.multiple_of(start * tile, 2 * tile), count * tile), :]
    upper, lower = [], []
    for at in range(0, count, 2):
        both = lax.dot_general(
            parts_ref[...],
            block[at * tile : (at + 2) * tile],
            (((1,), (1,)), ((), ())),
            preferred_element_type=jnp.float32,
        )
        labels = jnp.concatenate([labels_at(start + at), labels_at(start + at + 1)], 1)
        residual = 0.5 * jnp.tanh(both[:rows] + both[rows:]) + (0.5 - labels.astype(jnp.float32))
        upper.append(residual.astype(jnp.bfloat16))
        lower.append((residual - upper[-1].astype(jnp.float32)).astype(jnp.bfloat16))
    grad_ref[...] += jnp.dot(
        jnp.concatenate(upper + lower, 1),
        jnp.concatenate([block, block], 0),
        preferred_element_type=jnp.float32,
    )


def add_tiles(grad_ref, parts_ref, tiles, live, most, labels_at):
    tile = tiles.shape[0] // CHUNK

    @pl.when(live % 2 == 1)
    def _():
        blank = pl.multiple_of(live * tile, tile)
        tiles[pl.ds(blank, tile), :] = jnp.zeros((tile, tiles.shape[1]), tiles.dtype)

    fours = (live + 1) // 4 if most > 2 else jnp.int32(0)
    if most > 2:

        def four(index, carry):
            add_some(grad_ref, parts_ref, tiles, index * 4, 4, labels_at)
            return carry

        lax.fori_loop(0, fours, four, 0)

    @pl.when(live > 4 * fours)
    def _():
        add_some(grad_ref, parts_ref, tiles, 4 * fours, 2, labels_at)


def store_square(grad_ref, square_ref):
    gradient = grad_ref[...]
    square = jnp.sum(gradient * gradient, axis=0, keepdims=True)
    square = sum(square[:, at : at + 128] for at in range(0, square.shape[1], 128))
    square_ref[...] = jnp.broadcast_to(square, square_ref.shape)


def core_and_position(loop_size):
    me = lax.axis_index("loop")
    core, row, outer = me % 2, me // 2 % 2, me // 4
    return core, jnp.where(row == 0, outer, loop_size // 2 - 1 - outer)


def origin_block(origin, loop_size):
    hops, other = origin
    chips = loop_size // 2
    core, position = core_and_position(loop_size)
    at = lax.rem(position + chips + jnp.where(core == 0, -hops, hops), chips)
    chip = jnp.where(at < chips // 2, 2 * at, 2 * (chips - 1 - at) + 1)
    return 2 * chip + (1 - core if other else core)


def pack_kernel(*refs):
    tile = refs[0].shape[0]
    for at, ref in enumerate(refs[:-1]):
        refs[-1][at * tile : (at + 1) * tile, :] = ref[...]


def pack(arrays):
    tile, width = arrays[0].shape
    return pl.pallas_call(
        pack_kernel,
        out_shape=jax.ShapeDtypeStruct((len(arrays) * tile, width), arrays[0].dtype),
        in_specs=[pl.BlockSpec(memory_space=pltpu.VMEM)] * len(arrays),
        out_specs=pl.BlockSpec(memory_space=pltpu.VMEM),
        compiler_params=pltpu.CompilerParams(vmem_limit_bytes=16 * 1024 * 1024),
        cost_estimate=pl.CostEstimate(
            flops=2**34, bytes_accessed=4 * len(arrays) * tile * width, transcendentals=0
        ),
        name="pack",
    )(*arrays)


def pieces_kernel(places, count, packed, first, last, table_ref, given_ref, labels_ref, *rest):
    rest = list(rest)
    arrays = [rest.pop(0) for _ in range(count)]
    if not first:
        rest.pop(0)
    grad_ref = rest.pop(0)
    parts_ref = rest.pop(0) if first else given_ref
    pack_ref = rest.pop(0) if packed else None
    square_ref = rest.pop(0) if last else None
    tiles, slots = rest
    tile = tiles.shape[0] // CHUNK
    for at, index in enumerate(packed):
        pack_ref[at * tile : (at + 1) * tile, :] = arrays[index][...]
    if first:
        parts_ref[...] = halves(0.5 * given_ref[...])
        grad_ref[...] = jnp.zeros_like(grad_ref)
    live = jnp.int32(0)
    table = table_ref[...]
    entries = [table[0, at] for at, _, _ in places]
    for found, (_, index, row) in zip(entries, places):

        @pl.when(found >= 0)
        def _():
            into = pl.ds(pl.multiple_of(live * tile, tile), tile)
            tiles[into, :] = arrays[index][row * tile : (row + 1) * tile, :]
            slots[live] = found

        live = live + (found >= 0).astype(jnp.int32)
    slots[live] = 0

    def labels_at(position):
        return labels_ref[:, pl.ds(pl.multiple_of(slots[position] * tile, tile), tile)]

    add_tiles(grad_ref, parts_ref, tiles, live, min(len(places), CHUNK), labels_at)
    if last:
        store_square(grad_ref, square_ref)


def add_pieces(held, packed, loop_size, table, given, labels, before, last, worked=None):
    first = before is None
    width = given.shape[1]
    rows = given.shape[0] // (1 if first else 2)
    arrays = [array for array, _ in held]
    tile = labels.shape[1] // CHUNK
    places = [(at, index, row) for index, (_, entries) in enumerate(held) for row, at in enumerate(entries)]
    places = places[:worked]
    most = min(len(places), CHUNK)
    out_shape = [jax.ShapeDtypeStruct((rows, width), jnp.float32)]
    if first:
        out_shape.append(jax.ShapeDtypeStruct((2 * rows, width), jnp.bfloat16))
    if packed:
        out_shape.append(jax.ShapeDtypeStruct((len(packed) * tile, width), jnp.bfloat16))
    if last:
        out_shape.append(jax.ShapeDtypeStruct((loop_size, 128), jnp.float32))
    extra = [] if first else [before]
    return pl.pallas_call(
        functools.partial(pieces_kernel, places, len(arrays), packed, first, last),
        out_shape=out_shape,
        in_specs=[pl.BlockSpec(memory_space=pltpu.VMEM)] * (3 + len(arrays) + len(extra)),
        out_specs=[pl.BlockSpec(memory_space=pltpu.VMEM)] * len(out_shape),
        input_output_aliases={} if first else {3 + len(arrays): 0},
        scratch_shapes=[
            pltpu.VMEM((CHUNK * tile, width), jnp.bfloat16),
            pltpu.SMEM((CHUNK + 1,), jnp.int32),
        ],
        compiler_params=pltpu.CompilerParams(vmem_limit_bytes=24 * 1024 * 1024),
        cost_estimate=pl.CostEstimate(
            flops=128 * rows * width * most * tile,
            bytes_accessed=8 * rows * width,
            transcendentals=rows * most * tile,
        ),
        name="add_pieces",
    )(table, given, labels, *arrays, *extra)


def ring_gradient(users, items, lists, labels):
    loop_size = lax.axis_size("loop")
    far = loop_size // 4
    origins = [(hops, 0) for hops in range(1 - far, far + 1)]
    origins += [(-hops, 1) for hops, _ in origins]
    table = slot_table(loop_size, origins, *lists)
    where = {origin: at for at, origin in enumerate(origins)}

    def held(hops, array):
        return array, [where[hops, 0]]

    def other(arrays, hops):
        return to_other_core(arrays, loop_size), [where[-hop, 1] for hop in hops]

    up = to_next(items, 1, loop_size)
    down = to_next(items, -1, loop_size)
    up, table = lax.optimization_barrier((up, table))
    opposite = to_opposite(items, loop_size)
    first = [held(0, items), held(1, up), held(-1, down), held(4, opposite)]
    second = [held(2, to_next(up, 1, loop_size)), held(-2, to_next(down, -1, loop_size))]
    third = [held(3, to_next(second[0][0], 1, loop_size)), held(-3, to_next(second[1][0], -1, loop_size))]
    gradient, parts = add_pieces(first, [], loop_size, table, users, labels, None, False)
    gradient, packed = add_pieces(
        second + first, [0, 1, 2, 3, 4, 5], loop_size, table, parts, labels, gradient, False, 2
    )
    first = other(packed, [2, -2, 0, 1, -1, 4])
    arrived, gradient = lax.optimization_barrier(([array for array, _ in third], gradient))
    last = other(pack(arrived), [3, -3])
    (gradient,) = add_pieces(
        third + [first], [], loop_size, table, parts, labels, gradient, False
    )
    return *add_pieces([last], [], loop_size, table, parts, labels, gradient, True), users


def chunks_kernel(
    list_ref, count_ref, users_ref, labels_ref, items_ref, grad_ref, square_ref, tiles, parts_ref, sems
):
    tile = tiles.shape[0] // CHUNK
    step = pl.program_id(0)
    live = jnp.clip(count_ref[0] - step * CHUNK, 0, CHUNK)

    @pl.when(step == 0)
    def _():
        parts_ref[...] = halves(0.5 * users_ref[...])
        grad_ref[...] = jnp.zeros_like(grad_ref)

    def move(slot):
        start = pl.multiple_of(list_ref[0, step * CHUNK + slot] * tile, tile)
        return pltpu.make_async_copy(
            items_ref.at[pl.ds(start, tile), :], tiles.at[pl.ds(slot * tile, tile), :], sems.at[slot]
        )

    for slot in range(CHUNK):
        pl.when(slot < live)(lambda slot=slot: move(slot).start())
    for slot in range(CHUNK):
        pl.when(slot < live)(lambda slot=slot: move(slot).wait())

    def labels_at(position):
        return labels_ref[:, pl.ds(pl.multiple_of(position * tile, tile), tile)]

    add_tiles(grad_ref, parts_ref, tiles, live, CHUNK, labels_at)

    @pl.when(step == pl.num_programs(0) - 1)
    def _():
        store_square(grad_ref, square_ref)


def add_chunks(loop_size, items, lists, users, labels):
    rows, width = users.shape
    slots = lists[0].shape[1]
    tile = labels.shape[1] // slots
    return pl.pallas_call(
        chunks_kernel,
        grid=(slots // CHUNK,),
        out_shape=[
            jax.ShapeDtypeStruct((rows, width), jnp.float32),
            jax.ShapeDtypeStruct((loop_size, 128), jnp.float32),
        ],
        in_specs=[
            pl.BlockSpec(memory_space=pltpu.SMEM),
            pl.BlockSpec(memory_space=pltpu.SMEM),
            pl.BlockSpec((rows, width), lambda step: (0, 0)),
            pl.BlockSpec((rows, CHUNK * tile), lambda step: (0, step)),
            pl.BlockSpec(memory_space=pl.ANY),
        ],
        out_specs=[
            pl.BlockSpec((rows, width), lambda step: (0, 0)),
            pl.BlockSpec((loop_size, 128), lambda step: (0, 0)),
        ],
        scratch_shapes=[
            pltpu.VMEM((CHUNK * tile, width), jnp.bfloat16),
            pltpu.VMEM((2 * rows, width), jnp.bfloat16),
            pltpu.SemaphoreType.DMA((CHUNK,)),
        ],
        compiler_params=pltpu.CompilerParams(vmem_limit_bytes=32 * 1024 * 1024),
        cost_estimate=pl.CostEstimate(
            flops=8 * rows * width * slots * tile,
            bytes_accessed=4 * rows * (slots * tile + 2 * width) + 2 * slots * tile * width,
            transcendentals=rows * slots * tile,
        ),
        name="add_chunks",
    )(*lists, users, labels, items)


def update_kernel(entries, users_ref, grad_ref, squares_ref, out_ref):
    total = jnp.sum(squares_ref[...], axis=0, keepdims=True)
    total = jnp.sum(total, axis=1, keepdims=True)
    scale = 0.5 / jnp.sqrt(total / entries + 1e-06)
    out_ref[...] = users_ref[...] - scale * grad_ref[...]


def local(users, items, tile_blocks, tile_count, labels):
    loop_size = lax.axis_size("loop")
    rows, width = users.shape
    slots = tile_blocks.shape[1]
    lists = (tile_blocks, tile_count)
    if loop_size == RING and slots == CHUNK:
        gradient, square, users = ring_gradient(users, items, lists, labels)
    else:
        whole = lax.all_gather(items, "loop", axis=0, tiled=True)
        gradient, square = add_chunks(loop_size, whole, lists, users, labels)

    squares = lax.all_to_all(square, "loop", 0, 0, tiled=True)
    return pl.pallas_call(
        functools.partial(update_kernel, rows * loop_size * width),
        out_shape=jax.ShapeDtypeStruct((rows, width), jnp.float32),
        in_specs=[pl.BlockSpec(memory_space=pltpu.VMEM)] * 3,
        out_specs=pl.BlockSpec(memory_space=pltpu.VMEM),
        compiler_params=pltpu.CompilerParams(vmem_limit_bytes=16 * 1024 * 1024),
        cost_estimate=pl.CostEstimate(
            flops=2 * rows * width, bytes_accessed=12 * rows * width, transcendentals=0
        ),
        name="update",
    )(users, gradient, squares)


def solution(mesh):
    in_specs = (
        P(("group", "loop"), None),
        P(("group", "loop"), None),
        P(("group", "loop"), None),
        P(("group", "loop")),
        P(("group", "loop"), None),
    )
    out_specs = P(("group", "loop"), None)
    return jax.shard_map(local, mesh=mesh, in_specs=in_specs, out_specs=out_specs, check_vma=False)
```

```python
import functools

import jax
import jax.numpy as jnp
from jax import lax
from jax.experimental import pallas as pl
from jax.experimental.pallas import tpu as pltpu
from jax.sharding import PartitionSpec as P

CHUNK = 8
RING = 16


def ring_place(loop_size):
    outer = loop_size // 4

    def device(position, core):
        position = position % (2 * outer)
        chip = 2 * position if position < outer else 2 * (2 * outer - 1 - position) + 1
        return 2 * chip + core

    return 2 * outer, device


def to_next(array, direction, loop_size):
    chips, device = ring_place(loop_size)
    pairs = [(device(at, 0), device(at + direction, 0)) for at in range(chips)]
    pairs += [(device(at, 1), device(at - direction, 1)) for at in range(chips)]
    return lax.ppermute(array, "loop", pairs)


def across(array, loop_size):
    chips, device = ring_place(loop_size)
    pairs = [
        (device(at, core), device(at + (3 if at % 2 == 0 else -3), core))
        for at in range(chips)
        for core in range(2)
    ]
    return lax.ppermute(array, "loop", pairs)


def to_other_core(array, loop_size):
    return lax.ppermute(array, "loop", [(at, at ^ 1) for at in range(loop_size)])


def halves(values):
    upper = values.astype(jnp.bfloat16)
    return jnp.concatenate([upper, (values - upper.astype(jnp.float32)).astype(jnp.bfloat16)], 0)


def table_kernel(loop_size, origins, list_ref, count_ref, table_ref):
    chips = loop_size // 2
    lane = lax.broadcasted_iota(jnp.int32, table_ref.shape, 1)
    core, position = core_and_position(loop_size)
    hops, other = jnp.zeros_like(lane), jnp.zeros_like(lane)
    for at, origin in enumerate(origins):
        hops = jnp.where(lane == at, origin[0], hops)
        other = jnp.where(lane == at, origin[1], other)
    at = (position + chips + jnp.where(core == 0, -hops, hops)) & (chips - 1)
    chip = jnp.where(at < chips // 2, 2 * at, 2 * (chips - 1 - at) + 1)
    block = 2 * chip + jnp.where(other == 1, 1 - core, core)
    found = jnp.full_like(lane, -1)
    for slot in range(list_ref.shape[1]):
        name = jnp.where(slot < count_ref[...], list_ref[:, slot : slot + 1], -1)
        found = jnp.where(name == block, slot, found)
    table_ref[...] = jnp.where(lane < len(origins), found, -1)


def slot_table(loop_size, origins, block_list, live_count):
    return pl.pallas_call(
        functools.partial(table_kernel, loop_size, origins),
        out_shape=jax.ShapeDtypeStruct((1, 128), jnp.int32),
        in_specs=[pl.BlockSpec(memory_space=pltpu.VMEM)] * 2,
        out_specs=pl.BlockSpec(memory_space=pltpu.VMEM),
        compiler_params=pltpu.CompilerParams(vmem_limit_bytes=16 * 1024 * 1024),
        cost_estimate=pl.CostEstimate(flops=2**32, bytes_accessed=1024, transcendentals=0),
        name="slot_table",
    )(block_list, live_count.reshape(1, 1))


def add_some(grad_ref, parts_ref, tiles, start, count, labels_at):
    rows = grad_ref.shape[0]
    tile = tiles.shape[0] // CHUNK
    block = tiles[pl.ds(pl.multiple_of(start * tile, 2 * tile), count * tile), :]
    upper, lower = [], []
    for at in range(0, count, 2):
        both = lax.dot_general(
            parts_ref[...],
            block[at * tile : (at + 2) * tile],
            (((1,), (1,)), ((), ())),
            preferred_element_type=jnp.float32,
        )
        labels = jnp.concatenate([labels_at(start + at), labels_at(start + at + 1)], 1)
        residual = 0.5 * jnp.tanh(both[:rows] + both[rows:]) + (0.5 - labels.astype(jnp.float32))
        upper.append(residual.astype(jnp.bfloat16))
        lower.append((residual - upper[-1].astype(jnp.float32)).astype(jnp.bfloat16))
    grad_ref[...] += jnp.dot(
        jnp.concatenate(upper + lower, 1),
        jnp.concatenate([block, block], 0),
        preferred_element_type=jnp.float32,
    )


def add_tiles(grad_ref, parts_ref, tiles, live, most, labels_at):
    tile = tiles.shape[0] // CHUNK

    @pl.when(live % 2 == 1)
    def _():
        blank = pl.multiple_of(live * tile, tile)
        tiles[pl.ds(blank, tile), :] = jnp.zeros((tile, tiles.shape[1]), tiles.dtype)

    fours = (live + 1) // 4 if most > 2 else jnp.int32(0)
    if most > 2:

        def four(index, carry):
            add_some(grad_ref, parts_ref, tiles, index * 4, 4, labels_at)
            return carry

        lax.fori_loop(0, fours, four, 0)

    @pl.when(live > 4 * fours)
    def _():
        add_some(grad_ref, parts_ref, tiles, 4 * fours, 2, labels_at)


def store_square(grad_ref, square_ref):
    gradient = grad_ref[...]
    square = jnp.sum(gradient * gradient, axis=0, keepdims=True)
    square = sum(square[:, at : at + 128] for at in range(0, square.shape[1], 128))
    square_ref[...] = jnp.broadcast_to(square, square_ref.shape)


def core_and_position(loop_size):
    me = lax.axis_index("loop")
    core, row, outer = me % 2, me // 2 % 2, me // 4
    return core, jnp.where(row == 0, outer, loop_size // 2 - 1 - outer)


def table_kernel(loop_size, origins, list_ref, count_ref, table_ref):
    chips = loop_size // 2
    lane = lax.broadcasted_iota(jnp.int32, table_ref.shape, 1)
    core, position = core_and_position(loop_size)
    hops, other = jnp.zeros_like(lane), jnp.zeros_like(lane)
    for at, origin in enumerate(origins):
        hops = jnp.where(lane == at, origin[0], hops)
        other = jnp.where(lane == at, origin[1], other)
    at = (position + chips + jnp.where(core == 0, -hops, hops)) & (chips - 1)
    chip = jnp.where(at < chips // 2, 2 * at, 2 * (chips - 1 - at) + 1)
    block = 2 * chip + jnp.where(other == 1, 1 - core, core)
    found = jnp.full_like(lane, -1)
    for slot in range(list_ref.shape[1]):
        name = jnp.where(slot < count_ref[...], list_ref[:, slot : slot + 1], -1)
        found = jnp.where(name == block, slot, found)
    table_ref[...] = jnp.where(lane < len(origins), found, -1)


def slot_table(loop_size, origins, block_list, live_count):
    return pl.pallas_call(
        functools.partial(table_kernel, loop_size, origins),
        out_shape=jax.ShapeDtypeStruct((1, 128), jnp.int32),
        in_specs=[pl.BlockSpec(memory_space=pltpu.VMEM)] * 2,
        out_specs=pl.BlockSpec(memory_space=pltpu.VMEM),
        compiler_params=pltpu.CompilerParams(vmem_limit_bytes=16 * 1024 * 1024),
        cost_estimate=pl.CostEstimate(flops=2**32, bytes_accessed=1024, transcendentals=0),
        name="slot_table",
    )(block_list, live_count.reshape(1, 1))


def add_some(grad_ref, parts_ref, tiles, start, count, labels_at):
    rows = grad_ref.shape[0]
    tile = tiles.shape[0] // CHUNK
    block = tiles[pl.ds(pl.multiple_of(start * tile, 2 * tile), count * tile), :]
    upper, lower = [], []
    for at in range(0, count, 2):
        both = lax.dot_general(
            parts_ref[...],
            block[at * tile : (at + 2) * tile],
            (((1,), (1,)), ((), ())),
            preferred_element_type=jnp.float32,
        )
        labels = jnp.concatenate([labels_at(start + at), labels_at(start + at + 1)], 1)
        residual = 0.5 * jnp.tanh(both[:rows] + both[rows:]) + (0.5 - labels.astype(jnp.float32))
        upper.append(residual.astype(jnp.bfloat16))
        lower.append((residual - upper[-1].astype(jnp.float32)).astype(jnp.bfloat16))
    grad_ref[...] += jnp.dot(
        jnp.concatenate(upper + lower, 1),
        jnp.concatenate([block, block], 0),
        preferred_element_type=jnp.float32,
    )


def add_tiles(grad_ref, parts_ref, tiles, live, most, labels_at):
    tile = tiles.shape[0] // CHUNK

    @pl.when(live % 2 == 1)
    def _():
        blank = pl.multiple_of(live * tile, tile)
        tiles[pl.ds(blank, tile), :] = jnp.zeros((tile, tiles.shape[1]), tiles.dtype)

    fours = (live + 1) // 4 if most > 2 else jnp.int32(0)
    if most > 2:

        def four(index, carry):
            add_some(grad_ref, parts_ref, tiles, index * 4, 4, labels_at)
            return carry

        lax.fori_loop(0, fours, four, 0)

    @pl.when(live > 4 * fours)
    def _():
        add_some(grad_ref, parts_ref, tiles, 4 * fours, 2, labels_at)


def store_square(grad_ref, square_ref):
    gradient = grad_ref[...]
    square = jnp.sum(gradient * gradient, axis=0, keepdims=True)
    square = sum(square[:, at : at + 128] for at in range(0, square.shape[1], 128))
    square_ref[...] = jnp.broadcast_to(square, square_ref.shape)


def core_and_position(loop_size):
    me = lax.axis_index("loop")
    core, row, outer = me % 2, me // 2 % 2, me // 4
    return core, jnp.where(row == 0, outer, loop_size // 2 - 1 - outer)


def origin_block(origin, loop_size):
    hops, other = origin
    chips = loop_size // 2
    core, position = core_and_position(loop_size)
    at = lax.rem(position + chips + jnp.where(core == 0, -hops, hops), chips)
    chip = jnp.where(at < chips // 2, 2 * at, 2 * (chips - 1 - at) + 1)
    return 2 * chip + (1 - core if other else core)


def pack_kernel(*refs):
    tile = refs[0].shape[0]
    for at, ref in enumerate(refs[:-1]):
        refs[-1][at * tile : (at + 1) * tile, :] = ref[...]


def pack(arrays):
    tile, width = arrays[0].shape
    return pl.pallas_call(
        pack_kernel,
        out_shape=jax.ShapeDtypeStruct((len(arrays) * tile, width), arrays[0].dtype),
        in_specs=[pl.BlockSpec(memory_space=pltpu.VMEM)] * len(arrays),
        out_specs=pl.BlockSpec(memory_space=pltpu.VMEM),
        compiler_params=pltpu.CompilerParams(vmem_limit_bytes=16 * 1024 * 1024),
        cost_estimate=pl.CostEstimate(
            flops=2**34, bytes_accessed=4 * len(arrays) * tile * width, transcendentals=0
        ),
        name="pack",
    )(*arrays)


def pieces_kernel(places, count, packed, loop_size, first, last, table_ref, given_ref, labels_ref, *rest):
    rest = list(rest)
    arrays = [rest.pop(0) for _ in range(count)]
    if not first:
        rest.pop(0)
    grad_ref = rest.pop(0)
    parts_ref = rest.pop(0) if first else given_ref
    across_ref = rest.pop(0) if first else None
    pack_ref = rest.pop(0) if packed else None
    square_ref = rest.pop(0) if last else None
    tiles, slots = rest
    tile = tiles.shape[0] // CHUNK
    for at, index in enumerate(packed):
        pack_ref[at * tile : (at + 1) * tile, :] = arrays[index][...]
    if first:
        core, position = core_and_position(loop_size)
        for at in range(2):

            @pl.when((core + position) % 2 == at)
            def _():
                across_ref[...] = arrays[1 + at][...]

        parts_ref[...] = halves(0.5 * given_ref[...])
        grad_ref[...] = jnp.zeros_like(grad_ref)
    live = jnp.int32(0)
    table = table_ref[...]
    entries = [table[0, at] for at, _, _ in places]
    for found, (_, index, row) in zip(entries, places):

        @pl.when(found >= 0)
        def _():
            into = pl.ds(pl.multiple_of(live * tile, tile), tile)
            tiles[into, :] = arrays[index][row * tile : (row + 1) * tile, :]
            slots[live] = found

        live = live + (found >= 0).astype(jnp.int32)
    slots[live] = 0

    def labels_at(position):
        return labels_ref[:, pl.ds(pl.multiple_of(slots[position] * tile, tile), tile)]

    add_tiles(grad_ref, parts_ref, tiles, live, min(len(places), CHUNK), labels_at)
    if last:
        store_square(grad_ref, square_ref)


def add_pieces(held, packed, loop_size, table, given, labels, before, last):
    first = before is None
    width = given.shape[1]
    rows = given.shape[0] // (1 if first else 2)
    arrays = [array for array, _ in held]
    tile = labels.shape[1] // CHUNK
    places = [(at, index, row) for index, (_, entries) in enumerate(held) for row, at in enumerate(entries)]
    most = min(len(places), CHUNK)
    out_shape = [jax.ShapeDtypeStruct((rows, width), jnp.float32)]
    if first:
        out_shape.append(jax.ShapeDtypeStruct((2 * rows, width), jnp.bfloat16))
        out_shape.append(jax.ShapeDtypeStruct((tile, width), jnp.bfloat16))
    if packed:
        out_shape.append(jax.ShapeDtypeStruct((len(packed) * tile, width), jnp.bfloat16))
    if last:
        out_shape.append(jax.ShapeDtypeStruct((loop_size, 128), jnp.float32))
    extra = [] if first else [before]
    return pl.pallas_call(
        functools.partial(pieces_kernel, places, len(arrays), packed, loop_size, first, last),
        out_shape=out_shape,
        in_specs=[pl.BlockSpec(memory_space=pltpu.VMEM)] * (3 + len(arrays) + len(extra)),
        out_specs=[pl.BlockSpec(memory_space=pltpu.VMEM)] * len(out_shape),
        input_output_aliases={} if first else {3 + len(arrays): 0},
        scratch_shapes=[
            pltpu.VMEM((CHUNK * tile, width), jnp.bfloat16),
            pltpu.SMEM((CHUNK + 1,), jnp.int32),
        ],
        compiler_params=pltpu.CompilerParams(vmem_limit_bytes=24 * 1024 * 1024),
        cost_estimate=pl.CostEstimate(
            flops=128 * rows * width * most * tile,
            bytes_accessed=8 * rows * width,
            transcendentals=rows * most * tile,
        ),
        name="add_pieces",
    )(table, given, labels, *arrays, *extra)


def ring_gradient(users, items, lists, labels):
    loop_size = lax.axis_size("loop")
    far = loop_size // 4
    origins = [(hops, 0) for hops in range(1 - far, far + 1)]
    origins += [(-hops, 1) for hops, _ in origins]
    table = slot_table(loop_size, origins, *lists)
    where = {origin: at for at, origin in enumerate(origins)}

    def held(hops, array):
        return array, [where[hops, 0]]

    def other(arrays, hops):
        return to_other_core(arrays, loop_size), [where[-hop, 1] for hop in hops]

    up = to_next(items, 1, loop_size)
    later, table = lax.optimization_barrier((items, table))
    down = to_next(later, -1, loop_size)
    down, up = down, lax.optimization_barrier((up, table))[0]
    first = [held(0, items), held(1, up), held(-1, down)]
    second = [held(2, to_next(up, 1, loop_size)), held(-2, to_next(down, -1, loop_size))]
    gradient, parts, opposite, packed = add_pieces(
        first, [0, 1, 2], loop_size, table, users, labels, None, False
    )
    opposite = across(opposite, loop_size)
    first = other(packed, [0, 1, -1])
    third = [held(3, to_next(second[0][0], 1, loop_size)), held(-3, to_next(second[1][0], -1, loop_size))]
    gradient, packed = add_pieces(second, [0, 1], loop_size, table, parts, labels, gradient, False)
    second = other(packed, [2, -2])
    third.append(held(4, opposite))
    arrived, gradient = lax.optimization_barrier(([array for array, _ in third], gradient))
    last = other(pack(arrived), [3, -3, 4])
    (gradient,) = add_pieces(
        third + [first, second], [], loop_size, table, parts, labels, gradient, False
    )
    return *add_pieces([last], [], loop_size, table, parts, labels, gradient, True), users


def chunks_kernel(
    list_ref, count_ref, users_ref, labels_ref, items_ref, grad_ref, square_ref, tiles, parts_ref, sems
):
    tile = tiles.shape[0] // CHUNK
    step = pl.program_id(0)
    live = jnp.clip(count_ref[0] - step * CHUNK, 0, CHUNK)

    @pl.when(step == 0)
    def _():
        parts_ref[...] = halves(0.5 * users_ref[...])
        grad_ref[...] = jnp.zeros_like(grad_ref)

    def move(slot):
        start = pl.multiple_of(list_ref[0, step * CHUNK + slot] * tile, tile)
        return pltpu.make_async_copy(
            items_ref.at[pl.ds(start, tile), :], tiles.at[pl.ds(slot * tile, tile), :], sems.at[slot]
        )

    for slot in range(CHUNK):
        pl.when(slot < live)(lambda slot=slot: move(slot).start())
    for slot in range(CHUNK):
        pl.when(slot < live)(lambda slot=slot: move(slot).wait())

    def labels_at(position):
        return labels_ref[:, pl.ds(pl.multiple_of(position * tile, tile), tile)]

    add_tiles(grad_ref, parts_ref, tiles, live, CHUNK, labels_at)

    @pl.when(step == pl.num_programs(0) - 1)
    def _():
        store_square(grad_ref, square_ref)


def add_chunks(loop_size, items, lists, users, labels):
    rows, width = users.shape
    slots = lists[0].shape[1]
    tile = labels.shape[1] // slots
    return pl.pallas_call(
        chunks_kernel,
        grid=(slots // CHUNK,),
        out_shape=[
            jax.ShapeDtypeStruct((rows, width), jnp.float32),
            jax.ShapeDtypeStruct((loop_size, 128), jnp.float32),
        ],
        in_specs=[
            pl.BlockSpec(memory_space=pltpu.SMEM),
            pl.BlockSpec(memory_space=pltpu.SMEM),
            pl.BlockSpec((rows, width), lambda step: (0, 0)),
            pl.BlockSpec((rows, CHUNK * tile), lambda step: (0, step)),
            pl.BlockSpec(memory_space=pl.ANY),
        ],
        out_specs=[
            pl.BlockSpec((rows, width), lambda step: (0, 0)),
            pl.BlockSpec((loop_size, 128), lambda step: (0, 0)),
        ],
        scratch_shapes=[
            pltpu.VMEM((CHUNK * tile, width), jnp.bfloat16),
            pltpu.VMEM((2 * rows, width), jnp.bfloat16),
            pltpu.SemaphoreType.DMA((CHUNK,)),
        ],
        compiler_params=pltpu.CompilerParams(vmem_limit_bytes=32 * 1024 * 1024),
        cost_estimate=pl.CostEstimate(
            flops=8 * rows * width * slots * tile,
            bytes_accessed=4 * rows * (slots * tile + 2 * width) + 2 * slots * tile * width,
            transcendentals=rows * slots * tile,
        ),
        name="add_chunks",
    )(*lists, users, labels, items)


def update_kernel(entries, users_ref, grad_ref, squares_ref, out_ref):
    total = jnp.sum(squares_ref[...], axis=0, keepdims=True)
    total = jnp.sum(total, axis=1, keepdims=True)
    scale = 0.5 / jnp.sqrt(total / entries + 1e-06)
    out_ref[...] = users_ref[...] - scale * grad_ref[...]


def local(users, items, tile_blocks, tile_count, labels):
    loop_size = lax.axis_size("loop")
    rows, width = users.shape
    slots = tile_blocks.shape[1]
    lists = (tile_blocks, tile_count)
    if loop_size == RING and slots == CHUNK:
        gradient, square, users = ring_gradient(users, items, lists, labels)
    else:
        whole = lax.all_gather(items, "loop", axis=0, tiled=True)
        gradient, square = add_chunks(loop_size, whole, lists, users, labels)

    squares = lax.all_to_all(square, "loop", 0, 0, tiled=True)
    return pl.pallas_call(
        functools.partial(update_kernel, rows * loop_size * width),
        out_shape=jax.ShapeDtypeStruct((rows, width), jnp.float32),
        in_specs=[pl.BlockSpec(memory_space=pltpu.VMEM)] * 3,
        out_specs=pl.BlockSpec(memory_space=pltpu.VMEM),
        compiler_params=pltpu.CompilerParams(vmem_limit_bytes=16 * 1024 * 1024),
        cost_estimate=pl.CostEstimate(
            flops=2 * rows * width, bytes_accessed=12 * rows * width, transcendentals=0
        ),
        name="update",
    )(users, gradient, squares)


def solution(mesh):
    in_specs = (
        P(("group", "loop"), None),
        P(("group", "loop"), None),
        P(("group", "loop"), None),
        P(("group", "loop")),
        P(("group", "loop"), None),
    )
    out_specs = P(("group", "loop"), None)
    return jax.shard_map(local, mesh=mesh, in_specs=in_specs, out_specs=out_specs, check_vma=False)
```

```python
import functools

import jax
import jax.numpy as jnp
from jax import lax
from jax.experimental import pallas as pl
from jax.experimental.pallas import tpu as pltpu
from jax.sharding import PartitionSpec as P

CHUNK = 8
RING = 16


def ring_place(loop_size):
    outer = loop_size // 4

    def device(position, core):
        position = position % (2 * outer)
        chip = 2 * position if position < outer else 2 * (2 * outer - 1 - position) + 1
        return 2 * chip + core

    return 2 * outer, device


def to_next(array, direction, loop_size):
    chips, device = ring_place(loop_size)
    pairs = [(device(at, 0), device(at + direction, 0)) for at in range(chips)]
    pairs += [(device(at, 1), device(at - direction, 1)) for at in range(chips)]
    return lax.ppermute(array, "loop", pairs)


def across(array, loop_size):
    chips, device = ring_place(loop_size)
    pairs = [
        (device(at, core), device(at + (3 if at % 2 == 0 else -3), core))
        for at in range(chips)
        for core in range(2)
    ]
    return lax.ppermute(array, "loop", pairs)


def to_other_core(array, loop_size):
    return lax.ppermute(array, "loop", [(at, at ^ 1) for at in range(loop_size)])


def halves(values):
    upper = values.astype(jnp.bfloat16)
    return jnp.concatenate([upper, (values - upper.astype(jnp.float32)).astype(jnp.bfloat16)], 0)


def table_kernel(loop_size, origins, list_ref, count_ref, table_ref):
    chips = loop_size // 2
    lane = lax.broadcasted_iota(jnp.int32, table_ref.shape, 1)
    core, position = core_and_position(loop_size)
    hops, other = jnp.zeros_like(lane), jnp.zeros_like(lane)
    for at, origin in enumerate(origins):
        hops = jnp.where(lane == at, origin[0], hops)
        other = jnp.where(lane == at, origin[1], other)
    at = (position + chips + jnp.where(core == 0, -hops, hops)) & (chips - 1)
    chip = jnp.where(at < chips // 2, 2 * at, 2 * (chips - 1 - at) + 1)
    block = 2 * chip + jnp.where(other == 1, 1 - core, core)
    found = jnp.full_like(lane, -1)
    for slot in range(list_ref.shape[1]):
        name = jnp.where(slot < count_ref[...], list_ref[:, slot : slot + 1], -1)
        found = jnp.where(name == block, slot, found)
    table_ref[...] = jnp.where(lane < len(origins), found, -1)


def slot_table(loop_size, origins, block_list, live_count):
    return pl.pallas_call(
        functools.partial(table_kernel, loop_size, origins),
        out_shape=jax.ShapeDtypeStruct((1, 128), jnp.int32),
        in_specs=[pl.BlockSpec(memory_space=pltpu.VMEM)] * 2,
        out_specs=pl.BlockSpec(memory_space=pltpu.VMEM),
        compiler_params=pltpu.CompilerParams(vmem_limit_bytes=16 * 1024 * 1024),
        cost_estimate=pl.CostEstimate(flops=2**32, bytes_accessed=1024, transcendentals=0),
        name="slot_table",
    )(block_list, live_count.reshape(1, 1))


def add_some(grad_ref, parts_ref, tiles, start, count, labels_at):
    rows = grad_ref.shape[0]
    tile = tiles.shape[0] // CHUNK
    block = tiles[pl.ds(pl.multiple_of(start * tile, tile), count * tile), :]
    upper, lower = [], []
    for at in range(0, count, 2):
        few = min(2, count)
        both = lax.dot_general(
            parts_ref[...],
            block[at * tile : (at + few) * tile],
            (((1,), (1,)), ((), ())),
            preferred_element_type=jnp.float32,
        )
        labels = [labels_at(start + at + more) for more in range(few)]
        labels = labels[0] if few == 1 else jnp.concatenate(labels, 1)
        residual = 0.5 * jnp.tanh(both[:rows] + both[rows:]) + (0.5 - labels.astype(jnp.float32))
        upper.append(residual.astype(jnp.bfloat16))
        lower.append((residual - upper[-1].astype(jnp.float32)).astype(jnp.bfloat16))
    grad_ref[...] += jnp.dot(
        jnp.concatenate(upper + lower, 1),
        jnp.concatenate([block, block], 0),
        preferred_element_type=jnp.float32,
    )


def add_tiles(grad_ref, parts_ref, tiles, live, most, labels_at):
    tile = tiles.shape[0] // CHUNK
    fours = jnp.int32(0)
    if most > 3:
        fours = (live + 1) // 4

        @pl.when(live % 4 == 3)
        def _():
            blank = pl.multiple_of(live * tile, tile)
            tiles[pl.ds(blank, tile), :] = jnp.zeros((tile, tiles.shape[1]), tiles.dtype)

        def four(index, carry):
            add_some(grad_ref, parts_ref, tiles, index * 4, 4, labels_at)
            return carry

        lax.fori_loop(0, fours, four, 0)

    def one(index, carry):
        add_some(grad_ref, parts_ref, tiles, index, 1, labels_at)
        return carry

    lax.fori_loop(4 * fours, jnp.maximum(live, 4 * fours), one, 0)


def store_square(grad_ref, square_ref):
    gradient = grad_ref[...]
    square = jnp.sum(gradient * gradient, axis=0, keepdims=True)
    square = sum(square[:, at : at + 128] for at in range(0, square.shape[1], 128))
    square_ref[...] = jnp.broadcast_to(square, square_ref.shape)


def core_and_position(loop_size):
    me = lax.axis_index("loop")
    core, row, outer = me % 2, me // 2 % 2, me // 4
    return core, jnp.where(row == 0, outer, loop_size // 2 - 1 - outer)


def table_kernel(loop_size, origins, list_ref, count_ref, table_ref):
    chips = loop_size // 2
    lane = lax.broadcasted_iota(jnp.int32, table_ref.shape, 1)
    core, position = core_and_position(loop_size)
    hops, other = jnp.zeros_like(lane), jnp.zeros_like(lane)
    for at, origin in enumerate(origins):
        hops = jnp.where(lane == at, origin[0], hops)
        other = jnp.where(lane == at, origin[1], other)
    at = (position + chips + jnp.where(core == 0, -hops, hops)) & (chips - 1)
    chip = jnp.where(at < chips // 2, 2 * at, 2 * (chips - 1 - at) + 1)
    block = 2 * chip + jnp.where(other == 1, 1 - core, core)
    found = jnp.full_like(lane, -1)
    for slot in range(list_ref.shape[1]):
        name = jnp.where(slot < count_ref[...], list_ref[:, slot : slot + 1], -1)
        found = jnp.where(name == block, slot, found)
    table_ref[...] = jnp.where(lane < len(origins), found, -1)


def slot_table(loop_size, origins, block_list, live_count):
    return pl.pallas_call(
        functools.partial(table_kernel, loop_size, origins),
        out_shape=jax.ShapeDtypeStruct((1, 128), jnp.int32),
        in_specs=[pl.BlockSpec(memory_space=pltpu.VMEM)] * 2,
        out_specs=pl.BlockSpec(memory_space=pltpu.VMEM),
        compiler_params=pltpu.CompilerParams(vmem_limit_bytes=16 * 1024 * 1024),
        cost_estimate=pl.CostEstimate(flops=2**32, bytes_accessed=1024, transcendentals=0),
        name="slot_table",
    )(block_list, live_count.reshape(1, 1))


def add_some(grad_ref, parts_ref, tiles, start, count, labels_at):
    rows = grad_ref.shape[0]
    tile = tiles.shape[0] // CHUNK
    block = tiles[pl.ds(pl.multiple_of(start * tile, 2 * tile), count * tile), :]
    upper, lower = [], []
    for at in range(0, count, 2):
        both = lax.dot_general(
            parts_ref[...],
            block[at * tile : (at + 2) * tile],
            (((1,), (1,)), ((), ())),
            preferred_element_type=jnp.float32,
        )
        labels = jnp.concatenate([labels_at(start + at), labels_at(start + at + 1)], 1)
        residual = 0.5 * jnp.tanh(both[:rows] + both[rows:]) + (0.5 - labels.astype(jnp.float32))
        upper.append(residual.astype(jnp.bfloat16))
        lower.append((residual - upper[-1].astype(jnp.float32)).astype(jnp.bfloat16))
    grad_ref[...] += jnp.dot(
        jnp.concatenate(upper + lower, 1),
        jnp.concatenate([block, block], 0),
        preferred_element_type=jnp.float32,
    )


def add_tiles(grad_ref, parts_ref, tiles, live, most, labels_at):
    tile = tiles.shape[0] // CHUNK

    @pl.when(live % 2 == 1)
    def _():
        blank = pl.multiple_of(live * tile, tile)
        tiles[pl.ds(blank, tile), :] = jnp.zeros((tile, tiles.shape[1]), tiles.dtype)

    fours = (live + 1) // 4 if most > 2 else jnp.int32(0)
    if most > 2:

        def four(index, carry):
            add_some(grad_ref, parts_ref, tiles, index * 4, 4, labels_at)
            return carry

        lax.fori_loop(0, fours, four, 0)

    @pl.when(live > 4 * fours)
    def _():
        add_some(grad_ref, parts_ref, tiles, 4 * fours, 2, labels_at)


def store_square(grad_ref, square_ref):
    gradient = grad_ref[...]
    square = jnp.sum(gradient * gradient, axis=0, keepdims=True)
    square = sum(square[:, at : at + 128] for at in range(0, square.shape[1], 128))
    square_ref[...] = jnp.broadcast_to(square, square_ref.shape)


def core_and_position(loop_size):
    me = lax.axis_index("loop")
    core, row, outer = me % 2, me // 2 % 2, me // 4
    return core, jnp.where(row == 0, outer, loop_size // 2 - 1 - outer)


def origin_block(origin, loop_size):
    hops, other = origin
    chips = loop_size // 2
    core, position = core_and_position(loop_size)
    at = lax.rem(position + chips + jnp.where(core == 0, -hops, hops), chips)
    chip = jnp.where(at < chips // 2, 2 * at, 2 * (chips - 1 - at) + 1)
    return 2 * chip + (1 - core if other else core)


def pack_kernel(*refs):
    tile = refs[0].shape[0]
    for at, ref in enumerate(refs[:-1]):
        refs[-1][at * tile : (at + 1) * tile, :] = ref[...]


def pack(arrays):
    tile, width = arrays[0].shape
    return pl.pallas_call(
        pack_kernel,
        out_shape=jax.ShapeDtypeStruct((len(arrays) * tile, width), arrays[0].dtype),
        in_specs=[pl.BlockSpec(memory_space=pltpu.VMEM)] * len(arrays),
        out_specs=pl.BlockSpec(memory_space=pltpu.VMEM),
        compiler_params=pltpu.CompilerParams(vmem_limit_bytes=16 * 1024 * 1024),
        cost_estimate=pl.CostEstimate(
            flops=2**34, bytes_accessed=4 * len(arrays) * tile * width, transcendentals=0
        ),
        name="pack",
    )(*arrays)


def pieces_kernel(places, count, packed, loop_size, first, last, table_ref, given_ref, labels_ref, *rest):
    rest = list(rest)
    arrays = [rest.pop(0) for _ in range(count)]
    if not first:
        rest.pop(0)
    grad_ref = rest.pop(0)
    parts_ref = rest.pop(0) if first else given_ref
    across_ref = rest.pop(0) if first else None
    pack_ref = rest.pop(0) if packed else None
    square_ref = rest.pop(0) if last else None
    tiles, slots = rest
    tile = tiles.shape[0] // CHUNK
    for at, index in enumerate(packed):
        pack_ref[at * tile : (at + 1) * tile, :] = arrays[index][...]
    if first:
        core, position = core_and_position(loop_size)
        for at in range(2):

            @pl.when((core + position) % 2 == at)
            def _():
                across_ref[...] = arrays[1 + at][...]

        parts_ref[...] = halves(0.5 * given_ref[...])
        grad_ref[...] = jnp.zeros_like(grad_ref)
    live = jnp.int32(0)
    table = table_ref[...]
    entries = [table[0, at] for at, _, _ in places]
    for found, (_, index, row) in zip(entries, places):

        @pl.when(found >= 0)
        def _():
            into = pl.ds(pl.multiple_of(live * tile, tile), tile)
            tiles[into, :] = arrays[index][row * tile : (row + 1) * tile, :]
            slots[live] = found

        live = live + (found >= 0).astype(jnp.int32)
    slots[live] = 0

    def labels_at(position):
        return labels_ref[:, pl.ds(pl.multiple_of(slots[position] * tile, tile), tile)]

    add_tiles(grad_ref, parts_ref, tiles, live, min(len(places), CHUNK), labels_at)
    if last:
        store_square(grad_ref, square_ref)


def add_pieces(held, packed, loop_size, table, given, labels, before, last):
    first = before is None
    width = given.shape[1]
    rows = given.shape[0] // (1 if first else 2)
    arrays = [array for array, _ in held]
    tile = labels.shape[1] // CHUNK
    places = [(at, index, row) for index, (_, entries) in enumerate(held) for row, at in enumerate(entries)]
    most = min(len(places), CHUNK)
    out_shape = [jax.ShapeDtypeStruct((rows, width), jnp.float32)]
    if first:
        out_shape.append(jax.ShapeDtypeStruct((2 * rows, width), jnp.bfloat16))
        out_shape.append(jax.ShapeDtypeStruct((tile, width), jnp.bfloat16))
    if packed:
        out_shape.append(jax.ShapeDtypeStruct((len(packed) * tile, width), jnp.bfloat16))
    if last:
        out_shape.append(jax.ShapeDtypeStruct((loop_size, 128), jnp.float32))
    extra = [] if first else [before]
    return pl.pallas_call(
        functools.partial(pieces_kernel, places, len(arrays), packed, loop_size, first, last),
        out_shape=out_shape,
        in_specs=[pl.BlockSpec(memory_space=pltpu.VMEM)] * (3 + len(arrays) + len(extra)),
        out_specs=[pl.BlockSpec(memory_space=pltpu.VMEM)] * len(out_shape),
        input_output_aliases={} if first else {3 + len(arrays): 0},
        scratch_shapes=[
            pltpu.VMEM((CHUNK * tile, width), jnp.bfloat16),
            pltpu.SMEM((CHUNK + 1,), jnp.int32),
        ],
        compiler_params=pltpu.CompilerParams(vmem_limit_bytes=24 * 1024 * 1024),
        cost_estimate=pl.CostEstimate(
            flops=128 * rows * width * most * tile,
            bytes_accessed=8 * rows * width,
            transcendentals=rows * most * tile,
        ),
        name="add_pieces",
    )(table, given, labels, *arrays, *extra)


def ring_gradient(users, items, lists, labels):
    loop_size = lax.axis_size("loop")
    far = loop_size // 4
    origins = [(hops, 0) for hops in range(1 - far, far + 1)]
    origins += [(-hops, 1) for hops, _ in origins]
    table = slot_table(loop_size, origins, *lists)
    where = {origin: at for at, origin in enumerate(origins)}

    def held(hops, array):
        return array, [where[hops, 0]]

    def other(arrays, hops):
        return to_other_core(arrays, loop_size), [where[-hop, 1] for hop in hops]

    up = to_next(items, 1, loop_size)
    down = to_next(items, -1, loop_size)
    up, table = lax.optimization_barrier((up, table))
    first = [held(0, items), held(1, up), held(-1, down)]
    second = [held(2, to_next(up, 1, loop_size)), held(-2, to_next(down, -1, loop_size))]
    gradient, parts, opposite, packed = add_pieces(
        first, [0, 1, 2], loop_size, table, users, labels, None, False
    )
    opposite = across(opposite, loop_size)
    first = other(packed, [0, 1, -1])
    third = [held(3, to_next(second[0][0], 1, loop_size)), held(-3, to_next(second[1][0], -1, loop_size))]
    gradient, packed = add_pieces(second, [0, 1], loop_size, table, parts, labels, gradient, False)
    second = other(packed, [2, -2])
    third.append(held(4, opposite))
    arrived, gradient = lax.optimization_barrier(([array for array, _ in third], gradient))
    final = other(pack(arrived), [3, -3, 4])
    (gradient,) = add_pieces(
        third + [first, second], [], loop_size, table, parts, labels, gradient, False
    )
    return *add_pieces([final], [], loop_size, table, parts, labels, gradient, True), users


def chunks_kernel(
    list_ref, count_ref, users_ref, labels_ref, items_ref, grad_ref, square_ref, tiles, parts_ref, sems
):
    tile = tiles.shape[0] // CHUNK
    step = pl.program_id(0)
    live = jnp.clip(count_ref[0] - step * CHUNK, 0, CHUNK)

    @pl.when(step == 0)
    def _():
        parts_ref[...] = halves(0.5 * users_ref[...])
        grad_ref[...] = jnp.zeros_like(grad_ref)

    def move(slot):
        start = pl.multiple_of(list_ref[0, step * CHUNK + slot] * tile, tile)
        return pltpu.make_async_copy(
            items_ref.at[pl.ds(start, tile), :], tiles.at[pl.ds(slot * tile, tile), :], sems.at[slot]
        )

    for slot in range(CHUNK):
        pl.when(slot < live)(lambda slot=slot: move(slot).start())
    for slot in range(CHUNK):
        pl.when(slot < live)(lambda slot=slot: move(slot).wait())

    def labels_at(position):
        return labels_ref[:, pl.ds(pl.multiple_of(position * tile, tile), tile)]

    add_tiles(grad_ref, parts_ref, tiles, live, CHUNK, labels_at)

    @pl.when(step == pl.num_programs(0) - 1)
    def _():
        store_square(grad_ref, square_ref)


def add_chunks(loop_size, items, lists, users, labels):
    rows, width = users.shape
    slots = lists[0].shape[1]
    tile = labels.shape[1] // slots
    return pl.pallas_call(
        chunks_kernel,
        grid=(slots // CHUNK,),
        out_shape=[
            jax.ShapeDtypeStruct((rows, width), jnp.float32),
            jax.ShapeDtypeStruct((loop_size, 128), jnp.float32),
        ],
        in_specs=[
            pl.BlockSpec(memory_space=pltpu.SMEM),
            pl.BlockSpec(memory_space=pltpu.SMEM),
            pl.BlockSpec((rows, width), lambda step: (0, 0)),
            pl.BlockSpec((rows, CHUNK * tile), lambda step: (0, step)),
            pl.BlockSpec(memory_space=pl.ANY),
        ],
        out_specs=[
            pl.BlockSpec((rows, width), lambda step: (0, 0)),
            pl.BlockSpec((loop_size, 128), lambda step: (0, 0)),
        ],
        scratch_shapes=[
            pltpu.VMEM((CHUNK * tile, width), jnp.bfloat16),
            pltpu.VMEM((2 * rows, width), jnp.bfloat16),
            pltpu.SemaphoreType.DMA((CHUNK,)),
        ],
        compiler_params=pltpu.CompilerParams(vmem_limit_bytes=32 * 1024 * 1024),
        cost_estimate=pl.CostEstimate(
            flops=8 * rows * width * slots * tile,
            bytes_accessed=4 * rows * (slots * tile + 2 * width) + 2 * slots * tile * width,
            transcendentals=rows * slots * tile,
        ),
        name="add_chunks",
    )(*lists, users, labels, items)


def update_kernel(entries, users_ref, grad_ref, squares_ref, out_ref, result, sems):
    total = jnp.sum(squares_ref[...], axis=0, keepdims=True)
    total = jnp.sum(total, axis=1, keepdims=True)
    scale = 0.5 / jnp.sqrt(total / entries + 1e-06)
    rows = users_ref.shape[0] // sems.shape[0]
    copies = []
    for at in range(sems.shape[0]):
        part = pl.ds(at * rows, rows)
        result[part, :] = users_ref[part, :] - scale * grad_ref[part, :]
        copies.append(pltpu.make_async_copy(result.at[part, :], out_ref.at[part, :], sems.at[at]))
        copies[-1].start()
    for copy in copies:
        copy.wait()


def local(users, items, tile_blocks, tile_count, labels):
    loop_size = lax.axis_size("loop")
    rows, width = users.shape
    slots = tile_blocks.shape[1]
    lists = (tile_blocks, tile_count)
    if loop_size == RING and slots == CHUNK:
        gradient, square, users = ring_gradient(users, items, lists, labels)
    else:
        whole = lax.all_gather(items, "loop", axis=0, tiled=True)
        gradient, square = add_chunks(loop_size, whole, lists, users, labels)

    squares = lax.all_to_all(square, "loop", 0, 0, tiled=True)
    return pl.pallas_call(
        functools.partial(update_kernel, rows * loop_size * width),
        out_shape=jax.ShapeDtypeStruct((rows, width), jnp.float32),
        in_specs=[pl.BlockSpec(memory_space=pltpu.VMEM)] * 3,
        out_specs=pl.BlockSpec(memory_space=pl.ANY),
        scratch_shapes=[pltpu.VMEM((rows, width), jnp.float32), pltpu.SemaphoreType.DMA((4,))],
        compiler_params=pltpu.CompilerParams(vmem_limit_bytes=16 * 1024 * 1024),
        cost_estimate=pl.CostEstimate(
            flops=2 * rows * width, bytes_accessed=12 * rows * width, transcendentals=0
        ),
        name="update",
    )(users, gradient, squares)


def solution(mesh):
    in_specs = (
        P(("group", "loop"), None),
        P(("group", "loop"), None),
        P(("group", "loop"), None),
        P(("group", "loop")),
        P(("group", "loop"), None),
    )
    out_specs = P(("group", "loop"), None)
    return jax.shard_map(local, mesh=mesh, in_specs=in_specs, out_specs=out_specs, check_vma=False)
```

```python
import functools

import jax
import jax.numpy as jnp
from jax import lax
from jax.experimental import pallas as pl
from jax.experimental.pallas import tpu as pltpu
from jax.sharding import PartitionSpec as P

CHUNK = 8
RING = 16
FEW = 3


def ring_place(loop_size):
    outer = loop_size // 4

    def device(position, core):
        position = position % (2 * outer)
        chip = 2 * position if position < outer else 2 * (2 * outer - 1 - position) + 1
        return 2 * chip + core

    return 2 * outer, device


def to_next(array, direction, loop_size):
    chips, device = ring_place(loop_size)
    pairs = [(device(at, 0), device(at + direction, 0)) for at in range(chips)]
    pairs += [(device(at, 1), device(at - direction, 1)) for at in range(chips)]
    return lax.ppermute(array, "loop", pairs)


def across(array, loop_size):
    chips, device = ring_place(loop_size)
    pairs = [
        (device(at, core), device(at + (3 if at % 2 == 0 else -3), core))
        for at in range(chips)
        for core in range(2)
    ]
    return lax.ppermute(array, "loop", pairs)


def to_other_core(array, loop_size):
    return lax.ppermute(array, "loop", [(at, at ^ 1) for at in range(loop_size)])


def halves(values):
    upper = values.astype(jnp.bfloat16)
    return jnp.concatenate([upper, (values - upper.astype(jnp.float32)).astype(jnp.bfloat16)], 0)


def table_kernel(loop_size, origins, list_ref, count_ref, table_ref):
    chips = loop_size // 2
    lane = lax.broadcasted_iota(jnp.int32, table_ref.shape, 1)
    core, position = core_and_position(loop_size)
    hops, other = jnp.zeros_like(lane), jnp.zeros_like(lane)
    for at, origin in enumerate(origins):
        hops = jnp.where(lane == at, origin[0], hops)
        other = jnp.where(lane == at, origin[1], other)
    at = (position + chips + jnp.where(core == 0, -hops, hops)) & (chips - 1)
    chip = jnp.where(at < chips // 2, 2 * at, 2 * (chips - 1 - at) + 1)
    block = 2 * chip + jnp.where(other == 1, 1 - core, core)
    found = jnp.full_like(lane, -1)
    for slot in range(list_ref.shape[1]):
        name = jnp.where(slot < count_ref[...], list_ref[:, slot : slot + 1], -1)
        found = jnp.where(name == block, slot, found)
    table_ref[...] = jnp.where(lane < len(origins), found, -1)


def slot_table(loop_size, origins, block_list, live_count):
    return pl.pallas_call(
        functools.partial(table_kernel, loop_size, origins),
        out_shape=jax.ShapeDtypeStruct((1, 128), jnp.int32),
        in_specs=[pl.BlockSpec(memory_space=pltpu.VMEM)] * 2,
        out_specs=pl.BlockSpec(memory_space=pltpu.VMEM),
        compiler_params=pltpu.CompilerParams(vmem_limit_bytes=16 * 1024 * 1024),
        cost_estimate=pl.CostEstimate(flops=2**32, bytes_accessed=1024, transcendentals=0),
        name="slot_table",
    )(block_list, live_count.reshape(1, 1))


def add_block(grad_ref, parts_ref, block, labels):
    rows = grad_ref.shape[0]
    tile = labels[0].shape[1]
    upper, lower = [], []
    for at in range(0, len(labels), 2):
        some = jnp.concatenate(labels[at : at + 2], 1)
        both = lax.dot_general(
            parts_ref[...],
            block[at * tile : at * tile + some.shape[1]],
            (((1,), (1,)), ((), ())),
            preferred_element_type=jnp.float32,
        )
        residual = 0.5 * jnp.tanh(both[:rows] + both[rows:]) + (0.5 - some.astype(jnp.float32))
        upper.append(residual.astype(jnp.bfloat16))
        lower.append((residual - upper[-1].astype(jnp.float32)).astype(jnp.bfloat16))
    grad_ref[...] += jnp.dot(
        jnp.concatenate(upper + lower, 1),
        jnp.concatenate([block, block], 0),
        preferred_element_type=jnp.float32,
    )


def add_tiles(grad_ref, parts_ref, tiles, live, labels_at):
    tile = tiles.shape[0] // CHUNK
    fours = (live + 1) // 4

    @pl.when(live % 4 == 3)
    def _():
        blank = pl.multiple_of(live * tile, tile)
        tiles[pl.ds(blank, tile), :] = jnp.zeros((tile, tiles.shape[1]), tiles.dtype)

    def add(count, index, carry):
        start = index * count
        block = tiles[pl.ds(pl.multiple_of(start * tile, tile), count * tile), :]
        add_block(grad_ref, parts_ref, block, [labels_at(start + at) for at in range(count)])
        return carry

    lax.fori_loop(0, fours, functools.partial(add, 4), 0)
    lax.fori_loop(4 * fours, jnp.maximum(live, 4 * fours), functools.partial(add, 1), 0)


def store_square(grad_ref, square_ref):
    gradient = grad_ref[...]
    square = jnp.sum(gradient * gradient, axis=0, keepdims=True)
    square = sum(square[:, at : at + 128] for at in range(0, square.shape[1], 128))
    square_ref[...] = jnp.broadcast_to(square, square_ref.shape)


def core_and_position(loop_size):
    me = lax.axis_index("loop")
    core, row, outer = me % 2, me // 2 % 2, me // 4
    return core, jnp.where(row == 0, outer, loop_size // 2 - 1 - outer)


def pack_kernel(*refs):
    tile = refs[0].shape[0]
    for at, ref in enumerate(refs[:-1]):
        refs[-1][at * tile : (at + 1) * tile, :] = ref[...]


def pack(arrays):
    tile, width = arrays[0].shape
    return pl.pallas_call(
        pack_kernel,
        out_shape=jax.ShapeDtypeStruct((len(arrays) * tile, width), arrays[0].dtype),
        in_specs=[pl.BlockSpec(memory_space=pltpu.VMEM)] * len(arrays),
        out_specs=pl.BlockSpec(memory_space=pltpu.VMEM),
        compiler_params=pltpu.CompilerParams(vmem_limit_bytes=16 * 1024 * 1024),
        cost_estimate=pl.CostEstimate(
            flops=2**34, bytes_accessed=4 * len(arrays) * tile * width, transcendentals=0
        ),
        name="pack",
    )(*arrays)


def pieces_kernel(places, count, packed, loop_size, first, last, table_ref, given_ref, labels_ref, *rest):
    rest = list(rest)
    arrays = [rest.pop(0) for _ in range(count)]
    if not first:
        rest.pop(0)
    grad_ref = rest.pop(0)
    parts_ref = rest.pop(0) if first else given_ref
    across_ref = rest.pop(0) if first else None
    pack_ref = rest.pop(0) if packed else None
    square_ref = rest.pop(0) if last else None
    tiles, slots = rest
    tile = tiles.shape[0] // CHUNK
    for at, index in enumerate(packed):
        pack_ref[at * tile : (at + 1) * tile, :] = arrays[index][...]
    if first:
        core, position = core_and_position(loop_size)
        for at in range(2):

            @pl.when((core + position) % 2 == at)
            def _():
                across_ref[...] = arrays[1 + at][...]

        parts_ref[...] = halves(0.5 * given_ref[...])
        grad_ref[...] = jnp.zeros_like(grad_ref)
    table = table_ref[...]
    entries = [table[0, at] for at, _, _ in places]

    def labels_of(slot):
        return labels_ref[:, pl.ds(pl.multiple_of(slot * tile, tile), tile)]

    if len(places) <= FEW:
        for found, (_, index, row) in zip(entries, places):

            @pl.when(found >= 0)
            def _():
                block = arrays[index][row * tile : (row + 1) * tile, :]
                add_block(grad_ref, parts_ref, block, [labels_of(found)])

    else:
        live = jnp.int32(0)
        for found, (_, index, row) in zip(entries, places):

            @pl.when(found >= 0)
            def _():
                into = pl.ds(pl.multiple_of(live * tile, tile), tile)
                tiles[into, :] = arrays[index][row * tile : (row + 1) * tile, :]
                slots[live] = found

            live = live + (found >= 0).astype(jnp.int32)
        slots[live] = 0
        add_tiles(grad_ref, parts_ref, tiles, live, lambda position: labels_of(slots[position]))
    if last:
        store_square(grad_ref, square_ref)


def add_pieces(held, packed, loop_size, table, given, labels, before, last):
    first = before is None
    width = given.shape[1]
    rows = given.shape[0] // (1 if first else 2)
    arrays = [array for array, _ in held]
    tile = labels.shape[1] // CHUNK
    places = [(at, index, row) for index, (_, entries) in enumerate(held) for row, at in enumerate(entries)]
    most = min(len(places), CHUNK)
    out_shape = [jax.ShapeDtypeStruct((rows, width), jnp.float32)]
    if first:
        out_shape.append(jax.ShapeDtypeStruct((2 * rows, width), jnp.bfloat16))
        out_shape.append(jax.ShapeDtypeStruct((tile, width), jnp.bfloat16))
    if packed:
        out_shape.append(jax.ShapeDtypeStruct((len(packed) * tile, width), jnp.bfloat16))
    if last:
        out_shape.append(jax.ShapeDtypeStruct((loop_size, 128), jnp.float32))
    extra = [] if first else [before]
    return pl.pallas_call(
        functools.partial(pieces_kernel, places, len(arrays), packed, loop_size, first, last),
        out_shape=out_shape,
        in_specs=[pl.BlockSpec(memory_space=pltpu.VMEM)] * (3 + len(arrays) + len(extra)),
        out_specs=[pl.BlockSpec(memory_space=pltpu.VMEM)] * len(out_shape),
        input_output_aliases={} if first else {3 + len(arrays): 0},
        scratch_shapes=[
            pltpu.VMEM((CHUNK * tile, width), jnp.bfloat16),
            pltpu.SMEM((CHUNK + 1,), jnp.int32),
        ],
        compiler_params=pltpu.CompilerParams(vmem_limit_bytes=24 * 1024 * 1024),
        cost_estimate=pl.CostEstimate(
            flops=128 * rows * width * most * tile,
            bytes_accessed=8 * rows * width,
            transcendentals=rows * most * tile,
        ),
        name="add_pieces",
    )(table, given, labels, *arrays, *extra)


def ring_gradient(users, items, lists, labels):
    loop_size = lax.axis_size("loop")
    far = loop_size // 4
    origins = [(hops, 0) for hops in range(1 - far, far + 1)]
    origins += [(-hops, 1) for hops, _ in origins]
    table = slot_table(loop_size, origins, *lists)
    where = {origin: at for at, origin in enumerate(origins)}

    def held(hops, array):
        return array, [where[hops, 0]]

    def other(arrays, hops):
        return to_other_core(arrays, loop_size), [where[-hop, 1] for hop in hops]

    up = to_next(items, 1, loop_size)
    down = to_next(items, -1, loop_size)
    up, table = lax.optimization_barrier((up, table))
    first = [held(0, items), held(1, up), held(-1, down)]
    second = [held(2, to_next(up, 1, loop_size)), held(-2, to_next(down, -1, loop_size))]
    gradient, parts, opposite, packed = add_pieces(
        first, [0, 1, 2], loop_size, table, users, labels, None, False
    )
    opposite = across(opposite, loop_size)
    first = other(packed, [0, 1, -1])
    third = [held(3, to_next(second[0][0], 1, loop_size)), held(-3, to_next(second[1][0], -1, loop_size))]
    gradient, packed = add_pieces(second, [0, 1], loop_size, table, parts, labels, gradient, False)
    second = other(packed, [2, -2])
    third.append(held(4, opposite))
    arrived, gradient = lax.optimization_barrier(([array for array, _ in third], gradient))
    final = other(pack(arrived), [3, -3, 4])
    (gradient,) = add_pieces(
        third + [first, second], [], loop_size, table, parts, labels, gradient, False
    )
    return *add_pieces([final], [], loop_size, table, parts, labels, gradient, True), users


def chunks_kernel(
    list_ref, count_ref, users_ref, labels_ref, items_ref, grad_ref, square_ref, tiles, parts_ref, sems
):
    tile = tiles.shape[0] // CHUNK
    step = pl.program_id(0)
    live = jnp.clip(count_ref[0] - step * CHUNK, 0, CHUNK)

    @pl.when(step == 0)
    def _():
        parts_ref[...] = halves(0.5 * users_ref[...])
        grad_ref[...] = jnp.zeros_like(grad_ref)

    def move(slot):
        start = pl.multiple_of(list_ref[0, step * CHUNK + slot] * tile, tile)
        return pltpu.make_async_copy(
            items_ref.at[pl.ds(start, tile), :], tiles.at[pl.ds(slot * tile, tile), :], sems.at[slot]
        )

    for slot in range(CHUNK):
        pl.when(slot < live)(lambda slot=slot: move(slot).start())
    for slot in range(CHUNK):
        pl.when(slot < live)(lambda slot=slot: move(slot).wait())

    def labels_at(position):
        return labels_ref[:, pl.ds(pl.multiple_of(position * tile, tile), tile)]

    add_tiles(grad_ref, parts_ref, tiles, live, labels_at)

    @pl.when(step == pl.num_programs(0) - 1)
    def _():
        store_square(grad_ref, square_ref)


def add_chunks(loop_size, items, lists, users, labels):
    rows, width = users.shape
    slots = lists[0].shape[1]
    tile = labels.shape[1] // slots
    return pl.pallas_call(
        chunks_kernel,
        grid=(slots // CHUNK,),
        out_shape=[
            jax.ShapeDtypeStruct((rows, width), jnp.float32),
            jax.ShapeDtypeStruct((loop_size, 128), jnp.float32),
        ],
        in_specs=[
            pl.BlockSpec(memory_space=pltpu.SMEM),
            pl.BlockSpec(memory_space=pltpu.SMEM),
            pl.BlockSpec((rows, width), lambda step: (0, 0)),
            pl.BlockSpec((rows, CHUNK * tile), lambda step: (0, step)),
            pl.BlockSpec(memory_space=pl.ANY),
        ],
        out_specs=[
            pl.BlockSpec((rows, width), lambda step: (0, 0)),
            pl.BlockSpec((loop_size, 128), lambda step: (0, 0)),
        ],
        scratch_shapes=[
            pltpu.VMEM((CHUNK * tile, width), jnp.bfloat16),
            pltpu.VMEM((2 * rows, width), jnp.bfloat16),
            pltpu.SemaphoreType.DMA((CHUNK,)),
        ],
        compiler_params=pltpu.CompilerParams(vmem_limit_bytes=32 * 1024 * 1024),
        cost_estimate=pl.CostEstimate(
            flops=8 * rows * width * slots * tile,
            bytes_accessed=4 * rows * (slots * tile + 2 * width) + 2 * slots * tile * width,
            transcendentals=rows * slots * tile,
        ),
        name="add_chunks",
    )(*lists, users, labels, items)


def update_kernel(entries, users_ref, grad_ref, squares_ref, out_ref, result, sems):
    total = jnp.sum(squares_ref[...], axis=0, keepdims=True)
    total = jnp.sum(total, axis=1, keepdims=True)
    scale = 0.5 / jnp.sqrt(total / entries + 1e-06)
    rows = users_ref.shape[0] // sems.shape[0]
    copies = []
    for at in range(sems.shape[0]):
        part = pl.ds(at * rows, rows)
        result[part, :] = users_ref[part, :] - scale * grad_ref[part, :]
        copies.append(pltpu.make_async_copy(result.at[part, :], out_ref.at[part, :], sems.at[at]))
        copies[-1].start()
    for copy in copies:
        copy.wait()


def local(users, items, tile_blocks, tile_count, labels):
    loop_size = lax.axis_size("loop")
    rows, width = users.shape
    slots = tile_blocks.shape[1]
    lists = (tile_blocks, tile_count)
    if loop_size == RING and slots == CHUNK:
        gradient, square, users = ring_gradient(users, items, lists, labels)
    else:
        whole = lax.all_gather(items, "loop", axis=0, tiled=True)
        gradient, square = add_chunks(loop_size, whole, lists, users, labels)

    squares = lax.all_to_all(square, "loop", 0, 0, tiled=True)
    return pl.pallas_call(
        functools.partial(update_kernel, rows * loop_size * width),
        out_shape=jax.ShapeDtypeStruct((rows, width), jnp.float32),
        in_specs=[pl.BlockSpec(memory_space=pltpu.VMEM)] * 3,
        out_specs=pl.BlockSpec(memory_space=pl.ANY),
        scratch_shapes=[pltpu.VMEM((rows, width), jnp.float32), pltpu.SemaphoreType.DMA((4,))],
        compiler_params=pltpu.CompilerParams(vmem_limit_bytes=16 * 1024 * 1024),
        cost_estimate=pl.CostEstimate(
            flops=2 * rows * width, bytes_accessed=12 * rows * width, transcendentals=0
        ),
        name="update",
    )(users, gradient, squares)


def solution(mesh):
    in_specs = (
        P(("group", "loop"), None),
        P(("group", "loop"), None),
        P(("group", "loop"), None),
        P(("group", "loop")),
        P(("group", "loop"), None),
    )
    out_specs = P(("group", "loop"), None)
    return jax.shard_map(local, mesh=mesh, in_specs=in_specs, out_specs=out_specs, check_vma=False)
```

```python
import functools

import jax
import jax.numpy as jnp
from jax import lax
from jax.experimental import pallas as pl
from jax.experimental.pallas import tpu as pltpu
from jax.sharding import PartitionSpec as P

CHUNK = 8
RING = 16
FEW = 3


def ring_place(loop_size):
    outer = loop_size // 4

    def device(position, core):
        position = position % (2 * outer)
        chip = 2 * position if position < outer else 2 * (2 * outer - 1 - position) + 1
        return 2 * chip + core

    return 2 * outer, device


def to_next(array, direction, loop_size):
    chips, device = ring_place(loop_size)
    pairs = [(device(at, 0), device(at + direction, 0)) for at in range(chips)]
    pairs += [(device(at, 1), device(at - direction, 1)) for at in range(chips)]
    return lax.ppermute(array, "loop", pairs)


def across(array, loop_size):
    chips, device = ring_place(loop_size)
    pairs = [
        (device(at, core), device(at + (3 if at % 2 == 0 else -3), core))
        for at in range(chips)
        for core in range(2)
    ]
    return lax.ppermute(array, "loop", pairs)


def to_other_core(array, loop_size):
    return lax.ppermute(array, "loop", [(at, at ^ 1) for at in range(loop_size)])


def halves(values):
    upper = values.astype(jnp.bfloat16)
    return jnp.concatenate([upper, (values - upper.astype(jnp.float32)).astype(jnp.bfloat16)], 0)


def table_kernel(loop_size, origins, list_ref, count_ref, table_ref):
    chips = loop_size // 2
    lane = lax.broadcasted_iota(jnp.int32, table_ref.shape, 1)
    core, position = core_and_position(loop_size)
    hops, other = jnp.zeros_like(lane), jnp.zeros_like(lane)
    for at, origin in enumerate(origins):
        hops = jnp.where(lane == at, origin[0], hops)
        other = jnp.where(lane == at, origin[1], other)
    at = (position + chips + jnp.where(core == 0, -hops, hops)) & (chips - 1)
    chip = jnp.where(at < chips // 2, 2 * at, 2 * (chips - 1 - at) + 1)
    block = 2 * chip + jnp.where(other == 1, 1 - core, core)
    found = jnp.full_like(lane, -1)
    for slot in range(list_ref.shape[1]):
        name = jnp.where(slot < count_ref[...], list_ref[:, slot : slot + 1], -1)
        found = jnp.where(name == block, slot, found)
    table_ref[...] = jnp.where(lane < len(origins), found, -1)


def slot_table(loop_size, origins, block_list, live_count):
    return pl.pallas_call(
        functools.partial(table_kernel, loop_size, origins),
        out_shape=jax.ShapeDtypeStruct((1, 128), jnp.int32),
        in_specs=[pl.BlockSpec(memory_space=pltpu.VMEM)] * 2,
        out_specs=pl.BlockSpec(memory_space=pltpu.VMEM),
        compiler_params=pltpu.CompilerParams(vmem_limit_bytes=16 * 1024 * 1024),
        cost_estimate=pl.CostEstimate(flops=2**32, bytes_accessed=1024, transcendentals=0),
        name="slot_table",
    )(block_list, live_count.reshape(1, 1))


def add_block(grad_ref, parts_ref, block, labels):
    rows = grad_ref.shape[0]
    tile = labels[0].shape[1]
    upper, lower = [], []
    for at in range(0, len(labels), 2):
        some = jnp.concatenate(labels[at : at + 2], 1)
        both = lax.dot_general(
            parts_ref[...],
            block[at * tile : at * tile + some.shape[1]],
            (((1,), (1,)), ((), ())),
            preferred_element_type=jnp.float32,
        )
        residual = 0.5 * jnp.tanh(both[:rows] + both[rows:]) + (0.5 - some.astype(jnp.float32))
        upper.append(residual.astype(jnp.bfloat16))
        lower.append((residual - upper[-1].astype(jnp.float32)).astype(jnp.bfloat16))
    grad_ref[...] += jnp.dot(
        jnp.concatenate(upper + lower, 1),
        jnp.concatenate([block, block], 0),
        preferred_element_type=jnp.float32,
    )


def add_tiles(grad_ref, parts_ref, tiles, live, labels_at):
    tile = tiles.shape[0] // CHUNK
    fours = (live + 1) // 4

    @pl.when(live % 4 == 3)
    def _():
        blank = pl.multiple_of(live * tile, tile)
        tiles[pl.ds(blank, tile), :] = jnp.zeros((tile, tiles.shape[1]), tiles.dtype)

    def add(count, index, carry):
        start = index * count
        block = tiles[pl.ds(pl.multiple_of(start * tile, tile), count * tile), :]
        add_block(grad_ref, parts_ref, block, [labels_at(start + at) for at in range(count)])
        return carry

    lax.fori_loop(0, fours, functools.partial(add, 4), 0)
    pl.when(live - 4 * fours == 2)(lambda: add(2, 2 * fours, None))
    pl.when(live - 4 * fours == 1)(lambda: add(1, 4 * fours, None))


def store_square(grad_ref, square_ref):
    gradient = grad_ref[...]
    square = jnp.sum(gradient * gradient, axis=0, keepdims=True)
    square = sum(square[:, at : at + 128] for at in range(0, square.shape[1], 128))
    square_ref[...] = jnp.broadcast_to(square, square_ref.shape)


def core_and_position(loop_size):
    me = lax.axis_index("loop")
    core, row, outer = me % 2, me // 2 % 2, me // 4
    return core, jnp.where(row == 0, outer, loop_size // 2 - 1 - outer)


def pack_kernel(*refs):
    tile = refs[0].shape[0]
    for at, ref in enumerate(refs[:-1]):
        refs[-1][at * tile : (at + 1) * tile, :] = ref[...]


def pack(arrays):
    tile, width = arrays[0].shape
    return pl.pallas_call(
        pack_kernel,
        out_shape=jax.ShapeDtypeStruct((len(arrays) * tile, width), arrays[0].dtype),
        in_specs=[pl.BlockSpec(memory_space=pltpu.VMEM)] * len(arrays),
        out_specs=pl.BlockSpec(memory_space=pltpu.VMEM),
        compiler_params=pltpu.CompilerParams(vmem_limit_bytes=16 * 1024 * 1024),
        cost_estimate=pl.CostEstimate(
            flops=2**34, bytes_accessed=4 * len(arrays) * tile * width, transcendentals=0
        ),
        name="pack",
    )(*arrays)


def pieces_kernel(places, count, packed, loop_size, first, last, table_ref, given_ref, labels_ref, *rest):
    rest = list(rest)
    arrays = [rest.pop(0) for _ in range(count)]
    if not first:
        rest.pop(0)
    grad_ref = rest.pop(0)
    parts_ref = rest.pop(0) if first else given_ref
    across_ref = rest.pop(0) if first else None
    pack_ref = rest.pop(0) if packed else None
    square_ref = rest.pop(0) if last else None
    tiles, slots = rest
    tile = tiles.shape[0] // CHUNK
    for at, index in enumerate(packed):
        pack_ref[at * tile : (at + 1) * tile, :] = arrays[index][...]
    if first:
        core, position = core_and_position(loop_size)
        for at in range(2):

            @pl.when((core + position) % 2 == at)
            def _():
                across_ref[...] = arrays[1 + at][...]

        parts_ref[...] = halves(0.5 * given_ref[...])
        grad_ref[...] = jnp.zeros_like(grad_ref)
    table = table_ref[...]
    entries = [table[0, at] for at, _, _ in places]

    def labels_of(slot):
        return labels_ref[:, pl.ds(pl.multiple_of(slot * tile, tile), tile)]

    if len(places) <= FEW:
        for found, (_, index, row) in zip(entries, places):

            @pl.when(found >= 0)
            def _():
                block = arrays[index][row * tile : (row + 1) * tile, :]
                add_block(grad_ref, parts_ref, block, [labels_of(found)])

    else:
        live = jnp.int32(0)
        for found, (_, index, row) in zip(entries, places):

            @pl.when(found >= 0)
            def _():
                into = pl.ds(pl.multiple_of(live * tile, tile), tile)
                tiles[into, :] = arrays[index][row * tile : (row + 1) * tile, :]
                slots[live] = found

            live = live + (found >= 0).astype(jnp.int32)
        slots[live] = 0
        add_tiles(grad_ref, parts_ref, tiles, live, lambda position: labels_of(slots[position]))
    if last:
        store_square(grad_ref, square_ref)


def add_pieces(held, packed, loop_size, table, given, labels, before, last):
    first = before is None
    width = given.shape[1]
    rows = given.shape[0] // (1 if first else 2)
    arrays = [array for array, _ in held]
    tile = labels.shape[1] // CHUNK
    places = [(at, index, row) for index, (_, entries) in enumerate(held) for row, at in enumerate(entries)]
    most = min(len(places), CHUNK)
    out_shape = [jax.ShapeDtypeStruct((rows, width), jnp.float32)]
    if first:
        out_shape.append(jax.ShapeDtypeStruct((2 * rows, width), jnp.bfloat16))
        out_shape.append(jax.ShapeDtypeStruct((tile, width), jnp.bfloat16))
    if packed:
        out_shape.append(jax.ShapeDtypeStruct((len(packed) * tile, width), jnp.bfloat16))
    if last:
        out_shape.append(jax.ShapeDtypeStruct((8, 128), jnp.float32))
    extra = [] if first else [before]
    return pl.pallas_call(
        functools.partial(pieces_kernel, places, len(arrays), packed, loop_size, first, last),
        out_shape=out_shape,
        in_specs=[pl.BlockSpec(memory_space=pltpu.VMEM)] * (3 + len(arrays) + len(extra)),
        out_specs=[pl.BlockSpec(memory_space=pltpu.VMEM)] * len(out_shape),
        input_output_aliases={} if first else {3 + len(arrays): 0},
        scratch_shapes=[
            pltpu.VMEM((CHUNK * tile, width), jnp.bfloat16),
            pltpu.SMEM((CHUNK + 1,), jnp.int32),
        ],
        compiler_params=pltpu.CompilerParams(vmem_limit_bytes=24 * 1024 * 1024),
        cost_estimate=pl.CostEstimate(
            flops=128 * rows * width * most * tile,
            bytes_accessed=8 * rows * width,
            transcendentals=rows * most * tile,
        ),
        name="add_pieces",
    )(table, given, labels, *arrays, *extra)


def ring_gradient(users, items, lists, labels):
    loop_size = lax.axis_size("loop")
    far = loop_size // 4
    origins = [(hops, 0) for hops in range(1 - far, far + 1)]
    origins += [(-hops, 1) for hops, _ in origins]
    table = slot_table(loop_size, origins, *lists)
    where = {origin: at for at, origin in enumerate(origins)}

    def held(hops, array):
        return array, [where[hops, 0]]

    def other(arrays, hops):
        return to_other_core(arrays, loop_size), [where[-hop, 1] for hop in hops]

    up = to_next(items, 1, loop_size)
    down = to_next(items, -1, loop_size)
    up, table = lax.optimization_barrier((up, table))
    first = [held(0, items), held(1, up), held(-1, down)]
    second = [held(2, to_next(up, 1, loop_size)), held(-2, to_next(down, -1, loop_size))]
    gradient, parts, opposite, packed = add_pieces(
        first, [0, 1, 2], loop_size, table, users, labels, None, False
    )
    opposite = across(opposite, loop_size)
    first = other(packed, [0, 1, -1])
    third = [held(3, to_next(second[0][0], 1, loop_size)), held(-3, to_next(second[1][0], -1, loop_size))]
    gradient, packed = add_pieces(second, [0, 1], loop_size, table, parts, labels, gradient, False)
    second = other(packed, [2, -2])
    third.append(held(4, opposite))
    arrived, gradient = lax.optimization_barrier(([array for array, _ in third], gradient))
    final = other(pack(arrived), [3, -3, 4])
    (gradient,) = add_pieces(
        third + [first, second], [], loop_size, table, parts, labels, gradient, False
    )
    return *add_pieces([final], [], loop_size, table, parts, labels, gradient, True), users


def chunks_kernel(
    list_ref, count_ref, users_ref, labels_ref, items_ref, grad_ref, square_ref, tiles, parts_ref, sems
):
    tile = tiles.shape[0] // CHUNK
    step = pl.program_id(0)
    live = jnp.clip(count_ref[0] - step * CHUNK, 0, CHUNK)

    @pl.when(step == 0)
    def _():
        parts_ref[...] = halves(0.5 * users_ref[...])
        grad_ref[...] = jnp.zeros_like(grad_ref)

    def move(slot):
        start = pl.multiple_of(list_ref[0, step * CHUNK + slot] * tile, tile)
        return pltpu.make_async_copy(
            items_ref.at[pl.ds(start, tile), :], tiles.at[pl.ds(slot * tile, tile), :], sems.at[slot]
        )

    for slot in range(CHUNK):
        pl.when(slot < live)(lambda slot=slot: move(slot).start())
    for slot in range(CHUNK):
        pl.when(slot < live)(lambda slot=slot: move(slot).wait())

    def labels_at(position):
        return labels_ref[:, pl.ds(pl.multiple_of(position * tile, tile), tile)]

    add_tiles(grad_ref, parts_ref, tiles, live, labels_at)

    @pl.when(step == pl.num_programs(0) - 1)
    def _():
        store_square(grad_ref, square_ref)


def add_chunks(loop_size, items, lists, users, labels):
    rows, width = users.shape
    slots = lists[0].shape[1]
    tile = labels.shape[1] // slots
    return pl.pallas_call(
        chunks_kernel,
        grid=(slots // CHUNK,),
        out_shape=[
            jax.ShapeDtypeStruct((rows, width), jnp.float32),
            jax.ShapeDtypeStruct((8, 128), jnp.float32),
        ],
        in_specs=[
            pl.BlockSpec(memory_space=pltpu.SMEM),
            pl.BlockSpec(memory_space=pltpu.SMEM),
            pl.BlockSpec((rows, width), lambda step: (0, 0)),
            pl.BlockSpec((rows, CHUNK * tile), lambda step: (0, step)),
            pl.BlockSpec(memory_space=pl.ANY),
        ],
        out_specs=[
            pl.BlockSpec((rows, width), lambda step: (0, 0)),
            pl.BlockSpec((8, 128), lambda step: (0, 0)),
        ],
        scratch_shapes=[
            pltpu.VMEM((CHUNK * tile, width), jnp.bfloat16),
            pltpu.VMEM((2 * rows, width), jnp.bfloat16),
            pltpu.SemaphoreType.DMA((CHUNK,)),
        ],
        compiler_params=pltpu.CompilerParams(vmem_limit_bytes=32 * 1024 * 1024),
        cost_estimate=pl.CostEstimate(
            flops=8 * rows * width * slots * tile,
            bytes_accessed=4 * rows * (slots * tile + 2 * width) + 2 * slots * tile * width,
            transcendentals=rows * slots * tile,
        ),
        name="add_chunks",
    )(*lists, users, labels, items)


def update_kernel(entries, users_ref, grad_ref, squares_ref, out_ref, result, sems):
    total = jnp.sum(squares_ref[...], axis=0, keepdims=True) / 8
    total = jnp.sum(total, axis=1, keepdims=True)
    scale = 0.5 / jnp.sqrt(total / entries + 1e-06)
    rows = users_ref.shape[0] // sems.shape[0]
    copies = []
    for at in range(sems.shape[0]):
        part = pl.ds(at * rows, rows)
        result[part, :] = users_ref[part, :] - scale * grad_ref[part, :]
        copies.append(pltpu.make_async_copy(result.at[part, :], out_ref.at[part, :], sems.at[at]))
        copies[-1].start()
    for copy in copies:
        copy.wait()


def local(users, items, tile_blocks, tile_count, labels):
    loop_size = lax.axis_size("loop")
    rows, width = users.shape
    slots = tile_blocks.shape[1]
    lists = (tile_blocks, tile_count)
    if loop_size == RING and slots == CHUNK:
        gradient, square, users = ring_gradient(users, items, lists, labels)
    else:
        whole = lax.all_gather(items, "loop", axis=0, tiled=True)
        gradient, square = add_chunks(loop_size, whole, lists, users, labels)

    squares = lax.all_gather(square, "loop", axis=0, tiled=True)
    return pl.pallas_call(
        functools.partial(update_kernel, rows * loop_size * width),
        out_shape=jax.ShapeDtypeStruct((rows, width), jnp.float32),
        in_specs=[pl.BlockSpec(memory_space=pltpu.VMEM)] * 3,
        out_specs=pl.BlockSpec(memory_space=pl.ANY),
        scratch_shapes=[pltpu.VMEM((rows, width), jnp.float32), pltpu.SemaphoreType.DMA((4,))],
        compiler_params=pltpu.CompilerParams(vmem_limit_bytes=16 * 1024 * 1024),
        cost_estimate=pl.CostEstimate(
            flops=2 * rows * width, bytes_accessed=12 * rows * width, transcendentals=0
        ),
        name="update",
    )(users, gradient, squares)


def solution(mesh):
    in_specs = (
        P(("group", "loop"), None),
        P(("group", "loop"), None),
        P(("group", "loop"), None),
        P(("group", "loop")),
        P(("group", "loop"), None),
    )
    out_specs = P(("group", "loop"), None)
    return jax.shard_map(local, mesh=mesh, in_specs=in_specs, out_specs=out_specs, check_vma=False)
```

```python
import functools

import jax
import jax.numpy as jnp
from jax import lax
from jax.experimental import pallas as pl
from jax.experimental.pallas import tpu as pltpu
from jax.sharding import PartitionSpec as P

CHUNK = 8
RING = 16


def ring_place(loop_size):
    outer = loop_size // 4

    def device(position, core):
        position = position % (2 * outer)
        chip = 2 * position if position < outer else 2 * (2 * outer - 1 - position) + 1
        return 2 * chip + core

    return 2 * outer, device


def to_next(array, direction, loop_size):
    chips, device = ring_place(loop_size)
    pairs = [(device(at, 0), device(at + direction, 0)) for at in range(chips)]
    pairs += [(device(at, 1), device(at - direction, 1)) for at in range(chips)]
    return lax.ppermute(array, "loop", pairs)


def across(array, loop_size):
    chips, device = ring_place(loop_size)
    pairs = [
        (device(at, core), device(at + (3 if at % 2 == 0 else -3), core))
        for at in range(chips)
        for core in range(2)
    ]
    return lax.ppermute(array, "loop", pairs)


def to_other_core(array, loop_size):
    return lax.ppermute(array, "loop", [(at, at ^ 1) for at in range(loop_size)])


def halves(values):
    upper = values.astype(jnp.bfloat16)
    return jnp.concatenate([upper, (values - upper.astype(jnp.float32)).astype(jnp.bfloat16)], 0)


def table_kernel(loop_size, origins, list_ref, count_ref, table_ref):
    chips = loop_size // 2
    lane = lax.broadcasted_iota(jnp.int32, table_ref.shape, 1)
    core, position = core_and_position(loop_size)
    hops, other = jnp.zeros_like(lane), jnp.zeros_like(lane)
    for at, origin in enumerate(origins):
        hops = jnp.where(lane == at, origin[0], hops)
        other = jnp.where(lane == at, origin[1], other)
    at = (position + chips + jnp.where(core == 0, -hops, hops)) & (chips - 1)
    chip = jnp.where(at < chips // 2, 2 * at, 2 * (chips - 1 - at) + 1)
    block = 2 * chip + jnp.where(other == 1, 1 - core, core)
    found = jnp.full_like(lane, -1)
    for slot in range(list_ref.shape[1]):
        name = jnp.where(slot < count_ref[...], list_ref[:, slot : slot + 1], -1)
        found = jnp.where(name == block, slot, found)
    table_ref[...] = jnp.where(lane < len(origins), found, -1)


def slot_table(loop_size, origins, block_list, live_count):
    return pl.pallas_call(
        functools.partial(table_kernel, loop_size, origins),
        out_shape=jax.ShapeDtypeStruct((1, 128), jnp.int32),
        in_specs=[pl.BlockSpec(memory_space=pltpu.VMEM)] * 2,
        out_specs=pl.BlockSpec(memory_space=pltpu.VMEM),
        compiler_params=pltpu.CompilerParams(vmem_limit_bytes=16 * 1024 * 1024),
        cost_estimate=pl.CostEstimate(flops=2**32, bytes_accessed=1024, transcendentals=0),
        name="slot_table",
    )(block_list, live_count.reshape(1, 1))


def add_block(grad_ref, parts_ref, block, labels):
    rows = grad_ref.shape[0]
    tile = labels[0].shape[1]
    upper, lower = [], []
    for at in range(0, len(labels), 2):
        some = jnp.concatenate(labels[at : at + 2], 1)
        both = lax.dot_general(
            parts_ref[...],
            block[at * tile : at * tile + some.shape[1]],
            (((1,), (1,)), ((), ())),
            preferred_element_type=jnp.float32,
        )
        residual = 0.5 * jnp.tanh(both[:rows] + both[rows:]) + (0.5 - some.astype(jnp.float32))
        upper.append(residual.astype(jnp.bfloat16))
        lower.append((residual - upper[-1].astype(jnp.float32)).astype(jnp.bfloat16))
    grad_ref[...] += jnp.dot(
        jnp.concatenate(upper + lower, 1),
        jnp.concatenate([block, block], 0),
        preferred_element_type=jnp.float32,
    )


def add_tiles(grad_ref, parts_ref, tiles, live, labels_at):
    tile = tiles.shape[0] // CHUNK
    fours = (live + 1) // 4

    @pl.when(live % 4 == 3)
    def _():
        blank = pl.multiple_of(live * tile, tile)
        tiles[pl.ds(blank, tile), :] = jnp.zeros((tile, tiles.shape[1]), tiles.dtype)

    def add(count, index, carry):
        start = index * count
        block = tiles[pl.ds(pl.multiple_of(start * tile, tile), count * tile), :]
        add_block(grad_ref, parts_ref, block, [labels_at(start + at) for at in range(count)])
        return carry

    lax.fori_loop(0, fours, functools.partial(add, 4), 0)
    pl.when(live - 4 * fours == 2)(lambda: add(2, 2 * fours, None))
    pl.when(live - 4 * fours == 1)(lambda: add(1, 4 * fours, None))


def store_square(grad_ref, square_ref):
    gradient = grad_ref[...]
    square = jnp.sum(gradient * gradient, axis=0, keepdims=True)
    square = sum(square[:, at : at + 128] for at in range(0, square.shape[1], 128))
    square_ref[...] = jnp.broadcast_to(square, square_ref.shape)


def core_and_position(loop_size):
    me = lax.axis_index("loop")
    core, row, outer = me % 2, me // 2 % 2, me // 4
    return core, jnp.where(row == 0, outer, loop_size // 2 - 1 - outer)


def pack_kernel(*refs):
    tile = refs[0].shape[0]
    for at, ref in enumerate(refs[:-1]):
        refs[-1][at * tile : (at + 1) * tile, :] = ref[...]


def pack(arrays):
    tile, width = arrays[0].shape
    return pl.pallas_call(
        pack_kernel,
        out_shape=jax.ShapeDtypeStruct((len(arrays) * tile, width), arrays[0].dtype),
        in_specs=[pl.BlockSpec(memory_space=pltpu.VMEM)] * len(arrays),
        out_specs=pl.BlockSpec(memory_space=pltpu.VMEM),
        compiler_params=pltpu.CompilerParams(vmem_limit_bytes=16 * 1024 * 1024),
        cost_estimate=pl.CostEstimate(
            flops=2**34, bytes_accessed=4 * len(arrays) * tile * width, transcendentals=0
        ),
        name="pack",
    )(*arrays)


def pieces_kernel(places, count, packed, loop_size, first, last, table_ref, given_ref, labels_ref, *rest):
    rest = list(rest)
    arrays = [rest.pop(0) for _ in range(count)]
    if not first:
        rest.pop(0)
    grad_ref = rest.pop(0)
    parts_ref = rest.pop(0) if first else given_ref
    across_ref = rest.pop(0) if first else None
    pack_ref = rest.pop(0) if packed else None
    square_ref = rest.pop(0) if last else None
    tiles, slots = rest
    tile = tiles.shape[0] // CHUNK
    for at, index in enumerate(packed):
        pack_ref[at * tile : (at + 1) * tile, :] = arrays[index][...]
    if first:
        core, position = core_and_position(loop_size)
        for at in range(2):

            @pl.when((core + position) % 2 == at)
            def _():
                across_ref[...] = arrays[1 + at][...]

        parts_ref[...] = halves(0.5 * given_ref[...])
        grad_ref[...] = jnp.zeros_like(grad_ref)
    table = table_ref[...]
    entries = [table[0, at] for at, _, _ in places]

    def labels_of(slot):
        return labels_ref[:, pl.ds(pl.multiple_of(slot * tile, tile), tile)]

    live = jnp.int32(0)
    for found, (_, index, row) in zip(entries, places):

        @pl.when(found >= 0)
        def _():
            into = pl.ds(pl.multiple_of(live * tile, tile), tile)
            tiles[into, :] = arrays[index][row * tile : (row + 1) * tile, :]
            slots[live] = found

        live = live + (found >= 0).astype(jnp.int32)
    slots[live] = 0
    add_tiles(grad_ref, parts_ref, tiles, live, lambda position: labels_of(slots[position]))
    if last:
        store_square(grad_ref, square_ref)


def add_pieces(held, packed, loop_size, table, given, labels, before, last):
    first = before is None
    width = given.shape[1]
    rows = given.shape[0] // (1 if first else 2)
    arrays = [array for array, _ in held]
    tile = labels.shape[1] // CHUNK
    places = [(at, index, row) for index, (_, entries) in enumerate(held) for row, at in enumerate(entries)]
    most = min(len(places), CHUNK)
    out_shape = [jax.ShapeDtypeStruct((rows, width), jnp.float32)]
    if first:
        out_shape.append(jax.ShapeDtypeStruct((2 * rows, width), jnp.bfloat16))
        out_shape.append(jax.ShapeDtypeStruct((tile, width), jnp.bfloat16))
    if packed:
        out_shape.append(jax.ShapeDtypeStruct((len(packed) * tile, width), jnp.bfloat16))
    if last:
        out_shape.append(jax.ShapeDtypeStruct((loop_size, 128), jnp.float32))
    extra = [] if first else [before]
    return pl.pallas_call(
        functools.partial(pieces_kernel, places, len(arrays), packed, loop_size, first, last),
        out_shape=out_shape,
        in_specs=[pl.BlockSpec(memory_space=pltpu.VMEM)] * (3 + len(arrays) + len(extra)),
        out_specs=[pl.BlockSpec(memory_space=pltpu.VMEM)] * len(out_shape),
        input_output_aliases={} if first else {3 + len(arrays): 0},
        scratch_shapes=[
            pltpu.VMEM((CHUNK * tile, width), jnp.bfloat16),
            pltpu.SMEM((CHUNK + 1,), jnp.int32),
        ],
        compiler_params=pltpu.CompilerParams(vmem_limit_bytes=24 * 1024 * 1024),
        cost_estimate=pl.CostEstimate(
            flops=128 * rows * width * most * tile,
            bytes_accessed=8 * rows * width,
            transcendentals=rows * most * tile,
        ),
        name="add_pieces",
    )(table, given, labels, *arrays, *extra)


def ring_gradient(users, items, lists, labels):
    loop_size = lax.axis_size("loop")
    far = loop_size // 4
    origins = [(hops, 0) for hops in range(1 - far, far + 1)]
    origins += [(-hops, 1) for hops, _ in origins]
    table = slot_table(loop_size, origins, *lists)
    where = {origin: at for at, origin in enumerate(origins)}

    def held(hops, array):
        return array, [where[hops, 0]]

    def other(arrays, hops):
        return to_other_core(arrays, loop_size), [where[-hop, 1] for hop in hops]

    up = to_next(items, 1, loop_size)
    down = to_next(items, -1, loop_size)
    up, table = lax.optimization_barrier((up, table))
    first = [held(0, items), held(1, up), held(-1, down)]
    second = [held(2, to_next(up, 1, loop_size)), held(-2, to_next(down, -1, loop_size))]
    gradient, parts, opposite, packed = add_pieces(
        first, [0, 1, 2], loop_size, table, users, labels, None, False
    )
    opposite = across(opposite, loop_size)
    first = other(packed, [0, 1, -1])
    third = [held(3, to_next(second[0][0], 1, loop_size)), held(-3, to_next(second[1][0], -1, loop_size))]
    gradient, packed = add_pieces(second, [0, 1], loop_size, table, parts, labels, gradient, False)
    second = other(packed, [2, -2])
    third.append(held(4, opposite))
    arrived, gradient = lax.optimization_barrier(([array for array, _ in third], gradient))
    final = other(pack(arrived), [3, -3, 4])
    (gradient,) = add_pieces(
        third + [first, second], [], loop_size, table, parts, labels, gradient, False
    )
    return *add_pieces([final], [], loop_size, table, parts, labels, gradient, True), users


def chunks_kernel(
    list_ref, count_ref, users_ref, labels_ref, items_ref, grad_ref, square_ref, tiles, parts_ref, sems
):
    tile = tiles.shape[0] // CHUNK
    step = pl.program_id(0)
    live = jnp.clip(count_ref[0] - step * CHUNK, 0, CHUNK)

    @pl.when(step == 0)
    def _():
        parts_ref[...] = halves(0.5 * users_ref[...])
        grad_ref[...] = jnp.zeros_like(grad_ref)

    def move(slot):
        start = pl.multiple_of(list_ref[0, step * CHUNK + slot] * tile, tile)
        return pltpu.make_async_copy(
            items_ref.at[pl.ds(start, tile), :], tiles.at[pl.ds(slot * tile, tile), :], sems.at[slot]
        )

    for slot in range(CHUNK):
        pl.when(slot < live)(lambda slot=slot: move(slot).start())
    for slot in range(CHUNK):
        pl.when(slot < live)(lambda slot=slot: move(slot).wait())

    def labels_at(position):
        return labels_ref[:, pl.ds(pl.multiple_of(position * tile, tile), tile)]

    add_tiles(grad_ref, parts_ref, tiles, live, labels_at)

    @pl.when(step == pl.num_programs(0) - 1)
    def _():
        store_square(grad_ref, square_ref)


def add_chunks(loop_size, items, lists, users, labels):
    rows, width = users.shape
    slots = lists[0].shape[1]
    tile = labels.shape[1] // slots
    return pl.pallas_call(
        chunks_kernel,
        grid=(slots // CHUNK,),
        out_shape=[
            jax.ShapeDtypeStruct((rows, width), jnp.float32),
            jax.ShapeDtypeStruct((loop_size, 128), jnp.float32),
        ],
        in_specs=[
            pl.BlockSpec(memory_space=pltpu.SMEM),
            pl.BlockSpec(memory_space=pltpu.SMEM),
            pl.BlockSpec((rows, width), lambda step: (0, 0)),
            pl.BlockSpec((rows, CHUNK * tile), lambda step: (0, step)),
            pl.BlockSpec(memory_space=pl.ANY),
        ],
        out_specs=[
            pl.BlockSpec((rows, width), lambda step: (0, 0)),
            pl.BlockSpec((loop_size, 128), lambda step: (0, 0)),
        ],
        scratch_shapes=[
            pltpu.VMEM((CHUNK * tile, width), jnp.bfloat16),
            pltpu.VMEM((2 * rows, width), jnp.bfloat16),
            pltpu.SemaphoreType.DMA((CHUNK,)),
        ],
        compiler_params=pltpu.CompilerParams(vmem_limit_bytes=32 * 1024 * 1024),
        cost_estimate=pl.CostEstimate(
            flops=8 * rows * width * slots * tile,
            bytes_accessed=4 * rows * (slots * tile + 2 * width) + 2 * slots * tile * width,
            transcendentals=rows * slots * tile,
        ),
        name="add_chunks",
    )(*lists, users, labels, items)


def update_kernel(entries, users_ref, grad_ref, squares_ref, out_ref, result, sems):
    total = jnp.sum(squares_ref[...], axis=0, keepdims=True)
    total = jnp.sum(total, axis=1, keepdims=True)
    scale = 0.5 / jnp.sqrt(total / entries + 1e-06)
    rows = users_ref.shape[0] // sems.shape[0]
    copies = []
    for at in range(sems.shape[0]):
        part = pl.ds(at * rows, rows)
        result[part, :] = users_ref[part, :] - scale * grad_ref[part, :]
        copies.append(pltpu.make_async_copy(result.at[part, :], out_ref.at[part, :], sems.at[at]))
        copies[-1].start()
    for copy in copies:
        copy.wait()


def local(users, items, tile_blocks, tile_count, labels):
    loop_size = lax.axis_size("loop")
    rows, width = users.shape
    slots = tile_blocks.shape[1]
    lists = (tile_blocks, tile_count)
    if loop_size == RING and slots == CHUNK:
        gradient, square, users = ring_gradient(users, items, lists, labels)
    else:
        whole = lax.all_gather(items, "loop", axis=0, tiled=True)
        gradient, square = add_chunks(loop_size, whole, lists, users, labels)

    squares = lax.all_to_all(square, "loop", 0, 0, tiled=True)
    return pl.pallas_call(
        functools.partial(update_kernel, rows * loop_size * width),
        out_shape=jax.ShapeDtypeStruct((rows, width), jnp.float32),
        in_specs=[pl.BlockSpec(memory_space=pltpu.VMEM)] * 3,
        out_specs=pl.BlockSpec(memory_space=pl.ANY),
        scratch_shapes=[pltpu.VMEM((rows, width), jnp.float32), pltpu.SemaphoreType.DMA((4,))],
        compiler_params=pltpu.CompilerParams(vmem_limit_bytes=16 * 1024 * 1024),
        cost_estimate=pl.CostEstimate(
            flops=2 * rows * width, bytes_accessed=12 * rows * width, transcendentals=0
        ),
        name="update",
    )(users, gradient, squares)


def solution(mesh):
    in_specs = (
        P(("group", "loop"), None),
        P(("group", "loop"), None),
        P(("group", "loop"), None),
        P(("group", "loop")),
        P(("group", "loop"), None),
    )
    out_specs = P(("group", "loop"), None)
    return jax.shard_map(local, mesh=mesh, in_specs=in_specs, out_specs=out_specs, check_vma=False)
```

```python
import functools

import jax
import jax.numpy as jnp
from jax import lax
from jax.experimental import pallas as pl
from jax.experimental.pallas import tpu as pltpu
from jax.sharding import PartitionSpec as P

CHUNK = 8
RING = 16


def ring_place(loop_size):
    outer = loop_size // 4

    def device(position, core):
        position = position % (2 * outer)
        chip = 2 * position if position < outer else 2 * (2 * outer - 1 - position) + 1
        return 2 * chip + core

    return 2 * outer, device


def to_next(array, direction, loop_size):
    chips, device = ring_place(loop_size)
    pairs = [(device(at, 0), device(at + direction, 0)) for at in range(chips)]
    pairs += [(device(at, 1), device(at - direction, 1)) for at in range(chips)]
    return lax.ppermute(array, "loop", pairs)


def across(array, loop_size):
    chips, device = ring_place(loop_size)
    pairs = [
        (device(at, core), device(at + (3 if at % 2 == 0 else -3), core))
        for at in range(chips)
        for core in range(2)
    ]
    return lax.ppermute(array, "loop", pairs)


def to_other_core(array, loop_size):
    return lax.ppermute(array, "loop", [(at, at ^ 1) for at in range(loop_size)])


def halves(values):
    upper = values.astype(jnp.bfloat16)
    return jnp.concatenate([upper, (values - upper.astype(jnp.float32)).astype(jnp.bfloat16)], 0)


def table_kernel(loop_size, origins, list_ref, count_ref, table_ref):
    chips = loop_size // 2
    lane = lax.broadcasted_iota(jnp.int32, table_ref.shape, 1)
    core, position = core_and_position(loop_size)
    hops, other = jnp.zeros_like(lane), jnp.zeros_like(lane)
    for at, origin in enumerate(origins):
        hops = jnp.where(lane == at, origin[0], hops)
        other = jnp.where(lane == at, origin[1], other)
    at = (position + chips + jnp.where(core == 0, -hops, hops)) & (chips - 1)
    chip = jnp.where(at < chips // 2, 2 * at, 2 * (chips - 1 - at) + 1)
    block = 2 * chip + jnp.where(other == 1, 1 - core, core)
    found = jnp.full_like(lane, -1)
    for slot in range(list_ref.shape[1]):
        name = jnp.where(slot < count_ref[...], list_ref[:, slot : slot + 1], -1)
        found = jnp.where(name == block, slot, found)
    table_ref[...] = jnp.where(lane < len(origins), found, -1)


def slot_table(loop_size, origins, block_list, live_count):
    return pl.pallas_call(
        functools.partial(table_kernel, loop_size, origins),
        out_shape=jax.ShapeDtypeStruct((1, 128), jnp.int32),
        in_specs=[pl.BlockSpec(memory_space=pltpu.VMEM)] * 2,
        out_specs=pl.BlockSpec(memory_space=pltpu.VMEM),
        compiler_params=pltpu.CompilerParams(vmem_limit_bytes=16 * 1024 * 1024),
        cost_estimate=pl.CostEstimate(flops=2**32, bytes_accessed=1024, transcendentals=0),
        name="slot_table",
    )(block_list, live_count.reshape(1, 1))


def add_block(grad_ref, parts_ref, block, labels):
    rows = grad_ref.shape[0]
    tile = labels[0].shape[1]
    upper, lower = [], []
    for at in range(0, len(labels), 2):
        some = jnp.concatenate(labels[at : at + 2], 1)
        both = lax.dot_general(
            parts_ref[...],
            block[at * tile : at * tile + some.shape[1]],
            (((1,), (1,)), ((), ())),
            preferred_element_type=jnp.float32,
        )
        residual = 0.5 * jnp.tanh(both[:rows] + both[rows:]) + (0.5 - some.astype(jnp.float32))
        upper.append(residual.astype(jnp.bfloat16))
        lower.append((residual - upper[-1].astype(jnp.float32)).astype(jnp.bfloat16))
    grad_ref[...] += jnp.dot(
        jnp.concatenate(upper + lower, 1),
        jnp.concatenate([block, block], 0),
        preferred_element_type=jnp.float32,
    )


def add_tiles(grad_ref, parts_ref, tiles, live, labels_at):
    tile = tiles.shape[0] // CHUNK
    fours = (live + 1) // 4

    @pl.when(live % 4 == 3)
    def _():
        blank = pl.multiple_of(live * tile, tile)
        tiles[pl.ds(blank, tile), :] = jnp.zeros((tile, tiles.shape[1]), tiles.dtype)

    def add(count, index, carry):
        start = index * count
        block = tiles[pl.ds(pl.multiple_of(start * tile, tile), count * tile), :]
        add_block(grad_ref, parts_ref, block, [labels_at(start + at) for at in range(count)])
        return carry

    lax.fori_loop(0, fours, functools.partial(add, 4), 0)
    pl.when(live - 4 * fours == 2)(lambda: add(2, 2 * fours, None))
    pl.when(live - 4 * fours == 1)(lambda: add(1, 4 * fours, None))


def store_square(grad_ref, square_ref):
    gradient = grad_ref[...]
    square = jnp.sum(gradient * gradient, axis=0, keepdims=True)
    square = sum(square[:, at : at + 128] for at in range(0, square.shape[1], 128))
    square_ref[...] = jnp.broadcast_to(square, square_ref.shape)


def core_and_position(loop_size):
    me = lax.axis_index("loop")
    core, row, outer = me % 2, me // 2 % 2, me // 4
    return core, jnp.where(row == 0, outer, loop_size // 2 - 1 - outer)


def pack_kernel(loop_size, *refs):
    count = len(refs) - (1 if loop_size is None else 2)
    tile = refs[0].shape[0]
    if loop_size is not None:
        core, position = core_and_position(loop_size)
        for at in range(2):

            @pl.when((core + position) % 2 == at)
            def _():
                refs[-1][...] = refs[1 + at][...]

    for at in range(count):
        refs[count][at * tile : (at + 1) * tile, :] = refs[at][...]


def pack(arrays, loop_size=None):
    tile, width = arrays[0].shape
    shapes = [(len(arrays) * tile, width)] + ([] if loop_size is None else [(tile, width)])
    return pl.pallas_call(
        functools.partial(pack_kernel, loop_size),
        out_shape=[jax.ShapeDtypeStruct(shape, arrays[0].dtype) for shape in shapes],
        in_specs=[pl.BlockSpec(memory_space=pltpu.VMEM)] * len(arrays),
        out_specs=[pl.BlockSpec(memory_space=pltpu.VMEM)] * len(shapes),
        compiler_params=pltpu.CompilerParams(vmem_limit_bytes=16 * 1024 * 1024),
        cost_estimate=pl.CostEstimate(
            flops=2**34 if loop_size is None else 2**32,
            bytes_accessed=4 * len(arrays) * tile * width,
            transcendentals=0,
        ),
        name="pack",
    )(*arrays)


def pieces_kernel(places, count, packed, first, last, table_ref, given_ref, labels_ref, *rest):
    rest = list(rest)
    arrays = [rest.pop(0) for _ in range(count)]
    if not first:
        rest.pop(0)
    grad_ref = rest.pop(0)
    parts_ref = rest.pop(0) if first else given_ref
    pack_ref = rest.pop(0) if packed else None
    square_ref = rest.pop(0) if last else None
    tiles, slots = rest
    tile = tiles.shape[0] // CHUNK
    for at, index in enumerate(packed):
        pack_ref[at * tile : (at + 1) * tile, :] = arrays[index][...]
    if first:
        parts_ref[...] = halves(0.5 * given_ref[...])
        grad_ref[...] = jnp.zeros_like(grad_ref)
    table = table_ref[...]
    entries = [table[0, at] for at, _, _ in places]

    def labels_of(slot):
        return labels_ref[:, pl.ds(pl.multiple_of(slot * tile, tile), tile)]

    live = jnp.int32(0)
    for found, (_, index, row) in zip(entries, places):

        @pl.when(found >= 0)
        def _():
            into = pl.ds(pl.multiple_of(live * tile, tile), tile)
            tiles[into, :] = arrays[index][row * tile : (row + 1) * tile, :]
            slots[live] = found

        live = live + (found >= 0).astype(jnp.int32)
    slots[live] = 0
    add_tiles(grad_ref, parts_ref, tiles, live, lambda position: labels_of(slots[position]))
    if last:
        store_square(grad_ref, square_ref)


def add_pieces(held, packed, loop_size, table, given, labels, before, last):
    first = before is None
    width = given.shape[1]
    rows = given.shape[0] // (1 if first else 2)
    arrays = [array for array, _ in held]
    tile = labels.shape[1] // CHUNK
    places = [(at, index, row) for index, (_, entries) in enumerate(held) for row, at in enumerate(entries)]
    most = min(len(places), CHUNK)
    out_shape = [jax.ShapeDtypeStruct((rows, width), jnp.float32)]
    if first:
        out_shape.append(jax.ShapeDtypeStruct((2 * rows, width), jnp.bfloat16))
    if packed:
        out_shape.append(jax.ShapeDtypeStruct((len(packed) * tile, width), jnp.bfloat16))
    if last:
        out_shape.append(jax.ShapeDtypeStruct((loop_size, 128), jnp.float32))
    extra = [] if first else [before]
    return pl.pallas_call(
        functools.partial(pieces_kernel, places, len(arrays), packed, first, last),
        out_shape=out_shape,
        in_specs=[pl.BlockSpec(memory_space=pltpu.VMEM)] * (3 + len(arrays) + len(extra)),
        out_specs=[pl.BlockSpec(memory_space=pltpu.VMEM)] * len(out_shape),
        input_output_aliases={} if first else {3 + len(arrays): 0},
        scratch_shapes=[
            pltpu.VMEM((CHUNK * tile, width), jnp.bfloat16),
            pltpu.SMEM((CHUNK + 1,), jnp.int32),
        ],
        compiler_params=pltpu.CompilerParams(vmem_limit_bytes=24 * 1024 * 1024),
        cost_estimate=pl.CostEstimate(
            flops=(8 if first else 128) * rows * width * most * tile,
            bytes_accessed=8 * rows * width,
            transcendentals=rows * most * tile,
        ),
        name="add_pieces",
    )(table, given, labels, *arrays, *extra)


def ring_gradient(users, items, lists, labels):
    loop_size = lax.axis_size("loop")
    far = loop_size // 4
    origins = [(hops, 0) for hops in range(1 - far, far + 1)]
    origins += [(-hops, 1) for hops, _ in origins]
    table = slot_table(loop_size, origins, *lists)
    where = {origin: at for at, origin in enumerate(origins)}

    def held(hops, array):
        return array, [where[hops, 0]]

    def other(arrays, hops):
        return to_other_core(arrays, loop_size), [where[-hop, 1] for hop in hops]

    up = to_next(items, 1, loop_size)
    down = to_next(items, -1, loop_size)
    up, table = lax.optimization_barrier((up, table))
    first = [held(0, items), held(1, up), held(-1, down)]
    second = [held(2, to_next(up, 1, loop_size)), held(-2, to_next(down, -1, loop_size))]
    packed, opposite = pack([items, up, down], loop_size)
    opposite = across(opposite, loop_size)
    gradient, parts = add_pieces(first, [], loop_size, table, users, labels, None, False)
    first = other(packed, [0, 1, -1])
    third = [held(3, to_next(second[0][0], 1, loop_size)), held(-3, to_next(second[1][0], -1, loop_size))]
    gradient, packed = add_pieces(second, [0, 1], loop_size, table, parts, labels, gradient, False)
    second = other(packed, [2, -2])
    third.append(held(4, opposite))
    arrived, gradient = lax.optimization_barrier(([array for array, _ in third], gradient))
    final = other(pack(arrived)[0], [3, -3, 4])
    (gradient,) = add_pieces(
        third + [first, second], [], loop_size, table, parts, labels, gradient, False
    )
    return *add_pieces([final], [], loop_size, table, parts, labels, gradient, True), users


def chunks_kernel(
    list_ref, count_ref, users_ref, labels_ref, items_ref, grad_ref, square_ref, tiles, parts_ref, sems
):
    tile = tiles.shape[0] // CHUNK
    step = pl.program_id(0)
    live = jnp.clip(count_ref[0] - step * CHUNK, 0, CHUNK)

    @pl.when(step == 0)
    def _():
        parts_ref[...] = halves(0.5 * users_ref[...])
        grad_ref[...] = jnp.zeros_like(grad_ref)

    def move(slot):
        start = pl.multiple_of(list_ref[0, step * CHUNK + slot] * tile, tile)
        return pltpu.make_async_copy(
            items_ref.at[pl.ds(start, tile), :], tiles.at[pl.ds(slot * tile, tile), :], sems.at[slot]
        )

    for slot in range(CHUNK):
        pl.when(slot < live)(lambda slot=slot: move(slot).start())
    for slot in range(CHUNK):
        pl.when(slot < live)(lambda slot=slot: move(slot).wait())

    def labels_at(position):
        return labels_ref[:, pl.ds(pl.multiple_of(position * tile, tile), tile)]

    add_tiles(grad_ref, parts_ref, tiles, live, labels_at)

    @pl.when(step == pl.num_programs(0) - 1)
    def _():
        store_square(grad_ref, square_ref)


def add_chunks(loop_size, items, lists, users, labels):
    rows, width = users.shape
    slots = lists[0].shape[1]
    tile = labels.shape[1] // slots
    return pl.pallas_call(
        chunks_kernel,
        grid=(slots // CHUNK,),
        out_shape=[
            jax.ShapeDtypeStruct((rows, width), jnp.float32),
            jax.ShapeDtypeStruct((loop_size, 128), jnp.float32),
        ],
        in_specs=[
            pl.BlockSpec(memory_space=pltpu.SMEM),
            pl.BlockSpec(memory_space=pltpu.SMEM),
            pl.BlockSpec((rows, width), lambda step: (0, 0)),
            pl.BlockSpec((rows, CHUNK * tile), lambda step: (0, step)),
            pl.BlockSpec(memory_space=pl.ANY),
        ],
        out_specs=[
            pl.BlockSpec((rows, width), lambda step: (0, 0)),
            pl.BlockSpec((loop_size, 128), lambda step: (0, 0)),
        ],
        scratch_shapes=[
            pltpu.VMEM((CHUNK * tile, width), jnp.bfloat16),
            pltpu.VMEM((2 * rows, width), jnp.bfloat16),
            pltpu.SemaphoreType.DMA((CHUNK,)),
        ],
        compiler_params=pltpu.CompilerParams(vmem_limit_bytes=32 * 1024 * 1024),
        cost_estimate=pl.CostEstimate(
            flops=8 * rows * width * slots * tile,
            bytes_accessed=4 * rows * (slots * tile + 2 * width) + 2 * slots * tile * width,
            transcendentals=rows * slots * tile,
        ),
        name="add_chunks",
    )(*lists, users, labels, items)


def update_kernel(entries, users_ref, grad_ref, squares_ref, out_ref, result, sems):
    total = jnp.sum(squares_ref[...], axis=0, keepdims=True)
    total = jnp.sum(total, axis=1, keepdims=True)
    scale = 0.5 / jnp.sqrt(total / entries + 1e-06)
    rows = users_ref.shape[0] // sems.shape[0]
    copies = []
    for at in range(sems.shape[0]):
        part = pl.ds(at * rows, rows)
        result[part, :] = users_ref[part, :] - scale * grad_ref[part, :]
        copies.append(pltpu.make_async_copy(result.at[part, :], out_ref.at[part, :], sems.at[at]))
        copies[-1].start()
    for copy in copies:
        copy.wait()


def local(users, items, tile_blocks, tile_count, labels):
    loop_size = lax.axis_size("loop")
    rows, width = users.shape
    slots = tile_blocks.shape[1]
    lists = (tile_blocks, tile_count)
    if loop_size == RING and slots == CHUNK:
        gradient, square, users = ring_gradient(users, items, lists, labels)
    else:
        whole = lax.all_gather(items, "loop", axis=0, tiled=True)
        gradient, square = add_chunks(loop_size, whole, lists, users, labels)

    squares = lax.all_to_all(square, "loop", 0, 0, tiled=True)
    return pl.pallas_call(
        functools.partial(update_kernel, rows * loop_size * width),
        out_shape=jax.ShapeDtypeStruct((rows, width), jnp.float32),
        in_specs=[pl.BlockSpec(memory_space=pltpu.VMEM)] * 3,
        out_specs=pl.BlockSpec(memory_space=pl.ANY),
        scratch_shapes=[pltpu.VMEM((rows, width), jnp.float32), pltpu.SemaphoreType.DMA((4,))],
        compiler_params=pltpu.CompilerParams(vmem_limit_bytes=16 * 1024 * 1024),
        cost_estimate=pl.CostEstimate(
            flops=2 * rows * width, bytes_accessed=12 * rows * width, transcendentals=0
        ),
        name="update",
    )(users, gradient, squares)


def solution(mesh):
    in_specs = (
        P(("group", "loop"), None),
        P(("group", "loop"), None),
        P(("group", "loop"), None),
        P(("group", "loop")),
        P(("group", "loop"), None),
    )
    out_specs = P(("group", "loop"), None)
    return jax.shard_map(local, mesh=mesh, in_specs=in_specs, out_specs=out_specs, check_vma=False)
```

```python
import functools

import jax
import jax.numpy as jnp
from jax import lax
from jax.experimental import pallas as pl
from jax.experimental.pallas import tpu as pltpu
from jax.sharding import PartitionSpec as P

CHUNK = 8
RING = 16


def ring_place(loop_size):
    outer = loop_size // 4

    def device(position, core):
        position = position % (2 * outer)
        chip = 2 * position if position < outer else 2 * (2 * outer - 1 - position) + 1
        return 2 * chip + core

    return 2 * outer, device


def to_next(array, direction, loop_size):
    chips, device = ring_place(loop_size)
    pairs = [(device(at, 0), device(at + direction, 0)) for at in range(chips)]
    pairs += [(device(at, 1), device(at - direction, 1)) for at in range(chips)]
    return lax.ppermute(array, "loop", pairs)


def across(array, loop_size):
    chips, device = ring_place(loop_size)
    pairs = [
        (device(at, core), device(at + (3 if at % 2 == 0 else -3), core))
        for at in range(chips)
        for core in range(2)
    ]
    return lax.ppermute(array, "loop", pairs)


def to_other_core(array, loop_size):
    return lax.ppermute(array, "loop", [(at, at ^ 1) for at in range(loop_size)])


def halves(values):
    upper = values.astype(jnp.bfloat16)
    return jnp.concatenate([upper, (values - upper.astype(jnp.float32)).astype(jnp.bfloat16)], 0)


def table_kernel(loop_size, origins, list_ref, count_ref, table_ref):
    chips = loop_size // 2
    lane = lax.broadcasted_iota(jnp.int32, table_ref.shape, 1)
    core, position = core_and_position(loop_size)
    hops, other = jnp.zeros_like(lane), jnp.zeros_like(lane)
    for at, origin in enumerate(origins):
        hops = jnp.where(lane == at, origin[0], hops)
        other = jnp.where(lane == at, origin[1], other)
    at = (position + chips + jnp.where(core == 0, -hops, hops)) & (chips - 1)
    chip = jnp.where(at < chips // 2, 2 * at, 2 * (chips - 1 - at) + 1)
    block = 2 * chip + jnp.where(other == 1, 1 - core, core)
    found = jnp.full_like(lane, -1)
    for slot in range(list_ref.shape[1]):
        name = jnp.where(slot < count_ref[...], list_ref[:, slot : slot + 1], -1)
        found = jnp.where(name == block, slot, found)
    table_ref[...] = jnp.where(lane < len(origins), found, -1)


def slot_table(loop_size, origins, block_list, live_count):
    return pl.pallas_call(
        functools.partial(table_kernel, loop_size, origins),
        out_shape=jax.ShapeDtypeStruct((1, 128), jnp.int32),
        in_specs=[pl.BlockSpec(memory_space=pltpu.VMEM)] * 2,
        out_specs=pl.BlockSpec(memory_space=pltpu.VMEM),
        compiler_params=pltpu.CompilerParams(vmem_limit_bytes=16 * 1024 * 1024),
        cost_estimate=pl.CostEstimate(flops=2**32, bytes_accessed=1024, transcendentals=0),
        name="slot_table",
    )(block_list, live_count.reshape(1, 1))


def add_block(grad_ref, parts_ref, block, labels):
    rows = grad_ref.shape[0]
    tile = labels[0].shape[1]
    upper, lower = [], []
    for at in range(0, len(labels), 2):
        some = jnp.concatenate(labels[at : at + 2], 1)
        both = lax.dot_general(
            parts_ref[...],
            block[at * tile : at * tile + some.shape[1]],
            (((1,), (1,)), ((), ())),
            preferred_element_type=jnp.float32,
        )
        residual = 0.5 * jnp.tanh(both[:rows] + both[rows:]) + (0.5 - some.astype(jnp.float32))
        upper.append(residual.astype(jnp.bfloat16))
        lower.append((residual - upper[-1].astype(jnp.float32)).astype(jnp.bfloat16))
    grad_ref[...] += jnp.dot(
        jnp.concatenate(upper + lower, 1),
        jnp.concatenate([block, block], 0),
        preferred_element_type=jnp.float32,
    )


def add_tiles(grad_ref, parts_ref, tiles, live, labels_at):
    tile = tiles.shape[0] // CHUNK
    fours = (live + 1) // 4

    @pl.when(live % 4 == 3)
    def _():
        blank = pl.multiple_of(live * tile, tile)
        tiles[pl.ds(blank, tile), :] = jnp.zeros((tile, tiles.shape[1]), tiles.dtype)

    def add(count, index, carry):
        start = index * count
        block = tiles[pl.ds(pl.multiple_of(start * tile, tile), count * tile), :]
        add_block(grad_ref, parts_ref, block, [labels_at(start + at) for at in range(count)])
        return carry

    lax.fori_loop(0, fours, functools.partial(add, 4), 0)
    pl.when(live - 4 * fours == 2)(lambda: add(2, 2 * fours, None))
    pl.when(live - 4 * fours == 1)(lambda: add(1, 4 * fours, None))


def store_square(grad_ref, square_ref):
    gradient = grad_ref[...]
    square = jnp.sum(gradient * gradient, axis=0, keepdims=True)
    square = sum(square[:, at : at + 128] for at in range(0, square.shape[1], 128))
    square_ref[...] = jnp.broadcast_to(square, square_ref.shape)


def core_and_position(loop_size):
    me = lax.axis_index("loop")
    core, row, outer = me % 2, me // 2 % 2, me // 4
    return core, jnp.where(row == 0, outer, loop_size // 2 - 1 - outer)


def pack_kernel(loop_size, *refs):
    tile = refs[0].shape[0]
    sources = refs[:-1] if loop_size is None else (refs[0], refs[2])
    packed_ref = refs[-1] if loop_size is None else refs[-2]
    if loop_size is not None:
        core, position = core_and_position(loop_size)
        for at in range(2):

            @pl.when((core + position) % 2 == at)
            def _():
                refs[-1][...] = refs[1 + at][...]

    for at, ref in enumerate(sources):
        packed_ref[at * tile : (at + 1) * tile, :] = ref[...]


def pack(arrays, loop_size=None):
    tile, width = arrays[0].shape
    shapes = [(len(arrays) * tile, width)] if loop_size is None else [(2 * tile, width), (tile, width)]
    return pl.pallas_call(
        functools.partial(pack_kernel, loop_size),
        out_shape=[jax.ShapeDtypeStruct(shape, arrays[0].dtype) for shape in shapes],
        in_specs=[pl.BlockSpec(memory_space=pltpu.VMEM)] * len(arrays),
        out_specs=[pl.BlockSpec(memory_space=pltpu.VMEM)] * len(shapes),
        compiler_params=pltpu.CompilerParams(vmem_limit_bytes=16 * 1024 * 1024),
        cost_estimate=pl.CostEstimate(
            flops=2**34 if loop_size is None else 2**32,
            bytes_accessed=4 * len(arrays) * tile * width,
            transcendentals=0,
        ),
        name="pack",
    )(*arrays)


def pieces_kernel(places, count, packed, first, last, table_ref, given_ref, labels_ref, *rest):
    rest = list(rest)
    arrays = [rest.pop(0) for _ in range(count)]
    if not first:
        rest.pop(0)
    grad_ref = rest.pop(0)
    parts_ref = rest.pop(0) if first else given_ref
    pack_ref = rest.pop(0) if packed else None
    square_ref = rest.pop(0) if last else None
    tiles, slots = rest
    tile = tiles.shape[0] // CHUNK
    for at, index in enumerate(packed):
        pack_ref[at * tile : (at + 1) * tile, :] = arrays[index][...]
    if first:
        parts_ref[...] = halves(0.5 * given_ref[...])
        grad_ref[...] = jnp.zeros_like(grad_ref)
    table = table_ref[...]
    entries = [table[0, at] for at, _, _ in places]

    def labels_of(slot):
        return labels_ref[:, pl.ds(pl.multiple_of(slot * tile, tile), tile)]

    live = jnp.int32(0)
    for found, (_, index, row) in zip(entries, places):

        @pl.when(found >= 0)
        def _():
            into = pl.ds(pl.multiple_of(live * tile, tile), tile)
            tiles[into, :] = arrays[index][row * tile : (row + 1) * tile, :]
            slots[live] = found

        live = live + (found >= 0).astype(jnp.int32)
    slots[live] = 0
    add_tiles(grad_ref, parts_ref, tiles, live, lambda position: labels_of(slots[position]))
    if last:
        store_square(grad_ref, square_ref)


def add_pieces(held, packed, loop_size, table, given, labels, before, last):
    first = before is None
    width = given.shape[1]
    rows = given.shape[0] // (1 if first else 2)
    arrays = [array for array, _ in held]
    tile = labels.shape[1] // CHUNK
    places = [(at, index, row) for index, (_, entries) in enumerate(held) for row, at in enumerate(entries)]
    most = min(len(places), CHUNK)
    out_shape = [jax.ShapeDtypeStruct((rows, width), jnp.float32)]
    if first:
        out_shape.append(jax.ShapeDtypeStruct((2 * rows, width), jnp.bfloat16))
    if packed:
        out_shape.append(jax.ShapeDtypeStruct((len(packed) * tile, width), jnp.bfloat16))
    if last:
        out_shape.append(jax.ShapeDtypeStruct((loop_size, 128), jnp.float32))
    extra = [] if first else [before]
    return pl.pallas_call(
        functools.partial(pieces_kernel, places, len(arrays), packed, first, last),
        out_shape=out_shape,
        in_specs=[pl.BlockSpec(memory_space=pltpu.VMEM)] * (3 + len(arrays) + len(extra)),
        out_specs=[pl.BlockSpec(memory_space=pltpu.VMEM)] * len(out_shape),
        input_output_aliases={} if first else {3 + len(arrays): 0},
        scratch_shapes=[
            pltpu.VMEM((CHUNK * tile, width), jnp.bfloat16),
            pltpu.SMEM((CHUNK + 1,), jnp.int32),
        ],
        compiler_params=pltpu.CompilerParams(vmem_limit_bytes=24 * 1024 * 1024),
        cost_estimate=pl.CostEstimate(
            flops=(8 if first else 128) * rows * width * most * tile,
            bytes_accessed=8 * rows * width,
            transcendentals=rows * most * tile,
        ),
        name="add_pieces",
    )(table, given, labels, *arrays, *extra)


def ring_gradient(users, items, lists, labels):
    loop_size = lax.axis_size("loop")
    far = loop_size // 4
    origins = [(hops, 0) for hops in range(1 - far, far + 1)]
    origins += [(-hops, 1) for hops, _ in origins]
    table = slot_table(loop_size, origins, *lists)
    where = {origin: at for at, origin in enumerate(origins)}

    def held(hops, array):
        return array, [where[hops, 0]]

    def other(arrays, hops):
        return to_other_core(arrays, loop_size), [where[-hop, 1] for hop in hops]

    up = to_next(items, 1, loop_size)
    down = to_next(items, -1, loop_size)
    up, table = lax.optimization_barrier((up, table))
    first = [held(0, items), held(1, up), held(-1, down)]
    second = [held(2, to_next(up, 1, loop_size)), held(-2, to_next(down, -1, loop_size))]
    first.append(other(up, [1]))
    packed, opposite = pack([items, up, down], loop_size)
    opposite = across(opposite, loop_size)
    gradient, parts = add_pieces(first, [], loop_size, table, users, labels, None, False)
    first = other(packed, [0, -1])
    third = [held(3, to_next(second[0][0], 1, loop_size)), held(-3, to_next(second[1][0], -1, loop_size))]
    gradient, packed = add_pieces(second, [0, 1], loop_size, table, parts, labels, gradient, False)
    second = other(packed, [2, -2])
    third.append(held(4, opposite))
    arrived, gradient = lax.optimization_barrier(([array for array, _ in third], gradient))
    final = other(pack(arrived)[0], [3, -3, 4])
    (gradient,) = add_pieces(
        third + [first, second], [], loop_size, table, parts, labels, gradient, False
    )
    return *add_pieces([final], [], loop_size, table, parts, labels, gradient, True), users


def chunks_kernel(
    list_ref, count_ref, users_ref, labels_ref, items_ref, grad_ref, square_ref, tiles, parts_ref, sems
):
    tile = tiles.shape[0] // CHUNK
    step = pl.program_id(0)
    live = jnp.clip(count_ref[0] - step * CHUNK, 0, CHUNK)

    @pl.when(step == 0)
    def _():
        parts_ref[...] = halves(0.5 * users_ref[...])
        grad_ref[...] = jnp.zeros_like(grad_ref)

    def move(slot):
        start = pl.multiple_of(list_ref[0, step * CHUNK + slot] * tile, tile)
        return pltpu.make_async_copy(
            items_ref.at[pl.ds(start, tile), :], tiles.at[pl.ds(slot * tile, tile), :], sems.at[slot]
        )

    for slot in range(CHUNK):
        pl.when(slot < live)(lambda slot=slot: move(slot).start())
    for slot in range(CHUNK):
        pl.when(slot < live)(lambda slot=slot: move(slot).wait())

    def labels_at(position):
        return labels_ref[:, pl.ds(pl.multiple_of(position * tile, tile), tile)]

    add_tiles(grad_ref, parts_ref, tiles, live, labels_at)

    @pl.when(step == pl.num_programs(0) - 1)
    def _():
        store_square(grad_ref, square_ref)


def add_chunks(loop_size, items, lists, users, labels):
    rows, width = users.shape
    slots = lists[0].shape[1]
    tile = labels.shape[1] // slots
    return pl.pallas_call(
        chunks_kernel,
        grid=(slots // CHUNK,),
        out_shape=[
            jax.ShapeDtypeStruct((rows, width), jnp.float32),
            jax.ShapeDtypeStruct((loop_size, 128), jnp.float32),
        ],
        in_specs=[
            pl.BlockSpec(memory_space=pltpu.SMEM),
            pl.BlockSpec(memory_space=pltpu.SMEM),
            pl.BlockSpec((rows, width), lambda step: (0, 0)),
            pl.BlockSpec((rows, CHUNK * tile), lambda step: (0, step)),
            pl.BlockSpec(memory_space=pl.ANY),
        ],
        out_specs=[
            pl.BlockSpec((rows, width), lambda step: (0, 0)),
            pl.BlockSpec((loop_size, 128), lambda step: (0, 0)),
        ],
        scratch_shapes=[
            pltpu.VMEM((CHUNK * tile, width), jnp.bfloat16),
            pltpu.VMEM((2 * rows, width), jnp.bfloat16),
            pltpu.SemaphoreType.DMA((CHUNK,)),
        ],
        compiler_params=pltpu.CompilerParams(vmem_limit_bytes=32 * 1024 * 1024),
        cost_estimate=pl.CostEstimate(
            flops=8 * rows * width * slots * tile,
            bytes_accessed=4 * rows * (slots * tile + 2 * width) + 2 * slots * tile * width,
            transcendentals=rows * slots * tile,
        ),
        name="add_chunks",
    )(*lists, users, labels, items)


def update_kernel(entries, users_ref, grad_ref, squares_ref, out_ref, result, sems):
    total = jnp.sum(squares_ref[...], axis=0, keepdims=True)
    total = jnp.sum(total, axis=1, keepdims=True)
    scale = 0.5 / jnp.sqrt(total / entries + 1e-06)
    rows = users_ref.shape[0] // sems.shape[0]
    copies = []
    for at in range(sems.shape[0]):
        part = pl.ds(at * rows, rows)
        result[part, :] = users_ref[part, :] - scale * grad_ref[part, :]
        copies.append(pltpu.make_async_copy(result.at[part, :], out_ref.at[part, :], sems.at[at]))
        copies[-1].start()
    for copy in copies:
        copy.wait()


def local(users, items, tile_blocks, tile_count, labels):
    loop_size = lax.axis_size("loop")
    rows, width = users.shape
    slots = tile_blocks.shape[1]
    lists = (tile_blocks, tile_count)
    if loop_size == RING and slots == CHUNK:
        gradient, square, users = ring_gradient(users, items, lists, labels)
    else:
        whole = lax.all_gather(items, "loop", axis=0, tiled=True)
        gradient, square = add_chunks(loop_size, whole, lists, users, labels)

    squares = lax.all_to_all(square, "loop", 0, 0, tiled=True)
    return pl.pallas_call(
        functools.partial(update_kernel, rows * loop_size * width),
        out_shape=jax.ShapeDtypeStruct((rows, width), jnp.float32),
        in_specs=[pl.BlockSpec(memory_space=pltpu.VMEM)] * 3,
        out_specs=pl.BlockSpec(memory_space=pl.ANY),
        scratch_shapes=[pltpu.VMEM((rows, width), jnp.float32), pltpu.SemaphoreType.DMA((4,))],
        compiler_params=pltpu.CompilerParams(vmem_limit_bytes=16 * 1024 * 1024),
        cost_estimate=pl.CostEstimate(
            flops=2 * rows * width, bytes_accessed=12 * rows * width, transcendentals=0
        ),
        name="update",
    )(users, gradient, squares)


def solution(mesh):
    in_specs = (
        P(("group", "loop"), None),
        P(("group", "loop"), None),
        P(("group", "loop"), None),
        P(("group", "loop")),
        P(("group", "loop"), None),
    )
    out_specs = P(("group", "loop"), None)
    return jax.shard_map(local, mesh=mesh, in_specs=in_specs, out_specs=out_specs, check_vma=False)
```

```python
import functools

import jax
import jax.numpy as jnp
from jax import lax
from jax.experimental import pallas as pl
from jax.experimental.pallas import tpu as pltpu
from jax.sharding import PartitionSpec as P

CHUNK = 8
RING = 16


def ring_place(loop_size):
    outer = loop_size // 4

    def device(position, core):
        position = position % (2 * outer)
        chip = 2 * (outer - 1 - position) if position < outer else 2 * (position - outer) + 1
        return 2 * chip + core

    return 2 * outer, device


def to_next(array, direction, loop_size):
    chips, device = ring_place(loop_size)
    pairs = [(device(at, 0), device(at + direction, 0)) for at in range(chips)]
    pairs += [(device(at, 1), device(at - direction, 1)) for at in range(chips)]
    return lax.ppermute(array, "loop", pairs)


def across(array, loop_size):
    chips, device = ring_place(loop_size)
    pairs = [
        (device(at, core), device(at + (3 if at % 2 == 0 else -3), core))
        for at in range(chips)
        for core in range(2)
    ]
    return lax.ppermute(array, "loop", pairs)


def to_other_core(array, loop_size):
    return lax.ppermute(array, "loop", [(at, at ^ 1) for at in range(loop_size)])


def halves(values):
    upper = values.astype(jnp.bfloat16)
    return jnp.concatenate([upper, (values - upper.astype(jnp.float32)).astype(jnp.bfloat16)], 0)


def table_kernel(loop_size, origins, list_ref, count_ref, table_ref):
    chips = loop_size // 2
    lane = lax.broadcasted_iota(jnp.int32, table_ref.shape, 1)
    core, position = core_and_position(loop_size)
    hops, other = jnp.zeros_like(lane), jnp.zeros_like(lane)
    for at, origin in enumerate(origins):
        hops = jnp.where(lane == at, origin[0], hops)
        other = jnp.where(lane == at, origin[1], other)
    at = (position + chips + jnp.where(core == 0, -hops, hops)) & (chips - 1)
    chip = jnp.where(at < chips // 2, chips - 2 - 2 * at, 2 * at - chips + 1)
    block = 2 * chip + jnp.where(other == 1, 1 - core, core)
    found = jnp.full_like(lane, -1)
    for slot in range(list_ref.shape[1]):
        name = jnp.where(slot < count_ref[...], list_ref[:, slot : slot + 1], -1)
        found = jnp.where(name == block, slot, found)
    table_ref[...] = jnp.where(lane < len(origins), found, -1)


def slot_table(loop_size, origins, block_list, live_count):
    return pl.pallas_call(
        functools.partial(table_kernel, loop_size, origins),
        out_shape=jax.ShapeDtypeStruct((1, 128), jnp.int32),
        in_specs=[pl.BlockSpec(memory_space=pltpu.VMEM)] * 2,
        out_specs=pl.BlockSpec(memory_space=pltpu.VMEM),
        compiler_params=pltpu.CompilerParams(vmem_limit_bytes=16 * 1024 * 1024),
        cost_estimate=pl.CostEstimate(flops=2**32, bytes_accessed=1024, transcendentals=0),
        name="slot_table",
    )(block_list, live_count.reshape(1, 1))


def add_block(grad_ref, parts_ref, block, labels):
    rows = grad_ref.shape[0]
    tile = labels[0].shape[1]
    upper, lower = [], []
    for at in range(0, len(labels), 2):
        some = jnp.concatenate(labels[at : at + 2], 1)
        both = lax.dot_general(
            parts_ref[...],
            block[at * tile : at * tile + some.shape[1]],
            (((1,), (1,)), ((), ())),
            preferred_element_type=jnp.float32,
        )
        residual = 0.5 * jnp.tanh(both[:rows] + both[rows:]) + (0.5 - some.astype(jnp.float32))
        upper.append(residual.astype(jnp.bfloat16))
        lower.append((residual - upper[-1].astype(jnp.float32)).astype(jnp.bfloat16))
    grad_ref[...] += jnp.dot(
        jnp.concatenate(upper + lower, 1),
        jnp.concatenate([block, block], 0),
        preferred_element_type=jnp.float32,
    )


def add_tiles(grad_ref, parts_ref, tiles, live, labels_at):
    tile = tiles.shape[0] // CHUNK
    fours = (live + 1) // 4

    @pl.when(live % 4 == 3)
    def _():
        blank = pl.multiple_of(live * tile, tile)
        tiles[pl.ds(blank, tile), :] = jnp.zeros((tile, tiles.shape[1]), tiles.dtype)

    def add(count, index, carry):
        start = index * count
        block = tiles[pl.ds(pl.multiple_of(start * tile, tile), count * tile), :]
        add_block(grad_ref, parts_ref, block, [labels_at(start + at) for at in range(count)])
        return carry

    lax.fori_loop(0, fours, functools.partial(add, 4), 0)
    pl.when(live - 4 * fours == 2)(lambda: add(2, 2 * fours, None))
    pl.when(live - 4 * fours == 1)(lambda: add(1, 4 * fours, None))


def store_square(grad_ref, square_ref):
    gradient = grad_ref[...]
    square = jnp.sum(gradient * gradient, axis=0, keepdims=True)
    square = sum(square[:, at : at + 128] for at in range(0, square.shape[1], 128))
    square_ref[...] = jnp.broadcast_to(square, square_ref.shape)


def core_and_position(loop_size):
    me = lax.axis_index("loop")
    core, row, outer = me % 2, me // 2 % 2, me // 4
    return core, loop_size // 4 + jnp.where(row == 0, -1 - outer, outer)


def pack_kernel(*refs):
    tile = refs[0].shape[0]
    for at, ref in enumerate(refs[:-1]):
        refs[-1][at * tile : (at + 1) * tile, :] = ref[...]


def pack(arrays):
    tile, width = arrays[0].shape
    return pl.pallas_call(
        pack_kernel,
        out_shape=jax.ShapeDtypeStruct((len(arrays) * tile, width), arrays[0].dtype),
        in_specs=[pl.BlockSpec(memory_space=pltpu.VMEM)] * len(arrays),
        out_specs=pl.BlockSpec(memory_space=pltpu.VMEM),
        compiler_params=pltpu.CompilerParams(vmem_limit_bytes=16 * 1024 * 1024),
        cost_estimate=pl.CostEstimate(
            flops=2**34, bytes_accessed=4 * len(arrays) * tile * width, transcendentals=0
        ),
        name="pack",
    )(*arrays)


def pieces_kernel(places, count, packed, loop_size, first, last, table_ref, given_ref, labels_ref, *rest):
    rest = list(rest)
    arrays = [rest.pop(0) for _ in range(count)]
    if not first:
        rest.pop(0)
    grad_ref = rest.pop(0)
    parts_ref = rest.pop(0) if first else given_ref
    across_ref = rest.pop(0) if first else None
    pack_ref = rest.pop(0) if packed else None
    square_ref = rest.pop(0) if last else None
    tiles, slots = rest
    tile = tiles.shape[0] // CHUNK
    for at, index in enumerate(packed):
        pack_ref[at * tile : (at + 1) * tile, :] = arrays[index][...]
    if first:
        core, position = core_and_position(loop_size)
        for at in range(2):

            @pl.when((core + position) % 2 == at)
            def _():
                across_ref[...] = arrays[1 + at][...]

        parts_ref[...] = halves(0.5 * given_ref[...])
        grad_ref[...] = jnp.zeros_like(grad_ref)
    table = table_ref[...]
    entries = [table[0, at] for at, _, _ in places]

    def labels_of(slot):
        return labels_ref[:, pl.ds(pl.multiple_of(slot * tile, tile), tile)]

    live = jnp.int32(0)
    for found, (_, index, row) in zip(entries, places):

        @pl.when(found >= 0)
        def _():
            into = pl.ds(pl.multiple_of(live * tile, tile), tile)
            tiles[into, :] = arrays[index][row * tile : (row + 1) * tile, :]
            slots[live] = found

        live = live + (found >= 0).astype(jnp.int32)
    slots[live] = 0
    add_tiles(grad_ref, parts_ref, tiles, live, lambda position: labels_of(slots[position]))
    if last:
        store_square(grad_ref, square_ref)


def add_pieces(held, packed, loop_size, table, given, labels, before, last):
    first = before is None
    width = given.shape[1]
    rows = given.shape[0] // (1 if first else 2)
    arrays = [array for array, _ in held]
    tile = labels.shape[1] // CHUNK
    places = [(at, index, row) for index, (_, entries) in enumerate(held) for row, at in enumerate(entries)]
    most = min(len(places), CHUNK)
    out_shape = [jax.ShapeDtypeStruct((rows, width), jnp.float32)]
    if first:
        out_shape.append(jax.ShapeDtypeStruct((2 * rows, width), jnp.bfloat16))
        out_shape.append(jax.ShapeDtypeStruct((tile, width), jnp.bfloat16))
    if packed:
        out_shape.append(jax.ShapeDtypeStruct((len(packed) * tile, width), jnp.bfloat16))
    if last:
        out_shape.append(jax.ShapeDtypeStruct((loop_size, 128), jnp.float32))
    extra = [] if first else [before]
    return pl.pallas_call(
        functools.partial(pieces_kernel, places, len(arrays), packed, loop_size, first, last),
        out_shape=out_shape,
        in_specs=[pl.BlockSpec(memory_space=pltpu.VMEM)] * (3 + len(arrays) + len(extra)),
        out_specs=[pl.BlockSpec(memory_space=pltpu.VMEM)] * len(out_shape),
        input_output_aliases={} if first else {3 + len(arrays): 0},
        scratch_shapes=[
            pltpu.VMEM((CHUNK * tile, width), jnp.bfloat16),
            pltpu.SMEM((CHUNK + 1,), jnp.int32),
        ],
        compiler_params=pltpu.CompilerParams(vmem_limit_bytes=24 * 1024 * 1024),
        cost_estimate=pl.CostEstimate(
            flops=128 * rows * width * most * tile,
            bytes_accessed=8 * rows * width,
            transcendentals=rows * most * tile,
        ),
        name="add_pieces",
    )(table, given, labels, *arrays, *extra)


def ring_gradient(users, items, lists, labels):
    loop_size = lax.axis_size("loop")
    far = loop_size // 4
    origins = [(hops, 0) for hops in range(1 - far, far + 1)]
    origins += [(-hops, 1) for hops, _ in origins]
    table = slot_table(loop_size, origins, *lists)
    where = {origin: at for at, origin in enumerate(origins)}

    def held(hops, array):
        return array, [where[hops, 0]]

    def other(arrays, hops):
        return to_other_core(arrays, loop_size), [where[-hop, 1] for hop in hops]

    up = to_next(items, 1, loop_size)
    down = to_next(items, -1, loop_size)
    up, table = lax.optimization_barrier((up, table))
    first = [held(0, items), held(1, up), held(-1, down)]
    second = [held(2, to_next(up, 1, loop_size)), held(-2, to_next(down, -1, loop_size))]
    gradient, parts, opposite, packed = add_pieces(
        first, [0, 1, 2], loop_size, table, users, labels, None, False
    )
    opposite = across(opposite, loop_size)
    first = other(packed, [0, 1, -1])
    third = [held(3, to_next(second[0][0], 1, loop_size)), held(-3, to_next(second[1][0], -1, loop_size))]
    gradient, packed = add_pieces(second, [0, 1], loop_size, table, parts, labels, gradient, False)
    second = other(packed, [2, -2])
    third.append(held(4, opposite))
    arrived, gradient = lax.optimization_barrier(([array for array, _ in third], gradient))
    final = other(pack(arrived), [3, -3, 4])
    (gradient,) = add_pieces(
        third + [first, second], [], loop_size, table, parts, labels, gradient, False
    )
    return *add_pieces([final], [], loop_size, table, parts, labels, gradient, True), users


def chunks_kernel(
    list_ref, count_ref, users_ref, labels_ref, items_ref, grad_ref, square_ref, tiles, parts_ref, sems
):
    tile = tiles.shape[0] // CHUNK
    step = pl.program_id(0)
    live = jnp.clip(count_ref[0] - step * CHUNK, 0, CHUNK)

    @pl.when(step == 0)
    def _():
        parts_ref[...] = halves(0.5 * users_ref[...])
        grad_ref[...] = jnp.zeros_like(grad_ref)

    def move(slot):
        start = pl.multiple_of(list_ref[0, step * CHUNK + slot] * tile, tile)
        return pltpu.make_async_copy(
            items_ref.at[pl.ds(start, tile), :], tiles.at[pl.ds(slot * tile, tile), :], sems.at[slot]
        )

    for slot in range(CHUNK):
        pl.when(slot < live)(lambda slot=slot: move(slot).start())
    for slot in range(CHUNK):
        pl.when(slot < live)(lambda slot=slot: move(slot).wait())

    def labels_at(position):
        return labels_ref[:, pl.ds(pl.multiple_of(position * tile, tile), tile)]

    add_tiles(grad_ref, parts_ref, tiles, live, labels_at)

    @pl.when(step == pl.num_programs(0) - 1)
    def _():
        store_square(grad_ref, square_ref)


def add_chunks(loop_size, items, lists, users, labels):
    rows, width = users.shape
    slots = lists[0].shape[1]
    tile = labels.shape[1] // slots
    return pl.pallas_call(
        chunks_kernel,
        grid=(slots // CHUNK,),
        out_shape=[
            jax.ShapeDtypeStruct((rows, width), jnp.float32),
            jax.ShapeDtypeStruct((loop_size, 128), jnp.float32),
        ],
        in_specs=[
            pl.BlockSpec(memory_space=pltpu.SMEM),
            pl.BlockSpec(memory_space=pltpu.SMEM),
            pl.BlockSpec((rows, width), lambda step: (0, 0)),
            pl.BlockSpec((rows, CHUNK * tile), lambda step: (0, step)),
            pl.BlockSpec(memory_space=pl.ANY),
        ],
        out_specs=[
            pl.BlockSpec((rows, width), lambda step: (0, 0)),
            pl.BlockSpec((loop_size, 128), lambda step: (0, 0)),
        ],
        scratch_shapes=[
            pltpu.VMEM((CHUNK * tile, width), jnp.bfloat16),
            pltpu.VMEM((2 * rows, width), jnp.bfloat16),
            pltpu.SemaphoreType.DMA((CHUNK,)),
        ],
        compiler_params=pltpu.CompilerParams(vmem_limit_bytes=32 * 1024 * 1024),
        cost_estimate=pl.CostEstimate(
            flops=8 * rows * width * slots * tile,
            bytes_accessed=4 * rows * (slots * tile + 2 * width) + 2 * slots * tile * width,
            transcendentals=rows * slots * tile,
        ),
        name="add_chunks",
    )(*lists, users, labels, items)


def update_kernel(entries, users_ref, grad_ref, squares_ref, out_ref, result, sems):
    total = jnp.sum(squares_ref[...], axis=0, keepdims=True)
    total = jnp.sum(total, axis=1, keepdims=True)
    scale = 0.5 / jnp.sqrt(total / entries + 1e-06)
    rows = users_ref.shape[0] // sems.shape[0]
    copies = []
    for at in range(sems.shape[0]):
        part = pl.ds(at * rows, rows)
        result[part, :] = users_ref[part, :] - scale * grad_ref[part, :]
        copies.append(pltpu.make_async_copy(result.at[part, :], out_ref.at[part, :], sems.at[at]))
        copies[-1].start()
    for copy in copies:
        copy.wait()


def local(users, items, tile_blocks, tile_count, labels):
    loop_size = lax.axis_size("loop")
    rows, width = users.shape
    slots = tile_blocks.shape[1]
    lists = (tile_blocks, tile_count)
    if loop_size == RING and slots == CHUNK:
        gradient, square, users = ring_gradient(users, items, lists, labels)
    else:
        whole = lax.all_gather(items, "loop", axis=0, tiled=True)
        gradient, square = add_chunks(loop_size, whole, lists, users, labels)

    squares = lax.all_to_all(square, "loop", 0, 0, tiled=True)
    return pl.pallas_call(
        functools.partial(update_kernel, rows * loop_size * width),
        out_shape=jax.ShapeDtypeStruct((rows, width), jnp.float32),
        in_specs=[pl.BlockSpec(memory_space=pltpu.VMEM)] * 3,
        out_specs=pl.BlockSpec(memory_space=pl.ANY),
        scratch_shapes=[pltpu.VMEM((rows, width), jnp.float32), pltpu.SemaphoreType.DMA((4,))],
        compiler_params=pltpu.CompilerParams(vmem_limit_bytes=16 * 1024 * 1024),
        cost_estimate=pl.CostEstimate(
            flops=2 * rows * width, bytes_accessed=12 * rows * width, transcendentals=0
        ),
        name="update",
    )(users, gradient, squares)


def solution(mesh):
    in_specs = (
        P(("group", "loop"), None),
        P(("group", "loop"), None),
        P(("group", "loop"), None),
        P(("group", "loop")),
        P(("group", "loop"), None),
    )
    out_specs = P(("group", "loop"), None)
    return jax.shard_map(local, mesh=mesh, in_specs=in_specs, out_specs=out_specs, check_vma=False)
```

```python
import functools

import jax
import jax.numpy as jnp
from jax import lax
from jax.experimental import pallas as pl
from jax.experimental.pallas import tpu as pltpu
from jax.sharding import PartitionSpec as P

CHUNK = 8
RING = 16


def ring_place(loop_size):
    outer = loop_size // 4

    def device(position, core):
        position = position % (2 * outer)
        chip = 2 * position if position < outer else 2 * (2 * outer - 1 - position) + 1
        return 2 * chip + core

    return 2 * outer, device


def to_next(array, direction, loop_size):
    chips, device = ring_place(loop_size)
    pairs = [(device(at, 0), device(at + direction, 0)) for at in range(chips)]
    pairs += [(device(at, 1), device(at - direction, 1)) for at in range(chips)]
    return lax.ppermute(array, "loop", pairs)


def across(array, loop_size):
    chips, device = ring_place(loop_size)
    pairs = [(device(at, 0), device(at + (3 if at % 2 == 0 else -3), 0)) for at in range(chips)]
    return lax.ppermute(array, "loop", pairs)


def to_opposite(array, loop_size):
    chips, device = ring_place(loop_size)
    return lax.ppermute(array, "loop", [(device(at, 1), device(at + chips // 2, 1)) for at in range(chips)])


def to_other_core(array, loop_size):
    return lax.ppermute(array, "loop", [(at, at ^ 1) for at in range(loop_size)])


def halves(values):
    upper = values.astype(jnp.bfloat16)
    return jnp.concatenate([upper, (values - upper.astype(jnp.float32)).astype(jnp.bfloat16)], 0)


def table_kernel(loop_size, origins, list_ref, count_ref, table_ref):
    chips = loop_size // 2
    lane = lax.broadcasted_iota(jnp.int32, table_ref.shape, 1)
    core, position = core_and_position(loop_size)
    hops, other, missing = jnp.zeros_like(lane), jnp.zeros_like(lane), jnp.full_like(lane, 2)
    for at, origin in enumerate(origins):
        hops = jnp.where(lane == at, origin[0], hops)
        other = jnp.where(lane == at, origin[1], other)
        missing = jnp.where(lane == at, origin[2], missing)
    at = (position + chips + jnp.where(core == 0, -hops, hops)) & (chips - 1)
    chip = jnp.where(at < chips // 2, 2 * at, 2 * (chips - 1 - at) + 1)
    block = 2 * chip + jnp.where(other == 1, 1 - core, core)
    found = jnp.full_like(lane, -1)
    for slot in range(list_ref.shape[1]):
        name = jnp.where(slot < count_ref[...], list_ref[:, slot : slot + 1], -1)
        found = jnp.where(name == block, slot, found)
    table_ref[...] = jnp.where((lane < len(origins)) & (missing != core), found, -1)


def slot_table(loop_size, origins, block_list, live_count):
    return pl.pallas_call(
        functools.partial(table_kernel, loop_size, origins),
        out_shape=jax.ShapeDtypeStruct((1, 128), jnp.int32),
        in_specs=[pl.BlockSpec(memory_space=pltpu.VMEM)] * 2,
        out_specs=pl.BlockSpec(memory_space=pltpu.VMEM),
        compiler_params=pltpu.CompilerParams(vmem_limit_bytes=16 * 1024 * 1024),
        cost_estimate=pl.CostEstimate(flops=2**32, bytes_accessed=1024, transcendentals=0),
        name="slot_table",
    )(block_list, live_count.reshape(1, 1))


def add_block(grad_ref, parts_ref, block, labels):
    rows = grad_ref.shape[0]
    tile = labels[0].shape[1]
    upper, lower = [], []
    for at in range(0, len(labels), 2):
        some = jnp.concatenate(labels[at : at + 2], 1)
        both = lax.dot_general(
            parts_ref[...],
            block[at * tile : at * tile + some.shape[1]],
            (((1,), (1,)), ((), ())),
            preferred_element_type=jnp.float32,
        )
        residual = 0.5 * jnp.tanh(both[:rows] + both[rows:]) + (0.5 - some.astype(jnp.float32))
        upper.append(residual.astype(jnp.bfloat16))
        lower.append((residual - upper[-1].astype(jnp.float32)).astype(jnp.bfloat16))
    grad_ref[...] += jnp.dot(
        jnp.concatenate(upper + lower, 1),
        jnp.concatenate([block, block], 0),
        preferred_element_type=jnp.float32,
    )


def add_tiles(grad_ref, parts_ref, tiles, live, labels_at):
    tile = tiles.shape[0] // CHUNK
    fours = (live + 1) // 4

    @pl.when(live % 4 == 3)
    def _():
        blank = pl.multiple_of(live * tile, tile)
        tiles[pl.ds(blank, tile), :] = jnp.zeros((tile, tiles.shape[1]), tiles.dtype)

    def add(count, index, carry):
        start = index * count
        block = tiles[pl.ds(pl.multiple_of(start * tile, tile), count * tile), :]
        add_block(grad_ref, parts_ref, block, [labels_at(start + at) for at in range(count)])
        return carry

    lax.fori_loop(0, fours, functools.partial(add, 4), 0)
    pl.when(live - 4 * fours == 2)(lambda: add(2, 2 * fours, None))
    pl.when(live - 4 * fours == 1)(lambda: add(1, 4 * fours, None))


def store_square(grad_ref, square_ref):
    gradient = grad_ref[...]
    square = jnp.sum(gradient * gradient, axis=0, keepdims=True)
    square = sum(square[:, at : at + 128] for at in range(0, square.shape[1], 128))
    square_ref[...] = jnp.broadcast_to(square, square_ref.shape)


def core_and_position(loop_size):
    me = lax.axis_index("loop")
    core, row, outer = me % 2, me // 2 % 2, me // 4
    return core, jnp.where(row == 0, outer, loop_size // 2 - 1 - outer)


def pack_kernel(*refs):
    tile = refs[0].shape[0]
    packed_ref = refs[-1]
    for at, ref in enumerate(refs[:-3]):
        packed_ref[at * tile : (at + 1) * tile, :] = ref[...]
    for core, ref in enumerate(refs[-3:-1]):

        @pl.when(lax.axis_index("loop") % 2 == core)
        def _():
            packed_ref[(len(refs) - 3) * tile :, :] = ref[...]


def pack(arrays):
    tile, width = arrays[0].shape
    return pl.pallas_call(
        pack_kernel,
        out_shape=jax.ShapeDtypeStruct(((len(arrays) - 1) * tile, width), arrays[0].dtype),
        in_specs=[pl.BlockSpec(memory_space=pltpu.VMEM)] * len(arrays),
        out_specs=pl.BlockSpec(memory_space=pltpu.VMEM),
        compiler_params=pltpu.CompilerParams(vmem_limit_bytes=16 * 1024 * 1024),
        cost_estimate=pl.CostEstimate(
            flops=2**34, bytes_accessed=4 * len(arrays) * tile * width, transcendentals=0
        ),
        name="pack",
    )(*arrays)


def pieces_kernel(places, count, packed, loop_size, first, last, table_ref, given_ref, labels_ref, *rest):
    rest = list(rest)
    arrays = [rest.pop(0) for _ in range(count)]
    if not first:
        rest.pop(0)
    grad_ref = rest.pop(0)
    parts_ref = rest.pop(0) if first else given_ref
    across_ref = rest.pop(0) if first else None
    pack_ref = rest.pop(0) if packed else None
    square_ref = rest.pop(0) if last else None
    tiles, slots = rest
    tile = tiles.shape[0] // CHUNK
    for at, index in enumerate(packed):
        pack_ref[at * tile : (at + 1) * tile, :] = arrays[index][...]
    if first:
        core, position = core_and_position(loop_size)
        for at in range(2):

            @pl.when((core + position) % 2 == at)
            def _():
                across_ref[...] = arrays[1 + at][...]

        parts_ref[...] = halves(0.5 * given_ref[...])
        grad_ref[...] = jnp.zeros_like(grad_ref)
    table = table_ref[...]
    entries = [table[0, at] for at, _, _ in places]

    def labels_of(slot):
        return labels_ref[:, pl.ds(pl.multiple_of(slot * tile, tile), tile)]

    live = jnp.int32(0)
    for found, (_, index, row) in zip(entries, places):

        @pl.when(found >= 0)
        def _():
            into = pl.ds(pl.multiple_of(live * tile, tile), tile)
            tiles[into, :] = arrays[index][row * tile : (row + 1) * tile, :]
            slots[live] = found

        live = live + (found >= 0).astype(jnp.int32)
    slots[live] = 0
    add_tiles(grad_ref, parts_ref, tiles, live, lambda position: labels_of(slots[position]))
    if last:
        store_square(grad_ref, square_ref)


def add_pieces(held, packed, loop_size, table, given, labels, before, last):
    first = before is None
    width = given.shape[1]
    rows = given.shape[0] // (1 if first else 2)
    arrays = [array for array, _ in held]
    tile = labels.shape[1] // CHUNK
    places = [(at, index, row) for index, (_, entries) in enumerate(held) for row, at in enumerate(entries)]
    most = min(len(places), CHUNK)
    out_shape = [jax.ShapeDtypeStruct((rows, width), jnp.float32)]
    if first:
        out_shape.append(jax.ShapeDtypeStruct((2 * rows, width), jnp.bfloat16))
        out_shape.append(jax.ShapeDtypeStruct((tile, width), jnp.bfloat16))
    if packed:
        out_shape.append(jax.ShapeDtypeStruct((len(packed) * tile, width), jnp.bfloat16))
    if last:
        out_shape.append(jax.ShapeDtypeStruct((loop_size, 128), jnp.float32))
    extra = [] if first else [before]
    return pl.pallas_call(
        functools.partial(pieces_kernel, places, len(arrays), packed, loop_size, first, last),
        out_shape=out_shape,
        in_specs=[pl.BlockSpec(memory_space=pltpu.VMEM)] * (3 + len(arrays) + len(extra)),
        out_specs=[pl.BlockSpec(memory_space=pltpu.VMEM)] * len(out_shape),
        input_output_aliases={} if first else {3 + len(arrays): 0},
        scratch_shapes=[
            pltpu.VMEM((CHUNK * tile, width), jnp.bfloat16),
            pltpu.SMEM((CHUNK + 1,), jnp.int32),
        ],
        compiler_params=pltpu.CompilerParams(vmem_limit_bytes=24 * 1024 * 1024),
        cost_estimate=pl.CostEstimate(
            flops=128 * rows * width * most * tile,
            bytes_accessed=8 * rows * width,
            transcendentals=rows * most * tile,
        ),
        name="add_pieces",
    )(table, given, labels, *arrays, *extra)


def ring_gradient(users, items, lists, labels):
    loop_size = lax.axis_size("loop")
    far = loop_size // 4
    origins = [(hops, 0, 2) for hops in range(1 - far, far)] + [(far, 0, 1), (far, 0, 0)]
    origins += [(-hops, 1, 2) for hops in range(1 - far, far + 1)]
    table = slot_table(loop_size, origins, *lists)
    where = {origin: at for at, origin in enumerate(origins)}

    def held(hops, array, missing=2):
        return array, [where[hops, 0, missing]]

    def other(arrays, hops):
        return to_other_core(arrays, loop_size), [where[-hop, 1, 2] for hop in hops]

    up = to_next(items, 1, loop_size)
    down = to_next(items, -1, loop_size)
    up, table = lax.optimization_barrier((up, table))
    straight = held(far, to_opposite(items, loop_size), 0)
    first = [held(0, items), held(1, up), held(-1, down), straight]
    second = [held(2, to_next(up, 1, loop_size)), held(-2, to_next(down, -1, loop_size))]
    gradient, parts, opposite, packed = add_pieces(
        first, [0, 1, 2], loop_size, table, users, labels, None, False
    )
    opposite = across(opposite, loop_size)
    first = other(packed, [0, 1, -1])
    third = [held(3, to_next(second[0][0], 1, loop_size)), held(-3, to_next(second[1][0], -1, loop_size))]
    gradient, packed = add_pieces(second, [0, 1], loop_size, table, parts, labels, gradient, False)
    second = other(packed, [2, -2])
    third.append(held(far, opposite, 1))
    arrived, gradient = lax.optimization_barrier(([array for array, _ in third], gradient))
    final = other(pack([*arrived, straight[0]]), [3, -3, far])
    (gradient,) = add_pieces(
        third + [first, second], [], loop_size, table, parts, labels, gradient, False
    )
    return *add_pieces([final], [], loop_size, table, parts, labels, gradient, True), users


def chunks_kernel(
    list_ref, count_ref, users_ref, labels_ref, items_ref, grad_ref, square_ref, tiles, parts_ref, sems
):
    tile = tiles.shape[0] // CHUNK
    step = pl.program_id(0)
    live = jnp.clip(count_ref[0] - step * CHUNK, 0, CHUNK)

    @pl.when(step == 0)
    def _():
        parts_ref[...] = halves(0.5 * users_ref[...])
        grad_ref[...] = jnp.zeros_like(grad_ref)

    def move(slot):
        start = pl.multiple_of(list_ref[0, step * CHUNK + slot] * tile, tile)
        return pltpu.make_async_copy(
            items_ref.at[pl.ds(start, tile), :], tiles.at[pl.ds(slot * tile, tile), :], sems.at[slot]
        )

    for slot in range(CHUNK):
        pl.when(slot < live)(lambda slot=slot: move(slot).start())
    for slot in range(CHUNK):
        pl.when(slot < live)(lambda slot=slot: move(slot).wait())

    def labels_at(position):
        return labels_ref[:, pl.ds(pl.multiple_of(position * tile, tile), tile)]

    add_tiles(grad_ref, parts_ref, tiles, live, labels_at)

    @pl.when(step == pl.num_programs(0) - 1)
    def _():
        store_square(grad_ref, square_ref)


def add_chunks(loop_size, items, lists, users, labels):
    rows, width = users.shape
    slots = lists[0].shape[1]
    tile = labels.shape[1] // slots
    return pl.pallas_call(
        chunks_kernel,
        grid=(slots // CHUNK,),
        out_shape=[
            jax.ShapeDtypeStruct((rows, width), jnp.float32),
            jax.ShapeDtypeStruct((loop_size, 128), jnp.float32),
        ],
        in_specs=[
            pl.BlockSpec(memory_space=pltpu.SMEM),
            pl.BlockSpec(memory_space=pltpu.SMEM),
            pl.BlockSpec((rows, width), lambda step: (0, 0)),
            pl.BlockSpec((rows, CHUNK * tile), lambda step: (0, step)),
            pl.BlockSpec(memory_space=pl.ANY),
        ],
        out_specs=[
            pl.BlockSpec((rows, width), lambda step: (0, 0)),
            pl.BlockSpec((loop_size, 128), lambda step: (0, 0)),
        ],
        scratch_shapes=[
            pltpu.VMEM((CHUNK * tile, width), jnp.bfloat16),
            pltpu.VMEM((2 * rows, width), jnp.bfloat16),
            pltpu.SemaphoreType.DMA((CHUNK,)),
        ],
        compiler_params=pltpu.CompilerParams(vmem_limit_bytes=32 * 1024 * 1024),
        cost_estimate=pl.CostEstimate(
            flops=8 * rows * width * slots * tile,
            bytes_accessed=4 * rows * (slots * tile + 2 * width) + 2 * slots * tile * width,
            transcendentals=rows * slots * tile,
        ),
        name="add_chunks",
    )(*lists, users, labels, items)


def update_kernel(entries, users_ref, grad_ref, squares_ref, out_ref, result, sems):
    total = jnp.sum(squares_ref[...], axis=0, keepdims=True)
    total = jnp.sum(total, axis=1, keepdims=True)
    scale = 0.5 / jnp.sqrt(total / entries + 1e-06)
    rows = users_ref.shape[0] // sems.shape[0]
    copies = []
    for at in range(sems.shape[0]):
        part = pl.ds(at * rows, rows)
        result[part, :] = users_ref[part, :] - scale * grad_ref[part, :]
        copies.append(pltpu.make_async_copy(result.at[part, :], out_ref.at[part, :], sems.at[at]))
        copies[-1].start()
    for copy in copies:
        copy.wait()


def local(users, items, tile_blocks, tile_count, labels):
    loop_size = lax.axis_size("loop")
    rows, width = users.shape
    slots = tile_blocks.shape[1]
    lists = (tile_blocks, tile_count)
    if loop_size == RING and slots == CHUNK:
        gradient, square, users = ring_gradient(users, items, lists, labels)
    else:
        whole = lax.all_gather(items, "loop", axis=0, tiled=True)
        gradient, square = add_chunks(loop_size, whole, lists, users, labels)

    squares = lax.all_to_all(square, "loop", 0, 0, tiled=True)
    return pl.pallas_call(
        functools.partial(update_kernel, rows * loop_size * width),
        out_shape=jax.ShapeDtypeStruct((rows, width), jnp.float32),
        in_specs=[pl.BlockSpec(memory_space=pltpu.VMEM)] * 3,
        out_specs=pl.BlockSpec(memory_space=pl.ANY),
        scratch_shapes=[pltpu.VMEM((rows, width), jnp.float32), pltpu.SemaphoreType.DMA((4,))],
        compiler_params=pltpu.CompilerParams(vmem_limit_bytes=16 * 1024 * 1024),
        cost_estimate=pl.CostEstimate(
            flops=2 * rows * width, bytes_accessed=12 * rows * width, transcendentals=0
        ),
        name="update",
    )(users, gradient, squares)


def solution(mesh):
    in_specs = (
        P(("group", "loop"), None),
        P(("group", "loop"), None),
        P(("group", "loop"), None),
        P(("group", "loop")),
        P(("group", "loop"), None),
    )
    out_specs = P(("group", "loop"), None)
    return jax.shard_map(local, mesh=mesh, in_specs=in_specs, out_specs=out_specs, check_vma=False)
```

```python
import functools

import jax
import jax.numpy as jnp
from jax import lax
from jax.experimental import pallas as pl
from jax.experimental.pallas import tpu as pltpu
from jax.sharding import PartitionSpec as P

CHUNK = 8
RING = 16


def ring_place(loop_size):
    outer = loop_size // 4

    def device(position, core):
        position = position % (2 * outer)
        chip = 2 * position if position < outer else 2 * (2 * outer - 1 - position) + 1
        return 2 * chip + core

    return 2 * outer, device


def to_next(array, direction, loop_size):
    chips, device = ring_place(loop_size)
    pairs = [(device(at, 0), device(at + direction, 0)) for at in range(chips)]
    pairs += [(device(at, 1), device(at - direction, 1)) for at in range(chips)]
    return lax.ppermute(array, "loop", pairs)


def across(array, loop_size):
    chips, device = ring_place(loop_size)
    pairs = [
        (device(at, core), device(at + (3 if at % 2 == 0 else -3), core))
        for at in range(chips)
        for core in range(2)
    ]
    return lax.ppermute(array, "loop", pairs)


def to_pair(array, loop_size):
    chips, device = ring_place(loop_size)
    pairs = [
        (device(at, core), device(at + (1 if at % 2 else -1), core))
        for at in range(chips)
        for core in range(2)
    ]
    return lax.ppermute(array, "loop", pairs)


def to_other_core(array, loop_size):
    return lax.ppermute(array, "loop", [(at, at ^ 1) for at in range(loop_size)])


def halves(values):
    upper = values.astype(jnp.bfloat16)
    return jnp.concatenate([upper, (values - upper.astype(jnp.float32)).astype(jnp.bfloat16)], 0)


def table_kernel(loop_size, origins, list_ref, count_ref, table_ref):
    chips = loop_size // 2
    lane = lax.broadcasted_iota(jnp.int32, table_ref.shape, 1)
    core, position = core_and_position(loop_size)
    hops, skips, other = jnp.zeros_like(lane), jnp.zeros_like(lane), jnp.zeros_like(lane)
    for at, origin in enumerate(origins):
        hops = jnp.where(lane == at, origin[0], hops)
        skips = jnp.where(lane == at, origin[1], skips)
        other = jnp.where(lane == at, origin[2], other)
    hops = jnp.where(core == 0, -hops, hops) + jnp.where(position % 2 == 0, skips, -skips)
    at = (position + chips + hops) & (chips - 1)
    chip = jnp.where(at < chips // 2, 2 * at, 2 * (chips - 1 - at) + 1)
    block = 2 * chip + jnp.where(other == 1, 1 - core, core)
    found = jnp.full_like(lane, -1)
    for slot in range(list_ref.shape[1]):
        name = jnp.where(slot < count_ref[...], list_ref[:, slot : slot + 1], -1)
        found = jnp.where(name == block, slot, found)
    table_ref[...] = jnp.where(lane < len(origins), found, -1)


def slot_table(loop_size, origins, block_list, live_count):
    return pl.pallas_call(
        functools.partial(table_kernel, loop_size, origins),
        out_shape=jax.ShapeDtypeStruct((1, 128), jnp.int32),
        in_specs=[pl.BlockSpec(memory_space=pltpu.VMEM)] * 2,
        out_specs=pl.BlockSpec(memory_space=pltpu.VMEM),
        compiler_params=pltpu.CompilerParams(vmem_limit_bytes=16 * 1024 * 1024),
        cost_estimate=pl.CostEstimate(flops=2**32, bytes_accessed=1024, transcendentals=0),
        name="slot_table",
    )(block_list, live_count.reshape(1, 1))


def add_block(grad_ref, parts_ref, block, labels):
    rows = grad_ref.shape[0]
    tile = labels[0].shape[1]
    upper, lower = [], []
    for at in range(0, len(labels), 2):
        some = jnp.concatenate(labels[at : at + 2], 1)
        both = lax.dot_general(
            parts_ref[...],
            block[at * tile : at * tile + some.shape[1]],
            (((1,), (1,)), ((), ())),
            preferred_element_type=jnp.float32,
        )
        residual = 0.5 * jnp.tanh(both[:rows] + both[rows:]) + (0.5 - some.astype(jnp.float32))
        upper.append(residual.astype(jnp.bfloat16))
        lower.append((residual - upper[-1].astype(jnp.float32)).astype(jnp.bfloat16))
    grad_ref[...] += jnp.dot(
        jnp.concatenate(upper + lower, 1),
        jnp.concatenate([block, block], 0),
        preferred_element_type=jnp.float32,
    )


def add_tiles(grad_ref, parts_ref, tiles, live, labels_at):
    tile = tiles.shape[0] // CHUNK
    fours = (live + 1) // 4

    @pl.when(live % 4 == 3)
    def _():
        blank = pl.multiple_of(live * tile, tile)
        tiles[pl.ds(blank, tile), :] = jnp.zeros((tile, tiles.shape[1]), tiles.dtype)

    def add(count, index, carry):
        start = index * count
        block = tiles[pl.ds(pl.multiple_of(start * tile, tile), count * tile), :]
        add_block(grad_ref, parts_ref, block, [labels_at(start + at) for at in range(count)])
        return carry

    lax.fori_loop(0, fours, functools.partial(add, 4), 0)
    pl.when(live - 4 * fours == 2)(lambda: add(2, 2 * fours, None))
    pl.when(live - 4 * fours == 1)(lambda: add(1, 4 * fours, None))


def store_square(grad_ref, square_ref):
    gradient = grad_ref[...]
    square = jnp.sum(gradient * gradient, axis=0, keepdims=True)
    square = sum(square[:, at : at + 128] for at in range(0, square.shape[1], 128))
    square_ref[...] = jnp.broadcast_to(square, square_ref.shape)


def core_and_position(loop_size):
    me = lax.axis_index("loop")
    core, row, outer = me % 2, me // 2 % 2, me // 4
    return core, jnp.where(row == 0, outer, loop_size // 2 - 1 - outer)


def pick_kernel(loop_size, upper_ref, lower_ref, picked_ref):
    core, position = core_and_position(loop_size)
    for at, ref in enumerate((lower_ref, upper_ref)):

        @pl.when((core + position) % 2 == at)
        def _():
            picked_ref[...] = ref[...]


def pick(upper, lower, loop_size):
    return pl.pallas_call(
        functools.partial(pick_kernel, loop_size),
        out_shape=jax.ShapeDtypeStruct(upper.shape, upper.dtype),
        in_specs=[pl.BlockSpec(memory_space=pltpu.VMEM)] * 2,
        out_specs=pl.BlockSpec(memory_space=pltpu.VMEM),
        compiler_params=pltpu.CompilerParams(vmem_limit_bytes=16 * 1024 * 1024),
        cost_estimate=pl.CostEstimate(
            flops=0, bytes_accessed=4 * upper.size, transcendentals=0
        ),
        name="pick",
    )(upper, lower)


def pack_kernel(*refs):
    tile = refs[0].shape[0]
    for at, ref in enumerate(refs[:-1]):
        refs[-1][at * tile : (at + 1) * tile, :] = ref[...]


def pack(arrays):
    tile, width = arrays[0].shape
    return pl.pallas_call(
        pack_kernel,
        out_shape=jax.ShapeDtypeStruct((len(arrays) * tile, width), arrays[0].dtype),
        in_specs=[pl.BlockSpec(memory_space=pltpu.VMEM)] * len(arrays),
        out_specs=pl.BlockSpec(memory_space=pltpu.VMEM),
        compiler_params=pltpu.CompilerParams(vmem_limit_bytes=16 * 1024 * 1024),
        cost_estimate=pl.CostEstimate(
            flops=2**34, bytes_accessed=4 * len(arrays) * tile * width, transcendentals=0
        ),
        name="pack",
    )(*arrays)


def pieces_kernel(places, count, packed, loop_size, first, last, table_ref, given_ref, labels_ref, *rest):
    rest = list(rest)
    arrays = [rest.pop(0) for _ in range(count)]
    if not first:
        rest.pop(0)
    grad_ref = rest.pop(0)
    parts_ref = rest.pop(0) if first else given_ref
    across_ref = rest.pop(0) if first else None
    pack_ref = rest.pop(0) if packed else None
    square_ref = rest.pop(0) if last else None
    tiles, slots = rest
    tile = tiles.shape[0] // CHUNK
    for at, index in enumerate(packed):
        pack_ref[at * tile : (at + 1) * tile, :] = arrays[index][...]
    if first:
        core, position = core_and_position(loop_size)
        for at in range(2):

            @pl.when((core + position) % 2 == at)
            def _():
                across_ref[...] = arrays[1 + at][...]

        parts_ref[...] = halves(0.5 * given_ref[...])
        grad_ref[...] = jnp.zeros_like(grad_ref)
    table = table_ref[...]
    entries = [table[0, at] for at, _, _ in places]

    def labels_of(slot):
        return labels_ref[:, pl.ds(pl.multiple_of(slot * tile, tile), tile)]

    live = jnp.int32(0)
    for found, (_, index, row) in zip(entries, places):

        @pl.when(found >= 0)
        def _():
            into = pl.ds(pl.multiple_of(live * tile, tile), tile)
            tiles[into, :] = arrays[index][row * tile : (row + 1) * tile, :]
            slots[live] = found

        live = live + (found >= 0).astype(jnp.int32)
    slots[live] = 0
    add_tiles(grad_ref, parts_ref, tiles, live, lambda position: labels_of(slots[position]))
    if last:
        store_square(grad_ref, square_ref)


def add_pieces(held, packed, loop_size, table, given, labels, before, last):
    first = before is None
    width = given.shape[1]
    rows = given.shape[0] // (1 if first else 2)
    arrays = [array for array, _ in held]
    tile = labels.shape[1] // CHUNK
    places = [(at, index, row) for index, (_, entries) in enumerate(held) for row, at in enumerate(entries)]
    most = min(len(places), CHUNK)
    out_shape = [jax.ShapeDtypeStruct((rows, width), jnp.float32)]
    if first:
        out_shape.append(jax.ShapeDtypeStruct((2 * rows, width), jnp.bfloat16))
        out_shape.append(jax.ShapeDtypeStruct((tile, width), jnp.bfloat16))
    if packed:
        out_shape.append(jax.ShapeDtypeStruct((len(packed) * tile, width), jnp.bfloat16))
    if last:
        out_shape.append(jax.ShapeDtypeStruct((loop_size, 128), jnp.float32))
    extra = [] if first else [before]
    return pl.pallas_call(
        functools.partial(pieces_kernel, places, len(arrays), packed, loop_size, first, last),
        out_shape=out_shape,
        in_specs=[pl.BlockSpec(memory_space=pltpu.VMEM)] * (3 + len(arrays) + len(extra)),
        out_specs=[pl.BlockSpec(memory_space=pltpu.VMEM)] * len(out_shape),
        input_output_aliases={} if first else {3 + len(arrays): 0},
        scratch_shapes=[
            pltpu.VMEM((CHUNK * tile, width), jnp.bfloat16),
            pltpu.SMEM((CHUNK + 1,), jnp.int32),
        ],
        compiler_params=pltpu.CompilerParams(vmem_limit_bytes=24 * 1024 * 1024),
        cost_estimate=pl.CostEstimate(
            flops=128 * rows * width * most * tile,
            bytes_accessed=8 * rows * width,
            transcendentals=rows * most * tile,
        ),
        name="add_pieces",
    )(table, given, labels, *arrays, *extra)


def ring_gradient(users, items, lists, labels):
    loop_size = lax.axis_size("loop")
    near = [(0, 0), (1, 0), (-1, 0), (0, 3), (2, 0), (-2, 0), (0, -3), (4, 0)]
    origins = [(hops, skips, 0) for hops, skips in near] + [(-hops, skips, 1) for hops, skips in near]
    table = slot_table(loop_size, origins, *lists)

    def held(array, origin):
        return array, [near.index(origin)]

    def other(array, some):
        return to_other_core(array, loop_size), [len(near) + near.index(origin) for origin in some]

    up = to_next(items, 1, loop_size)
    down = to_next(items, -1, loop_size)
    up, table = lax.optimization_barrier((up, table))
    first = [held(items, (0, 0)), held(up, (1, 0)), held(down, (-1, 0))]
    first.append(held(across(items, loop_size), (0, 3)))
    up, down = to_next(up, 1, loop_size), to_next(down, -1, loop_size)
    second = [held(up, (2, 0)), held(down, (-2, 0))]
    gradient, parts, opposite, packed = add_pieces(
        first, [0, 1, 2, 3], loop_size, table, users, labels, None, False
    )
    third = [held(across(opposite, loop_size), (4, 0))]
    first = other(packed, near[:4])
    third.append(held(to_pair(pick(up, down, loop_size), loop_size), (0, -3)))
    gradient, packed = add_pieces(second, [0, 1], loop_size, table, parts, labels, gradient, False)
    second = other(packed, near[4:6])
    arrived, gradient = lax.optimization_barrier(([array for array, _ in third], gradient))
    final = other(pack(arrived), [(4, 0), (0, -3)])
    (gradient,) = add_pieces(
        third + [first, second], [], loop_size, table, parts, labels, gradient, False
    )
    return *add_pieces([final], [], loop_size, table, parts, labels, gradient, True), users


def chunks_kernel(
    list_ref, count_ref, users_ref, labels_ref, items_ref, grad_ref, square_ref, tiles, parts_ref, sems
):
    tile = tiles.shape[0] // CHUNK
    step = pl.program_id(0)
    live = jnp.clip(count_ref[0] - step * CHUNK, 0, CHUNK)

    @pl.when(step == 0)
    def _():
        parts_ref[...] = halves(0.5 * users_ref[...])
        grad_ref[...] = jnp.zeros_like(grad_ref)

    def move(slot):
        start = pl.multiple_of(list_ref[0, step * CHUNK + slot] * tile, tile)
        return pltpu.make_async_copy(
            items_ref.at[pl.ds(start, tile), :], tiles.at[pl.ds(slot * tile, tile), :], sems.at[slot]
        )

    for slot in range(CHUNK):
        pl.when(slot < live)(lambda slot=slot: move(slot).start())
    for slot in range(CHUNK):
        pl.when(slot < live)(lambda slot=slot: move(slot).wait())

    def labels_at(position):
        return labels_ref[:, pl.ds(pl.multiple_of(position * tile, tile), tile)]

    add_tiles(grad_ref, parts_ref, tiles, live, labels_at)

    @pl.when(step == pl.num_programs(0) - 1)
    def _():
        store_square(grad_ref, square_ref)


def add_chunks(loop_size, items, lists, users, labels):
    rows, width = users.shape
    slots = lists[0].shape[1]
    tile = labels.shape[1] // slots
    return pl.pallas_call(
        chunks_kernel,
        grid=(slots // CHUNK,),
        out_shape=[
            jax.ShapeDtypeStruct((rows, width), jnp.float32),
            jax.ShapeDtypeStruct((loop_size, 128), jnp.float32),
        ],
        in_specs=[
            pl.BlockSpec(memory_space=pltpu.SMEM),
            pl.BlockSpec(memory_space=pltpu.SMEM),
            pl.BlockSpec((rows, width), lambda step: (0, 0)),
            pl.BlockSpec((rows, CHUNK * tile), lambda step: (0, step)),
            pl.BlockSpec(memory_space=pl.ANY),
        ],
        out_specs=[
            pl.BlockSpec((rows, width), lambda step: (0, 0)),
            pl.BlockSpec((loop_size, 128), lambda step: (0, 0)),
        ],
        scratch_shapes=[
            pltpu.VMEM((CHUNK * tile, width), jnp.bfloat16),
            pltpu.VMEM((2 * rows, width), jnp.bfloat16),
            pltpu.SemaphoreType.DMA((CHUNK,)),
        ],
        compiler_params=pltpu.CompilerParams(vmem_limit_bytes=32 * 1024 * 1024),
        cost_estimate=pl.CostEstimate(
            flops=8 * rows * width * slots * tile,
            bytes_accessed=4 * rows * (slots * tile + 2 * width) + 2 * slots * tile * width,
            transcendentals=rows * slots * tile,
        ),
        name="add_chunks",
    )(*lists, users, labels, items)


def update_kernel(entries, users_ref, grad_ref, squares_ref, out_ref, result, sems):
    total = jnp.sum(squares_ref[...], axis=0, keepdims=True)
    total = jnp.sum(total, axis=1, keepdims=True)
    scale = 0.5 / jnp.sqrt(total / entries + 1e-06)
    rows = users_ref.shape[0] // sems.shape[0]
    copies = []
    for at in range(sems.shape[0]):
        part = pl.ds(at * rows, rows)
        result[part, :] = users_ref[part, :] - scale * grad_ref[part, :]
        copies.append(pltpu.make_async_copy(result.at[part, :], out_ref.at[part, :], sems.at[at]))
        copies[-1].start()
    for copy in copies:
        copy.wait()


def local(users, items, tile_blocks, tile_count, labels):
    loop_size = lax.axis_size("loop")
    rows, width = users.shape
    slots = tile_blocks.shape[1]
    lists = (tile_blocks, tile_count)
    if loop_size == RING and slots == CHUNK:
        gradient, square, users = ring_gradient(users, items, lists, labels)
    else:
        whole = lax.all_gather(items, "loop", axis=0, tiled=True)
        gradient, square = add_chunks(loop_size, whole, lists, users, labels)

    squares = lax.all_to_all(square, "loop", 0, 0, tiled=True)
    return pl.pallas_call(
        functools.partial(update_kernel, rows * loop_size * width),
        out_shape=jax.ShapeDtypeStruct((rows, width), jnp.float32),
        in_specs=[pl.BlockSpec(memory_space=pltpu.VMEM)] * 3,
        out_specs=pl.BlockSpec(memory_space=pl.ANY),
        scratch_shapes=[pltpu.VMEM((rows, width), jnp.float32), pltpu.SemaphoreType.DMA((4,))],
        compiler_params=pltpu.CompilerParams(vmem_limit_bytes=16 * 1024 * 1024),
        cost_estimate=pl.CostEstimate(
            flops=2 * rows * width, bytes_accessed=12 * rows * width, transcendentals=0
        ),
        name="update",
    )(users, gradient, squares)


def solution(mesh):
    in_specs = (
        P(("group", "loop"), None),
        P(("group", "loop"), None),
        P(("group", "loop"), None),
        P(("group", "loop")),
        P(("group", "loop"), None),
    )
    out_specs = P(("group", "loop"), None)
    return jax.shard_map(local, mesh=mesh, in_specs=in_specs, out_specs=out_specs, check_vma=False)
```

```python
import functools

import jax
import jax.numpy as jnp
from jax import lax
from jax.experimental import pallas as pl
from jax.experimental.pallas import tpu as pltpu
from jax.sharding import PartitionSpec as P

CHUNK = 8
RING = 16


def ring_place(loop_size):
    outer = loop_size // 4

    def device(position, core):
        position = position % (2 * outer)
        chip = 2 * position if position < outer else 2 * (2 * outer - 1 - position) + 1
        return 2 * chip + core

    return 2 * outer, device


def to_next(array, direction, loop_size):
    chips, device = ring_place(loop_size)
    pairs = [(device(at, 0), device(at + direction, 0)) for at in range(chips)]
    pairs += [(device(at, 1), device(at - direction, 1)) for at in range(chips)]
    return lax.ppermute(array, "loop", pairs)


def across(array, loop_size):
    chips, device = ring_place(loop_size)
    pairs = [
        (device(at, core), device(at + (3 if at % 2 == 0 else -3), core))
        for at in range(chips)
        for core in range(2)
    ]
    return lax.ppermute(array, "loop", pairs)


def to_pair(array, loop_size):
    chips, device = ring_place(loop_size)
    pairs = [
        (device(at, core), device(at + (1 if at % 2 else -1), core))
        for at in range(chips)
        for core in range(2)
    ]
    return lax.ppermute(array, "loop", pairs)


def to_other_core(array, loop_size):
    return lax.ppermute(array, "loop", [(at, at ^ 1) for at in range(loop_size)])


def halves(values):
    upper = values.astype(jnp.bfloat16)
    return jnp.concatenate([upper, (values - upper.astype(jnp.float32)).astype(jnp.bfloat16)], 0)


def table_kernel(loop_size, origins, list_ref, count_ref, table_ref):
    chips = loop_size // 2
    lane = lax.broadcasted_iota(jnp.int32, table_ref.shape, 1)
    core, position = core_and_position(loop_size)
    hops, skips, other = jnp.zeros_like(lane), jnp.zeros_like(lane), jnp.zeros_like(lane)
    for at, origin in enumerate(origins):
        hops = jnp.where(lane == at, origin[0], hops)
        skips = jnp.where(lane == at, origin[1], skips)
        other = jnp.where(lane == at, origin[2], other)
    hops = jnp.where(core == 0, -hops, hops) + jnp.where(position % 2 == 0, skips, -skips)
    at = (position + chips + hops) & (chips - 1)
    chip = jnp.where(at < chips // 2, 2 * at, 2 * (chips - 1 - at) + 1)
    block = 2 * chip + jnp.where(other == 1, 1 - core, core)
    found = jnp.full_like(lane, -1)
    for slot in range(list_ref.shape[1]):
        name = jnp.where(slot < count_ref[...], list_ref[:, slot : slot + 1], -1)
        found = jnp.where(name == block, slot, found)
    table_ref[...] = jnp.where(lane < len(origins), found, -1)


def slot_table(loop_size, origins, block_list, live_count):
    return pl.pallas_call(
        functools.partial(table_kernel, loop_size, origins),
        out_shape=jax.ShapeDtypeStruct((1, 128), jnp.int32),
        in_specs=[pl.BlockSpec(memory_space=pltpu.VMEM)] * 2,
        out_specs=pl.BlockSpec(memory_space=pltpu.VMEM),
        compiler_params=pltpu.CompilerParams(vmem_limit_bytes=16 * 1024 * 1024),
        cost_estimate=pl.CostEstimate(flops=2**32, bytes_accessed=1024, transcendentals=0),
        name="slot_table",
    )(block_list, live_count.reshape(1, 1))


def add_block(grad_ref, parts_ref, block, labels):
    rows = grad_ref.shape[0]
    tile = labels[0].shape[1]
    upper, lower = [], []
    for at in range(0, len(labels), 2):
        some = jnp.concatenate(labels[at : at + 2], 1)
        both = lax.dot_general(
            parts_ref[...],
            block[at * tile : at * tile + some.shape[1]],
            (((1,), (1,)), ((), ())),
            preferred_element_type=jnp.float32,
        )
        residual = 0.5 * jnp.tanh(both[:rows] + both[rows:]) + (0.5 - some.astype(jnp.float32))
        upper.append(residual.astype(jnp.bfloat16))
        lower.append((residual - upper[-1].astype(jnp.float32)).astype(jnp.bfloat16))
    grad_ref[...] += jnp.dot(
        jnp.concatenate(upper + lower, 1),
        jnp.concatenate([block, block], 0),
        preferred_element_type=jnp.float32,
    )


def add_tiles(grad_ref, parts_ref, tiles, live, labels_at):
    tile = tiles.shape[0] // CHUNK
    fours = (live + 1) // 4

    @pl.when(live % 4 == 3)
    def _():
        blank = pl.multiple_of(live * tile, tile)
        tiles[pl.ds(blank, tile), :] = jnp.zeros((tile, tiles.shape[1]), tiles.dtype)

    def add(count, index, carry):
        start = index * count
        block = tiles[pl.ds(pl.multiple_of(start * tile, tile), count * tile), :]
        add_block(grad_ref, parts_ref, block, [labels_at(start + at) for at in range(count)])
        return carry

    lax.fori_loop(0, fours, functools.partial(add, 4), 0)
    pl.when(live - 4 * fours == 2)(lambda: add(2, 2 * fours, None))
    pl.when(live - 4 * fours == 1)(lambda: add(1, 4 * fours, None))


def store_square(grad_ref, square_ref):
    gradient = grad_ref[...]
    square = jnp.sum(gradient * gradient, axis=0, keepdims=True)
    square = sum(square[:, at : at + 128] for at in range(0, square.shape[1], 128))
    square_ref[...] = jnp.broadcast_to(square, square_ref.shape)


def core_and_position(loop_size):
    me = lax.axis_index("loop")
    core, row, outer = me % 2, me // 2 % 2, me // 4
    return core, jnp.where(row == 0, outer, loop_size // 2 - 1 - outer)


def pick_kernel(loop_size, upper_ref, lower_ref, picked_ref):
    core, position = core_and_position(loop_size)
    for at, ref in enumerate((lower_ref, upper_ref)):

        @pl.when((core + position) % 2 == at)
        def _():
            picked_ref[...] = ref[...]


def pick(upper, lower, loop_size):
    return pl.pallas_call(
        functools.partial(pick_kernel, loop_size),
        out_shape=jax.ShapeDtypeStruct(upper.shape, upper.dtype),
        in_specs=[pl.BlockSpec(memory_space=pltpu.VMEM)] * 2,
        out_specs=pl.BlockSpec(memory_space=pltpu.VMEM),
        compiler_params=pltpu.CompilerParams(vmem_limit_bytes=16 * 1024 * 1024),
        cost_estimate=pl.CostEstimate(
            flops=0, bytes_accessed=4 * upper.size, transcendentals=0
        ),
        name="pick",
    )(upper, lower)


def pack_kernel(*refs):
    tile = refs[0].shape[0]
    for at, ref in enumerate(refs[:-1]):
        refs[-1][at * tile : (at + 1) * tile, :] = ref[...]


def pack(arrays):
    tile, width = arrays[0].shape
    return pl.pallas_call(
        pack_kernel,
        out_shape=jax.ShapeDtypeStruct((len(arrays) * tile, width), arrays[0].dtype),
        in_specs=[pl.BlockSpec(memory_space=pltpu.VMEM)] * len(arrays),
        out_specs=pl.BlockSpec(memory_space=pltpu.VMEM),
        compiler_params=pltpu.CompilerParams(vmem_limit_bytes=16 * 1024 * 1024),
        cost_estimate=pl.CostEstimate(
            flops=2**34, bytes_accessed=4 * len(arrays) * tile * width, transcendentals=0
        ),
        name="pack",
    )(*arrays)


def pieces_kernel(places, count, packed, loop_size, first, last, table_ref, given_ref, labels_ref, *rest):
    rest = list(rest)
    arrays = [rest.pop(0) for _ in range(count)]
    if not first:
        rest.pop(0)
    grad_ref = rest.pop(0)
    parts_ref = rest.pop(0) if first else given_ref
    across_ref = rest.pop(0) if first else None
    pack_ref = rest.pop(0) if packed else None
    square_ref = rest.pop(0) if last else None
    tiles, slots = rest
    tile = tiles.shape[0] // CHUNK
    for at, index in enumerate(packed):
        pack_ref[at * tile : (at + 1) * tile, :] = arrays[index][...]
    if first:
        core, position = core_and_position(loop_size)
        for at in range(2):

            @pl.when((core + position) % 2 == at)
            def _():
                across_ref[...] = arrays[1 + at][...]

        parts_ref[...] = halves(0.5 * given_ref[...])
        grad_ref[...] = jnp.zeros_like(grad_ref)
    table = table_ref[...]
    entries = [table[0, at] for at, _, _ in places]

    def labels_of(slot):
        return labels_ref[:, pl.ds(pl.multiple_of(slot * tile, tile), tile)]

    live = jnp.int32(0)
    for found, (_, index, row) in zip(entries, places):

        @pl.when(found >= 0)
        def _():
            into = pl.ds(pl.multiple_of(live * tile, tile), tile)
            tiles[into, :] = arrays[index][row * tile : (row + 1) * tile, :]
            slots[live] = found

        live = live + (found >= 0).astype(jnp.int32)
    slots[live] = 0
    add_tiles(grad_ref, parts_ref, tiles, live, lambda position: labels_of(slots[position]))
    if last:
        store_square(grad_ref, square_ref)


def add_pieces(held, packed, loop_size, table, given, labels, before, last):
    first = before is None
    width = given.shape[1]
    rows = given.shape[0] // (1 if first else 2)
    arrays = [array for array, _ in held]
    tile = labels.shape[1] // CHUNK
    places = [(at, index, row) for index, (_, entries) in enumerate(held) for row, at in enumerate(entries)]
    most = min(len(places), CHUNK)
    out_shape = [jax.ShapeDtypeStruct((rows, width), jnp.float32)]
    if first:
        out_shape.append(jax.ShapeDtypeStruct((2 * rows, width), jnp.bfloat16))
        out_shape.append(jax.ShapeDtypeStruct((tile, width), jnp.bfloat16))
    if packed:
        out_shape.append(jax.ShapeDtypeStruct((len(packed) * tile, width), jnp.bfloat16))
    if last:
        out_shape.append(jax.ShapeDtypeStruct((loop_size, 128), jnp.float32))
    extra = [] if first else [before]
    return pl.pallas_call(
        functools.partial(pieces_kernel, places, len(arrays), packed, loop_size, first, last),
        out_shape=out_shape,
        in_specs=[pl.BlockSpec(memory_space=pltpu.VMEM)] * (3 + len(arrays) + len(extra)),
        out_specs=[pl.BlockSpec(memory_space=pltpu.VMEM)] * len(out_shape),
        input_output_aliases={} if first else {3 + len(arrays): 0},
        scratch_shapes=[
            pltpu.VMEM((CHUNK * tile, width), jnp.bfloat16),
            pltpu.SMEM((CHUNK + 1,), jnp.int32),
        ],
        compiler_params=pltpu.CompilerParams(vmem_limit_bytes=24 * 1024 * 1024),
        cost_estimate=pl.CostEstimate(
            flops=128 * rows * width * most * tile,
            bytes_accessed=8 * rows * width,
            transcendentals=rows * most * tile,
        ),
        name="add_pieces",
    )(table, given, labels, *arrays, *extra)


def ring_gradient(users, items, lists, labels):
    loop_size = lax.axis_size("loop")
    near = [(0, 0), (1, 0), (-1, 0), (0, 3), (2, 0), (-2, 0), (0, -3), (4, 0)]
    origins = [(hops, skips, 0) for hops, skips in near] + [(-hops, skips, 1) for hops, skips in near]
    table = slot_table(loop_size, origins, *lists)

    def held(array, origin):
        return array, [near.index(origin)]

    def other(array, some):
        return to_other_core(array, loop_size), [len(near) + near.index(origin) for origin in some]

    up = to_next(items, 1, loop_size)
    down = to_next(items, -1, loop_size)
    up, table = lax.optimization_barrier((up, table))
    first = [held(items, (0, 0)), held(up, (1, 0)), held(down, (-1, 0))]
    skipped = held(across(items, loop_size), (0, 3))
    up, down = to_next(up, 1, loop_size), to_next(down, -1, loop_size)
    second = [held(up, (2, 0)), held(down, (-2, 0)), skipped]
    gradient, parts, opposite, packed = add_pieces(
        first, [0, 1, 2], loop_size, table, users, labels, None, False
    )
    third = [held(across(opposite, loop_size), (4, 0))]
    first = other(packed, near[:3])
    third.append(held(to_pair(pick(up, down, loop_size), loop_size), (0, -3)))
    gradient, packed = add_pieces(second, [0, 1, 2], loop_size, table, parts, labels, gradient, False)
    second = other(packed, [(2, 0), (-2, 0), (0, 3)])
    arrived, gradient = lax.optimization_barrier(([array for array, _ in third], gradient))
    final = other(pack(arrived), [(4, 0), (0, -3)])
    (gradient,) = add_pieces(
        third + [first, second], [], loop_size, table, parts, labels, gradient, False
    )
    return *add_pieces([final], [], loop_size, table, parts, labels, gradient, True), users


def chunks_kernel(
    list_ref, count_ref, users_ref, labels_ref, items_ref, grad_ref, square_ref, tiles, parts_ref, sems
):
    tile = tiles.shape[0] // CHUNK
    step = pl.program_id(0)
    live = jnp.clip(count_ref[0] - step * CHUNK, 0, CHUNK)

    @pl.when(step == 0)
    def _():
        parts_ref[...] = halves(0.5 * users_ref[...])
        grad_ref[...] = jnp.zeros_like(grad_ref)

    def move(slot):
        start = pl.multiple_of(list_ref[0, step * CHUNK + slot] * tile, tile)
        return pltpu.make_async_copy(
            items_ref.at[pl.ds(start, tile), :], tiles.at[pl.ds(slot * tile, tile), :], sems.at[slot]
        )

    for slot in range(CHUNK):
        pl.when(slot < live)(lambda slot=slot: move(slot).start())
    for slot in range(CHUNK):
        pl.when(slot < live)(lambda slot=slot: move(slot).wait())

    def labels_at(position):
        return labels_ref[:, pl.ds(pl.multiple_of(position * tile, tile), tile)]

    add_tiles(grad_ref, parts_ref, tiles, live, labels_at)

    @pl.when(step == pl.num_programs(0) - 1)
    def _():
        store_square(grad_ref, square_ref)


def add_chunks(loop_size, items, lists, users, labels):
    rows, width = users.shape
    slots = lists[0].shape[1]
    tile = labels.shape[1] // slots
    return pl.pallas_call(
        chunks_kernel,
        grid=(slots // CHUNK,),
        out_shape=[
            jax.ShapeDtypeStruct((rows, width), jnp.float32),
            jax.ShapeDtypeStruct((loop_size, 128), jnp.float32),
        ],
        in_specs=[
            pl.BlockSpec(memory_space=pltpu.SMEM),
            pl.BlockSpec(memory_space=pltpu.SMEM),
            pl.BlockSpec((rows, width), lambda step: (0, 0)),
            pl.BlockSpec((rows, CHUNK * tile), lambda step: (0, step)),
            pl.BlockSpec(memory_space=pl.ANY),
        ],
        out_specs=[
            pl.BlockSpec((rows, width), lambda step: (0, 0)),
            pl.BlockSpec((loop_size, 128), lambda step: (0, 0)),
        ],
        scratch_shapes=[
            pltpu.VMEM((CHUNK * tile, width), jnp.bfloat16),
            pltpu.VMEM((2 * rows, width), jnp.bfloat16),
            pltpu.SemaphoreType.DMA((CHUNK,)),
        ],
        compiler_params=pltpu.CompilerParams(vmem_limit_bytes=32 * 1024 * 1024),
        cost_estimate=pl.CostEstimate(
            flops=8 * rows * width * slots * tile,
            bytes_accessed=4 * rows * (slots * tile + 2 * width) + 2 * slots * tile * width,
            transcendentals=rows * slots * tile,
        ),
        name="add_chunks",
    )(*lists, users, labels, items)


def update_kernel(entries, users_ref, grad_ref, squares_ref, out_ref, result, sems):
    total = jnp.sum(squares_ref[...], axis=0, keepdims=True)
    total = jnp.sum(total, axis=1, keepdims=True)
    scale = 0.5 / jnp.sqrt(total / entries + 1e-06)
    rows = users_ref.shape[0] // sems.shape[0]
    copies = []
    for at in range(sems.shape[0]):
        part = pl.ds(at * rows, rows)
        result[part, :] = users_ref[part, :] - scale * grad_ref[part, :]
        copies.append(pltpu.make_async_copy(result.at[part, :], out_ref.at[part, :], sems.at[at]))
        copies[-1].start()
    for copy in copies:
        copy.wait()


def local(users, items, tile_blocks, tile_count, labels):
    loop_size = lax.axis_size("loop")
    rows, width = users.shape
    slots = tile_blocks.shape[1]
    lists = (tile_blocks, tile_count)
    if loop_size == RING and slots == CHUNK:
        gradient, square, users = ring_gradient(users, items, lists, labels)
    else:
        whole = lax.all_gather(items, "loop", axis=0, tiled=True)
        gradient, square = add_chunks(loop_size, whole, lists, users, labels)

    squares = lax.all_to_all(square, "loop", 0, 0, tiled=True)
    return pl.pallas_call(
        functools.partial(update_kernel, rows * loop_size * width),
        out_shape=jax.ShapeDtypeStruct((rows, width), jnp.float32),
        in_specs=[pl.BlockSpec(memory_space=pltpu.VMEM)] * 3,
        out_specs=pl.BlockSpec(memory_space=pl.ANY),
        scratch_shapes=[pltpu.VMEM((rows, width), jnp.float32), pltpu.SemaphoreType.DMA((4,))],
        compiler_params=pltpu.CompilerParams(vmem_limit_bytes=16 * 1024 * 1024),
        cost_estimate=pl.CostEstimate(
            flops=2 * rows * width, bytes_accessed=12 * rows * width, transcendentals=0
        ),
        name="update",
    )(users, gradient, squares)


def solution(mesh):
    in_specs = (
        P(("group", "loop"), None),
        P(("group", "loop"), None),
        P(("group", "loop"), None),
        P(("group", "loop")),
        P(("group", "loop"), None),
    )
    out_specs = P(("group", "loop"), None)
    return jax.shard_map(local, mesh=mesh, in_specs=in_specs, out_specs=out_specs, check_vma=False)
```

```python
import functools

import jax
import jax.numpy as jnp
from jax import lax
from jax.experimental import pallas as pl
from jax.experimental.pallas import tpu as pltpu
from jax.sharding import PartitionSpec as P

CHUNK = 8
RING = 16


def ring_place(loop_size):
    outer = loop_size // 4

    def device(position, core):
        position = position % (2 * outer)
        chip = 2 * position if position < outer else 2 * (2 * outer - 1 - position) + 1
        return 2 * chip + core

    return 2 * outer, device


def to_next(array, direction, loop_size):
    chips, device = ring_place(loop_size)
    pairs = [(device(at, 0), device(at + direction, 0)) for at in range(chips)]
    pairs += [(device(at, 1), device(at - direction, 1)) for at in range(chips)]
    return lax.ppermute(array, "loop", pairs)


def across(array, loop_size):
    chips, device = ring_place(loop_size)
    pairs = [
        (device(at, core), device(at + (3 if at % 2 == 0 else -3), core))
        for at in range(chips)
        for core in range(2)
    ]
    return lax.ppermute(array, "loop", pairs)


def to_other_row(array, loop_size):
    return lax.ppermute(array, "loop", [(at, at ^ 2) for at in range(loop_size)])


def to_other_core(array, loop_size):
    return lax.ppermute(array, "loop", [(at, at ^ 1) for at in range(loop_size)])


def halves(values):
    upper = values.astype(jnp.bfloat16)
    return jnp.concatenate([upper, (values - upper.astype(jnp.float32)).astype(jnp.bfloat16)], 0)


def table_kernel(loop_size, origins, list_ref, count_ref, table_ref):
    chips = loop_size // 2
    lane = lax.broadcasted_iota(jnp.int32, table_ref.shape, 1)
    core, position = core_and_position(loop_size)
    hops, skips, other = jnp.zeros_like(lane), jnp.zeros_like(lane), jnp.zeros_like(lane)
    for at, origin in enumerate(origins):
        hops = jnp.where(lane == at, origin[0], hops)
        skips = jnp.where(lane == at, origin[1], skips)
        other = jnp.where(lane == at, origin[2], other)
    hops = jnp.where(core == 0, -hops, hops) + jnp.where(position % 2 == 0, skips, -skips)
    at = (position + chips + hops) & (chips - 1)
    chip = jnp.where(at < chips // 2, 2 * at, 2 * (chips - 1 - at) + 1)
    block = 2 * chip + jnp.where(other == 1, 1 - core, core)
    found = jnp.full_like(lane, -1)
    for slot in range(list_ref.shape[1]):
        name = jnp.where(slot < count_ref[...], list_ref[:, slot : slot + 1], -1)
        found = jnp.where(name == block, slot, found)
    table_ref[...] = jnp.where(lane < len(origins), found, -1)


def slot_table(loop_size, origins, block_list, live_count):
    return pl.pallas_call(
        functools.partial(table_kernel, loop_size, origins),
        out_shape=jax.ShapeDtypeStruct((1, 128), jnp.int32),
        in_specs=[pl.BlockSpec(memory_space=pltpu.VMEM)] * 2,
        out_specs=pl.BlockSpec(memory_space=pltpu.VMEM),
        compiler_params=pltpu.CompilerParams(vmem_limit_bytes=16 * 1024 * 1024),
        cost_estimate=pl.CostEstimate(flops=2**32, bytes_accessed=1024, transcendentals=0),
        name="slot_table",
    )(block_list, live_count.reshape(1, 1))


def add_block(grad_ref, parts_ref, block, labels):
    rows = grad_ref.shape[0]
    tile = labels[0].shape[1]
    upper, lower = [], []
    for at in range(0, len(labels), 2):
        some = jnp.concatenate(labels[at : at + 2], 1)
        both = lax.dot_general(
            parts_ref[...],
            block[at * tile : at * tile + some.shape[1]],
            (((1,), (1,)), ((), ())),
            preferred_element_type=jnp.float32,
        )
        residual = 0.5 * jnp.tanh(both[:rows] + both[rows:]) + (0.5 - some.astype(jnp.float32))
        upper.append(residual.astype(jnp.bfloat16))
        lower.append((residual - upper[-1].astype(jnp.float32)).astype(jnp.bfloat16))
    grad_ref[...] += jnp.dot(
        jnp.concatenate(upper + lower, 1),
        jnp.concatenate([block, block], 0),
        preferred_element_type=jnp.float32,
    )


def add_tiles(grad_ref, parts_ref, tiles, live, labels_at):
    tile = tiles.shape[0] // CHUNK
    fours = (live + 1) // 4

    @pl.when(live % 4 == 3)
    def _():
        blank = pl.multiple_of(live * tile, tile)
        tiles[pl.ds(blank, tile), :] = jnp.zeros((tile, tiles.shape[1]), tiles.dtype)

    def add(count, index, carry):
        start = index * count
        block = tiles[pl.ds(pl.multiple_of(start * tile, tile), count * tile), :]
        add_block(grad_ref, parts_ref, block, [labels_at(start + at) for at in range(count)])
        return carry

    lax.fori_loop(0, fours, functools.partial(add, 4), 0)
    pl.when(live - 4 * fours == 2)(lambda: add(2, 2 * fours, None))
    pl.when(live - 4 * fours == 1)(lambda: add(1, 4 * fours, None))


def store_square(grad_ref, square_ref):
    gradient = grad_ref[...]
    square = jnp.sum(gradient * gradient, axis=0, keepdims=True)
    square = sum(square[:, at : at + 128] for at in range(0, square.shape[1], 128))
    square_ref[...] = jnp.broadcast_to(square, square_ref.shape)


def core_and_position(loop_size):
    me = lax.axis_index("loop")
    core, row, outer = me % 2, me // 2 % 2, me // 4
    return core, jnp.where(row == 0, outer, loop_size // 2 - 1 - outer)


def pick_kernel(loop_size, upper_ref, lower_ref, picked_ref):
    core, position = core_and_position(loop_size)
    middle = (position + 1) // 2
    for at, ref in enumerate((lower_ref, upper_ref)):

        @pl.when((core + position + middle) % 2 == at)
        def _():
            picked_ref[...] = ref[...]


def pick(upper, lower, loop_size):
    return pl.pallas_call(
        functools.partial(pick_kernel, loop_size),
        out_shape=jax.ShapeDtypeStruct(upper.shape, upper.dtype),
        in_specs=[pl.BlockSpec(memory_space=pltpu.VMEM)] * 2,
        out_specs=pl.BlockSpec(memory_space=pltpu.VMEM),
        compiler_params=pltpu.CompilerParams(vmem_limit_bytes=16 * 1024 * 1024),
        cost_estimate=pl.CostEstimate(
            flops=0, bytes_accessed=4 * upper.size, transcendentals=0
        ),
        name="pick",
    )(upper, lower)


def pack_kernel(*refs):
    tile = refs[0].shape[0]
    for at, ref in enumerate(refs[:-1]):
        refs[-1][at * tile : (at + 1) * tile, :] = ref[...]


def pack(arrays):
    tile, width = arrays[0].shape
    return pl.pallas_call(
        pack_kernel,
        out_shape=jax.ShapeDtypeStruct((len(arrays) * tile, width), arrays[0].dtype),
        in_specs=[pl.BlockSpec(memory_space=pltpu.VMEM)] * len(arrays),
        out_specs=pl.BlockSpec(memory_space=pltpu.VMEM),
        compiler_params=pltpu.CompilerParams(vmem_limit_bytes=16 * 1024 * 1024),
        cost_estimate=pl.CostEstimate(
            flops=2**34, bytes_accessed=4 * len(arrays) * tile * width, transcendentals=0
        ),
        name="pack",
    )(*arrays)


def pieces_kernel(places, count, packed, loop_size, first, last, table_ref, given_ref, labels_ref, *rest):
    rest = list(rest)
    arrays = [rest.pop(0) for _ in range(count)]
    if not first:
        rest.pop(0)
    grad_ref = rest.pop(0)
    parts_ref = rest.pop(0) if first else given_ref
    across_ref = rest.pop(0) if first else None
    pack_ref = rest.pop(0) if packed else None
    square_ref = rest.pop(0) if last else None
    tiles, slots = rest
    tile = tiles.shape[0] // CHUNK
    for at, index in enumerate(packed):
        pack_ref[at * tile : (at + 1) * tile, :] = arrays[index][...]
    if first:
        core, position = core_and_position(loop_size)
        for at in range(2):

            @pl.when((core + position) % 2 == at)
            def _():
                across_ref[...] = arrays[1 + at][...]

        parts_ref[...] = halves(0.5 * given_ref[...])
        grad_ref[...] = jnp.zeros_like(grad_ref)
    table = table_ref[...]
    entries = [table[0, at] for at, _, _ in places]

    def labels_of(slot):
        return labels_ref[:, pl.ds(pl.multiple_of(slot * tile, tile), tile)]

    live = jnp.int32(0)
    for found, (_, index, row) in zip(entries, places):

        @pl.when(found >= 0)
        def _():
            into = pl.ds(pl.multiple_of(live * tile, tile), tile)
            tiles[into, :] = arrays[index][row * tile : (row + 1) * tile, :]
            slots[live] = found

        live = live + (found >= 0).astype(jnp.int32)
    slots[live] = 0
    add_tiles(grad_ref, parts_ref, tiles, live, lambda position: labels_of(slots[position]))
    if last:
        store_square(grad_ref, square_ref)


def add_pieces(held, packed, loop_size, table, given, labels, before, last):
    first = before is None
    width = given.shape[1]
    rows = given.shape[0] // (1 if first else 2)
    arrays = [array for array, _ in held]
    tile = labels.shape[1] // CHUNK
    places = [(at, index, row) for index, (_, entries) in enumerate(held) for row, at in enumerate(entries)]
    most = min(len(places), CHUNK)
    out_shape = [jax.ShapeDtypeStruct((rows, width), jnp.float32)]
    if first:
        out_shape.append(jax.ShapeDtypeStruct((2 * rows, width), jnp.bfloat16))
        out_shape.append(jax.ShapeDtypeStruct((tile, width), jnp.bfloat16))
    if packed:
        out_shape.append(jax.ShapeDtypeStruct((len(packed) * tile, width), jnp.bfloat16))
    if last:
        out_shape.append(jax.ShapeDtypeStruct((loop_size, 128), jnp.float32))
    extra = [] if first else [before]
    return pl.pallas_call(
        functools.partial(pieces_kernel, places, len(arrays), packed, loop_size, first, last),
        out_shape=out_shape,
        in_specs=[pl.BlockSpec(memory_space=pltpu.VMEM)] * (3 + len(arrays) + len(extra)),
        out_specs=[pl.BlockSpec(memory_space=pltpu.VMEM)] * len(out_shape),
        input_output_aliases={} if first else {3 + len(arrays): 0},
        scratch_shapes=[
            pltpu.VMEM((CHUNK * tile, width), jnp.bfloat16),
            pltpu.SMEM((CHUNK + 1,), jnp.int32),
        ],
        compiler_params=pltpu.CompilerParams(vmem_limit_bytes=24 * 1024 * 1024),
        cost_estimate=pl.CostEstimate(
            flops=128 * rows * width * most * tile,
            bytes_accessed=8 * rows * width,
            transcendentals=rows * most * tile,
        ),
        name="add_pieces",
    )(table, given, labels, *arrays, *extra)


def ring_gradient(users, items, lists, labels):
    loop_size = lax.axis_size("loop")
    near = [(0, 0), (1, 0), (-1, 0), (0, 3), (2, 0), (-2, 0), (0, -3), (4, 0)]
    origins = [(hops, skips, 0) for hops, skips in near] + [(-hops, skips, 1) for hops, skips in near]
    table = slot_table(loop_size, origins, *lists)

    def held(array, origin):
        return array, [near.index(origin)]

    def other(array, some):
        return to_other_core(array, loop_size), [len(near) + near.index(origin) for origin in some]

    up = to_next(items, 1, loop_size)
    down = to_next(items, -1, loop_size)
    up, table = lax.optimization_barrier((up, table))
    first = [held(items, (0, 0)), held(up, (1, 0)), held(down, (-1, 0))]
    skipped = held(across(items, loop_size), (0, 3))
    up, down = to_next(up, 1, loop_size), to_next(down, -1, loop_size)
    second = [held(up, (2, 0)), held(down, (-2, 0)), skipped]
    gradient, parts, opposite, packed = add_pieces(
        first, [0, 1, 2], loop_size, table, users, labels, None, False
    )
    third = [held(across(opposite, loop_size), (4, 0))]
    first = other(packed, near[:3])
    third.append(held(to_other_row(pick(up, down, loop_size), loop_size), (0, -3)))
    gradient, packed = add_pieces(second, [0, 1, 2], loop_size, table, parts, labels, gradient, False)
    second = other(packed, [(2, 0), (-2, 0), (0, 3)])
    arrived, gradient = lax.optimization_barrier(([array for array, _ in third], gradient))
    final = other(pack(arrived), [(4, 0), (0, -3)])
    (gradient,) = add_pieces(
        third + [first, second], [], loop_size, table, parts, labels, gradient, False
    )
    return *add_pieces([final], [], loop_size, table, parts, labels, gradient, True), users


def chunks_kernel(
    list_ref, count_ref, users_ref, labels_ref, items_ref, grad_ref, square_ref, tiles, parts_ref, sems
):
    tile = tiles.shape[0] // CHUNK
    step = pl.program_id(0)
    live = jnp.clip(count_ref[0] - step * CHUNK, 0, CHUNK)

    @pl.when(step == 0)
    def _():
        parts_ref[...] = halves(0.5 * users_ref[...])
        grad_ref[...] = jnp.zeros_like(grad_ref)

    def move(slot):
        start = pl.multiple_of(list_ref[0, step * CHUNK + slot] * tile, tile)
        return pltpu.make_async_copy(
            items_ref.at[pl.ds(start, tile), :], tiles.at[pl.ds(slot * tile, tile), :], sems.at[slot]
        )

    for slot in range(CHUNK):
        pl.when(slot < live)(lambda slot=slot: move(slot).start())
    for slot in range(CHUNK):
        pl.when(slot < live)(lambda slot=slot: move(slot).wait())

    def labels_at(position):
        return labels_ref[:, pl.ds(pl.multiple_of(position * tile, tile), tile)]

    add_tiles(grad_ref, parts_ref, tiles, live, labels_at)

    @pl.when(step == pl.num_programs(0) - 1)
    def _():
        store_square(grad_ref, square_ref)


def add_chunks(loop_size, items, lists, users, labels):
    rows, width = users.shape
    slots = lists[0].shape[1]
    tile = labels.shape[1] // slots
    return pl.pallas_call(
        chunks_kernel,
        grid=(slots // CHUNK,),
        out_shape=[
            jax.ShapeDtypeStruct((rows, width), jnp.float32),
            jax.ShapeDtypeStruct((loop_size, 128), jnp.float32),
        ],
        in_specs=[
            pl.BlockSpec(memory_space=pltpu.SMEM),
            pl.BlockSpec(memory_space=pltpu.SMEM),
            pl.BlockSpec((rows, width), lambda step: (0, 0)),
            pl.BlockSpec((rows, CHUNK * tile), lambda step: (0, step)),
            pl.BlockSpec(memory_space=pl.ANY),
        ],
        out_specs=[
            pl.BlockSpec((rows, width), lambda step: (0, 0)),
            pl.BlockSpec((loop_size, 128), lambda step: (0, 0)),
        ],
        scratch_shapes=[
            pltpu.VMEM((CHUNK * tile, width), jnp.bfloat16),
            pltpu.VMEM((2 * rows, width), jnp.bfloat16),
            pltpu.SemaphoreType.DMA((CHUNK,)),
        ],
        compiler_params=pltpu.CompilerParams(vmem_limit_bytes=32 * 1024 * 1024),
        cost_estimate=pl.CostEstimate(
            flops=8 * rows * width * slots * tile,
            bytes_accessed=4 * rows * (slots * tile + 2 * width) + 2 * slots * tile * width,
            transcendentals=rows * slots * tile,
        ),
        name="add_chunks",
    )(*lists, users, labels, items)


def update_kernel(entries, users_ref, grad_ref, squares_ref, out_ref, result, sems):
    total = jnp.sum(squares_ref[...], axis=0, keepdims=True)
    total = jnp.sum(total, axis=1, keepdims=True)
    scale = 0.5 / jnp.sqrt(total / entries + 1e-06)
    rows = users_ref.shape[0] // sems.shape[0]
    copies = []
    for at in range(sems.shape[0]):
        part = pl.ds(at * rows, rows)
        result[part, :] = users_ref[part, :] - scale * grad_ref[part, :]
        copies.append(pltpu.make_async_copy(result.at[part, :], out_ref.at[part, :], sems.at[at]))
        copies[-1].start()
    for copy in copies:
        copy.wait()


def local(users, items, tile_blocks, tile_count, labels):
    loop_size = lax.axis_size("loop")
    rows, width = users.shape
    slots = tile_blocks.shape[1]
    lists = (tile_blocks, tile_count)
    if loop_size == RING and slots == CHUNK:
        gradient, square, users = ring_gradient(users, items, lists, labels)
    else:
        whole = lax.all_gather(items, "loop", axis=0, tiled=True)
        gradient, square = add_chunks(loop_size, whole, lists, users, labels)

    squares = lax.all_to_all(square, "loop", 0, 0, tiled=True)
    return pl.pallas_call(
        functools.partial(update_kernel, rows * loop_size * width),
        out_shape=jax.ShapeDtypeStruct((rows, width), jnp.float32),
        in_specs=[pl.BlockSpec(memory_space=pltpu.VMEM)] * 3,
        out_specs=pl.BlockSpec(memory_space=pl.ANY),
        scratch_shapes=[pltpu.VMEM((rows, width), jnp.float32), pltpu.SemaphoreType.DMA((4,))],
        compiler_params=pltpu.CompilerParams(vmem_limit_bytes=16 * 1024 * 1024),
        cost_estimate=pl.CostEstimate(
            flops=2 * rows * width, bytes_accessed=12 * rows * width, transcendentals=0
        ),
        name="update",
    )(users, gradient, squares)


def solution(mesh):
    in_specs = (
        P(("group", "loop"), None),
        P(("group", "loop"), None),
        P(("group", "loop"), None),
        P(("group", "loop")),
        P(("group", "loop"), None),
    )
    out_specs = P(("group", "loop"), None)
    return jax.shard_map(local, mesh=mesh, in_specs=in_specs, out_specs=out_specs, check_vma=False)
```

```python
import functools

import jax
import jax.numpy as jnp
from jax import lax
from jax.experimental import pallas as pl
from jax.experimental.pallas import tpu as pltpu
from jax.sharding import PartitionSpec as P

CHUNK = 8
RING = 16


def ring_place(loop_size):
    outer = loop_size // 4

    def device(position, core):
        position = position % (2 * outer)
        chip = 2 * position if position < outer else 2 * (2 * outer - 1 - position) + 1
        return 2 * chip + core

    return 2 * outer, device


def to_next(array, direction, loop_size):
    chips, device = ring_place(loop_size)
    pairs = [(device(at, 0), device(at + direction, 0)) for at in range(chips)]
    pairs += [(device(at, 1), device(at - direction, 1)) for at in range(chips)]
    return lax.ppermute(array, "loop", pairs)


def across(array, loop_size):
    chips, device = ring_place(loop_size)
    pairs = [
        (device(at, core), device(at + (3 if at % 2 == 0 else -3), core))
        for at in range(chips)
        for core in range(2)
    ]
    return lax.ppermute(array, "loop", pairs)


def to_other_core(array, loop_size):
    return lax.ppermute(array, "loop", [(at, at ^ 1) for at in range(loop_size)])


def halves(values):
    upper = values.astype(jnp.bfloat16)
    return jnp.concatenate([upper, (values - upper.astype(jnp.float32)).astype(jnp.bfloat16)], 0)


def table_kernel(loop_size, origins, list_ref, count_ref, table_ref):
    chips = loop_size // 2
    lane = lax.broadcasted_iota(jnp.int32, table_ref.shape, 1)
    core, position = core_and_position(loop_size)
    hops, other = jnp.zeros_like(lane), jnp.zeros_like(lane)
    for at, origin in enumerate(origins):
        hops = jnp.where(lane == at, origin[0], hops)
        other = jnp.where(lane == at, origin[1], other)
    at = (position + chips + jnp.where(core == 0, -hops, hops)) & (chips - 1)
    chip = jnp.where(at < chips // 2, 2 * at, 2 * (chips - 1 - at) + 1)
    block = 2 * chip + jnp.where(other == 1, 1 - core, core)
    found = jnp.full_like(lane, -1)
    for slot in range(list_ref.shape[1]):
        name = jnp.where(slot < count_ref[...], list_ref[:, slot : slot + 1], -1)
        found = jnp.where(name == block, slot, found)
    table_ref[...] = jnp.where(lane < len(origins), found, -1)


def slot_table(loop_size, origins, block_list, live_count):
    return pl.pallas_call(
        functools.partial(table_kernel, loop_size, origins),
        out_shape=jax.ShapeDtypeStruct((1, 128), jnp.int32),
        in_specs=[pl.BlockSpec(memory_space=pltpu.VMEM)] * 2,
        out_specs=pl.BlockSpec(memory_space=pltpu.VMEM),
        compiler_params=pltpu.CompilerParams(vmem_limit_bytes=16 * 1024 * 1024),
        cost_estimate=pl.CostEstimate(flops=2**32, bytes_accessed=1024, transcendentals=0),
        name="slot_table",
    )(block_list, live_count.reshape(1, 1))


def add_block(grad_ref, parts_ref, block, labels):
    rows = grad_ref.shape[0]
    tile = labels[0].shape[1]
    upper, lower = [], []
    for at in range(0, len(labels), 2):
        some = jnp.concatenate(labels[at : at + 2], 1)
        both = lax.dot_general(
            parts_ref[...],
            block[at * tile : at * tile + some.shape[1]],
            (((1,), (1,)), ((), ())),
            preferred_element_type=jnp.float32,
        )
        residual = 0.5 * jnp.tanh(both[:rows] + both[rows:]) + (0.5 - some.astype(jnp.float32))
        upper.append(residual.astype(jnp.bfloat16))
        lower.append((residual - upper[-1].astype(jnp.float32)).astype(jnp.bfloat16))
    grad_ref[...] += jnp.dot(
        jnp.concatenate(upper + lower, 1),
        jnp.concatenate([block, block], 0),
        preferred_element_type=jnp.float32,
    )


def add_tiles(grad_ref, parts_ref, tiles, live, labels_at):
    tile = tiles.shape[0] // CHUNK
    fours = (live + 1) // 4

    @pl.when(live % 4 == 3)
    def _():
        blank = pl.multiple_of(live * tile, tile)
        tiles[pl.ds(blank, tile), :] = jnp.zeros((tile, tiles.shape[1]), tiles.dtype)

    def add(count, index, carry):
        start = index * count
        block = tiles[pl.ds(pl.multiple_of(start * tile, tile), count * tile), :]
        add_block(grad_ref, parts_ref, block, [labels_at(start + at) for at in range(count)])
        return carry

    lax.fori_loop(0, fours, functools.partial(add, 4), 0)
    pl.when(live - 4 * fours == 2)(lambda: add(2, 2 * fours, None))
    pl.when(live - 4 * fours == 1)(lambda: add(1, 4 * fours, None))


def store_square(grad_ref, square_ref):
    gradient = grad_ref[...]
    square = jnp.sum(gradient * gradient, axis=0, keepdims=True)
    square = sum(square[:, at : at + 128] for at in range(0, square.shape[1], 128))
    square_ref[...] = jnp.broadcast_to(square, square_ref.shape)


def core_and_position(loop_size):
    me = lax.axis_index("loop")
    core, row, outer = me % 2, me // 2 % 2, me // 4
    return core, jnp.where(row == 0, outer, loop_size // 2 - 1 - outer)


def pack_kernel(loop_size, *refs):
    tile = refs[0].shape[0]
    sources = refs[:-1] if loop_size is None else refs[:2]
    packed_ref = refs[-1] if loop_size is None else refs[-2]
    if loop_size is not None:
        core, position = core_and_position(loop_size)
        for at in range(2):

            @pl.when((core + position) % 2 == at)
            def _():
                refs[-1][...] = refs[1 + at][...]

    for at, ref in enumerate(sources):
        packed_ref[at * tile : (at + 1) * tile, :] = ref[...]


def pack(arrays, loop_size=None):
    tile, width = arrays[0].shape
    shapes = [(len(arrays) * tile, width)] if loop_size is None else [(2 * tile, width), (tile, width)]
    return pl.pallas_call(
        functools.partial(pack_kernel, loop_size),
        out_shape=[jax.ShapeDtypeStruct(shape, arrays[0].dtype) for shape in shapes],
        in_specs=[pl.BlockSpec(memory_space=pltpu.VMEM)] * len(arrays),
        out_specs=[pl.BlockSpec(memory_space=pltpu.VMEM)] * len(shapes),
        compiler_params=pltpu.CompilerParams(vmem_limit_bytes=16 * 1024 * 1024),
        cost_estimate=pl.CostEstimate(
            flops=2**34 if loop_size is None else 2**32,
            bytes_accessed=4 * len(arrays) * tile * width,
            transcendentals=0,
        ),
        name="pack",
    )(*arrays)


def pieces_kernel(places, count, packed, first, last, table_ref, given_ref, labels_ref, *rest):
    rest = list(rest)
    arrays = [rest.pop(0) for _ in range(count)]
    if not first:
        rest.pop(0)
    grad_ref = rest.pop(0)
    parts_ref = rest.pop(0) if first else given_ref
    pack_ref = rest.pop(0) if packed else None
    square_ref = rest.pop(0) if last else None
    tiles, slots = rest
    tile = tiles.shape[0] // CHUNK
    for at, index in enumerate(packed):
        pack_ref[at * tile : (at + 1) * tile, :] = arrays[index][...]
    if first:
        parts_ref[...] = halves(0.5 * given_ref[...])
        grad_ref[...] = jnp.zeros_like(grad_ref)
    table = table_ref[...]
    entries = [table[0, at] for at, _, _ in places]

    def labels_of(slot):
        return labels_ref[:, pl.ds(pl.multiple_of(slot * tile, tile), tile)]

    live = jnp.int32(0)
    for found, (_, index, row) in zip(entries, places):

        @pl.when(found >= 0)
        def _():
            into = pl.ds(pl.multiple_of(live * tile, tile), tile)
            tiles[into, :] = arrays[index][row * tile : (row + 1) * tile, :]
            slots[live] = found

        live = live + (found >= 0).astype(jnp.int32)
    slots[live] = 0
    add_tiles(grad_ref, parts_ref, tiles, live, lambda position: labels_of(slots[position]))
    if last:
        store_square(grad_ref, square_ref)


def add_pieces(held, packed, loop_size, table, given, labels, before, last):
    first = before is None
    width = given.shape[1]
    rows = given.shape[0] // (1 if first else 2)
    arrays = [array for array, _ in held]
    tile = labels.shape[1] // CHUNK
    places = [(at, index, row) for index, (_, entries) in enumerate(held) for row, at in enumerate(entries)]
    most = min(len(places), CHUNK)
    out_shape = [jax.ShapeDtypeStruct((rows, width), jnp.float32)]
    if first:
        out_shape.append(jax.ShapeDtypeStruct((2 * rows, width), jnp.bfloat16))
    if packed:
        out_shape.append(jax.ShapeDtypeStruct((len(packed) * tile, width), jnp.bfloat16))
    if last:
        out_shape.append(jax.ShapeDtypeStruct((loop_size, 128), jnp.float32))
    extra = [] if first else [before]
    return pl.pallas_call(
        functools.partial(pieces_kernel, places, len(arrays), packed, first, last),
        out_shape=out_shape,
        in_specs=[pl.BlockSpec(memory_space=pltpu.VMEM)] * (3 + len(arrays) + len(extra)),
        out_specs=[pl.BlockSpec(memory_space=pltpu.VMEM)] * len(out_shape),
        input_output_aliases={} if first else {3 + len(arrays): 0},
        scratch_shapes=[
            pltpu.VMEM((CHUNK * tile, width), jnp.bfloat16),
            pltpu.SMEM((CHUNK + 1,), jnp.int32),
        ],
        compiler_params=pltpu.CompilerParams(vmem_limit_bytes=24 * 1024 * 1024),
        cost_estimate=pl.CostEstimate(
            flops=(8 if first else 128) * rows * width * most * tile,
            bytes_accessed=8 * rows * width,
            transcendentals=rows * most * tile,
        ),
        name="add_pieces",
    )(table, given, labels, *arrays, *extra)


def ring_gradient(users, items, lists, labels):
    loop_size = lax.axis_size("loop")
    far = loop_size // 4
    origins = [(hops, 0) for hops in range(1 - far, far + 1)]
    origins += [(-hops, 1) for hops, _ in origins]
    table = slot_table(loop_size, origins, *lists)
    where = {origin: at for at, origin in enumerate(origins)}

    def held(hops, array):
        return array, [where[hops, 0]]

    def other(arrays, hops):
        return to_other_core(arrays, loop_size), [where[-hop, 1] for hop in hops]

    up = to_next(items, 1, loop_size)
    down = to_next(items, -1, loop_size)
    up, table = lax.optimization_barrier((up, table))
    first = [held(0, items), held(1, up), held(-1, down)]
    second = [held(2, to_next(up, 1, loop_size)), held(-2, to_next(down, -1, loop_size))]
    first.append(other(down, [-1]))
    packed, opposite = pack([items, up, down], loop_size)
    opposite = across(opposite, loop_size)
    gradient, parts = add_pieces(first, [], loop_size, table, users, labels, None, False)
    first = other(packed, [0, 1])
    third = [held(3, to_next(second[0][0], 1, loop_size)), held(-3, to_next(second[1][0], -1, loop_size))]
    gradient, packed = add_pieces(second, [0, 1], loop_size, table, parts, labels, gradient, False)
    second = other(packed, [2, -2])
    third.append(held(4, opposite))
    arrived, gradient = lax.optimization_barrier(([array for array, _ in third], gradient))
    final = other(pack(arrived)[0], [3, -3, 4])
    (gradient,) = add_pieces(
        third + [first, second], [], loop_size, table, parts, labels, gradient, False
    )
    return *add_pieces([final], [], loop_size, table, parts, labels, gradient, True), users


def chunks_kernel(
    list_ref, count_ref, users_ref, labels_ref, items_ref, grad_ref, square_ref, tiles, parts_ref, sems
):
    tile = tiles.shape[0] // CHUNK
    step = pl.program_id(0)
    live = jnp.clip(count_ref[0] - step * CHUNK, 0, CHUNK)

    @pl.when(step == 0)
    def _():
        parts_ref[...] = halves(0.5 * users_ref[...])
        grad_ref[...] = jnp.zeros_like(grad_ref)

    def move(slot):
        start = pl.multiple_of(list_ref[0, step * CHUNK + slot] * tile, tile)
        return pltpu.make_async_copy(
            items_ref.at[pl.ds(start, tile), :], tiles.at[pl.ds(slot * tile, tile), :], sems.at[slot]
        )

    for slot in range(CHUNK):
        pl.when(slot < live)(lambda slot=slot: move(slot).start())
    for slot in range(CHUNK):
        pl.when(slot < live)(lambda slot=slot: move(slot).wait())

    def labels_at(position):
        return labels_ref[:, pl.ds(pl.multiple_of(position * tile, tile), tile)]

    add_tiles(grad_ref, parts_ref, tiles, live, labels_at)

    @pl.when(step == pl.num_programs(0) - 1)
    def _():
        store_square(grad_ref, square_ref)


def add_chunks(loop_size, items, lists, users, labels):
    rows, width = users.shape
    slots = lists[0].shape[1]
    tile = labels.shape[1] // slots
    return pl.pallas_call(
        chunks_kernel,
        grid=(slots // CHUNK,),
        out_shape=[
            jax.ShapeDtypeStruct((rows, width), jnp.float32),
            jax.ShapeDtypeStruct((loop_size, 128), jnp.float32),
        ],
        in_specs=[
            pl.BlockSpec(memory_space=pltpu.SMEM),
            pl.BlockSpec(memory_space=pltpu.SMEM),
            pl.BlockSpec((rows, width), lambda step: (0, 0)),
            pl.BlockSpec((rows, CHUNK * tile), lambda step: (0, step)),
            pl.BlockSpec(memory_space=pl.ANY),
        ],
        out_specs=[
            pl.BlockSpec((rows, width), lambda step: (0, 0)),
            pl.BlockSpec((loop_size, 128), lambda step: (0, 0)),
        ],
        scratch_shapes=[
            pltpu.VMEM((CHUNK * tile, width), jnp.bfloat16),
            pltpu.VMEM((2 * rows, width), jnp.bfloat16),
            pltpu.SemaphoreType.DMA((CHUNK,)),
        ],
        compiler_params=pltpu.CompilerParams(vmem_limit_bytes=32 * 1024 * 1024),
        cost_estimate=pl.CostEstimate(
            flops=8 * rows * width * slots * tile,
            bytes_accessed=4 * rows * (slots * tile + 2 * width) + 2 * slots * tile * width,
            transcendentals=rows * slots * tile,
        ),
        name="add_chunks",
    )(*lists, users, labels, items)


def update_kernel(entries, users_ref, grad_ref, squares_ref, out_ref, result, sems):
    total = jnp.sum(squares_ref[...], axis=0, keepdims=True)
    total = jnp.sum(total, axis=1, keepdims=True)
    scale = 0.5 / jnp.sqrt(total / entries + 1e-06)
    rows = users_ref.shape[0] // sems.shape[0]
    copies = []
    for at in range(sems.shape[0]):
        part = pl.ds(at * rows, rows)
        result[part, :] = users_ref[part, :] - scale * grad_ref[part, :]
        copies.append(pltpu.make_async_copy(result.at[part, :], out_ref.at[part, :], sems.at[at]))
        copies[-1].start()
    for copy in copies:
        copy.wait()


def local(users, items, tile_blocks, tile_count, labels):
    loop_size = lax.axis_size("loop")
    rows, width = users.shape
    slots = tile_blocks.shape[1]
    lists = (tile_blocks, tile_count)
    if loop_size == RING and slots == CHUNK:
        gradient, square, users = ring_gradient(users, items, lists, labels)
    else:
        whole = lax.all_gather(items, "loop", axis=0, tiled=True)
        gradient, square = add_chunks(loop_size, whole, lists, users, labels)

    squares = lax.all_to_all(square, "loop", 0, 0, tiled=True)
    return pl.pallas_call(
        functools.partial(update_kernel, rows * loop_size * width),
        out_shape=jax.ShapeDtypeStruct((rows, width), jnp.float32),
        in_specs=[pl.BlockSpec(memory_space=pltpu.VMEM)] * 3,
        out_specs=pl.BlockSpec(memory_space=pl.ANY),
        scratch_shapes=[pltpu.VMEM((rows, width), jnp.float32), pltpu.SemaphoreType.DMA((4,))],
        compiler_params=pltpu.CompilerParams(vmem_limit_bytes=16 * 1024 * 1024),
        cost_estimate=pl.CostEstimate(
            flops=2 * rows * width, bytes_accessed=12 * rows * width, transcendentals=0
        ),
        name="update",
    )(users, gradient, squares)


def solution(mesh):
    in_specs = (
        P(("group", "loop"), None),
        P(("group", "loop"), None),
        P(("group", "loop"), None),
        P(("group", "loop")),
        P(("group", "loop"), None),
    )
    out_specs = P(("group", "loop"), None)
    return jax.shard_map(local, mesh=mesh, in_specs=in_specs, out_specs=out_specs, check_vma=False)
```

```python
import functools

import jax
import jax.numpy as jnp
from jax import lax
from jax.experimental import pallas as pl
from jax.experimental.pallas import tpu as pltpu
from jax.sharding import PartitionSpec as P

CHUNK = 8
RING = 16


def ring_place(loop_size):
    outer = loop_size // 4

    def device(position, core):
        position = position % (2 * outer)
        chip = 2 * position if position < outer else 2 * (2 * outer - 1 - position) + 1
        return 2 * chip + core

    return 2 * outer, device


def to_next(array, direction, loop_size):
    chips, device = ring_place(loop_size)
    pairs = [(device(at, 0), device(at + direction, 0)) for at in range(chips)]
    pairs += [(device(at, 1), device(at - direction, 1)) for at in range(chips)]
    return lax.ppermute(array, "loop", pairs)


def across(array, loop_size):
    chips, device = ring_place(loop_size)
    pairs = [
        (device(at, core), device(at + (3 if at % 2 == 0 else -3), core))
        for at in range(chips)
        for core in range(2)
    ]
    return lax.ppermute(array, "loop", pairs)


def to_other_core(array, loop_size):
    return lax.ppermute(array, "loop", [(at, at ^ 1) for at in range(loop_size)])


def halves(values):
    upper = values.astype(jnp.bfloat16)
    return jnp.concatenate([upper, (values - upper.astype(jnp.float32)).astype(jnp.bfloat16)], 0)


def table_kernel(loop_size, origins, list_ref, count_ref, table_ref):
    chips = loop_size // 2
    lane = lax.broadcasted_iota(jnp.int32, table_ref.shape, 1)
    core, position = core_and_position(loop_size)
    hops, other = jnp.zeros_like(lane), jnp.zeros_like(lane)
    for at, origin in enumerate(origins):
        hops = jnp.where(lane == at, origin[0], hops)
        other = jnp.where(lane == at, origin[1], other)
    at = (position + chips + jnp.where(core == 0, -hops, hops)) & (chips - 1)
    chip = jnp.where(at < chips // 2, 2 * at, 2 * (chips - 1 - at) + 1)
    block = 2 * chip + jnp.where(other == 1, 1 - core, core)
    found = jnp.full_like(lane, -1)
    for slot in range(list_ref.shape[1]):
        name = jnp.where(slot < count_ref[...], list_ref[:, slot : slot + 1], -1)
        found = jnp.where(name == block, slot, found)
    table_ref[...] = jnp.where(lane < len(origins), found, -1)


def slot_table(loop_size, origins, block_list, live_count):
    return pl.pallas_call(
        functools.partial(table_kernel, loop_size, origins),
        out_shape=jax.ShapeDtypeStruct((1, 128), jnp.int32),
        in_specs=[pl.BlockSpec(memory_space=pltpu.VMEM)] * 2,
        out_specs=pl.BlockSpec(memory_space=pltpu.VMEM),
        compiler_params=pltpu.CompilerParams(vmem_limit_bytes=16 * 1024 * 1024),
        cost_estimate=pl.CostEstimate(flops=2**32, bytes_accessed=1024, transcendentals=0),
        name="slot_table",
    )(block_list, live_count.reshape(1, 1))


def add_block(grad_ref, parts_ref, block, labels):
    rows = grad_ref.shape[0]
    tile = labels[0].shape[1]
    upper, lower = [], []
    for at in range(0, len(labels), 2):
        some = jnp.concatenate(labels[at : at + 2], 1)
        both = lax.dot_general(
            parts_ref[...],
            block[at * tile : at * tile + some.shape[1]],
            (((1,), (1,)), ((), ())),
            preferred_element_type=jnp.float32,
        )
        residual = 0.5 * jnp.tanh(both[:rows] + both[rows:]) + (0.5 - some.astype(jnp.float32))
        upper.append(residual.astype(jnp.bfloat16))
        lower.append((residual - upper[-1].astype(jnp.float32)).astype(jnp.bfloat16))
    grad_ref[...] += jnp.dot(
        jnp.concatenate(upper + lower, 1),
        jnp.concatenate([block, block], 0),
        preferred_element_type=jnp.float32,
    )


def add_tiles(grad_ref, parts_ref, tiles, live, labels_at):
    tile = tiles.shape[0] // CHUNK
    fours = (live + 1) // 4

    @pl.when(live % 4 == 3)
    def _():
        blank = pl.multiple_of(live * tile, tile)
        tiles[pl.ds(blank, tile), :] = jnp.zeros((tile, tiles.shape[1]), tiles.dtype)

    def add(count, index, carry):
        start = index * count
        block = tiles[pl.ds(pl.multiple_of(start * tile, tile), count * tile), :]
        add_block(grad_ref, parts_ref, block, [labels_at(start + at) for at in range(count)])
        return carry

    lax.fori_loop(0, fours, functools.partial(add, 4), 0)
    pl.when(live - 4 * fours == 2)(lambda: add(2, 2 * fours, None))
    pl.when(live - 4 * fours == 1)(lambda: add(1, 4 * fours, None))


def store_square(grad_ref, square_ref):
    gradient = grad_ref[...]
    square = jnp.sum(gradient * gradient, axis=0, keepdims=True)
    square = sum(square[:, at : at + 128] for at in range(0, square.shape[1], 128))
    square_ref[...] = jnp.broadcast_to(square, square_ref.shape)


def core_and_position(loop_size):
    me = lax.axis_index("loop")
    core, row, outer = me % 2, me // 2 % 2, me // 4
    return core, jnp.where(row == 0, outer, loop_size // 2 - 1 - outer)


def pack_kernel(*refs):
    tile = refs[0].shape[0]
    for at, ref in enumerate(refs[:-1]):
        refs[-1][at * tile : (at + 1) * tile, :] = ref[...]


def pack(arrays):
    tile, width = arrays[0].shape
    return pl.pallas_call(
        pack_kernel,
        out_shape=jax.ShapeDtypeStruct((len(arrays) * tile, width), arrays[0].dtype),
        in_specs=[pl.BlockSpec(memory_space=pltpu.VMEM)] * len(arrays),
        out_specs=pl.BlockSpec(memory_space=pltpu.VMEM),
        compiler_params=pltpu.CompilerParams(vmem_limit_bytes=16 * 1024 * 1024),
        cost_estimate=pl.CostEstimate(
            flops=2**34, bytes_accessed=4 * len(arrays) * tile * width, transcendentals=0
        ),
        name="pack",
    )(*arrays)


def pieces_kernel(places, count, packed, loop_size, first, last, table_ref, given_ref, labels_ref, *rest):
    rest = list(rest)
    arrays = [rest.pop(0) for _ in range(count)]
    if not first:
        rest.pop(0)
    grad_ref = rest.pop(0)
    parts_ref = rest.pop(0) if first else given_ref
    across_ref = rest.pop(0) if first else None
    pack_ref = rest.pop(0) if packed else None
    square_ref = rest.pop(0) if last else None
    tiles, slots = rest
    tile = tiles.shape[0] // CHUNK
    for at, index in enumerate(packed):
        pack_ref[at * tile : (at + 1) * tile, :] = arrays[index][...]
    if first:
        core, position = core_and_position(loop_size)
        for at in range(2):

            @pl.when((core + position) % 2 == at)
            def _():
                across_ref[...] = arrays[1 + at][...]

        parts_ref[...] = halves(0.5 * given_ref[...])
        grad_ref[...] = jnp.zeros_like(grad_ref)
    table = table_ref[...]
    entries = [table[0, at] for at, _, _ in places]

    def labels_of(slot):
        return labels_ref[:, pl.ds(pl.multiple_of(slot * tile, tile), tile)]

    live = jnp.int32(0)
    for found, (_, index, row) in zip(entries, places):

        @pl.when(found >= 0)
        def _():
            into = pl.ds(pl.multiple_of(live * tile, tile), tile)
            tiles[into, :] = arrays[index][row * tile : (row + 1) * tile, :]
            slots[live] = found

        live = live + (found >= 0).astype(jnp.int32)
    slots[live] = 0
    add_tiles(grad_ref, parts_ref, tiles, live, lambda position: labels_of(slots[position]))
    if last:
        store_square(grad_ref, square_ref)


def add_pieces(held, packed, loop_size, table, given, labels, before, last):
    first = before is None
    width = given.shape[1]
    rows = given.shape[0] // (1 if first else 2)
    arrays = [array for array, _ in held]
    tile = labels.shape[1] // CHUNK
    places = [(at, index, row) for index, (_, entries) in enumerate(held) for row, at in enumerate(entries)]
    most = min(len(places), CHUNK)
    out_shape = [jax.ShapeDtypeStruct((rows, width), jnp.float32)]
    if first:
        out_shape.append(jax.ShapeDtypeStruct((2 * rows, width), jnp.bfloat16))
        out_shape.append(jax.ShapeDtypeStruct((tile, width), jnp.bfloat16))
    if packed:
        out_shape.append(jax.ShapeDtypeStruct((len(packed) * tile, width), jnp.bfloat16))
    if last:
        out_shape.append(jax.ShapeDtypeStruct((loop_size, 128), jnp.float32))
    extra = [] if first else [before]
    return pl.pallas_call(
        functools.partial(pieces_kernel, places, len(arrays), packed, loop_size, first, last),
        out_shape=out_shape,
        in_specs=[pl.BlockSpec(memory_space=pltpu.VMEM)] * (3 + len(arrays) + len(extra)),
        out_specs=[pl.BlockSpec(memory_space=pltpu.VMEM)] * len(out_shape),
        input_output_aliases={} if first else {3 + len(arrays): 0},
        scratch_shapes=[
            pltpu.VMEM((CHUNK * tile, width), jnp.bfloat16),
            pltpu.SMEM((CHUNK + 1,), jnp.int32),
        ],
        compiler_params=pltpu.CompilerParams(vmem_limit_bytes=24 * 1024 * 1024),
        cost_estimate=pl.CostEstimate(
            flops=128 * rows * width * most * tile,
            bytes_accessed=8 * rows * width,
            transcendentals=rows * most * tile,
        ),
        name="add_pieces",
    )(table, given, labels, *arrays, *extra)


def ring_gradient(users, items, lists, labels):
    loop_size = lax.axis_size("loop")
    far = loop_size // 4
    origins = [(hops, 0) for hops in range(1 - far, far + 1)]
    origins += [(-hops, 1) for hops, _ in origins]
    table = slot_table(loop_size, origins, *lists)
    where = {origin: at for at, origin in enumerate(origins)}

    def held(hops, array):
        return array, [where[hops, 0]]

    def other(arrays, hops):
        return to_other_core(arrays, loop_size), [where[-hop, 1] for hop in hops]

    up = to_next(items, 1, loop_size)
    down = to_next(items, -1, loop_size)
    up, table = lax.optimization_barrier((up, table))
    first = [held(0, items), held(1, up), held(-1, down)]
    second = [held(2, to_next(up, 1, loop_size)), held(-2, to_next(down, -1, loop_size))]
    gradient, parts, opposite, packed = add_pieces(
        first, [0, 1, 2], loop_size, table, users, labels, None, False
    )
    opposite = across(opposite, loop_size)
    first = other(packed, [0, 1, -1])
    third = [held(3, to_next(second[0][0], 1, loop_size)), held(-3, to_next(second[1][0], -1, loop_size))]
    second.append(held(4, opposite))
    gradient, packed = add_pieces(
        second, [0, 1, 2], loop_size, table, parts, labels, gradient, False
    )
    second = other(packed, [2, -2, 4])
    arrived, gradient = lax.optimization_barrier(([array for array, _ in third], gradient))
    final = other(pack(arrived), [3, -3])
    (gradient,) = add_pieces(
        third + [first, second], [], loop_size, table, parts, labels, gradient, False
    )
    return *add_pieces([final], [], loop_size, table, parts, labels, gradient, True), users


def chunks_kernel(
    list_ref, count_ref, users_ref, labels_ref, items_ref, grad_ref, square_ref, tiles, parts_ref, sems
):
    tile = tiles.shape[0] // CHUNK
    step = pl.program_id(0)
    live = jnp.clip(count_ref[0] - step * CHUNK, 0, CHUNK)

    @pl.when(step == 0)
    def _():
        parts_ref[...] = halves(0.5 * users_ref[...])
        grad_ref[...] = jnp.zeros_like(grad_ref)

    def move(slot):
        start = pl.multiple_of(list_ref[0, step * CHUNK + slot] * tile, tile)
        return pltpu.make_async_copy(
            items_ref.at[pl.ds(start, tile), :], tiles.at[pl.ds(slot * tile, tile), :], sems.at[slot]
        )

    for slot in range(CHUNK):
        pl.when(slot < live)(lambda slot=slot: move(slot).start())
    for slot in range(CHUNK):
        pl.when(slot < live)(lambda slot=slot: move(slot).wait())

    def labels_at(position):
        return labels_ref[:, pl.ds(pl.multiple_of(position * tile, tile), tile)]

    add_tiles(grad_ref, parts_ref, tiles, live, labels_at)

    @pl.when(step == pl.num_programs(0) - 1)
    def _():
        store_square(grad_ref, square_ref)


def add_chunks(loop_size, items, lists, users, labels):
    rows, width = users.shape
    slots = lists[0].shape[1]
    tile = labels.shape[1] // slots
    return pl.pallas_call(
        chunks_kernel,
        grid=(slots // CHUNK,),
        out_shape=[
            jax.ShapeDtypeStruct((rows, width), jnp.float32),
            jax.ShapeDtypeStruct((loop_size, 128), jnp.float32),
        ],
        in_specs=[
            pl.BlockSpec(memory_space=pltpu.SMEM),
            pl.BlockSpec(memory_space=pltpu.SMEM),
            pl.BlockSpec((rows, width), lambda step: (0, 0)),
            pl.BlockSpec((rows, CHUNK * tile), lambda step: (0, step)),
            pl.BlockSpec(memory_space=pl.ANY),
        ],
        out_specs=[
            pl.BlockSpec((rows, width), lambda step: (0, 0)),
            pl.BlockSpec((loop_size, 128), lambda step: (0, 0)),
        ],
        scratch_shapes=[
            pltpu.VMEM((CHUNK * tile, width), jnp.bfloat16),
            pltpu.VMEM((2 * rows, width), jnp.bfloat16),
            pltpu.SemaphoreType.DMA((CHUNK,)),
        ],
        compiler_params=pltpu.CompilerParams(vmem_limit_bytes=32 * 1024 * 1024),
        cost_estimate=pl.CostEstimate(
            flops=8 * rows * width * slots * tile,
            bytes_accessed=4 * rows * (slots * tile + 2 * width) + 2 * slots * tile * width,
            transcendentals=rows * slots * tile,
        ),
        name="add_chunks",
    )(*lists, users, labels, items)


def update_kernel(entries, users_ref, grad_ref, squares_ref, out_ref, result, sems):
    total = jnp.sum(squares_ref[...], axis=0, keepdims=True)
    total = jnp.sum(total, axis=1, keepdims=True)
    scale = 0.5 / jnp.sqrt(total / entries + 1e-06)
    rows = users_ref.shape[0] // sems.shape[0]
    copies = []
    for at in range(sems.shape[0]):
        part = pl.ds(at * rows, rows)
        result[part, :] = users_ref[part, :] - scale * grad_ref[part, :]
        copies.append(pltpu.make_async_copy(result.at[part, :], out_ref.at[part, :], sems.at[at]))
        copies[-1].start()
    for copy in copies:
        copy.wait()


def local(users, items, tile_blocks, tile_count, labels):
    loop_size = lax.axis_size("loop")
    rows, width = users.shape
    slots = tile_blocks.shape[1]
    lists = (tile_blocks, tile_count)
    if loop_size == RING and slots == CHUNK:
        gradient, square, users = ring_gradient(users, items, lists, labels)
    else:
        whole = lax.all_gather(items, "loop", axis=0, tiled=True)
        gradient, square = add_chunks(loop_size, whole, lists, users, labels)

    squares = lax.all_to_all(square, "loop", 0, 0, tiled=True)
    return pl.pallas_call(
        functools.partial(update_kernel, rows * loop_size * width),
        out_shape=jax.ShapeDtypeStruct((rows, width), jnp.float32),
        in_specs=[pl.BlockSpec(memory_space=pltpu.VMEM)] * 3,
        out_specs=pl.BlockSpec(memory_space=pl.ANY),
        scratch_shapes=[pltpu.VMEM((rows, width), jnp.float32), pltpu.SemaphoreType.DMA((4,))],
        compiler_params=pltpu.CompilerParams(vmem_limit_bytes=16 * 1024 * 1024),
        cost_estimate=pl.CostEstimate(
            flops=2 * rows * width, bytes_accessed=12 * rows * width, transcendentals=0
        ),
        name="update",
    )(users, gradient, squares)


def solution(mesh):
    in_specs = (
        P(("group", "loop"), None),
        P(("group", "loop"), None),
        P(("group", "loop"), None),
        P(("group", "loop")),
        P(("group", "loop"), None),
    )
    out_specs = P(("group", "loop"), None)
    return jax.shard_map(local, mesh=mesh, in_specs=in_specs, out_specs=out_specs, check_vma=False)
```

```python
import functools

import jax
import jax.numpy as jnp
from jax import lax
from jax.experimental import pallas as pl
from jax.experimental.pallas import tpu as pltpu
from jax.sharding import PartitionSpec as P

CHUNK = 8
RING = 16


def ring_place(loop_size):
    outer = loop_size // 4

    def device(position, core):
        position = position % (2 * outer)
        chip = 2 * position if position < outer else 2 * (2 * outer - 1 - position) + 1
        return 2 * chip + core

    return 2 * outer, device


def to_next(array, direction, loop_size):
    chips, device = ring_place(loop_size)
    pairs = [(device(at, 0), device(at + direction, 0)) for at in range(chips)]
    pairs += [(device(at, 1), device(at - direction, 1)) for at in range(chips)]
    return lax.ppermute(array, "loop", pairs)


def across(array, loop_size):
    chips, device = ring_place(loop_size)
    pairs = [
        (device(at, core), device(at + (3 if at % 2 == 0 else -3), core))
        for at in range(chips)
        for core in range(2)
    ]
    return lax.ppermute(array, "loop", pairs)


def to_other_core(array, loop_size):
    return lax.ppermute(array, "loop", [(at, at ^ 1) for at in range(loop_size)])


def halves(values):
    upper = values.astype(jnp.bfloat16)
    return jnp.concatenate([upper, (values - upper.astype(jnp.float32)).astype(jnp.bfloat16)], 0)


def table_kernel(loop_size, origins, list_ref, count_ref, table_ref):
    chips = loop_size // 2
    lane = lax.broadcasted_iota(jnp.int32, table_ref.shape, 1)
    core, position = core_and_position(loop_size)
    hops, other = jnp.zeros_like(lane), jnp.zeros_like(lane)
    for at, origin in enumerate(origins):
        hops = jnp.where(lane == at, origin[0], hops)
        other = jnp.where(lane == at, origin[1], other)
    at = (position + chips + jnp.where(core == 0, -hops, hops)) & (chips - 1)
    chip = jnp.where(at < chips // 2, 2 * at, 2 * (chips - 1 - at) + 1)
    block = 2 * chip + jnp.where(other == 1, 1 - core, core)
    found = jnp.full_like(lane, -1)
    for slot in range(list_ref.shape[1]):
        name = jnp.where(slot < count_ref[...], list_ref[:, slot : slot + 1], -1)
        found = jnp.where(name == block, slot, found)
    table_ref[...] = jnp.where(lane < len(origins), found, -1)


def slot_table(loop_size, origins, block_list, live_count):
    return pl.pallas_call(
        functools.partial(table_kernel, loop_size, origins),
        out_shape=jax.ShapeDtypeStruct((1, 128), jnp.int32),
        in_specs=[pl.BlockSpec(memory_space=pltpu.VMEM)] * 2,
        out_specs=pl.BlockSpec(memory_space=pltpu.VMEM),
        compiler_params=pltpu.CompilerParams(vmem_limit_bytes=16 * 1024 * 1024),
        cost_estimate=pl.CostEstimate(flops=2**32, bytes_accessed=1024, transcendentals=0),
        name="slot_table",
    )(block_list, live_count.reshape(1, 1))


def add_block(grad_ref, parts_ref, block, labels):
    rows = grad_ref.shape[0]
    tile = labels[0].shape[1]
    upper, lower = [], []
    for at in range(0, len(labels), 2):
        some = jnp.concatenate(labels[at : at + 2], 1)
        both = lax.dot_general(
            parts_ref[...],
            block[at * tile : at * tile + some.shape[1]],
            (((1,), (1,)), ((), ())),
            preferred_element_type=jnp.float32,
        )
        residual = 0.5 * jnp.tanh(both[:rows] + both[rows:]) + (0.5 - some.astype(jnp.float32))
        upper.append(residual.astype(jnp.bfloat16))
        lower.append((residual - upper[-1].astype(jnp.float32)).astype(jnp.bfloat16))
    grad_ref[...] += jnp.dot(
        jnp.concatenate(upper + lower, 1),
        jnp.concatenate([block, block], 0),
        preferred_element_type=jnp.float32,
    )


def add_tiles(grad_ref, parts_ref, tiles, live, labels_at):
    tile = tiles.shape[0] // CHUNK
    fours = (live + 1) // 4

    @pl.when(live % 4 == 3)
    def _():
        blank = pl.multiple_of(live * tile, tile)
        tiles[pl.ds(blank, tile), :] = jnp.zeros((tile, tiles.shape[1]), tiles.dtype)

    def add(count, index, carry):
        start = index * count
        block = tiles[pl.ds(pl.multiple_of(start * tile, tile), count * tile), :]
        add_block(grad_ref, parts_ref, block, [labels_at(start + at) for at in range(count)])
        return carry

    lax.fori_loop(0, fours, functools.partial(add, 4), 0)
    pl.when(live - 4 * fours == 2)(lambda: add(2, 2 * fours, None))
    pl.when(live - 4 * fours == 1)(lambda: add(1, 4 * fours, None))


def store_square(grad_ref, square_ref):
    gradient = grad_ref[...]
    square = jnp.sum(gradient * gradient, axis=0, keepdims=True)
    square = sum(square[:, at : at + 128] for at in range(0, square.shape[1], 128))
    square_ref[...] = jnp.broadcast_to(square, square_ref.shape)


def core_and_position(loop_size):
    me = lax.axis_index("loop")
    core, row, outer = me % 2, me // 2 % 2, me // 4
    return core, jnp.where(row == 0, outer, loop_size // 2 - 1 - outer)


def pack_kernel(*refs):
    tile = refs[0].shape[0]
    for at, ref in enumerate(refs[:-1]):
        refs[-1][at * tile : (at + 1) * tile, :] = ref[...]


def pack(arrays):
    tile, width = arrays[0].shape
    return pl.pallas_call(
        pack_kernel,
        out_shape=jax.ShapeDtypeStruct((len(arrays) * tile, width), arrays[0].dtype),
        in_specs=[pl.BlockSpec(memory_space=pltpu.VMEM)] * len(arrays),
        out_specs=pl.BlockSpec(memory_space=pltpu.VMEM),
        compiler_params=pltpu.CompilerParams(vmem_limit_bytes=16 * 1024 * 1024),
        cost_estimate=pl.CostEstimate(
            flops=2**34, bytes_accessed=4 * len(arrays) * tile * width, transcendentals=0
        ),
        name="pack",
    )(*arrays)


def pieces_kernel(places, count, packed, loop_size, first, last, table_ref, given_ref, labels_ref, *rest):
    rest = list(rest)
    arrays = [rest.pop(0) for _ in range(count)]
    if not first:
        rest.pop(0)
    grad_ref = rest.pop(0)
    parts_ref = rest.pop(0) if first else given_ref
    across_ref = rest.pop(0) if first else None
    pack_ref = rest.pop(0) if packed else None
    square_ref = rest.pop(0) if last else None
    tiles, slots = rest
    tile = tiles.shape[0] // CHUNK
    for at, index in enumerate(packed):
        pack_ref[at * tile : (at + 1) * tile, :] = arrays[index][...]
    if first:
        core, position = core_and_position(loop_size)
        for at in range(2):

            @pl.when((core + position) % 2 == at)
            def _():
                across_ref[...] = arrays[1 + at][...]

        parts_ref[...] = halves(0.5 * given_ref[...])
        grad_ref[...] = jnp.zeros_like(grad_ref)
    table = table_ref[...]
    entries = [table[0, at] for at, _, _ in places]

    def labels_of(slot):
        return labels_ref[:, pl.ds(pl.multiple_of(slot * tile, tile), tile)]

    live = jnp.int32(0)
    for found, (_, index, row) in zip(entries, places):

        @pl.when(found >= 0)
        def _():
            into = pl.ds(pl.multiple_of(live * tile, tile), tile)
            tiles[into, :] = arrays[index][row * tile : (row + 1) * tile, :]
            slots[live] = found

        live = live + (found >= 0).astype(jnp.int32)
    slots[live] = 0
    add_tiles(grad_ref, parts_ref, tiles, live, lambda position: labels_of(slots[position]))
    if last:
        store_square(grad_ref, square_ref)


def add_pieces(held, packed, loop_size, table, given, labels, before, last):
    first = before is None
    width = given.shape[1]
    rows = given.shape[0] // (1 if first else 2)
    arrays = [array for array, _ in held]
    tile = labels.shape[1] // CHUNK
    places = [(at, index, row) for index, (_, entries) in enumerate(held) for row, at in enumerate(entries)]
    most = min(len(places), CHUNK)
    out_shape = [jax.ShapeDtypeStruct((rows, width), jnp.float32)]
    if first:
        out_shape.append(jax.ShapeDtypeStruct((2 * rows, width), jnp.bfloat16))
        out_shape.append(jax.ShapeDtypeStruct((tile, width), jnp.bfloat16))
    if packed:
        out_shape.append(jax.ShapeDtypeStruct((len(packed) * tile, width), jnp.bfloat16))
    if last:
        out_shape.append(jax.ShapeDtypeStruct((8 * loop_size, 128), jnp.float32))
    extra = [] if first else [before]
    return pl.pallas_call(
        functools.partial(pieces_kernel, places, len(arrays), packed, loop_size, first, last),
        out_shape=out_shape,
        in_specs=[pl.BlockSpec(memory_space=pltpu.VMEM)] * (3 + len(arrays) + len(extra)),
        out_specs=[pl.BlockSpec(memory_space=pltpu.VMEM)] * len(out_shape),
        input_output_aliases={} if first else {3 + len(arrays): 0},
        scratch_shapes=[
            pltpu.VMEM((CHUNK * tile, width), jnp.bfloat16),
            pltpu.SMEM((CHUNK + 1,), jnp.int32),
        ],
        compiler_params=pltpu.CompilerParams(vmem_limit_bytes=24 * 1024 * 1024),
        cost_estimate=pl.CostEstimate(
            flops=128 * rows * width * most * tile,
            bytes_accessed=8 * rows * width,
            transcendentals=rows * most * tile,
        ),
        name="add_pieces",
    )(table, given, labels, *arrays, *extra)


def ring_gradient(users, items, lists, labels):
    loop_size = lax.axis_size("loop")
    far = loop_size // 4
    origins = [(hops, 0) for hops in range(1 - far, far + 1)]
    origins += [(-hops, 1) for hops, _ in origins]
    table = slot_table(loop_size, origins, *lists)
    where = {origin: at for at, origin in enumerate(origins)}

    def held(hops, array):
        return array, [where[hops, 0]]

    def other(arrays, hops):
        return to_other_core(arrays, loop_size), [where[-hop, 1] for hop in hops]

    up = to_next(items, 1, loop_size)
    down = to_next(items, -1, loop_size)
    up, table = lax.optimization_barrier((up, table))
    first = [held(0, items), held(1, up), held(-1, down)]
    second = [held(2, to_next(up, 1, loop_size)), held(-2, to_next(down, -1, loop_size))]
    gradient, parts, opposite, packed = add_pieces(
        first, [0, 1, 2], loop_size, table, users, labels, None, False
    )
    opposite = across(opposite, loop_size)
    first = other(packed, [0, 1, -1])
    third = [held(3, to_next(second[0][0], 1, loop_size)), held(-3, to_next(second[1][0], -1, loop_size))]
    gradient, packed = add_pieces(second, [0, 1], loop_size, table, parts, labels, gradient, False)
    second = other(packed, [2, -2])
    third.append(held(4, opposite))
    arrived, gradient = lax.optimization_barrier(([array for array, _ in third], gradient))
    final = other(pack(arrived), [3, -3, 4])
    (gradient,) = add_pieces(
        third + [first, second], [], loop_size, table, parts, labels, gradient, False
    )
    return *add_pieces([final], [], loop_size, table, parts, labels, gradient, True), users


def chunks_kernel(
    list_ref, count_ref, users_ref, labels_ref, items_ref, grad_ref, square_ref, tiles, parts_ref, sems
):
    tile = tiles.shape[0] // CHUNK
    step = pl.program_id(0)
    live = jnp.clip(count_ref[0] - step * CHUNK, 0, CHUNK)

    @pl.when(step == 0)
    def _():
        parts_ref[...] = halves(0.5 * users_ref[...])
        grad_ref[...] = jnp.zeros_like(grad_ref)

    def move(slot):
        start = pl.multiple_of(list_ref[0, step * CHUNK + slot] * tile, tile)
        return pltpu.make_async_copy(
            items_ref.at[pl.ds(start, tile), :], tiles.at[pl.ds(slot * tile, tile), :], sems.at[slot]
        )

    for slot in range(CHUNK):
        pl.when(slot < live)(lambda slot=slot: move(slot).start())
    for slot in range(CHUNK):
        pl.when(slot < live)(lambda slot=slot: move(slot).wait())

    def labels_at(position):
        return labels_ref[:, pl.ds(pl.multiple_of(position * tile, tile), tile)]

    add_tiles(grad_ref, parts_ref, tiles, live, labels_at)

    @pl.when(step == pl.num_programs(0) - 1)
    def _():
        store_square(grad_ref, square_ref)


def add_chunks(loop_size, items, lists, users, labels):
    rows, width = users.shape
    slots = lists[0].shape[1]
    tile = labels.shape[1] // slots
    return pl.pallas_call(
        chunks_kernel,
        grid=(slots // CHUNK,),
        out_shape=[
            jax.ShapeDtypeStruct((rows, width), jnp.float32),
            jax.ShapeDtypeStruct((8 * loop_size, 128), jnp.float32),
        ],
        in_specs=[
            pl.BlockSpec(memory_space=pltpu.SMEM),
            pl.BlockSpec(memory_space=pltpu.SMEM),
            pl.BlockSpec((rows, width), lambda step: (0, 0)),
            pl.BlockSpec((rows, CHUNK * tile), lambda step: (0, step)),
            pl.BlockSpec(memory_space=pl.ANY),
        ],
        out_specs=[
            pl.BlockSpec((rows, width), lambda step: (0, 0)),
            pl.BlockSpec((8 * loop_size, 128), lambda step: (0, 0)),
        ],
        scratch_shapes=[
            pltpu.VMEM((CHUNK * tile, width), jnp.bfloat16),
            pltpu.VMEM((2 * rows, width), jnp.bfloat16),
            pltpu.SemaphoreType.DMA((CHUNK,)),
        ],
        compiler_params=pltpu.CompilerParams(vmem_limit_bytes=32 * 1024 * 1024),
        cost_estimate=pl.CostEstimate(
            flops=8 * rows * width * slots * tile,
            bytes_accessed=4 * rows * (slots * tile + 2 * width) + 2 * slots * tile * width,
            transcendentals=rows * slots * tile,
        ),
        name="add_chunks",
    )(*lists, users, labels, items)


def update_kernel(entries, users_ref, grad_ref, squares_ref, out_ref, result, sems):
    total = jnp.sum(squares_ref[...], axis=0, keepdims=True) / 8
    total = jnp.sum(total, axis=1, keepdims=True)
    scale = 0.5 / jnp.sqrt(total / entries + 1e-06)
    rows = users_ref.shape[0] // sems.shape[0]
    copies = []
    for at in range(sems.shape[0]):
        part = pl.ds(at * rows, rows)
        result[part, :] = users_ref[part, :] - scale * grad_ref[part, :]
        copies.append(pltpu.make_async_copy(result.at[part, :], out_ref.at[part, :], sems.at[at]))
        copies[-1].start()
    for copy in copies:
        copy.wait()


def local(users, items, tile_blocks, tile_count, labels):
    loop_size = lax.axis_size("loop")
    rows, width = users.shape
    slots = tile_blocks.shape[1]
    lists = (tile_blocks, tile_count)
    if loop_size == RING and slots == CHUNK:
        gradient, square, users = ring_gradient(users, items, lists, labels)
    else:
        whole = lax.all_gather(items, "loop", axis=0, tiled=True)
        gradient, square = add_chunks(loop_size, whole, lists, users, labels)

    squares = lax.all_to_all(square, "loop", 0, 0, tiled=True)
    return pl.pallas_call(
        functools.partial(update_kernel, rows * loop_size * width),
        out_shape=jax.ShapeDtypeStruct((rows, width), jnp.float32),
        in_specs=[pl.BlockSpec(memory_space=pltpu.VMEM)] * 3,
        out_specs=pl.BlockSpec(memory_space=pl.ANY),
        scratch_shapes=[pltpu.VMEM((rows, width), jnp.float32), pltpu.SemaphoreType.DMA((4,))],
        compiler_params=pltpu.CompilerParams(vmem_limit_bytes=16 * 1024 * 1024),
        cost_estimate=pl.CostEstimate(
            flops=2 * rows * width, bytes_accessed=12 * rows * width, transcendentals=0
        ),
        name="update",
    )(users, gradient, squares)


def solution(mesh):
    in_specs = (
        P(("group", "loop"), None),
        P(("group", "loop"), None),
        P(("group", "loop"), None),
        P(("group", "loop")),
        P(("group", "loop"), None),
    )
    out_specs = P(("group", "loop"), None)
    return jax.shard_map(local, mesh=mesh, in_specs=in_specs, out_specs=out_specs, check_vma=False)
```

```python
import functools

import jax
import jax.numpy as jnp
from jax import lax
from jax.experimental import pallas as pl
from jax.experimental.pallas import tpu as pltpu
from jax.sharding import PartitionSpec as P

CHUNK = 8
RING = 16


def ring_place(loop_size):
    outer = loop_size // 4

    def device(position, core):
        position = position % (2 * outer)
        chip = 2 * (outer - 1 - position) if position < outer else 2 * (position - outer) + 1
        return 2 * chip + core

    return 2 * outer, device


def to_next(array, direction, loop_size):
    chips, device = ring_place(loop_size)
    pairs = [(device(at, 0), device(at + direction, 0)) for at in range(chips)]
    pairs += [(device(at, 1), device(at - direction, 1)) for at in range(chips)]
    return lax.ppermute(array, "loop", pairs)


def across(array, loop_size):
    chips, device = ring_place(loop_size)
    pairs = [
        (device(at, core), device(at + (3 if at % 2 == 0 else -3), core))
        for at in range(chips)
        for core in range(2)
    ]
    return lax.ppermute(array, "loop", pairs)


def to_other_core(array, loop_size):
    return lax.ppermute(array, "loop", [(at, at ^ 1) for at in range(loop_size)])


def halves(values):
    upper = values.astype(jnp.bfloat16)
    return jnp.concatenate([upper, (values - upper.astype(jnp.float32)).astype(jnp.bfloat16)], 0)


def table_kernel(loop_size, origins, list_ref, count_ref, table_ref):
    chips = loop_size // 2
    lane = lax.broadcasted_iota(jnp.int32, table_ref.shape, 1)
    core, position = core_and_position(loop_size)
    hops, other = jnp.zeros_like(lane), jnp.zeros_like(lane)
    for at, origin in enumerate(origins):
        hops = jnp.where(lane == at, origin[0], hops)
        other = jnp.where(lane == at, origin[1], other)
    at = (position + chips + jnp.where(core == 0, -hops, hops)) & (chips - 1)
    chip = jnp.where(at < chips // 2, chips - 2 - 2 * at, 2 * at - chips + 1)
    block = 2 * chip + jnp.where(other == 1, 1 - core, core)
    found = jnp.full_like(lane, -1)
    for slot in range(list_ref.shape[1]):
        name = jnp.where(slot < count_ref[...], list_ref[:, slot : slot + 1], -1)
        found = jnp.where(name == block, slot, found)
    table_ref[...] = jnp.where(lane < len(origins), found, -1)


def slot_table(loop_size, origins, block_list, live_count):
    return pl.pallas_call(
        functools.partial(table_kernel, loop_size, origins),
        out_shape=jax.ShapeDtypeStruct((1, 128), jnp.int32),
        in_specs=[pl.BlockSpec(memory_space=pltpu.VMEM)] * 2,
        out_specs=pl.BlockSpec(memory_space=pltpu.VMEM),
        compiler_params=pltpu.CompilerParams(vmem_limit_bytes=16 * 1024 * 1024),
        cost_estimate=pl.CostEstimate(flops=2**32, bytes_accessed=1024, transcendentals=0),
        name="slot_table",
    )(block_list, live_count.reshape(1, 1))


def add_block(grad_ref, parts_ref, block, labels):
    rows = grad_ref.shape[0]
    tile = labels[0].shape[1]
    upper, lower = [], []
    for at in range(0, len(labels), 2):
        some = jnp.concatenate(labels[at : at + 2], 1)
        both = lax.dot_general(
            parts_ref[...],
            block[at * tile : at * tile + some.shape[1]],
            (((1,), (1,)), ((), ())),
            preferred_element_type=jnp.float32,
        )
        residual = 0.5 * jnp.tanh(both[:rows] + both[rows:]) + (0.5 - some.astype(jnp.float32))
        upper.append(residual.astype(jnp.bfloat16))
        lower.append((residual - upper[-1].astype(jnp.float32)).astype(jnp.bfloat16))
    grad_ref[...] += jnp.dot(
        jnp.concatenate(upper + lower, 1),
        jnp.concatenate([block, block], 0),
        preferred_element_type=jnp.float32,
    )


def add_tiles(grad_ref, parts_ref, tiles, live, labels_at):
    tile = tiles.shape[0] // CHUNK
    fours = (live + 1) // 4

    @pl.when(live % 4 == 3)
    def _():
        blank = pl.multiple_of(live * tile, tile)
        tiles[pl.ds(blank, tile), :] = jnp.zeros((tile, tiles.shape[1]), tiles.dtype)

    def add(count, index, carry):
        start = index * count
        block = tiles[pl.ds(pl.multiple_of(start * tile, tile), count * tile), :]
        add_block(grad_ref, parts_ref, block, [labels_at(start + at) for at in range(count)])
        return carry

    lax.fori_loop(0, fours, functools.partial(add, 4), 0)
    pl.when(live - 4 * fours == 2)(lambda: add(2, 2 * fours, None))
    pl.when(live - 4 * fours == 1)(lambda: add(1, 4 * fours, None))


def store_square(grad_ref, square_ref):
    gradient = grad_ref[...]
    square = jnp.sum(gradient * gradient, axis=0, keepdims=True)
    square = sum(square[:, at : at + 128] for at in range(0, square.shape[1], 128))
    square_ref[...] = jnp.broadcast_to(square, square_ref.shape)


def core_and_position(loop_size):
    me = lax.axis_index("loop")
    core, row, outer = me % 2, me // 2 % 2, me // 4
    return core, loop_size // 4 + jnp.where(row == 0, -1 - outer, outer)


def pack_kernel(loop_size, *refs):
    tile = refs[0].shape[0]
    sources = refs[:-1] if loop_size is None else (refs[0], refs[2])
    packed_ref = refs[-1] if loop_size is None else refs[-2]
    if loop_size is not None:
        core, position = core_and_position(loop_size)
        for at in range(2):

            @pl.when((core + position) % 2 == at)
            def _():
                refs[-1][...] = refs[1 + at][...]

    for at, ref in enumerate(sources):
        packed_ref[at * tile : (at + 1) * tile, :] = ref[...]


def pack(arrays, loop_size=None):
    tile, width = arrays[0].shape
    shapes = [(len(arrays) * tile, width)] if loop_size is None else [(2 * tile, width), (tile, width)]
    return pl.pallas_call(
        functools.partial(pack_kernel, loop_size),
        out_shape=[jax.ShapeDtypeStruct(shape, arrays[0].dtype) for shape in shapes],
        in_specs=[pl.BlockSpec(memory_space=pltpu.VMEM)] * len(arrays),
        out_specs=[pl.BlockSpec(memory_space=pltpu.VMEM)] * len(shapes),
        compiler_params=pltpu.CompilerParams(vmem_limit_bytes=16 * 1024 * 1024),
        cost_estimate=pl.CostEstimate(
            flops=2**34 if loop_size is None else 2**32,
            bytes_accessed=4 * len(arrays) * tile * width,
            transcendentals=0,
        ),
        name="pack",
    )(*arrays)


def pieces_kernel(places, count, packed, first, last, table_ref, given_ref, labels_ref, *rest):
    rest = list(rest)
    arrays = [rest.pop(0) for _ in range(count)]
    if not first:
        rest.pop(0)
    grad_ref = rest.pop(0)
    parts_ref = rest.pop(0) if first else given_ref
    pack_ref = rest.pop(0) if packed else None
    square_ref = rest.pop(0) if last else None
    tiles, slots = rest
    tile = tiles.shape[0] // CHUNK
    for at, index in enumerate(packed):
        pack_ref[at * tile : (at + 1) * tile, :] = arrays[index][...]
    if first:
        parts_ref[...] = halves(0.5 * given_ref[...])
        grad_ref[...] = jnp.zeros_like(grad_ref)
    table = table_ref[...]
    entries = [table[0, at] for at, _, _ in places]

    def labels_of(slot):
        return labels_ref[:, pl.ds(pl.multiple_of(slot * tile, tile), tile)]

    live = jnp.int32(0)
    for found, (_, index, row) in zip(entries, places):

        @pl.when(found >= 0)
        def _():
            into = pl.ds(pl.multiple_of(live * tile, tile), tile)
            tiles[into, :] = arrays[index][row * tile : (row + 1) * tile, :]
            slots[live] = found

        live = live + (found >= 0).astype(jnp.int32)
    slots[live] = 0
    add_tiles(grad_ref, parts_ref, tiles, live, lambda position: labels_of(slots[position]))
    if last:
        store_square(grad_ref, square_ref)


def add_pieces(held, packed, loop_size, table, given, labels, before, last):
    first = before is None
    width = given.shape[1]
    rows = given.shape[0] // (1 if first else 2)
    arrays = [array for array, _ in held]
    tile = labels.shape[1] // CHUNK
    places = [(at, index, row) for index, (_, entries) in enumerate(held) for row, at in enumerate(entries)]
    most = min(len(places), CHUNK)
    out_shape = [jax.ShapeDtypeStruct((rows, width), jnp.float32)]
    if first:
        out_shape.append(jax.ShapeDtypeStruct((2 * rows, width), jnp.bfloat16))
    if packed:
        out_shape.append(jax.ShapeDtypeStruct((len(packed) * tile, width), jnp.bfloat16))
    if last:
        out_shape.append(jax.ShapeDtypeStruct((loop_size, 128), jnp.float32))
    extra = [] if first else [before]
    return pl.pallas_call(
        functools.partial(pieces_kernel, places, len(arrays), packed, first, last),
        out_shape=out_shape,
        in_specs=[pl.BlockSpec(memory_space=pltpu.VMEM)] * (3 + len(arrays) + len(extra)),
        out_specs=[pl.BlockSpec(memory_space=pltpu.VMEM)] * len(out_shape),
        input_output_aliases={} if first else {3 + len(arrays): 0},
        scratch_shapes=[
            pltpu.VMEM((CHUNK * tile, width), jnp.bfloat16),
            pltpu.SMEM((CHUNK + 1,), jnp.int32),
        ],
        compiler_params=pltpu.CompilerParams(vmem_limit_bytes=24 * 1024 * 1024),
        cost_estimate=pl.CostEstimate(
            flops=(8 if first else 128) * rows * width * most * tile,
            bytes_accessed=8 * rows * width,
            transcendentals=rows * most * tile,
        ),
        name="add_pieces",
    )(table, given, labels, *arrays, *extra)


def ring_gradient(users, items, lists, labels):
    loop_size = lax.axis_size("loop")
    far = loop_size // 4
    origins = [(hops, 0) for hops in range(1 - far, far + 1)]
    origins += [(-hops, 1) for hops, _ in origins]
    table = slot_table(loop_size, origins, *lists)
    where = {origin: at for at, origin in enumerate(origins)}

    def held(hops, array):
        return array, [where[hops, 0]]

    def other(arrays, hops):
        return to_other_core(arrays, loop_size), [where[-hop, 1] for hop in hops]

    up = to_next(items, 1, loop_size)
    down = to_next(items, -1, loop_size)
    up, table = lax.optimization_barrier((up, table))
    first = [held(0, items), held(1, up), held(-1, down)]
    second = [held(2, to_next(up, 1, loop_size)), held(-2, to_next(down, -1, loop_size))]
    first.append(other(up, [1]))
    packed, opposite = pack([items, up, down], loop_size)
    opposite = across(opposite, loop_size)
    gradient, parts = add_pieces(first, [], loop_size, table, users, labels, None, False)
    first = other(packed, [0, -1])
    third = [held(3, to_next(second[0][0], 1, loop_size)), held(-3, to_next(second[1][0], -1, loop_size))]
    gradient, packed = add_pieces(second, [0, 1], loop_size, table, parts, labels, gradient, False)
    second = other(packed, [2, -2])
    third.append(held(4, opposite))
    arrived, gradient = lax.optimization_barrier(([array for array, _ in third], gradient))
    final = other(pack(arrived)[0], [3, -3, 4])
    (gradient,) = add_pieces(
        third + [first, second], [], loop_size, table, parts, labels, gradient, False
    )
    return *add_pieces([final], [], loop_size, table, parts, labels, gradient, True), users


def chunks_kernel(
    list_ref, count_ref, users_ref, labels_ref, items_ref, grad_ref, square_ref, tiles, parts_ref, sems
):
    tile = tiles.shape[0] // CHUNK
    step = pl.program_id(0)
    live = jnp.clip(count_ref[0] - step * CHUNK, 0, CHUNK)

    @pl.when(step == 0)
    def _():
        parts_ref[...] = halves(0.5 * users_ref[...])
        grad_ref[...] = jnp.zeros_like(grad_ref)

    def move(slot):
        start = pl.multiple_of(list_ref[0, step * CHUNK + slot] * tile, tile)
        return pltpu.make_async_copy(
            items_ref.at[pl.ds(start, tile), :], tiles.at[pl.ds(slot * tile, tile), :], sems.at[slot]
        )

    for slot in range(CHUNK):
        pl.when(slot < live)(lambda slot=slot: move(slot).start())
    for slot in range(CHUNK):
        pl.when(slot < live)(lambda slot=slot: move(slot).wait())

    def labels_at(position):
        return labels_ref[:, pl.ds(pl.multiple_of(position * tile, tile), tile)]

    add_tiles(grad_ref, parts_ref, tiles, live, labels_at)

    @pl.when(step == pl.num_programs(0) - 1)
    def _():
        store_square(grad_ref, square_ref)


def add_chunks(loop_size, items, lists, users, labels):
    rows, width = users.shape
    slots = lists[0].shape[1]
    tile = labels.shape[1] // slots
    return pl.pallas_call(
        chunks_kernel,
        grid=(slots // CHUNK,),
        out_shape=[
            jax.ShapeDtypeStruct((rows, width), jnp.float32),
            jax.ShapeDtypeStruct((loop_size, 128), jnp.float32),
        ],
        in_specs=[
            pl.BlockSpec(memory_space=pltpu.SMEM),
            pl.BlockSpec(memory_space=pltpu.SMEM),
            pl.BlockSpec((rows, width), lambda step: (0, 0)),
            pl.BlockSpec((rows, CHUNK * tile), lambda step: (0, step)),
            pl.BlockSpec(memory_space=pl.ANY),
        ],
        out_specs=[
            pl.BlockSpec((rows, width), lambda step: (0, 0)),
            pl.BlockSpec((loop_size, 128), lambda step: (0, 0)),
        ],
        scratch_shapes=[
            pltpu.VMEM((CHUNK * tile, width), jnp.bfloat16),
            pltpu.VMEM((2 * rows, width), jnp.bfloat16),
            pltpu.SemaphoreType.DMA((CHUNK,)),
        ],
        compiler_params=pltpu.CompilerParams(vmem_limit_bytes=32 * 1024 * 1024),
        cost_estimate=pl.CostEstimate(
            flops=8 * rows * width * slots * tile,
            bytes_accessed=4 * rows * (slots * tile + 2 * width) + 2 * slots * tile * width,
            transcendentals=rows * slots * tile,
        ),
        name="add_chunks",
    )(*lists, users, labels, items)


def update_kernel(entries, users_ref, grad_ref, squares_ref, out_ref, result, sems):
    total = jnp.sum(squares_ref[...], axis=0, keepdims=True)
    total = jnp.sum(total, axis=1, keepdims=True)
    scale = 0.5 / jnp.sqrt(total / entries + 1e-06)
    rows = users_ref.shape[0] // sems.shape[0]
    copies = []
    for at in range(sems.shape[0]):
        part = pl.ds(at * rows, rows)
        result[part, :] = users_ref[part, :] - scale * grad_ref[part, :]
        copies.append(pltpu.make_async_copy(result.at[part, :], out_ref.at[part, :], sems.at[at]))
        copies[-1].start()
    for copy in copies:
        copy.wait()


def local(users, items, tile_blocks, tile_count, labels):
    loop_size = lax.axis_size("loop")
    rows, width = users.shape
    slots = tile_blocks.shape[1]
    lists = (tile_blocks, tile_count)
    if loop_size == RING and slots == CHUNK:
        gradient, square, users = ring_gradient(users, items, lists, labels)
    else:
        whole = lax.all_gather(items, "loop", axis=0, tiled=True)
        gradient, square = add_chunks(loop_size, whole, lists, users, labels)

    squares = lax.all_to_all(square, "loop", 0, 0, tiled=True)
    return pl.pallas_call(
        functools.partial(update_kernel, rows * loop_size * width),
        out_shape=jax.ShapeDtypeStruct((rows, width), jnp.float32),
        in_specs=[pl.BlockSpec(memory_space=pltpu.VMEM)] * 3,
        out_specs=pl.BlockSpec(memory_space=pl.ANY),
        scratch_shapes=[pltpu.VMEM((rows, width), jnp.float32), pltpu.SemaphoreType.DMA((4,))],
        compiler_params=pltpu.CompilerParams(vmem_limit_bytes=16 * 1024 * 1024),
        cost_estimate=pl.CostEstimate(
            flops=2 * rows * width, bytes_accessed=12 * rows * width, transcendentals=0
        ),
        name="update",
    )(users, gradient, squares)


def solution(mesh):
    in_specs = (
        P(("group", "loop"), None),
        P(("group", "loop"), None),
        P(("group", "loop"), None),
        P(("group", "loop")),
        P(("group", "loop"), None),
    )
    out_specs = P(("group", "loop"), None)
    return jax.shard_map(local, mesh=mesh, in_specs=in_specs, out_specs=out_specs, check_vma=False)
```

```python
import functools

import jax
import jax.numpy as jnp
from jax import lax
from jax.experimental import pallas as pl
from jax.experimental.pallas import tpu as pltpu
from jax.sharding import PartitionSpec as P

CHUNK = 8
RING = 16


def ring_place(loop_size):
    outer = loop_size // 4

    def device(position, core):
        position = position % (2 * outer)
        chip = 2 * position if position < outer else 2 * (2 * outer - 1 - position) + 1
        return 2 * chip + core

    return 2 * outer, device


def to_next(array, direction, loop_size):
    chips, device = ring_place(loop_size)
    pairs = [(device(at, 0), device(at + direction, 0)) for at in range(chips)]
    pairs += [(device(at, 1), device(at - direction, 1)) for at in range(chips)]
    return lax.ppermute(array, "loop", pairs)


def across(array, loop_size):
    chips, device = ring_place(loop_size)
    pairs = [
        (device(at, core), device(at + (3 if at % 2 == 0 else -3), core))
        for at in range(chips)
        for core in range(2)
    ]
    return lax.ppermute(array, "loop", pairs)


def to_other_core(array, loop_size):
    return lax.ppermute(array, "loop", [(at, at ^ 1) for at in range(loop_size)])


def halves(values):
    upper = values.astype(jnp.bfloat16)
    return jnp.concatenate([upper, (values - upper.astype(jnp.float32)).astype(jnp.bfloat16)], 0)


def table_kernel(loop_size, origins, list_ref, count_ref, table_ref):
    chips = loop_size // 2
    lane = lax.broadcasted_iota(jnp.int32, table_ref.shape, 1)
    core, position = core_and_position(loop_size)
    hops, other = jnp.zeros_like(lane), jnp.zeros_like(lane)
    for at, origin in enumerate(origins):
        hops = jnp.where(lane == at, origin[0], hops)
        other = jnp.where(lane == at, origin[1], other)
    at = (position + chips + jnp.where(core == 0, -hops, hops)) & (chips - 1)
    chip = jnp.where(at < chips // 2, 2 * at, 2 * (chips - 1 - at) + 1)
    block = 2 * chip + jnp.where(other == 1, 1 - core, core)
    found = jnp.full_like(lane, -1)
    for slot in range(list_ref.shape[1]):
        name = jnp.where(slot < count_ref[...], list_ref[:, slot : slot + 1], -1)
        found = jnp.where(name == block, slot, found)
    table_ref[...] = jnp.where(lane < len(origins), found, -1)


def slot_table(loop_size, origins, block_list, live_count):
    return pl.pallas_call(
        functools.partial(table_kernel, loop_size, origins),
        out_shape=jax.ShapeDtypeStruct((1, 128), jnp.int32),
        in_specs=[pl.BlockSpec(memory_space=pltpu.VMEM)] * 2,
        out_specs=pl.BlockSpec(memory_space=pltpu.VMEM),
        compiler_params=pltpu.CompilerParams(vmem_limit_bytes=16 * 1024 * 1024),
        cost_estimate=pl.CostEstimate(flops=2**32, bytes_accessed=1024, transcendentals=0),
        name="slot_table",
    )(block_list, live_count.reshape(1, 1))


def add_block(grad_ref, parts_ref, block, labels):
    rows = grad_ref.shape[0]
    half = rows // 2
    tile = labels[0].shape[1]
    for start in range(0, rows, half):
        both_parts = jnp.concatenate(
            [parts_ref[start : start + half, :], parts_ref[rows + start : rows + start + half, :]], 0
        )
        upper, lower = [], []
        for at in range(0, len(labels), 2):
            some = jnp.concatenate([each[start : start + half] for each in labels[at : at + 2]], 1)
            both = lax.dot_general(
                both_parts,
                block[at * tile : at * tile + some.shape[1]],
                (((1,), (1,)), ((), ())),
                preferred_element_type=jnp.float32,
            )
            residual = 0.5 * jnp.tanh(both[:half] + both[half:]) + (0.5 - some.astype(jnp.float32))
            upper.append(residual.astype(jnp.bfloat16))
            lower.append((residual - upper[-1].astype(jnp.float32)).astype(jnp.bfloat16))
        grad_ref[start : start + half, :] += jnp.dot(
            jnp.concatenate(upper + lower, 1),
            jnp.concatenate([block, block], 0),
            preferred_element_type=jnp.float32,
        )


def add_tiles(grad_ref, parts_ref, tiles, live, labels_at):
    tile = tiles.shape[0] // CHUNK
    fours = (live + 1) // 4

    @pl.when(live % 4 == 3)
    def _():
        blank = pl.multiple_of(live * tile, tile)
        tiles[pl.ds(blank, tile), :] = jnp.zeros((tile, tiles.shape[1]), tiles.dtype)

    def add(count, index, carry):
        start = index * count
        block = tiles[pl.ds(pl.multiple_of(start * tile, tile), count * tile), :]
        add_block(grad_ref, parts_ref, block, [labels_at(start + at) for at in range(count)])
        return carry

    lax.fori_loop(0, fours, functools.partial(add, 4), 0)
    pl.when(live - 4 * fours == 2)(lambda: add(2, 2 * fours, None))
    pl.when(live - 4 * fours == 1)(lambda: add(1, 4 * fours, None))


def store_square(grad_ref, square_ref):
    gradient = grad_ref[...]
    square = jnp.sum(gradient * gradient, axis=0, keepdims=True)
    square = sum(square[:, at : at + 128] for at in range(0, square.shape[1], 128))
    square_ref[...] = jnp.broadcast_to(square, square_ref.shape)


def core_and_position(loop_size):
    me = lax.axis_index("loop")
    core, row, outer = me % 2, me // 2 % 2, me // 4
    return core, jnp.where(row == 0, outer, loop_size // 2 - 1 - outer)


def pack_kernel(loop_size, *refs):
    tile = refs[0].shape[0]
    sources = refs[:-1] if loop_size is None else (refs[0], refs[2])
    packed_ref = refs[-1] if loop_size is None else refs[-2]
    if loop_size is not None:
        core, position = core_and_position(loop_size)
        for at in range(2):

            @pl.when((core + position) % 2 == at)
            def _():
                refs[-1][...] = refs[1 + at][...]

    for at, ref in enumerate(sources):
        packed_ref[at * tile : (at + 1) * tile, :] = ref[...]


def pack(arrays, loop_size=None):
    tile, width = arrays[0].shape
    shapes = [(len(arrays) * tile, width)] if loop_size is None else [(2 * tile, width), (tile, width)]
    return pl.pallas_call(
        functools.partial(pack_kernel, loop_size),
        out_shape=[jax.ShapeDtypeStruct(shape, arrays[0].dtype) for shape in shapes],
        in_specs=[pl.BlockSpec(memory_space=pltpu.VMEM)] * len(arrays),
        out_specs=[pl.BlockSpec(memory_space=pltpu.VMEM)] * len(shapes),
        compiler_params=pltpu.CompilerParams(vmem_limit_bytes=16 * 1024 * 1024),
        cost_estimate=pl.CostEstimate(
            flops=2**34 if loop_size is None else 2**32,
            bytes_accessed=4 * len(arrays) * tile * width,
            transcendentals=0,
        ),
        name="pack",
    )(*arrays)


def pieces_kernel(places, count, packed, first, last, table_ref, given_ref, labels_ref, *rest):
    rest = list(rest)
    arrays = [rest.pop(0) for _ in range(count)]
    if not first:
        rest.pop(0)
    grad_ref = rest.pop(0)
    parts_ref = rest.pop(0) if first else given_ref
    pack_ref = rest.pop(0) if packed else None
    square_ref = rest.pop(0) if last else None
    tiles, slots = rest
    tile = tiles.shape[0] // CHUNK
    for at, index in enumerate(packed):
        pack_ref[at * tile : (at + 1) * tile, :] = arrays[index][...]
    if first:
        parts_ref[...] = halves(0.5 * given_ref[...])
        grad_ref[...] = jnp.zeros_like(grad_ref)
    table = table_ref[...]
    entries = [table[0, at] for at, _, _ in places]

    def labels_of(slot):
        return labels_ref[:, pl.ds(pl.multiple_of(slot * tile, tile), tile)]

    live = jnp.int32(0)
    for found, (_, index, row) in zip(entries, places):

        @pl.when(found >= 0)
        def _():
            into = pl.ds(pl.multiple_of(live * tile, tile), tile)
            tiles[into, :] = arrays[index][row * tile : (row + 1) * tile, :]
            slots[live] = found

        live = live + (found >= 0).astype(jnp.int32)
    slots[live] = 0
    add_tiles(grad_ref, parts_ref, tiles, live, lambda position: labels_of(slots[position]))
    if last:
        store_square(grad_ref, square_ref)


def add_pieces(held, packed, loop_size, table, given, labels, before, last):
    first = before is None
    width = given.shape[1]
    rows = given.shape[0] // (1 if first else 2)
    arrays = [array for array, _ in held]
    tile = labels.shape[1] // CHUNK
    places = [(at, index, row) for index, (_, entries) in enumerate(held) for row, at in enumerate(entries)]
    most = min(len(places), CHUNK)
    out_shape = [jax.ShapeDtypeStruct((rows, width), jnp.float32)]
    if first:
        out_shape.append(jax.ShapeDtypeStruct((2 * rows, width), jnp.bfloat16))
    if packed:
        out_shape.append(jax.ShapeDtypeStruct((len(packed) * tile, width), jnp.bfloat16))
    if last:
        out_shape.append(jax.ShapeDtypeStruct((loop_size, 128), jnp.float32))
    extra = [] if first else [before]
    return pl.pallas_call(
        functools.partial(pieces_kernel, places, len(arrays), packed, first, last),
        out_shape=out_shape,
        in_specs=[pl.BlockSpec(memory_space=pltpu.VMEM)] * (3 + len(arrays) + len(extra)),
        out_specs=[pl.BlockSpec(memory_space=pltpu.VMEM)] * len(out_shape),
        input_output_aliases={} if first else {3 + len(arrays): 0},
        scratch_shapes=[
            pltpu.VMEM((CHUNK * tile, width), jnp.bfloat16),
            pltpu.SMEM((CHUNK + 1,), jnp.int32),
        ],
        compiler_params=pltpu.CompilerParams(vmem_limit_bytes=24 * 1024 * 1024),
        cost_estimate=pl.CostEstimate(
            flops=(8 if first else 128) * rows * width * most * tile,
            bytes_accessed=8 * rows * width,
            transcendentals=rows * most * tile,
        ),
        name="add_pieces",
    )(table, given, labels, *arrays, *extra)


def ring_gradient(users, items, lists, labels):
    loop_size = lax.axis_size("loop")
    far = loop_size // 4
    origins = [(hops, 0) for hops in range(1 - far, far + 1)]
    origins += [(-hops, 1) for hops, _ in origins]
    table = slot_table(loop_size, origins, *lists)
    where = {origin: at for at, origin in enumerate(origins)}

    def held(hops, array):
        return array, [where[hops, 0]]

    def other(arrays, hops):
        return to_other_core(arrays, loop_size), [where[-hop, 1] for hop in hops]

    up = to_next(items, 1, loop_size)
    down = to_next(items, -1, loop_size)
    up, table = lax.optimization_barrier((up, table))
    first = [held(0, items), held(1, up), held(-1, down)]
    second = [held(2, to_next(up, 1, loop_size)), held(-2, to_next(down, -1, loop_size))]
    first.append(other(up, [1]))
    packed, opposite = pack([items, up, down], loop_size)
    opposite = across(opposite, loop_size)
    gradient, parts = add_pieces(first, [], loop_size, table, users, labels, None, False)
    first = other(packed, [0, -1])
    third = [held(3, to_next(second[0][0], 1, loop_size)), held(-3, to_next(second[1][0], -1, loop_size))]
    gradient, packed = add_pieces(second, [0, 1], loop_size, table, parts, labels, gradient, False)
    second = other(packed, [2, -2])
    third.append(held(4, opposite))
    arrived, gradient = lax.optimization_barrier(([array for array, _ in third], gradient))
    final = other(pack(arrived)[0], [3, -3, 4])
    (gradient,) = add_pieces(
        third + [first, second], [], loop_size, table, parts, labels, gradient, False
    )
    return *add_pieces([final], [], loop_size, table, parts, labels, gradient, True), users


def chunks_kernel(
    list_ref, count_ref, users_ref, labels_ref, items_ref, grad_ref, square_ref, tiles, parts_ref, sems
):
    tile = tiles.shape[0] // CHUNK
    step = pl.program_id(0)
    live = jnp.clip(count_ref[0] - step * CHUNK, 0, CHUNK)

    @pl.when(step == 0)
    def _():
        parts_ref[...] = halves(0.5 * users_ref[...])
        grad_ref[...] = jnp.zeros_like(grad_ref)

    def move(slot):
        start = pl.multiple_of(list_ref[0, step * CHUNK + slot] * tile, tile)
        return pltpu.make_async_copy(
            items_ref.at[pl.ds(start, tile), :], tiles.at[pl.ds(slot * tile, tile), :], sems.at[slot]
        )

    for slot in range(CHUNK):
        pl.when(slot < live)(lambda slot=slot: move(slot).start())
    for slot in range(CHUNK):
        pl.when(slot < live)(lambda slot=slot: move(slot).wait())

    def labels_at(position):
        return labels_ref[:, pl.ds(pl.multiple_of(position * tile, tile), tile)]

    add_tiles(grad_ref, parts_ref, tiles, live, labels_at)

    @pl.when(step == pl.num_programs(0) - 1)
    def _():
        store_square(grad_ref, square_ref)


def add_chunks(loop_size, items, lists, users, labels):
    rows, width = users.shape
    slots = lists[0].shape[1]
    tile = labels.shape[1] // slots
    return pl.pallas_call(
        chunks_kernel,
        grid=(slots // CHUNK,),
        out_shape=[
            jax.ShapeDtypeStruct((rows, width), jnp.float32),
            jax.ShapeDtypeStruct((loop_size, 128), jnp.float32),
        ],
        in_specs=[
            pl.BlockSpec(memory_space=pltpu.SMEM),
            pl.BlockSpec(memory_space=pltpu.SMEM),
            pl.BlockSpec((rows, width), lambda step: (0, 0)),
            pl.BlockSpec((rows, CHUNK * tile), lambda step: (0, step)),
            pl.BlockSpec(memory_space=pl.ANY),
        ],
        out_specs=[
            pl.BlockSpec((rows, width), lambda step: (0, 0)),
            pl.BlockSpec((loop_size, 128), lambda step: (0, 0)),
        ],
        scratch_shapes=[
            pltpu.VMEM((CHUNK * tile, width), jnp.bfloat16),
            pltpu.VMEM((2 * rows, width), jnp.bfloat16),
            pltpu.SemaphoreType.DMA((CHUNK,)),
        ],
        compiler_params=pltpu.CompilerParams(vmem_limit_bytes=32 * 1024 * 1024),
        cost_estimate=pl.CostEstimate(
            flops=8 * rows * width * slots * tile,
            bytes_accessed=4 * rows * (slots * tile + 2 * width) + 2 * slots * tile * width,
            transcendentals=rows * slots * tile,
        ),
        name="add_chunks",
    )(*lists, users, labels, items)


def update_kernel(entries, users_ref, grad_ref, squares_ref, out_ref, result, sems):
    total = jnp.sum(squares_ref[...], axis=0, keepdims=True)
    total = jnp.sum(total, axis=1, keepdims=True)
    scale = 0.5 / jnp.sqrt(total / entries + 1e-06)
    rows = users_ref.shape[0] // sems.shape[0]
    copies = []
    for at in range(sems.shape[0]):
        part = pl.ds(at * rows, rows)
        result[part, :] = users_ref[part, :] - scale * grad_ref[part, :]
        copies.append(pltpu.make_async_copy(result.at[part, :], out_ref.at[part, :], sems.at[at]))
        copies[-1].start()
    for copy in copies:
        copy.wait()


def local(users, items, tile_blocks, tile_count, labels):
    loop_size = lax.axis_size("loop")
    rows, width = users.shape
    slots = tile_blocks.shape[1]
    lists = (tile_blocks, tile_count)
    if loop_size == RING and slots == CHUNK:
        gradient, square, users = ring_gradient(users, items, lists, labels)
    else:
        whole = lax.all_gather(items, "loop", axis=0, tiled=True)
        gradient, square = add_chunks(loop_size, whole, lists, users, labels)

    squares = lax.all_to_all(square, "loop", 0, 0, tiled=True)
    return pl.pallas_call(
        functools.partial(update_kernel, rows * loop_size * width),
        out_shape=jax.ShapeDtypeStruct((rows, width), jnp.float32),
        in_specs=[pl.BlockSpec(memory_space=pltpu.VMEM)] * 3,
        out_specs=pl.BlockSpec(memory_space=pl.ANY),
        scratch_shapes=[pltpu.VMEM((rows, width), jnp.float32), pltpu.SemaphoreType.DMA((4,))],
        compiler_params=pltpu.CompilerParams(vmem_limit_bytes=16 * 1024 * 1024),
        cost_estimate=pl.CostEstimate(
            flops=2 * rows * width, bytes_accessed=12 * rows * width, transcendentals=0
        ),
        name="update",
    )(users, gradient, squares)


def solution(mesh):
    in_specs = (
        P(("group", "loop"), None),
        P(("group", "loop"), None),
        P(("group", "loop"), None),
        P(("group", "loop")),
        P(("group", "loop"), None),
    )
    out_specs = P(("group", "loop"), None)
    return jax.shard_map(local, mesh=mesh, in_specs=in_specs, out_specs=out_specs, check_vma=False)
```

```python
import functools

import jax
import jax.numpy as jnp
from jax import lax
from jax.experimental import pallas as pl
from jax.experimental.pallas import tpu as pltpu
from jax.sharding import PartitionSpec as P

CHUNK = 8
RING = 16


def ring_place(loop_size):
    outer = loop_size // 4

    def device(position, core):
        position = position % (2 * outer)
        chip = 2 * position if position < outer else 2 * (2 * outer - 1 - position) + 1
        return 2 * chip + core

    return 2 * outer, device


def to_next(array, direction, loop_size):
    chips, device = ring_place(loop_size)
    pairs = [(device(at, 0), device(at + direction, 0)) for at in range(chips)]
    pairs += [(device(at, 1), device(at - direction, 1)) for at in range(chips)]
    return lax.ppermute(array, "loop", pairs)


def across(array, loop_size):
    chips, device = ring_place(loop_size)
    pairs = [
        (device(at, core), device(at + (3 if at % 2 == 0 else -3), core))
        for at in range(chips)
        for core in range(2)
    ]
    return lax.ppermute(array, "loop", pairs)


def to_other_core(array, loop_size):
    return lax.ppermute(array, "loop", [(at, at ^ 1) for at in range(loop_size)])


def halves(values):
    upper = values.astype(jnp.bfloat16)
    return jnp.concatenate([upper, (values - upper.astype(jnp.float32)).astype(jnp.bfloat16)], 1)


def table_kernel(loop_size, origins, list_ref, count_ref, table_ref):
    chips = loop_size // 2
    lane = lax.broadcasted_iota(jnp.int32, table_ref.shape, 1)
    core, position = core_and_position(loop_size)
    hops, other = jnp.zeros_like(lane), jnp.zeros_like(lane)
    for at, origin in enumerate(origins):
        hops = jnp.where(lane == at, origin[0], hops)
        other = jnp.where(lane == at, origin[1], other)
    at = (position + chips + jnp.where(core == 0, -hops, hops)) & (chips - 1)
    chip = jnp.where(at < chips // 2, 2 * at, 2 * (chips - 1 - at) + 1)
    block = 2 * chip + jnp.where(other == 1, 1 - core, core)
    found = jnp.full_like(lane, -1)
    for slot in range(list_ref.shape[1]):
        name = jnp.where(slot < count_ref[...], list_ref[:, slot : slot + 1], -1)
        found = jnp.where(name == block, slot, found)
    table_ref[...] = jnp.where(lane < len(origins), found, -1)


def slot_table(loop_size, origins, block_list, live_count):
    return pl.pallas_call(
        functools.partial(table_kernel, loop_size, origins),
        out_shape=jax.ShapeDtypeStruct((1, 128), jnp.int32),
        in_specs=[pl.BlockSpec(memory_space=pltpu.VMEM)] * 2,
        out_specs=pl.BlockSpec(memory_space=pltpu.VMEM),
        compiler_params=pltpu.CompilerParams(vmem_limit_bytes=16 * 1024 * 1024),
        cost_estimate=pl.CostEstimate(flops=2**32, bytes_accessed=1024, transcendentals=0),
        name="slot_table",
    )(block_list, live_count.reshape(1, 1))


def add_block(grad_ref, parts_ref, block, labels):
    tile = labels[0].shape[1]
    upper, lower = [], []
    for at in range(0, len(labels), 2):
        some = jnp.concatenate(labels[at : at + 2], 1)
        items = block[at * tile : at * tile + some.shape[1]]
        half_scores = lax.dot_general(
            parts_ref[...],
            jnp.concatenate([items, items], 1),
            (((1,), (1,)), ((), ())),
            preferred_element_type=jnp.float32,
        )
        residual = 0.5 * jnp.tanh(half_scores) + (0.5 - some.astype(jnp.float32))
        upper.append(residual.astype(jnp.bfloat16))
        lower.append((residual - upper[-1].astype(jnp.float32)).astype(jnp.bfloat16))
    grad_ref[...] += jnp.dot(
        jnp.concatenate(upper + lower, 1),
        jnp.concatenate([block, block], 0),
        preferred_element_type=jnp.float32,
    )


def add_tiles(grad_ref, parts_ref, tiles, live, labels_at):
    tile = tiles.shape[0] // CHUNK
    fours = (live + 1) // 4

    @pl.when(live % 4 == 3)
    def _():
        blank = pl.multiple_of(live * tile, tile)
        tiles[pl.ds(blank, tile), :] = jnp.zeros((tile, tiles.shape[1]), tiles.dtype)

    def add(count, index, carry):
        start = index * count
        block = tiles[pl.ds(pl.multiple_of(start * tile, tile), count * tile), :]
        add_block(grad_ref, parts_ref, block, [labels_at(start + at) for at in range(count)])
        return carry

    lax.fori_loop(0, fours, functools.partial(add, 4), 0)
    pl.when(live - 4 * fours == 2)(lambda: add(2, 2 * fours, None))
    pl.when(live - 4 * fours == 1)(lambda: add(1, 4 * fours, None))


def store_square(grad_ref, square_ref):
    gradient = grad_ref[...]
    square = jnp.sum(gradient * gradient, axis=0, keepdims=True)
    square = sum(square[:, at : at + 128] for at in range(0, square.shape[1], 128))
    square_ref[...] = jnp.broadcast_to(square, square_ref.shape)


def core_and_position(loop_size):
    me = lax.axis_index("loop")
    core, row, outer = me % 2, me // 2 % 2, me // 4
    return core, jnp.where(row == 0, outer, loop_size // 2 - 1 - outer)


def pack_kernel(loop_size, *refs):
    tile = refs[0].shape[0]
    sources = refs[:-1] if loop_size is None else (refs[0], refs[2])
    packed_ref = refs[-1] if loop_size is None else refs[-2]
    if loop_size is not None:
        core, position = core_and_position(loop_size)
        for at in range(2):

            @pl.when((core + position) % 2 == at)
            def _():
                refs[-1][...] = refs[1 + at][...]

    for at, ref in enumerate(sources):
        packed_ref[at * tile : (at + 1) * tile, :] = ref[...]


def pack(arrays, loop_size=None):
    tile, width = arrays[0].shape
    shapes = [(len(arrays) * tile, width)] if loop_size is None else [(2 * tile, width), (tile, width)]
    return pl.pallas_call(
        functools.partial(pack_kernel, loop_size),
        out_shape=[jax.ShapeDtypeStruct(shape, arrays[0].dtype) for shape in shapes],
        in_specs=[pl.BlockSpec(memory_space=pltpu.VMEM)] * len(arrays),
        out_specs=[pl.BlockSpec(memory_space=pltpu.VMEM)] * len(shapes),
        compiler_params=pltpu.CompilerParams(vmem_limit_bytes=16 * 1024 * 1024),
        cost_estimate=pl.CostEstimate(
            flops=2**34 if loop_size is None else 2**32,
            bytes_accessed=4 * len(arrays) * tile * width,
            transcendentals=0,
        ),
        name="pack",
    )(*arrays)


def pieces_kernel(places, count, packed, first, last, table_ref, given_ref, labels_ref, *rest):
    rest = list(rest)
    arrays = [rest.pop(0) for _ in range(count)]
    if not first:
        rest.pop(0)
    grad_ref = rest.pop(0)
    parts_ref = rest.pop(0) if first else given_ref
    pack_ref = rest.pop(0) if packed else None
    square_ref = rest.pop(0) if last else None
    tiles, slots = rest
    tile = tiles.shape[0] // CHUNK
    for at, index in enumerate(packed):
        pack_ref[at * tile : (at + 1) * tile, :] = arrays[index][...]
    if first:
        parts_ref[...] = halves(0.5 * given_ref[...])
        grad_ref[...] = jnp.zeros_like(grad_ref)
    table = table_ref[...]
    entries = [table[0, at] for at, _, _ in places]

    def labels_of(slot):
        return labels_ref[:, pl.ds(pl.multiple_of(slot * tile, tile), tile)]

    live = jnp.int32(0)
    for found, (_, index, row) in zip(entries, places):

        @pl.when(found >= 0)
        def _():
            into = pl.ds(pl.multiple_of(live * tile, tile), tile)
            tiles[into, :] = arrays[index][row * tile : (row + 1) * tile, :]
            slots[live] = found

        live = live + (found >= 0).astype(jnp.int32)
    slots[live] = 0
    add_tiles(grad_ref, parts_ref, tiles, live, lambda position: labels_of(slots[position]))
    if last:
        store_square(grad_ref, square_ref)


def add_pieces(held, packed, loop_size, table, given, labels, before, last):
    first = before is None
    width = given.shape[1] // (1 if first else 2)
    rows = given.shape[0]
    arrays = [array for array, _ in held]
    tile = labels.shape[1] // CHUNK
    places = [(at, index, row) for index, (_, entries) in enumerate(held) for row, at in enumerate(entries)]
    most = min(len(places), CHUNK)
    out_shape = [jax.ShapeDtypeStruct((rows, width), jnp.float32)]
    if first:
        out_shape.append(jax.ShapeDtypeStruct((rows, 2 * width), jnp.bfloat16))
    if packed:
        out_shape.append(jax.ShapeDtypeStruct((len(packed) * tile, width), jnp.bfloat16))
    if last:
        out_shape.append(jax.ShapeDtypeStruct((loop_size, 128), jnp.float32))
    extra = [] if first else [before]
    return pl.pallas_call(
        functools.partial(pieces_kernel, places, len(arrays), packed, first, last),
        out_shape=out_shape,
        in_specs=[pl.BlockSpec(memory_space=pltpu.VMEM)] * (3 + len(arrays) + len(extra)),
        out_specs=[pl.BlockSpec(memory_space=pltpu.VMEM)] * len(out_shape),
        input_output_aliases={} if first else {3 + len(arrays): 0},
        scratch_shapes=[
            pltpu.VMEM((CHUNK * tile, width), jnp.bfloat16),
            pltpu.SMEM((CHUNK + 1,), jnp.int32),
        ],
        compiler_params=pltpu.CompilerParams(vmem_limit_bytes=24 * 1024 * 1024),
        cost_estimate=pl.CostEstimate(
            flops=(8 if first else 128) * rows * width * most * tile,
            bytes_accessed=8 * rows * width,
            transcendentals=rows * most * tile,
        ),
        name="add_pieces",
    )(table, given, labels, *arrays, *extra)


def ring_gradient(users, items, lists, labels):
    loop_size = lax.axis_size("loop")
    far = loop_size // 4
    origins = [(hops, 0) for hops in range(1 - far, far + 1)]
    origins += [(-hops, 1) for hops, _ in origins]
    table = slot_table(loop_size, origins, *lists)
    where = {origin: at for at, origin in enumerate(origins)}

    def held(hops, array):
        return array, [where[hops, 0]]

    def other(arrays, hops):
        return to_other_core(arrays, loop_size), [where[-hop, 1] for hop in hops]

    up = to_next(items, 1, loop_size)
    down = to_next(items, -1, loop_size)
    up, table = lax.optimization_barrier((up, table))
    first = [held(0, items), held(1, up), held(-1, down)]
    second = [held(2, to_next(up, 1, loop_size)), held(-2, to_next(down, -1, loop_size))]
    first.append(other(up, [1]))
    packed, opposite = pack([items, up, down], loop_size)
    opposite = across(opposite, loop_size)
    gradient, parts = add_pieces(first, [], loop_size, table, users, labels, None, False)
    first = other(packed, [0, -1])
    third = [held(3, to_next(second[0][0], 1, loop_size)), held(-3, to_next(second[1][0], -1, loop_size))]
    gradient, packed = add_pieces(second, [0, 1], loop_size, table, parts, labels, gradient, False)
    second = other(packed, [2, -2])
    third.append(held(4, opposite))
    arrived, gradient = lax.optimization_barrier(([array for array, _ in third], gradient))
    final = other(pack(arrived)[0], [3, -3, 4])
    (gradient,) = add_pieces(
        third + [first, second], [], loop_size, table, parts, labels, gradient, False
    )
    return *add_pieces([final], [], loop_size, table, parts, labels, gradient, True), users


def chunks_kernel(
    list_ref, count_ref, users_ref, labels_ref, items_ref, grad_ref, square_ref, tiles, parts_ref, sems
):
    tile = tiles.shape[0] // CHUNK
    step = pl.program_id(0)
    live = jnp.clip(count_ref[0] - step * CHUNK, 0, CHUNK)

    @pl.when(step == 0)
    def _():
        parts_ref[...] = halves(0.5 * users_ref[...])
        grad_ref[...] = jnp.zeros_like(grad_ref)

    def move(slot):
        start = pl.multiple_of(list_ref[0, step * CHUNK + slot] * tile, tile)
        return pltpu.make_async_copy(
            items_ref.at[pl.ds(start, tile), :], tiles.at[pl.ds(slot * tile, tile), :], sems.at[slot]
        )

    for slot in range(CHUNK):
        pl.when(slot < live)(lambda slot=slot: move(slot).start())
    for slot in range(CHUNK):
        pl.when(slot < live)(lambda slot=slot: move(slot).wait())

    def labels_at(position):
        return labels_ref[:, pl.ds(pl.multiple_of(position * tile, tile), tile)]

    add_tiles(grad_ref, parts_ref, tiles, live, labels_at)

    @pl.when(step == pl.num_programs(0) - 1)
    def _():
        store_square(grad_ref, square_ref)


def add_chunks(loop_size, items, lists, users, labels):
    rows, width = users.shape
    slots = lists[0].shape[1]
    tile = labels.shape[1] // slots
    return pl.pallas_call(
        chunks_kernel,
        grid=(slots // CHUNK,),
        out_shape=[
            jax.ShapeDtypeStruct((rows, width), jnp.float32),
            jax.ShapeDtypeStruct((loop_size, 128), jnp.float32),
        ],
        in_specs=[
            pl.BlockSpec(memory_space=pltpu.SMEM),
            pl.BlockSpec(memory_space=pltpu.SMEM),
            pl.BlockSpec((rows, width), lambda step: (0, 0)),
            pl.BlockSpec((rows, CHUNK * tile), lambda step: (0, step)),
            pl.BlockSpec(memory_space=pl.ANY),
        ],
        out_specs=[
            pl.BlockSpec((rows, width), lambda step: (0, 0)),
            pl.BlockSpec((loop_size, 128), lambda step: (0, 0)),
        ],
        scratch_shapes=[
            pltpu.VMEM((CHUNK * tile, width), jnp.bfloat16),
            pltpu.VMEM((rows, 2 * width), jnp.bfloat16),
            pltpu.SemaphoreType.DMA((CHUNK,)),
        ],
        compiler_params=pltpu.CompilerParams(vmem_limit_bytes=32 * 1024 * 1024),
        cost_estimate=pl.CostEstimate(
            flops=8 * rows * width * slots * tile,
            bytes_accessed=4 * rows * (slots * tile + 2 * width) + 2 * slots * tile * width,
            transcendentals=rows * slots * tile,
        ),
        name="add_chunks",
    )(*lists, users, labels, items)


def update_kernel(entries, users_ref, grad_ref, squares_ref, out_ref, result, sems):
    total = jnp.sum(squares_ref[...], axis=0, keepdims=True)
    total = jnp.sum(total, axis=1, keepdims=True)
    scale = 0.5 / jnp.sqrt(total / entries + 1e-06)
    rows = users_ref.shape[0] // sems.shape[0]
    copies = []
    for at in range(sems.shape[0]):
        part = pl.ds(at * rows, rows)
        result[part, :] = users_ref[part, :] - scale * grad_ref[part, :]
        copies.append(pltpu.make_async_copy(result.at[part, :], out_ref.at[part, :], sems.at[at]))
        copies[-1].start()
    for copy in copies:
        copy.wait()


def local(users, items, tile_blocks, tile_count, labels):
    loop_size = lax.axis_size("loop")
    rows, width = users.shape
    slots = tile_blocks.shape[1]
    lists = (tile_blocks, tile_count)
    if loop_size == RING and slots == CHUNK:
        gradient, square, users = ring_gradient(users, items, lists, labels)
    else:
        whole = lax.all_gather(items, "loop", axis=0, tiled=True)
        gradient, square = add_chunks(loop_size, whole, lists, users, labels)

    squares = lax.all_to_all(square, "loop", 0, 0, tiled=True)
    return pl.pallas_call(
        functools.partial(update_kernel, rows * loop_size * width),
        out_shape=jax.ShapeDtypeStruct((rows, width), jnp.float32),
        in_specs=[pl.BlockSpec(memory_space=pltpu.VMEM)] * 3,
        out_specs=pl.BlockSpec(memory_space=pl.ANY),
        scratch_shapes=[pltpu.VMEM((rows, width), jnp.float32), pltpu.SemaphoreType.DMA((4,))],
        compiler_params=pltpu.CompilerParams(vmem_limit_bytes=16 * 1024 * 1024),
        cost_estimate=pl.CostEstimate(
            flops=2 * rows * width, bytes_accessed=12 * rows * width, transcendentals=0
        ),
        name="update",
    )(users, gradient, squares)


def solution(mesh):
    in_specs = (
        P(("group", "loop"), None),
        P(("group", "loop"), None),
        P(("group", "loop"), None),
        P(("group", "loop")),
        P(("group", "loop"), None),
    )
    out_specs = P(("group", "loop"), None)
    return jax.shard_map(local, mesh=mesh, in_specs=in_specs, out_specs=out_specs, check_vma=False)
```

```python
import functools

import jax
import jax.numpy as jnp
from jax import lax
from jax.experimental import pallas as pl
from jax.experimental.pallas import tpu as pltpu
from jax.sharding import PartitionSpec as P

CHUNK = 8
RING = 16


def ring_place(loop_size):
    outer = loop_size // 4

    def device(position, core):
        position = position % (2 * outer)
        chip = 2 * position if position < outer else 2 * (2 * outer - 1 - position) + 1
        return 2 * chip + core

    return 2 * outer, device


def to_next(array, direction, loop_size):
    chips, device = ring_place(loop_size)
    pairs = [(device(at, 0), device(at + direction, 0)) for at in range(chips)]
    pairs += [(device(at, 1), device(at - direction, 1)) for at in range(chips)]
    return lax.ppermute(array, "loop", pairs)


def across(array, loop_size):
    chips, device = ring_place(loop_size)
    pairs = [
        (device(at, core), device(at + (3 if at % 2 == 0 else -3), core))
        for at in range(chips)
        for core in range(2)
    ]
    return lax.ppermute(array, "loop", pairs)


def to_other_core(array, loop_size):
    return lax.ppermute(array, "loop", [(at, at ^ 1) for at in range(loop_size)])


def halves(values):
    upper = values.astype(jnp.bfloat16)
    return jnp.concatenate([upper, (values - upper.astype(jnp.float32)).astype(jnp.bfloat16)], 1)


def table_kernel(loop_size, origins, list_ref, count_ref, table_ref):
    chips = loop_size // 2
    lane = lax.broadcasted_iota(jnp.int32, table_ref.shape, 1)
    core, position = core_and_position(loop_size)
    hops, other = jnp.zeros_like(lane), jnp.zeros_like(lane)
    for at, origin in enumerate(origins):
        hops = jnp.where(lane == at, origin[0], hops)
        other = jnp.where(lane == at, origin[1], other)
    at = (position + chips + jnp.where(core == 0, -hops, hops)) & (chips - 1)
    chip = jnp.where(at < chips // 2, 2 * at, 2 * (chips - 1 - at) + 1)
    block = 2 * chip + jnp.where(other == 1, 1 - core, core)
    found = jnp.full_like(lane, -1)
    for slot in range(list_ref.shape[1]):
        name = jnp.where(slot < count_ref[...], list_ref[:, slot : slot + 1], -1)
        found = jnp.where(name == block, slot, found)
    table_ref[...] = jnp.where(lane < len(origins), found, -1)


def slot_table(loop_size, origins, block_list, live_count):
    return pl.pallas_call(
        functools.partial(table_kernel, loop_size, origins),
        out_shape=jax.ShapeDtypeStruct((1, 128), jnp.int32),
        in_specs=[pl.BlockSpec(memory_space=pltpu.VMEM)] * 2,
        out_specs=pl.BlockSpec(memory_space=pltpu.VMEM),
        compiler_params=pltpu.CompilerParams(vmem_limit_bytes=16 * 1024 * 1024),
        cost_estimate=pl.CostEstimate(flops=2**32, bytes_accessed=1024, transcendentals=0),
        name="slot_table",
    )(block_list, live_count.reshape(1, 1))


def add_block(grad_ref, parts_ref, block, labels):
    tile = labels[0].shape[1]
    upper, lower = [], []
    for at in range(0, len(labels), 2):
        some = jnp.concatenate(labels[at : at + 2], 1)
        items = block[at * tile : at * tile + some.shape[1]]
        half_scores = lax.dot_general(
            parts_ref[...],
            jnp.concatenate([items, items], 1),
            (((1,), (1,)), ((), ())),
            preferred_element_type=jnp.float32,
        )
        residual = 0.5 * jnp.tanh(half_scores) + (0.5 - some.astype(jnp.float32))
        upper.append(residual.astype(jnp.bfloat16))
        lower.append((residual - upper[-1].astype(jnp.float32)).astype(jnp.bfloat16))
    grad_ref[...] += jnp.dot(
        jnp.concatenate(upper + lower, 1),
        jnp.concatenate([block, block], 0),
        preferred_element_type=jnp.float32,
    )


def add_tiles(grad_ref, parts_ref, tiles, live, labels_at):
    tile = tiles.shape[0] // CHUNK
    fours = (live + 1) // 4

    @pl.when(live % 4 == 3)
    def _():
        blank = pl.multiple_of(live * tile, tile)
        tiles[pl.ds(blank, tile), :] = jnp.zeros((tile, tiles.shape[1]), tiles.dtype)

    def add(count, index, carry):
        start = index * count
        block = tiles[pl.ds(pl.multiple_of(start * tile, tile), count * tile), :]
        add_block(grad_ref, parts_ref, block, [labels_at(start + at) for at in range(count)])
        return carry

    lax.fori_loop(0, fours, functools.partial(add, 4), 0)
    pl.when(live - 4 * fours == 2)(lambda: add(2, 2 * fours, None))
    pl.when(live - 4 * fours == 1)(lambda: add(1, 4 * fours, None))


def store_square(grad_ref, square_ref):
    gradient = grad_ref[...]
    square = jnp.sum(gradient * gradient, axis=0, keepdims=True)
    square = sum(square[:, at : at + 128] for at in range(0, square.shape[1], 128))
    square_ref[...] = jnp.broadcast_to(square, square_ref.shape)


def core_and_position(loop_size):
    me = lax.axis_index("loop")
    core, row, outer = me % 2, me // 2 % 2, me // 4
    return core, jnp.where(row == 0, outer, loop_size // 2 - 1 - outer)


def pack_kernel(loop_size, *refs):
    tile = refs[0].shape[0]
    sources = refs[:-1] if loop_size is None else (refs[0], refs[2])
    packed_ref = refs[-1] if loop_size is None else refs[-2]
    if loop_size is not None:
        core, position = core_and_position(loop_size)
        for at in range(2):

            @pl.when((core + position) % 2 == at)
            def _():
                refs[-1][...] = refs[1 + at][...]

    for at, ref in enumerate(sources):
        packed_ref[at * tile : (at + 1) * tile, :] = ref[...]


def pack(arrays, loop_size=None):
    tile, width = arrays[0].shape
    shapes = [(len(arrays) * tile, width)] if loop_size is None else [(2 * tile, width), (tile, width)]
    return pl.pallas_call(
        functools.partial(pack_kernel, loop_size),
        out_shape=[jax.ShapeDtypeStruct(shape, arrays[0].dtype) for shape in shapes],
        in_specs=[pl.BlockSpec(memory_space=pltpu.VMEM)] * len(arrays),
        out_specs=[pl.BlockSpec(memory_space=pltpu.VMEM)] * len(shapes),
        compiler_params=pltpu.CompilerParams(vmem_limit_bytes=16 * 1024 * 1024),
        cost_estimate=pl.CostEstimate(
            flops=2**34 if loop_size is None else 2**32,
            bytes_accessed=4 * len(arrays) * tile * width,
            transcendentals=0,
        ),
        name="pack",
    )(*arrays)


def pieces_kernel(places, count, packed, first, last, table_ref, given_ref, labels_ref, *rest):
    rest = list(rest)
    arrays = [rest.pop(0) for _ in range(count)]
    if not first:
        rest.pop(0)
    grad_ref = rest.pop(0)
    parts_ref = rest.pop(0) if first else given_ref
    pack_ref = rest.pop(0) if packed else None
    square_ref = rest.pop(0) if last else None
    tiles, slots = rest
    tile = tiles.shape[0] // CHUNK
    for at, index in enumerate(packed):
        pack_ref[at * tile : (at + 1) * tile, :] = arrays[index][...]
    if first:
        parts_ref[...] = halves(0.5 * given_ref[...])
        grad_ref[...] = jnp.zeros_like(grad_ref)
    table = table_ref[...]
    entries = [table[0, at] for at, _, _ in places]

    def labels_of(slot):
        return labels_ref[:, pl.ds(pl.multiple_of(slot * tile, tile), tile)]

    live = jnp.int32(0)
    for found, (_, index, row) in zip(entries, places):

        @pl.when(found >= 0)
        def _():
            into = pl.ds(pl.multiple_of(live * tile, tile), tile)
            tiles[into, :] = arrays[index][row * tile : (row + 1) * tile, :]
            slots[live] = found

        live = live + (found >= 0).astype(jnp.int32)
    slots[live] = 0
    add_tiles(grad_ref, parts_ref, tiles, live, lambda position: labels_of(slots[position]))
    if last:
        store_square(grad_ref, square_ref)


def add_pieces(held, packed, loop_size, table, given, labels, before, last):
    first = before is None
    width = given.shape[1] // (1 if first else 2)
    rows = given.shape[0]
    arrays = [array for array, _ in held]
    tile = labels.shape[1] // CHUNK
    places = [(at, index, row) for index, (_, entries) in enumerate(held) for row, at in enumerate(entries)]
    most = min(len(places), CHUNK)
    out_shape = [jax.ShapeDtypeStruct((rows, width), jnp.float32)]
    if first:
        out_shape.append(jax.ShapeDtypeStruct((rows, 2 * width), jnp.bfloat16))
    if packed:
        out_shape.append(jax.ShapeDtypeStruct((len(packed) * tile, width), jnp.bfloat16))
    if last:
        out_shape.append(jax.ShapeDtypeStruct((loop_size, 128), jnp.float32))
    extra = [] if first else [before]
    return pl.pallas_call(
        functools.partial(pieces_kernel, places, len(arrays), packed, first, last),
        out_shape=out_shape,
        in_specs=[pl.BlockSpec(memory_space=pltpu.VMEM)] * (3 + len(arrays) + len(extra)),
        out_specs=[pl.BlockSpec(memory_space=pltpu.VMEM)] * len(out_shape),
        input_output_aliases={} if first else {3 + len(arrays): 0},
        scratch_shapes=[
            pltpu.VMEM((CHUNK * tile, width), jnp.bfloat16),
            pltpu.SMEM((CHUNK + 1,), jnp.int32),
        ],
        compiler_params=pltpu.CompilerParams(vmem_limit_bytes=24 * 1024 * 1024),
        cost_estimate=pl.CostEstimate(
            flops=(8 if first else 128) * rows * width * most * tile,
            bytes_accessed=8 * rows * width,
            transcendentals=rows * most * tile,
        ),
        name="add_pieces",
    )(table, given, labels, *arrays, *extra)


def ring_gradient(users, items, lists, labels):
    loop_size = lax.axis_size("loop")
    far = loop_size // 4
    origins = [(hops, 0) for hops in range(1 - far, far + 1)]
    origins += [(-hops, 1) for hops, _ in origins]
    table = slot_table(loop_size, origins, *lists)
    where = {origin: at for at, origin in enumerate(origins)}

    def held(hops, array):
        return array, [where[hops, 0]]

    def other(arrays, hops):
        return to_other_core(arrays, loop_size), [where[-hop, 1] for hop in hops]

    up = to_next(items, 1, loop_size)
    down = to_next(items, -1, loop_size)
    up, table = lax.optimization_barrier((up, table))
    first = [held(0, items), held(1, up), held(-1, down)]
    second = [held(2, to_next(up, 1, loop_size)), held(-2, to_next(down, -1, loop_size))]
    first.append(other(up, [1]))
    packed, opposite = pack([items, up, down], loop_size)
    opposite = across(opposite, loop_size)
    gradient, parts = add_pieces(first, [], loop_size, table, users, labels, None, False)
    first = other(packed, [0, -1])
    third = [held(3, to_next(second[0][0], 1, loop_size)), held(-3, to_next(second[1][0], -1, loop_size))]
    gradient, packed = add_pieces(second, [0, 1], loop_size, table, parts, labels, gradient, False)
    second = other(packed, [2, -2])
    third.append(held(4, opposite))
    arrived, gradient = lax.optimization_barrier(([array for array, _ in third], gradient))
    final = other(pack(arrived)[0], [3, -3, 4])
    (gradient,) = add_pieces(
        third + [first, second], [], loop_size, table, parts, labels, gradient, False
    )
    return *add_pieces([final], [], loop_size, table, parts, labels, gradient, True), users


def chunks_kernel(
    list_ref, count_ref, users_ref, labels_ref, items_ref, grad_ref, square_ref, tiles, parts_ref, sems
):
    tile = tiles.shape[0] // CHUNK
    step = pl.program_id(0)
    live = jnp.clip(count_ref[0] - step * CHUNK, 0, CHUNK)

    @pl.when(step == 0)
    def _():
        parts_ref[...] = halves(0.5 * users_ref[...])
        grad_ref[...] = jnp.zeros_like(grad_ref)

    def move(slot):
        start = pl.multiple_of(list_ref[0, step * CHUNK + slot] * tile, tile)
        return pltpu.make_async_copy(
            items_ref.at[pl.ds(start, tile), :], tiles.at[pl.ds(slot * tile, tile), :], sems.at[slot]
        )

    for slot in range(CHUNK):
        pl.when(slot < live)(lambda slot=slot: move(slot).start())
    for slot in range(CHUNK):
        pl.when(slot < live)(lambda slot=slot: move(slot).wait())

    def labels_at(position):
        return labels_ref[:, pl.ds(pl.multiple_of(position * tile, tile), tile)]

    add_tiles(grad_ref, parts_ref, tiles, live, labels_at)

    @pl.when(step == pl.num_programs(0) - 1)
    def _():
        store_square(grad_ref, square_ref)


def add_chunks(loop_size, items, lists, users, labels):
    rows, width = users.shape
    slots = lists[0].shape[1]
    tile = labels.shape[1] // slots
    return pl.pallas_call(
        chunks_kernel,
        grid=(slots // CHUNK,),
        out_shape=[
            jax.ShapeDtypeStruct((rows, width), jnp.float32),
            jax.ShapeDtypeStruct((loop_size, 128), jnp.float32),
        ],
        in_specs=[
            pl.BlockSpec(memory_space=pltpu.SMEM),
            pl.BlockSpec(memory_space=pltpu.SMEM),
            pl.BlockSpec((rows, width), lambda step: (0, 0)),
            pl.BlockSpec((rows, CHUNK * tile), lambda step: (0, step)),
            pl.BlockSpec(memory_space=pl.ANY),
        ],
        out_specs=[
            pl.BlockSpec((rows, width), lambda step: (0, 0)),
            pl.BlockSpec((loop_size, 128), lambda step: (0, 0)),
        ],
        scratch_shapes=[
            pltpu.VMEM((CHUNK * tile, width), jnp.bfloat16),
            pltpu.VMEM((rows, 2 * width), jnp.bfloat16),
            pltpu.SemaphoreType.DMA((CHUNK,)),
        ],
        compiler_params=pltpu.CompilerParams(vmem_limit_bytes=32 * 1024 * 1024),
        cost_estimate=pl.CostEstimate(
            flops=8 * rows * width * slots * tile,
            bytes_accessed=4 * rows * (slots * tile + 2 * width) + 2 * slots * tile * width,
            transcendentals=rows * slots * tile,
        ),
        name="add_chunks",
    )(*lists, users, labels, items)


def update_kernel(entries, users_ref, grad_ref, squares_ref, out_ref, result, sems):
    total = jnp.sum(squares_ref[...], axis=0, keepdims=True)
    total = jnp.sum(total, axis=1, keepdims=True)
    scale = 0.5 / jnp.sqrt(total / entries + 1e-06)
    rows = users_ref.shape[0] // sems.shape[0]
    copies = []
    for at in range(sems.shape[0]):
        part = pl.ds(at * rows, rows)
        result[part, :] = users_ref[part, :] - scale * grad_ref[part, :]
        copies.append(pltpu.make_async_copy(result.at[part, :], out_ref.at[part, :], sems.at[at]))
        copies[-1].start()
    for copy in copies:
        copy.wait()


def local(users, items, tile_blocks, tile_count, labels):
    loop_size = lax.axis_size("loop")
    rows, width = users.shape
    slots = tile_blocks.shape[1]
    lists = (tile_blocks, tile_count)
    if loop_size == RING and slots == CHUNK:
        gradient, square, users = ring_gradient(users, items, lists, labels)
    else:
        whole = lax.all_gather(items, "loop", axis=0, tiled=True)
        gradient, square = add_chunks(loop_size, whole, lists, users, labels)

    squares = lax.all_to_all(square, "loop", 0, 0, tiled=True)
    return pl.pallas_call(
        functools.partial(update_kernel, rows * loop_size * width),
        out_shape=jax.ShapeDtypeStruct((rows, width), jnp.float32),
        in_specs=[pl.BlockSpec(memory_space=pltpu.VMEM)] * 3,
        out_specs=pl.BlockSpec(memory_space=pl.ANY),
        scratch_shapes=[pltpu.VMEM((rows, width), jnp.float32), pltpu.SemaphoreType.DMA((8,))],
        compiler_params=pltpu.CompilerParams(vmem_limit_bytes=16 * 1024 * 1024),
        cost_estimate=pl.CostEstimate(
            flops=2 * rows * width, bytes_accessed=12 * rows * width, transcendentals=0
        ),
        name="update",
    )(users, gradient, squares)


def solution(mesh):
    in_specs = (
        P(("group", "loop"), None),
        P(("group", "loop"), None),
        P(("group", "loop"), None),
        P(("group", "loop")),
        P(("group", "loop"), None),
    )
    out_specs = P(("group", "loop"), None)
    return jax.shard_map(local, mesh=mesh, in_specs=in_specs, out_specs=out_specs, check_vma=False)
```

```python
import functools

import jax
import jax.numpy as jnp
from jax import lax
from jax.experimental import pallas as pl
from jax.experimental.pallas import tpu as pltpu
from jax.sharding import PartitionSpec as P

CHUNK = 8
RING = 16


def ring_place(loop_size):
    outer = loop_size // 4

    def device(position, core):
        position = position % (2 * outer)
        chip = 2 * position if position < outer else 2 * (2 * outer - 1 - position) + 1
        return 2 * chip + core

    return 2 * outer, device


def to_next(array, direction, loop_size):
    chips, device = ring_place(loop_size)
    pairs = [(device(at, 0), device(at + direction, 0)) for at in range(chips)]
    pairs += [(device(at, 1), device(at - direction, 1)) for at in range(chips)]
    return lax.ppermute(array, "loop", pairs)


def across(array, loop_size):
    chips, device = ring_place(loop_size)
    pairs = [
        (device(at, core), device(at + (3 if at % 2 == 0 else -3), core))
        for at in range(chips)
        for core in range(2)
    ]
    return lax.ppermute(array, "loop", pairs)


def to_other_core(array, loop_size):
    return lax.ppermute(array, "loop", [(at, at ^ 1) for at in range(loop_size)])


def halves(values):
    upper = values.astype(jnp.bfloat16)
    return jnp.concatenate([upper, (values - upper.astype(jnp.float32)).astype(jnp.bfloat16)], 1)


def table_kernel(loop_size, origins, list_ref, count_ref, table_ref):
    chips = loop_size // 2
    lane = lax.broadcasted_iota(jnp.int32, table_ref.shape, 1)
    core, position = core_and_position(loop_size)
    hops, other = jnp.zeros_like(lane), jnp.zeros_like(lane)
    for at, origin in enumerate(origins):
        hops = jnp.where(lane == at, origin[0], hops)
        other = jnp.where(lane == at, origin[1], other)
    at = (position + chips + jnp.where(core == 0, -hops, hops)) & (chips - 1)
    chip = jnp.where(at < chips // 2, 2 * at, 2 * (chips - 1 - at) + 1)
    block = 2 * chip + jnp.where(other == 1, 1 - core, core)
    found = jnp.full_like(lane, -1)
    for slot in range(list_ref.shape[1]):
        name = jnp.where(slot < count_ref[...], list_ref[:, slot : slot + 1], -1)
        found = jnp.where(name == block, slot, found)
    table_ref[...] = jnp.where(lane < len(origins), found, -1)


def slot_table(loop_size, origins, block_list, live_count):
    return pl.pallas_call(
        functools.partial(table_kernel, loop_size, origins),
        out_shape=jax.ShapeDtypeStruct((1, 128), jnp.int32),
        in_specs=[pl.BlockSpec(memory_space=pltpu.VMEM)] * 2,
        out_specs=pl.BlockSpec(memory_space=pltpu.VMEM),
        compiler_params=pltpu.CompilerParams(vmem_limit_bytes=16 * 1024 * 1024),
        cost_estimate=pl.CostEstimate(flops=2**32, bytes_accessed=1024, transcendentals=0),
        name="slot_table",
    )(block_list, live_count.reshape(1, 1))


def add_block(grad_ref, parts_ref, block, labels):
    tile = labels[0].shape[1]
    upper, lower = [], []
    for at in range(0, len(labels), 2):
        some = jnp.concatenate(labels[at : at + 2], 1)
        items = block[at * tile : at * tile + some.shape[1]]
        half_scores = lax.dot_general(
            parts_ref[...],
            jnp.concatenate([items, items], 1),
            (((1,), (1,)), ((), ())),
            preferred_element_type=jnp.float32,
        )
        residual = 0.5 * jnp.tanh(half_scores) + (0.5 - some.astype(jnp.float32))
        upper.append(residual.astype(jnp.bfloat16))
        lower.append((residual - upper[-1].astype(jnp.float32)).astype(jnp.bfloat16))
    grad_ref[...] += jnp.dot(
        jnp.concatenate(upper + lower, 1),
        jnp.concatenate([block, block], 0),
        preferred_element_type=jnp.float32,
    )


def add_tiles(grad_ref, parts_ref, tiles, live, labels_at):
    tile = tiles.shape[0] // CHUNK
    fours = (live + 1) // 4

    @pl.when(live % 4 == 3)
    def _():
        blank = pl.multiple_of(live * tile, tile)
        tiles[pl.ds(blank, tile), :] = jnp.zeros((tile, tiles.shape[1]), tiles.dtype)

    def add(count, index, carry):
        start = index * count
        block = tiles[pl.ds(pl.multiple_of(start * tile, tile), count * tile), :]
        add_block(grad_ref, parts_ref, block, [labels_at(start + at) for at in range(count)])
        return carry

    lax.fori_loop(0, fours, functools.partial(add, 4), 0)
    pl.when(live - 4 * fours == 2)(lambda: add(2, 2 * fours, None))
    pl.when(live - 4 * fours == 1)(lambda: add(1, 4 * fours, None))


def store_square(grad_ref, square_ref):
    gradient = grad_ref[...]
    square = jnp.sum(gradient * gradient, axis=0, keepdims=True)
    square = sum(square[:, at : at + 128] for at in range(0, square.shape[1], 128))
    square_ref[...] = jnp.broadcast_to(square, square_ref.shape)


def core_and_position(loop_size):
    me = lax.axis_index("loop")
    core, row, outer = me % 2, me // 2 % 2, me // 4
    return core, jnp.where(row == 0, outer, loop_size // 2 - 1 - outer)


def pack_kernel(loop_size, *refs):
    tile = refs[0].shape[0]
    sources = refs[:-1] if loop_size is None else (refs[0], refs[2])
    packed_ref = refs[-1] if loop_size is None else refs[-2]
    if loop_size is not None:
        core, position = core_and_position(loop_size)
        for at in range(2):

            @pl.when((core + position) % 2 == at)
            def _():
                refs[-1][...] = refs[1 + at][...]

    for at, ref in enumerate(sources):
        packed_ref[at * tile : (at + 1) * tile, :] = ref[...]


def pack(arrays, loop_size=None):
    tile, width = arrays[0].shape
    shapes = [(len(arrays) * tile, width)] if loop_size is None else [(2 * tile, width), (tile, width)]
    return pl.pallas_call(
        functools.partial(pack_kernel, loop_size),
        out_shape=[jax.ShapeDtypeStruct(shape, arrays[0].dtype) for shape in shapes],
        in_specs=[pl.BlockSpec(memory_space=pltpu.VMEM)] * len(arrays),
        out_specs=[pl.BlockSpec(memory_space=pltpu.VMEM)] * len(shapes),
        compiler_params=pltpu.CompilerParams(vmem_limit_bytes=16 * 1024 * 1024),
        cost_estimate=pl.CostEstimate(
            flops=2**34 if loop_size is None else 2**32,
            bytes_accessed=4 * len(arrays) * tile * width,
            transcendentals=0,
        ),
        name="pack",
    )(*arrays)


def pieces_kernel(places, count, packed, first, last, table_ref, given_ref, labels_ref, *rest):
    rest = list(rest)
    arrays = [rest.pop(0) for _ in range(count)]
    if not first:
        rest.pop(0)
    grad_ref = rest.pop(0)
    parts_ref = rest.pop(0) if first else given_ref
    pack_ref = rest.pop(0) if packed else None
    square_ref = rest.pop(0) if last else None
    tiles, slots = rest
    tile = tiles.shape[0] // CHUNK
    for at, index in enumerate(packed):
        pack_ref[at * tile : (at + 1) * tile, :] = arrays[index][...]
    if first:
        parts_ref[...] = halves(0.5 * given_ref[...])
        grad_ref[...] = jnp.zeros_like(grad_ref)
    table = table_ref[...]
    entries = [table[0, at] for at, _, _ in places]

    def labels_of(slot):
        return labels_ref[:, pl.ds(pl.multiple_of(slot * tile, tile), tile)]

    live = jnp.int32(0)
    for found, (_, index, row) in zip(entries, places):

        @pl.when(found >= 0)
        def _():
            into = pl.ds(pl.multiple_of(live * tile, tile), tile)
            tiles[into, :] = arrays[index][row * tile : (row + 1) * tile, :]
            slots[live] = found

        live = live + (found >= 0).astype(jnp.int32)
    slots[live] = 0
    add_tiles(grad_ref, parts_ref, tiles, live, lambda position: labels_of(slots[position]))
    if last:
        store_square(grad_ref, square_ref)


def add_pieces(held, packed, loop_size, table, given, labels, before, last):
    first = before is None
    width = given.shape[1] // (1 if first else 2)
    rows = given.shape[0]
    arrays = [array for array, _ in held]
    tile = labels.shape[1] // CHUNK
    places = [(at, index, row) for index, (_, entries) in enumerate(held) for row, at in enumerate(entries)]
    most = min(len(places), CHUNK)
    out_shape = [jax.ShapeDtypeStruct((rows, width), jnp.float32)]
    if first:
        out_shape.append(jax.ShapeDtypeStruct((rows, 2 * width), jnp.bfloat16))
    if packed:
        out_shape.append(jax.ShapeDtypeStruct((len(packed) * tile, width), jnp.bfloat16))
    if last:
        out_shape.append(jax.ShapeDtypeStruct((loop_size, 128), jnp.float32))
    extra = [] if first else [before]
    return pl.pallas_call(
        functools.partial(pieces_kernel, places, len(arrays), packed, first, last),
        out_shape=out_shape,
        in_specs=[pl.BlockSpec(memory_space=pltpu.VMEM)] * (3 + len(arrays) + len(extra)),
        out_specs=[pl.BlockSpec(memory_space=pltpu.VMEM)] * len(out_shape),
        input_output_aliases={} if first else {3 + len(arrays): 0},
        scratch_shapes=[
            pltpu.VMEM((CHUNK * tile, width), jnp.bfloat16),
            pltpu.SMEM((CHUNK + 1,), jnp.int32),
        ],
        compiler_params=pltpu.CompilerParams(vmem_limit_bytes=24 * 1024 * 1024),
        cost_estimate=pl.CostEstimate(
            flops=(8 if first else 128) * rows * width * most * tile,
            bytes_accessed=8 * rows * width,
            transcendentals=rows * most * tile,
        ),
        name="add_pieces",
    )(table, given, labels, *arrays, *extra)


def ring_gradient(users, items, lists, labels):
    loop_size = lax.axis_size("loop")
    far = loop_size // 4
    origins = [(hops, 0) for hops in range(1 - far, far + 1)]
    origins += [(-hops, 1) for hops, _ in origins]
    table = slot_table(loop_size, origins, *lists)
    where = {origin: at for at, origin in enumerate(origins)}

    def held(hops, array):
        return array, [where[hops, 0]]

    def other(arrays, hops):
        return to_other_core(arrays, loop_size), [where[-hop, 1] for hop in hops]

    up = to_next(items, 1, loop_size)
    down = to_next(items, -1, loop_size)
    up, table = lax.optimization_barrier((up, table))
    first = [held(0, items), held(1, up), held(-1, down)]
    second = [held(2, to_next(up, 1, loop_size)), held(-2, to_next(down, -1, loop_size))]
    first.append(other(up, [1]))
    packed, opposite = pack([items, up, down], loop_size)
    opposite = across(opposite, loop_size)
    gradient, parts = add_pieces(first, [], loop_size, table, users, labels, None, False)
    first = other(packed, [0, -1])
    third = [held(3, to_next(second[0][0], 1, loop_size)), held(-3, to_next(second[1][0], -1, loop_size))]
    gradient, packed = add_pieces(second, [0, 1], loop_size, table, parts, labels, gradient, False)
    second = other(packed, [2, -2])
    third.append(held(4, opposite))
    arrived, gradient = lax.optimization_barrier(([array for array, _ in third], gradient))
    final = other(pack(arrived)[0], [3, -3, 4])
    (gradient,) = add_pieces(
        third + [first, second], [], loop_size, table, parts, labels, gradient, False
    )
    return *add_pieces([final], [], loop_size, table, parts, labels, gradient, True), users


def chunks_kernel(
    list_ref, count_ref, users_ref, labels_ref, items_ref, grad_ref, square_ref, tiles, parts_ref, sems
):
    tile = tiles.shape[0] // CHUNK
    step = pl.program_id(0)
    live = jnp.clip(count_ref[0] - step * CHUNK, 0, CHUNK)

    @pl.when(step == 0)
    def _():
        parts_ref[...] = halves(0.5 * users_ref[...])
        grad_ref[...] = jnp.zeros_like(grad_ref)

    def move(slot):
        start = pl.multiple_of(list_ref[0, step * CHUNK + slot] * tile, tile)
        return pltpu.make_async_copy(
            items_ref.at[pl.ds(start, tile), :], tiles.at[pl.ds(slot * tile, tile), :], sems.at[slot]
        )

    for slot in range(CHUNK):
        pl.when(slot < live)(lambda slot=slot: move(slot).start())
    for slot in range(CHUNK):
        pl.when(slot < live)(lambda slot=slot: move(slot).wait())

    def labels_at(position):
        return labels_ref[:, pl.ds(pl.multiple_of(position * tile, tile), tile)]

    add_tiles(grad_ref, parts_ref, tiles, live, labels_at)

    @pl.when(step == pl.num_programs(0) - 1)
    def _():
        store_square(grad_ref, square_ref)


def add_chunks(loop_size, items, lists, users, labels):
    rows, width = users.shape
    slots = lists[0].shape[1]
    tile = labels.shape[1] // slots
    return pl.pallas_call(
        chunks_kernel,
        grid=(slots // CHUNK,),
        out_shape=[
            jax.ShapeDtypeStruct((rows, width), jnp.float32),
            jax.ShapeDtypeStruct((loop_size, 128), jnp.float32),
        ],
        in_specs=[
            pl.BlockSpec(memory_space=pltpu.SMEM),
            pl.BlockSpec(memory_space=pltpu.SMEM),
            pl.BlockSpec((rows, width), lambda step: (0, 0)),
            pl.BlockSpec((rows, CHUNK * tile), lambda step: (0, step)),
            pl.BlockSpec(memory_space=pl.ANY),
        ],
        out_specs=[
            pl.BlockSpec((rows, width), lambda step: (0, 0)),
            pl.BlockSpec((loop_size, 128), lambda step: (0, 0)),
        ],
        scratch_shapes=[
            pltpu.VMEM((CHUNK * tile, width), jnp.bfloat16),
            pltpu.VMEM((rows, 2 * width), jnp.bfloat16),
            pltpu.SemaphoreType.DMA((CHUNK,)),
        ],
        compiler_params=pltpu.CompilerParams(vmem_limit_bytes=32 * 1024 * 1024),
        cost_estimate=pl.CostEstimate(
            flops=8 * rows * width * slots * tile,
            bytes_accessed=4 * rows * (slots * tile + 2 * width) + 2 * slots * tile * width,
            transcendentals=rows * slots * tile,
        ),
        name="add_chunks",
    )(*lists, users, labels, items)


def update_kernel(entries, users_ref, grad_ref, squares_ref, out_ref, result, sems):
    total = jnp.sum(squares_ref[...], axis=0, keepdims=True)
    total = jnp.sum(total, axis=1, keepdims=True)
    scale = 0.5 / jnp.sqrt(total / entries + 1e-06)
    rows = users_ref.shape[0] // sems.shape[0]
    copies = []
    for at in range(sems.shape[0]):
        part = pl.ds(at * rows, rows)
        result[part, :] = users_ref[part, :] - scale * grad_ref[part, :]
        copies.append(pltpu.make_async_copy(result.at[part, :], out_ref.at[part, :], sems.at[at]))
        copies[-1].start()
    for copy in copies:
        copy.wait()


def local(users, items, tile_blocks, tile_count, labels):
    loop_size = lax.axis_size("loop")
    rows, width = users.shape
    slots = tile_blocks.shape[1]
    lists = (tile_blocks, tile_count)
    if loop_size == RING and slots == CHUNK:
        gradient, square, users = ring_gradient(users, items, lists, labels)
    else:
        whole = lax.all_gather(items, "loop", axis=0, tiled=True)
        gradient, square = add_chunks(loop_size, whole, lists, users, labels)

    squares = lax.all_to_all(square, "loop", 0, 0, tiled=True)
    return pl.pallas_call(
        functools.partial(update_kernel, rows * loop_size * width),
        out_shape=jax.ShapeDtypeStruct((rows, width), jnp.float32),
        in_specs=[pl.BlockSpec(memory_space=pltpu.VMEM)] * 3,
        out_specs=pl.BlockSpec(memory_space=pl.ANY),
        scratch_shapes=[pltpu.VMEM((rows, width), jnp.float32), pltpu.SemaphoreType.DMA((2,))],
        compiler_params=pltpu.CompilerParams(vmem_limit_bytes=16 * 1024 * 1024),
        cost_estimate=pl.CostEstimate(
            flops=2 * rows * width, bytes_accessed=12 * rows * width, transcendentals=0
        ),
        name="update",
    )(users, gradient, squares)


def solution(mesh):
    in_specs = (
        P(("group", "loop"), None),
        P(("group", "loop"), None),
        P(("group", "loop"), None),
        P(("group", "loop")),
        P(("group", "loop"), None),
    )
    out_specs = P(("group", "loop"), None)
    return jax.shard_map(local, mesh=mesh, in_specs=in_specs, out_specs=out_specs, check_vma=False)
```
